32 devices in a mesh: coil: 4 (over x, core), tile: 8 (over z, y).
Axes of the slice: x: 2, y: 2, z: 4, core: 2. Of those that a mesh axis runs over, the one named last changes fastest.
Arguments:
- image_p: float32 [2, 128, 128, 128], P(None, 'tile', 'coil'), may hold values from -6 to 6
- image_x: float32 [2, 128, 128, 128], P(None, 'tile', 'coil'), may hold values from -6 to 6
- image_r: float32 [2, 128, 128, 128], P(None, 'tile', 'coil'), may hold values from -6 to 6
- sensitivity: float32 [4, 2, 128, 128, 128], P('coil', None, 'tile'), may hold values from -5 to 5
- kb_weights: float32 [256, 3, 4, 128], P('tile'), may hold values from -3 to 3
- block_owner: int32 [256], P('tile'), may hold values from 0 to 7, as said below
- owner_list: int32 [3, 8, 8, 16], P(None, 'tile'), may hold values from -1 to 124, as said below
Outputs:
- next_x: float32 [2, 128, 128, 128], P(None, 'tile', 'coil')
- next_r: float32 [2, 128, 128, 128], P(None, 'tile', 'coil')
- next_p: float32 [2, 128, 128, 128], P(None, 'tile', 'coil')
The draws below stay inside these ranges and needn't reach their ends.
Inputs may be any that keep to these rules, and one draw needn't show every extreme that they name: `block_owner`: of the 32 blocks handled by one index of tile (blocks h * 32 to h * 32 + 31), at most 16 have any one owner; in every draw each such device has exactly 16 blocks of one common owner. owner_list[:, o, h, k] holds the offsets (kx, ky within tile o, kz) of the block of rank k among the blocks of device h whose owner is o, in the order of their slots; all three are -1 where there is no such block. Offsets place the whole box inside the grid and inside tile o.
All inputs are finite; a program needn't handle non-finite values.
Results may differ from the reference program's by a relative error of at most 0.0002.
Values sent between devices are 32-bit elements; how exact they have to be, the bound alone decides.
No kernel may reach another device: no remote copies, remote signals or barrier semaphores. Data moves between devices by JAX's collectives and lax.ppermute only.
A program may use at most 256 MiB of HBM per device.

```python
import jax
import jax.numpy as jnp
from jax import lax

GRID = 128
COILS = 4
BOX = 4
BSAMP = 128
SLOTS = 32
BLOCKS = 256
CAP = 16
N_TILE = 8


def routing(key):
    key = jax.random.fold_in(key, 11)
    key_hot, key_shift, key_perm, key_x, key_y, key_z = jax.random.split(key, 6)
    hot = N_TILE // 4 + jax.random.randint(key_hot, (), 0, N_TILE // 2)
    index = jnp.arange(SLOTS, dtype=jnp.int32)
    shifts = jax.random.randint(key_shift, (N_TILE,), 0, N_TILE)
    spread = (hot + 1 + (index[None, :] + shifts[:, None]) % (N_TILE - 1)) % N_TILE
    base = jnp.where(index[None, :] < CAP, hot, spread).astype(jnp.int32)
    perms = jax.vmap(lambda k: jax.random.permutation(k, SLOTS))(jax.random.split(key_perm, N_TILE))
    owners = jnp.take_along_axis(base, perms, axis=1).astype(jnp.int32)
    onehot = (owners[:, :, None] == jnp.arange(N_TILE, dtype=jnp.int32)[None, None, :]).astype(jnp.int32)
    ranks = jnp.sum((jnp.cumsum(onehot, axis=1) - onehot) * onehot, axis=2)
    span = GRID - BOX + 1
    inner = GRID // N_TILE - BOX + 1
    off_x = jax.random.randint(key_x, (N_TILE, SLOTS), 0, span)
    off_y = jax.random.randint(key_y, (N_TILE, SLOTS), 0, inner)
    off_z = jax.random.randint(key_z, (N_TILE, SLOTS), 0, span)
    off_x = off_x.at[:, 0].set(GRID - BOX).at[:, 1].set(0)
    off_y = off_y.at[:, 0].set(GRID // N_TILE - BOX).at[:, 1].set(0)
    off_z = off_z.at[:, 0].set(GRID - BOX).at[:, 1].set(0)
    offsets = jnp.stack([off_x, off_y, off_z]).astype(jnp.int32)
    helpers = jnp.broadcast_to(jnp.arange(N_TILE, dtype=jnp.int32)[:, None], owners.shape)
    lists = jnp.full((3, N_TILE, N_TILE, CAP), -1, jnp.int32)
    lists = lists.at[:, owners, helpers, ranks].set(offsets)
    return (owners.reshape(-1), lists)


def draw_block_owner(key, part):
    return routing(key)[0]


def draw_owner_list(key, part):
    return routing(key)[1]


def block_levels(stream_key, shape, pieces, smallest, high):
    loudness = 1.0
    for axis_at, shards_of in pieces:
        draws = jax.random.uniform(jax.random.fold_in(jax.random.fold_in(stream_key, 6), axis_at), (shards_of,), jnp.float32, smallest / len(pieces), high / len(pieces))
        loudness = loudness * jnp.repeat(jnp.exp(draws), shape[axis_at] // shards_of).reshape((-1,) + (1,) * (len(shape) - 1 - axis_at))
    return loudness


def scatter_about(rng, dims, scale, limit, pieces=(), held_as=jnp.bfloat16):
    values = jax.random.normal(rng, dims, jnp.float32) * scale
    if len(pieces) > 0:
        values = block_levels(rng, dims, pieces, -0.22, 0.18) * values
    return jnp.clip(values, min=-limit, max=limit).astype(held_as)


def setup_inputs(seed: int = 0) -> dict:
    splits = jax.random.split(jax.random.key(seed), 8)
    return {
        "image_p": scatter_about(splits[0], (2, GRID, GRID, GRID), 1.0, 6.0, ((1, 8), (2, 4)), jnp.float32),
        "image_x": scatter_about(splits[1], (2, GRID, GRID, GRID), 1.0, 6.0, ((1, 8), (2, 4)), jnp.float32),
        "image_r": scatter_about(splits[2], (2, GRID, GRID, GRID), 1.0, 6.0, ((1, 8), (2, 4)), jnp.float32),
        "sensitivity": scatter_about(splits[3], (COILS, 2, GRID, GRID, GRID), 0.35, 5.0, ((0, 4), (2, 8)), jnp.float32),
        "kb_weights": scatter_about(splits[4], (BLOCKS, 3, BOX, BSAMP), BOX ** -0.5, 3.0, ((0, 8),), jnp.float32),
        "block_owner": draw_block_owner(jax.random.fold_in(splits[7], 71), 0),
        "owner_list": draw_owner_list(jax.random.fold_in(splits[7], 71), 0),
    }


def regrid(boxes, weights):
    count = boxes.shape[0]
    width = weights.shape[2]
    cube = boxes.reshape(count, 2, width, width, width)
    w_x = weights[:, 0]
    w_y = weights[:, 1]
    w_z = weights[:, 2]
    values = jnp.einsum("ncijk,nis,njs,nks->ncs", cube, w_x, w_y, w_z, precision=lax.Precision.HIGHEST)
    back = jnp.einsum("ncs,nis,njs,nks->ncijk", values, w_x, w_y, w_z, precision=lax.Precision.HIGHEST)
    return back.reshape(count, -1)


def regrid_groups(boxes, weights, group):
    count = boxes.shape[0]
    grouped = (boxes.reshape(count // group, group, boxes.shape[1]), weights.reshape((count // group, group) + weights.shape[1:]))
    done = lax.map(lambda pair: regrid(pair[0], pair[1]), grouped)
    return done.reshape(count, -1)


def cut_box(field, off_x, off_y, off_z, width):
    start = (jnp.zeros((), jnp.int32), off_x, off_y, off_z)
    return lax.dynamic_slice(field, start, (2, width, width, width))


def place_boxes(grid, boxes, off_x, off_y, off_z, width):
    count = boxes.shape[0]
    cells = jnp.arange(width, dtype=jnp.int32)
    index_x = off_x[:, None, None, None] + cells[None, :, None, None]
    index_y = off_y[:, None, None, None] + cells[None, None, :, None]
    index_z = off_z[:, None, None, None] + cells[None, None, None, :]
    values = jnp.transpose(boxes.reshape(count, 2, width, width, width), (1, 0, 2, 3, 4))
    return grid.at[:, index_x, index_y, index_z].add(values)


def ranks_of(owners, ntile):
    onehot = (owners[:, :, None] == jnp.arange(ntile, dtype=jnp.int32)[None, None, :]).astype(jnp.int32)
    return jnp.sum((jnp.cumsum(onehot, axis=1) - onehot) * onehot, axis=2)


def reference(image_p, image_x, image_r, sensitivity, kb_weights, block_owner, owner_list):
    width = BOX
    owners = block_owner.reshape(N_TILE, SLOTS)
    ranks = ranks_of(owners, N_TILE)
    helpers = jnp.broadcast_to(jnp.arange(N_TILE, dtype=jnp.int32)[:, None], owners.shape)
    offsets = owner_list[:, owners, helpers, ranks].reshape(3, -1).astype(jnp.int32)
    off_x = offsets[0]
    off_y = offsets[1] + block_owner.astype(jnp.int32) * (GRID // N_TILE)
    off_z = offsets[2]
    direction = lax.complex(image_p[0], image_p[1])

    def one_coil(total, sens):
        smap = lax.complex(sens[0], sens[1])
        kspace = jnp.fft.fftn(smap * direction, norm="ortho")
        kstack = jnp.stack([jnp.real(kspace), jnp.imag(kspace)])
        boxes = jax.vmap(cut_box, in_axes=(None, 0, 0, 0, None))(kstack, off_x, off_y, off_z, width)
        boxes = boxes.reshape(boxes.shape[0], -1)
        done = regrid_groups(boxes, kb_weights, SLOTS)
        gridded = place_boxes(jnp.zeros_like(kstack), done, off_x, off_y, off_z, width)
        image = jnp.fft.ifftn(lax.complex(gridded[0], gridded[1]), norm="ortho")
        back = jnp.conj(smap) * image
        return total + jnp.stack([jnp.real(back), jnp.imag(back)]), None

    normal, unused = lax.scan(one_coil, jnp.zeros_like(image_p), sensitivity)
    norm_now = jnp.sum(image_r * image_r)
    alpha = norm_now / jnp.sum(image_p * normal)
    next_x = image_x + alpha * image_p
    next_r = image_r - alpha * normal
    norm_next = jnp.sum(next_r * next_r)
    next_p = next_r + (norm_next / norm_now) * image_p
    return next_x, next_r, next_p
```

```python
import functools
import math

import jax
import jax.numpy as jnp
import ml_dtypes
import numpy as np
from jax import lax
from jax.experimental import pallas as pl
from jax.experimental.pallas import tpu as pltpu
from jax.sharding import PartitionSpec as P

LANES = 128
VMEM = 56 * 1024 * 1024


def halves(values):
    high = values.astype(jnp.bfloat16)
    low = (values - high.astype(jnp.float32)).astype(jnp.bfloat16)
    return high, low


def dot_bf16(left, right, dims):
    return lax.dot_general(left, right, (dims, ((), ())), preferred_element_type=jnp.float32)


def dot_left(table, values, dims=((1,), (0,))):
    high, low = halves(values)
    return (
        dot_bf16(table[0], high, dims)
        + dot_bf16(table[0], low, dims)
        + dot_bf16(table[1], high, dims)
    )


def dot_right(values, table, dims=((1,), (0,))):
    high, low = halves(values)
    return (
        dot_bf16(high, table[0], dims)
        + dot_bf16(low, table[0], dims)
        + dot_bf16(high, table[1], dims)
    )


def fourier_tables(length):
    cells = np.arange(length)
    angle = 2.0 * math.pi / length * (cells[:, None] * cells[None, :] % length)
    cos_t = np.cos(angle) / math.sqrt(length)
    sin_t = np.sin(angle) / math.sqrt(length)
    found = []
    for sign in (1.0, -1.0):
        whole = np.block([[cos_t, -sign * sin_t], [sign * sin_t, cos_t]])
        high = whole.astype(ml_dtypes.bfloat16)
        low = (whole - high.astype(np.float64)).astype(ml_dtypes.bfloat16)
        found += [jnp.asarray(high), jnp.asarray(low)]
    return found


def window_masks(first, chunk, rows, planes):
    lane = lax.broadcasted_iota(jnp.int32, (rows, LANES), 1)
    past = lane // planes % chunk - first
    here = jnp.logical_and(past >= 0, past < 4)
    after = jnp.logical_and(past + chunk >= 0, past + chunk < 4)
    return here, after


def forward_kernel(
    info, starts, *refs, length, planes, chunk, pieces, slots, handlers, batch
):
    p_refs = refs[:pieces]
    s_ref, a_hi, a_lo, b_hi, b_lo, cos_ref, sin_ref, x_hi, x_lo = refs[pieces : pieces + 9]
    out_ref = refs[pieces + 9]
    direction, ybuf, kbuf, gbuf = refs[pieces + 10 :]
    step = pl.program_id(0)
    rows = length * planes
    part = length // pieces
    left = (b_hi[...], b_lo[...])
    for pair in range(batch // 2):
        columns = []
        for inner in range(2):
            at = pair * 2 + inner
            for piece in range(pieces):
                to = pl.ds(pl.multiple_of(starts[piece], part), part)
                direction[0, to, :] = p_refs[piece][0, at]
                direction[1, to, :] = p_refs[piece][1, at]
            s_re = s_ref[0, at]
            s_im = s_ref[1, at]
            p_re = direction[0]
            p_im = direction[1]
            columns.append(
                jnp.concatenate([s_re * p_re - s_im * p_im, s_re * p_im + s_im * p_re], axis=0)
            )
        done = dot_left(left, jnp.concatenate(columns, axis=1))
        for inner in range(2):
            plane = step * batch + pair * 2 + inner
            for ri in range(2):
                ybuf[pl.ds(ri * rows + plane, length, stride=planes), :] = done[
                    ri * length : (ri + 1) * length, inner * LANES : (inner + 1) * LANES
                ]

    @pl.when(step == pl.num_programs(0) - 1)
    def _():
        right = (a_hi[...], a_lo[...])

        def along_z(at, carry):
            base = pl.multiple_of(at * 256, 256)
            both = jnp.concatenate(
                [ybuf[pl.ds(base, 256), :], ybuf[pl.ds(rows + base, 256), :]], axis=1
            )
            done = dot_right(both, right)
            for inner in range(4):
                band = done[inner * 64 : (inner + 1) * 64]
                tile = jnp.concatenate([band[:, :length], band[:, length:]], axis=0)
                to = pl.multiple_of((at * 4 + inner) * length, length)
                kbuf[pl.ds(to, length), :] = tile.T
            return carry

        lax.fori_loop(0, rows // 256, along_z, 0)

        def cut(group, carry):
            for inner in range(8):
                block = group * 8 + inner
                here, after = window_masks(info[2, block], chunk, 4, planes)
                first = kbuf[pl.ds(info[0, block], 4), :]
                second = kbuf[pl.ds(info[1, block], 4), :]
                cells = jnp.where(here, first, jnp.where(after, second, 0.0))
                to = block // slots * (4 * slots) + block % slots
                gbuf[pl.ds(to, 4, stride=slots), :] = cells
            return carry

        lax.fori_loop(0, handlers * slots // 8, cut, 0)
        table = (x_hi[...], x_lo[...])

        def along_x(handler, carry):
            rows_at = pl.ds(pl.multiple_of(handler * slots, slots), slots)
            cos_b = jnp.concatenate([cos_ref[rows_at, :]] * 4, axis=0)
            sin_b = jnp.concatenate([sin_ref[rows_at, :]] * 4, axis=0)
            cells = gbuf[pl.ds(pl.multiple_of(handler * LANES, LANES), LANES), :]
            turned = cells * cos_b + pltpu.roll(cells, LANES // 2, 1) * sin_b
            out_ref[handler] = dot_left(table, turned, ((1,), (1,)))
            return carry

        lax.fori_loop(0, handlers, along_x, 0)


def forward(info, starts, p_pieces, smap, tables, phases, shift, slots):
    planes, length = smap.shape[1], smap.shape[2]
    pieces = len(p_pieces)
    part = length // pieces
    batch = min(planes, 4)
    chunk = LANES // (2 * planes)
    handlers = info.shape[1] // slots
    rows = length * planes
    whole = lambda *shape: pl.BlockSpec(shape, lambda s: (0,) * len(shape))
    kernel = functools.partial(
        forward_kernel, length=length, planes=planes, chunk=chunk, pieces=pieces,
        slots=slots, handlers=handlers, batch=batch,
    )
    return pl.pallas_call(
        kernel,
        grid=(planes // batch,),
        in_specs=[pl.BlockSpec(memory_space=pltpu.SMEM)] * 2
        + [pl.BlockSpec((2, batch, part, length), lambda s: (0, s, 0, 0))] * pieces
        + [pl.BlockSpec((2, batch, length, length), lambda s: (0, s, 0, 0))]
        + [whole(2 * length, 2 * length)] * 4
        + [whole(handlers * slots, LANES)] * 2
        + [whole(32, LANES)] * 2,
        out_specs=whole(handlers, 32, LANES),
        out_shape=jax.ShapeDtypeStruct((handlers, 32, LANES), jnp.float32),
        scratch_shapes=[
            pltpu.VMEM((2, length, length), jnp.float32),
            pltpu.VMEM((2 * rows, length), jnp.float32),
            pltpu.VMEM((length * (length // chunk), LANES), jnp.float32),
            pltpu.VMEM((handlers * LANES, LANES), jnp.float32),
        ],
        compiler_params=pltpu.CompilerParams(vmem_limit_bytes=VMEM),
        name="forward",
    )(info, starts, *p_pieces, smap, *tables, *phases, *shift)


def regrid_kernel(parts_ref, matrix_ref, turn_ref, out_ref, *, handlers):
    total = parts_ref[0]
    for at in range(1, handlers):
        total = total + parts_ref[at]
    turn = turn_ref[...]
    cyclic = [total[8 * q : 8 * q + 8] for q in range(4)]

    def pick(values, sign, at):
        found = values[at]
        for by in range(1, 4):
            found = jnp.where(turn == by, values[(at + sign * by) % 4], found)
        return found

    cells = [pick(cyclic, 1, e) for e in range(4)]
    along = lax.broadcasted_iota(jnp.int32, (8, LANES), 0) % 4
    sums = [jnp.zeros((8, LANES), jnp.float32) for _ in range(4)]
    for source in range(4):
        for d_z in range(4):
            value = cells[source]
            if d_z:
                value = pltpu.roll(value, LANES - 32 * d_z, 1)
            for d_x in range(4):
                moved = value
                if d_x:
                    moved = jnp.where(
                        along + d_x < 4, pltpu.roll(value, 8 - d_x, 0), pltpu.roll(value, 4 - d_x, 0)
                    )
                for e in range(4):
                    sums[e] = sums[e] + matrix_ref[((e * 4 + source) * 4 + d_z) * 4 + d_x] * moved
    done = jnp.concatenate([pick(sums, -1, q) for q in range(4)], axis=0)
    for at in range(handlers):
        out_ref[at] = done


def regrid(parts, matrix, turn):
    handlers = parts.shape[0]
    return pl.pallas_call(
        functools.partial(regrid_kernel, handlers=handlers),
        out_shape=jax.ShapeDtypeStruct(parts.shape, jnp.float32),
        in_specs=[pl.BlockSpec(memory_space=pltpu.VMEM)] * 3,
        out_specs=pl.BlockSpec(memory_space=pltpu.VMEM),
        compiler_params=pltpu.CompilerParams(vmem_limit_bytes=VMEM),
        name="regrid",
    )(parts, matrix, turn)


def inverse_kernel(
    info, starts, u_ref, s_ref, a_hi, a_lo, b_hi, b_lo, cos_ref, sin_ref, x_hi, x_lo, *refs,
    length, planes, chunk, pieces, slots, handlers, batch
):
    out_refs = refs[:pieces]
    kbuf, gbuf, ybuf, image = refs[pieces:]
    step = pl.program_id(0)
    rows = length * planes
    part = length // pieces

    @pl.when(step == 0)
    def _():
        table = (x_hi[...], x_lo[...])

        def along_x(handler, carry):
            rows_at = pl.ds(pl.multiple_of(handler * slots, slots), slots)
            cos_b = jnp.concatenate([cos_ref[rows_at, :]] * 4, axis=0)
            sin_b = jnp.concatenate([sin_ref[rows_at, :]] * 4, axis=0)
            cells = dot_right(u_ref[handler].T, table)
            turned = cells * cos_b - pltpu.roll(cells, LANES // 2, 1) * sin_b
            gbuf[pl.ds(pl.multiple_of(handler * LANES, LANES), LANES), :] = turned
            return carry

        lax.fori_loop(0, handlers, along_x, 0)
        kbuf[...] = jnp.zeros_like(kbuf)

        def place(group, carry):
            for inner in range(8):
                block = group * 8 + inner
                here, after = window_masks(info[2, block], chunk, 4, planes)
                at = block // slots * (4 * slots) + block % slots
                cells = gbuf[pl.ds(at, 4, stride=slots), :]
                first = pl.ds(info[0, block], 4)
                kbuf[first, :] = kbuf[first, :] + jnp.where(here, cells, 0.0)
                second = pl.ds(info[1, block], 4)
                kbuf[second, :] = kbuf[second, :] + jnp.where(after, cells, 0.0)
            return carry

        lax.fori_loop(0, handlers * slots // 8, place, 0)
        right = (b_hi[...], b_lo[...])

        def along_z(at, carry):
            bands = []
            for inner in range(4):
                to = pl.multiple_of((at * 4 + inner) * length, length)
                tile = kbuf[pl.ds(to, length), :].T
                bands.append(jnp.concatenate([tile[:64], tile[64:]], axis=1))
            done = dot_right(jnp.concatenate(bands, axis=0), right)
            base = pl.multiple_of(at * 256, 256)
            ybuf[pl.ds(base, 256), :] = done[:, :length]
            ybuf[pl.ds(rows + base, 256), :] = done[:, length:]
            return carry

        lax.fori_loop(0, rows // 256, along_z, 0)

    left = (a_hi[...], a_lo[...])
    for pair in range(batch // 2):
        columns = []
        for inner in range(2):
            plane = step * batch + pair * 2 + inner
            columns.append(
                jnp.concatenate(
                    [ybuf[pl.ds(ri * rows + plane, length, stride=planes), :] for ri in range(2)],
                    axis=0,
                )
            )
        image[...] = dot_left(left, jnp.concatenate(columns, axis=1))
        for inner in range(2):
            at = pair * 2 + inner
            lanes = slice(inner * LANES, (inner + 1) * LANES)
            for piece in range(pieces):
                start = pl.multiple_of(starts[piece], part)
                i_re = image[pl.ds(start, part), lanes]
                i_im = image[pl.ds(length + start, part), lanes]
                s_re = s_ref[0, at, pl.ds(start, part), :]
                s_im = s_ref[1, at, pl.ds(start, part), :]
                out_refs[piece][0, at] = s_re * i_re + s_im * i_im
                out_refs[piece][1, at] = s_re * i_im - s_im * i_re


def inverse(info, starts, u, smap, tables, phases, shift, slots, pieces):
    planes, length = smap.shape[1], smap.shape[2]
    part = length // pieces
    batch = min(planes, 4)
    chunk = LANES // (2 * planes)
    handlers = info.shape[1] // slots
    rows = length * planes
    whole = lambda *shape: pl.BlockSpec(shape, lambda s: (0,) * len(shape))
    kernel = functools.partial(
        inverse_kernel, length=length, planes=planes, chunk=chunk, pieces=pieces,
        slots=slots, handlers=handlers, batch=batch,
    )
    return pl.pallas_call(
        kernel,
        grid=(planes // batch,),
        in_specs=[pl.BlockSpec(memory_space=pltpu.SMEM)] * 2
        + [whole(handlers, 32, LANES)]
        + [pl.BlockSpec((2, batch, length, length), lambda s: (0, s, 0, 0))]
        + [whole(2 * length, 2 * length)] * 4
        + [whole(handlers * slots, LANES)] * 2
        + [whole(32, LANES)] * 2,
        out_specs=[pl.BlockSpec((2, batch, part, length), lambda s: (0, s, 0, 0))] * pieces,
        out_shape=[jax.ShapeDtypeStruct((2, planes, part, length), jnp.float32)] * pieces,
        scratch_shapes=[
            pltpu.VMEM((length * (length // chunk), LANES), jnp.float32),
            pltpu.VMEM((handlers * LANES, LANES), jnp.float32),
            pltpu.VMEM((2 * rows, length), jnp.float32),
            pltpu.VMEM((2 * length, 2 * length), jnp.float32),
        ],
        compiler_params=pltpu.CompilerParams(vmem_limit_bytes=VMEM),
        name="inverse",
    )(info, starts, u, smap, *tables, *phases, *shift)


def sums_kernel(*refs, terms):
    term_refs = refs[:terms]
    p_ref, r_ref, normal_ref, out_ref, acc = refs[terms:]
    step = pl.program_id(0)

    @pl.when(step == 0)
    def _():
        acc[...] = jnp.zeros_like(acc)

    normal = term_refs[0][...]
    for term in term_refs[1:]:
        normal = normal + term[...]
    normal_ref[...] = normal
    p = p_ref[...]
    r = r_ref[...]
    for at, product in enumerate((r * r, p * normal, r * normal, normal * normal)):
        acc[at] = acc[at] + jnp.sum(product.reshape(-1, 8, LANES), axis=0)

    @pl.when(step == pl.num_programs(0) - 1)
    def _():
        lane = lax.broadcasted_iota(jnp.int32, out_ref.shape, 1)
        found = jnp.zeros(out_ref.shape, jnp.float32)
        for at in range(4):
            found = jnp.where(lane == at, jnp.sum(acc[at]), found)
        out_ref[...] = found


def sums(terms, p, r, devices):
    shape = p.shape
    batch = min(shape[1], 4)
    spec = pl.BlockSpec((2, batch) + shape[2:], lambda s: (0, s, 0, 0))
    return pl.pallas_call(
        functools.partial(sums_kernel, terms=len(terms)),
        grid=(shape[1] // batch,),
        in_specs=[spec] * (len(terms) + 2),
        out_specs=[spec, pl.BlockSpec((devices, LANES), lambda s: (0, 0))],
        out_shape=[
            jax.ShapeDtypeStruct(shape, jnp.float32),
            jax.ShapeDtypeStruct((devices, LANES), jnp.float32),
        ],
        scratch_shapes=[pltpu.VMEM((4, 8, LANES), jnp.float32)],
        compiler_params=pltpu.CompilerParams(vmem_limit_bytes=VMEM),
        name="sums",
    )(*terms, p, r)


def finish_kernel(sums_ref, x_ref, r_ref, p_ref, normal_ref, x_out, r_out, p_out):
    total = jnp.sum(sums_ref[...], axis=0, keepdims=True)
    r_r = total[:, 0:1]
    p_n = total[:, 1:2]
    r_n = total[:, 2:3]
    n_n = total[:, 3:4]
    alpha = r_r / p_n
    beta = (r_r + alpha * (alpha * n_n - 2.0 * r_n)) / r_r
    p = p_ref[...]
    next_r = r_ref[...] - alpha * normal_ref[...]
    x_out[...] = x_ref[...] + alpha * p
    r_out[...] = next_r
    p_out[...] = next_r + beta * p


def finish(total, x, r, p, normal):
    shape = x.shape
    batch = min(shape[1], 4)
    spec = pl.BlockSpec((2, batch) + shape[2:], lambda s: (0, s, 0, 0))
    return pl.pallas_call(
        finish_kernel,
        grid=(shape[1] // batch,),
        in_specs=[pl.BlockSpec(total.shape, lambda s: (0, 0))] + [spec] * 4,
        out_specs=[spec] * 3,
        out_shape=[jax.ShapeDtypeStruct(shape, jnp.float32)] * 3,
        compiler_params=pltpu.CompilerParams(vmem_limit_bytes=VMEM),
        name="finish",
    )(total, x, r, p, normal)


def block_matrices(weights):
    slots, _, width, _ = weights.shape
    w_x, w_y, w_z = weights[:, 0], weights[:, 1], weights[:, 2]
    pairs_x = jnp.stack([w_x * jnp.roll(w_x, -d, axis=1) for d in range(width)], axis=1)
    pairs_z = jnp.stack([w_z * jnp.roll(w_z, -d, axis=1) for d in range(width)], axis=1)
    pairs_y = w_y[:, :, None] * w_y[:, None, :]
    both = pairs_x[:, :, :, None, None] * pairs_z[:, None, None, :, :]
    found = jnp.einsum(
        "jxizfs,jabs->abzxifj", both, pairs_y, precision=lax.Precision.HIGHEST
    )
    found = jnp.stack([found, found], axis=4)
    return found.reshape(width**4, 2 * width, width * slots)


def block_offsets(gathered, slots, ntile, capacity):
    owners = gathered[:, :slots]
    lists = gathered[:, slots:].reshape(ntile, 3, ntile, capacity)
    earlier = jnp.tril(jnp.ones((slots, slots), jnp.int32), -1)
    same = (owners[:, :, None] == owners[:, None, :]).astype(jnp.int32)
    ranks = jnp.sum(same * earlier[None], axis=2)
    wanted = owners * capacity + ranks
    lists = jnp.transpose(lists, (1, 2, 0, 3)).reshape(3, ntile, 1, ntile * capacity)
    hit = wanted[:, :, None] == jnp.arange(ntile * capacity, dtype=jnp.int32)
    found = jnp.sum(jnp.where(hit[None], lists, 0), axis=3)
    return found[0], found[1] + owners * (LANES // ntile), found[2]


def shards(image_p, image_x, image_r, sensitivity, kb_weights, block_owner, owner_list):
    ntile = lax.axis_size("tile")
    ncoil = lax.axis_size("coil")
    chips = ncoil // 2
    slots = kb_weights.shape[0]
    capacity = owner_list.shape[3]
    planes, length = image_p.shape[1], image_p.shape[3]
    part = image_p.shape[2]
    chunk = LANES // (2 * planes)
    tile = lax.axis_index("tile")
    coil = lax.axis_index("coil")
    chip, core = coil // 2, coil % 2

    mine = jnp.concatenate([block_owner, owner_list[:, 0].reshape(-1)])
    gathered = lax.all_to_all(
        jnp.broadcast_to(mine[None], (ntile, mine.shape[0])), "tile", 0, 0, tiled=True
    )

    def from_chip(values, by):
        pairs = [
            (a * 2 + k, (a - by) % chips * 2 + k) for a in range(chips) for k in range(2)
        ]
        return lax.ppermute(values, "coil", pairs)

    def to_chip(values, by):
        pairs = [
            (a * 2 + k, (a + by) % chips * 2 + k) for a in range(chips) for k in range(2)
        ]
        return lax.ppermute(values, "coil", pairs)

    def other_core(values):
        pairs = [(a * 2 + k, a * 2 + 1 - k) for a in range(chips) for k in range(2)]
        return lax.ppermute(values, "coil", pairs)

    p_same = [image_p] + [from_chip(image_p, by) for by in range(1, chips)]
    p_pieces = p_same + [other_core(piece) for piece in p_same]
    hops = jnp.arange(chips, dtype=jnp.int32)
    starts = jnp.concatenate(
        [((chip + hops) % chips * 2 + at) * part for at in (core, 1 - core)]
    )

    off_x, off_y, off_z = block_offsets(gathered, slots, ntile, capacity)
    band = off_y // chunk
    after = jnp.minimum(band + 1, length // chunk - 1)
    info = jnp.stack(
        [
            (band * length + off_z).reshape(-1),
            (after * length + off_z).reshape(-1),
            (off_y % chunk).reshape(-1),
        ]
    )
    lane = jnp.arange(LANES, dtype=jnp.int32)
    lane_ri = lane // (LANES // 2)
    lane_q = lane // planes % chunk
    lane_x = lane % planes + tile * planes
    unit = 2.0 * math.pi / length
    angle = unit * (off_x.reshape(-1, 1) * lane_x[None] % length).astype(jnp.float32)
    phases = (jnp.cos(angle), jnp.sin(angle) * jnp.where(lane_ri == 0, 1.0, -1.0)[None])
    row = jnp.arange(32, dtype=jnp.int32)[:, None]
    row_q, row_ri, row_i = row // 8, row // 4 % 2, row % 4
    angle = unit * (row_i * lane_x[None] % length).astype(jnp.float32)
    sine = jnp.where(row_ri == 0, 1.0, -1.0) * jnp.sin(angle)
    shift = jnp.where(row_ri == lane_ri[None], jnp.cos(angle), sine)
    shift = jnp.where(lane_q[None] % 4 == row_q, shift / math.sqrt(length), 0.0)
    shift_hi = lax.reduce_precision(shift, 8, 7)
    shift = (shift_hi.astype(jnp.bfloat16), (shift - shift_hi).astype(jnp.bfloat16))
    tables = fourier_tables(length)
    matrix = block_matrices(kb_weights)
    own_y = lax.dynamic_index_in_dim(off_y, tile, 0, keepdims=True) % 4
    turn = jnp.broadcast_to(jnp.tile(own_y, (1, 4)), (8, LANES))

    smap = sensitivity[0]
    partial = forward(info, starts, p_pieces, smap, tables, phases, shift, slots)
    parts = lax.all_to_all(partial, "tile", 0, 0, tiled=True)
    done = regrid(parts, matrix, turn)
    spread = lax.all_to_all(done, "tile", 0, 0, tiled=True)
    images = inverse(info, starts, spread, smap, tables, phases, shift, slots, ncoil)
    kept, sent = images[:chips], images[chips:]
    terms = [kept[0], other_core(sent[0])]
    for by in range(1, chips):
        terms.append(to_chip(kept[by] + other_core(sent[by]), by))
    normal, found = sums(terms, image_p, image_r, ncoil * ntile)
    total = lax.all_to_all(found, ("coil", "tile"), 0, 0, tiled=True)
    return tuple(finish(total, image_x, image_r, image_p, normal))


def solution(mesh):
    return jax.shard_map(
        shards,
        mesh=mesh,
        in_specs=(
            P(None, "tile", "coil", None),
            P(None, "tile", "coil", None),
            P(None, "tile", "coil", None),
            P("coil", None, "tile", None, None),
            P("tile", None, None, None),
            P("tile"),
            P(None, "tile", None, None),
        ),
        out_specs=(
            P(None, "tile", "coil", None),
            P(None, "tile", "coil", None),
            P(None, "tile", "coil", None),
        ),
        check_vma=False,
    )
```

```python
import functools
import math

import jax
import jax.numpy as jnp
import ml_dtypes
import numpy as np
from jax import lax
from jax.experimental import pallas as pl
from jax.experimental.pallas import tpu as pltpu
from jax.sharding import PartitionSpec as P

LANES = 128
VMEM = 24 * 1024 * 1024


def halves(values):
    high = values.astype(jnp.bfloat16)
    low = (values - high.astype(jnp.float32)).astype(jnp.bfloat16)
    return high, low


def dot_bf16(left, right, dims):
    return lax.dot_general(left, right, (dims, ((), ())), preferred_element_type=jnp.float32)


def dot_left(table, values, dims=((1,), (0,))):
    high, low = halves(values)
    return (
        dot_bf16(table[0], high, dims)
        + dot_bf16(table[0], low, dims)
        + dot_bf16(table[1], high, dims)
    )


def dot_right(values, table, dims=((1,), (0,))):
    high, low = halves(values)
    return (
        dot_bf16(high, table[0], dims)
        + dot_bf16(low, table[0], dims)
        + dot_bf16(high, table[1], dims)
    )


def fourier_tables(length):
    cells = np.arange(length)
    angle = 2.0 * math.pi / length * (cells[:, None] * cells[None, :] % length)
    cos_t = np.cos(angle) / math.sqrt(length)
    sin_t = np.sin(angle) / math.sqrt(length)
    found = []
    for sign in (1.0, -1.0):
        whole = np.block([[cos_t, -sign * sin_t], [sign * sin_t, cos_t]])
        high = whole.astype(ml_dtypes.bfloat16)
        low = (whole - high.astype(np.float64)).astype(ml_dtypes.bfloat16)
        found += [jnp.asarray(high), jnp.asarray(low)]
    return found


def window_masks(first, chunk, rows, planes):
    lane = lax.broadcasted_iota(jnp.int32, (rows, LANES), 1)
    past = lane // planes % chunk - first
    here = jnp.logical_and(past >= 0, past < 4)
    after = jnp.logical_and(past + chunk >= 0, past + chunk < 4)
    return here, after


def forward_kernel(
    info, starts, *refs, length, planes, chunk, pieces, slots, handlers, batch
):
    p_refs = refs[:pieces]
    s_ref, a_hi, a_lo, b_hi, b_lo, cos_ref, sin_ref, x_hi, x_lo = refs[pieces : pieces + 9]
    out_ref = refs[pieces + 9]
    direction, ybuf, kbuf, gbuf = refs[pieces + 10 :]
    step = pl.program_id(0)
    rows = length * planes
    part = length // pieces
    left = (b_hi[...], b_lo[...])
    for pair in range(batch // 2):
        columns = []
        for inner in range(2):
            at = pair * 2 + inner
            for piece in range(pieces):
                to = pl.ds(pl.multiple_of(starts[piece], part), part)
                direction[0, to, :] = p_refs[piece][0, at]
                direction[1, to, :] = p_refs[piece][1, at]
            s_re = s_ref[0, at]
            s_im = s_ref[1, at]
            p_re = direction[0]
            p_im = direction[1]
            columns.append(
                jnp.concatenate([s_re * p_re - s_im * p_im, s_re * p_im + s_im * p_re], axis=0)
            )
        done = dot_left(left, jnp.concatenate(columns, axis=1))
        for inner in range(2):
            plane = step * batch + pair * 2 + inner
            for ri in range(2):
                ybuf[pl.ds(ri * rows + plane, length, stride=planes), :] = done[
                    ri * length : (ri + 1) * length, inner * LANES : (inner + 1) * LANES
                ]

    @pl.when(step == pl.num_programs(0) - 1)
    def _():
        right = (a_hi[...], a_lo[...])

        def along_z(at, carry):
            base = pl.multiple_of(at * 256, 256)
            both = jnp.concatenate(
                [ybuf[pl.ds(base, 256), :], ybuf[pl.ds(rows + base, 256), :]], axis=1
            )
            done = dot_right(both, right)
            for inner in range(4):
                band = done[inner * 64 : (inner + 1) * 64]
                tile = jnp.concatenate([band[:, :length], band[:, length:]], axis=0)
                to = pl.multiple_of((at * 4 + inner) * length, length)
                kbuf[pl.ds(to, length), :] = tile.T
            return carry

        lax.fori_loop(0, rows // 256, along_z, 0)

        def cut(group, carry):
            for inner in range(8):
                block = group * 8 + inner
                here, after = window_masks(info[2, block], chunk, 4, planes)
                first = kbuf[pl.ds(info[0, block], 4), :]
                second = kbuf[pl.ds(info[1, block], 4), :]
                cells = jnp.where(here, first, jnp.where(after, second, 0.0))
                to = block // slots * (4 * slots) + block % slots
                gbuf[pl.ds(to, 4, stride=slots), :] = cells
            return carry

        lax.fori_loop(0, handlers * slots // 8, cut, 0)
        table = (x_hi[...], x_lo[...])

        def along_x(handler, carry):
            rows_at = pl.ds(pl.multiple_of(handler * slots, slots), slots)
            cos_b = jnp.concatenate([cos_ref[rows_at, :]] * 4, axis=0)
            sin_b = jnp.concatenate([sin_ref[rows_at, :]] * 4, axis=0)
            cells = gbuf[pl.ds(pl.multiple_of(handler * LANES, LANES), LANES), :]
            turned = cells * cos_b + pltpu.roll(cells, LANES // 2, 1) * sin_b
            out_ref[handler] = dot_left(table, turned, ((1,), (1,)))
            return carry

        lax.fori_loop(0, handlers, along_x, 0)


def forward(info, starts, p_pieces, smap, tables, phases, shift, slots):
    planes, length = smap.shape[1], smap.shape[2]
    pieces = len(p_pieces)
    part = length // pieces
    batch = min(planes, 4)
    chunk = LANES // (2 * planes)
    handlers = info.shape[1] // slots
    rows = length * planes
    whole = lambda *shape: pl.BlockSpec(shape, lambda s: (0,) * len(shape))
    kernel = functools.partial(
        forward_kernel, length=length, planes=planes, chunk=chunk, pieces=pieces,
        slots=slots, handlers=handlers, batch=batch,
    )
    return pl.pallas_call(
        kernel,
        grid=(planes // batch,),
        in_specs=[pl.BlockSpec(memory_space=pltpu.SMEM)] * 2
        + [pl.BlockSpec((2, batch, part, length), lambda s: (0, s, 0, 0))] * pieces
        + [pl.BlockSpec((2, batch, length, length), lambda s: (0, s, 0, 0))]
        + [whole(2 * length, 2 * length)] * 4
        + [whole(handlers * slots, LANES)] * 2
        + [whole(32, LANES)] * 2,
        out_specs=whole(handlers, 32, LANES),
        out_shape=jax.ShapeDtypeStruct((handlers, 32, LANES), jnp.float32),
        scratch_shapes=[
            pltpu.VMEM((2, length, length), jnp.float32),
            pltpu.VMEM((2 * rows, length), jnp.float32),
            pltpu.VMEM((length * (length // chunk), LANES), jnp.float32),
            pltpu.VMEM((handlers * LANES, LANES), jnp.float32),
        ],
        compiler_params=pltpu.CompilerParams(vmem_limit_bytes=VMEM),
        name="forward",
    )(info, starts, *p_pieces, smap, *tables, *phases, *shift)


def regrid_kernel(parts_ref, matrix_ref, turn_ref, out_ref, *, handlers):
    total = parts_ref[0]
    for at in range(1, handlers):
        total = total + parts_ref[at]
    turn = turn_ref[...]
    cyclic = [total[8 * q : 8 * q + 8] for q in range(4)]

    def pick(values, sign, at):
        found = values[at]
        for by in range(1, 4):
            found = jnp.where(turn == by, values[(at + sign * by) % 4], found)
        return found

    cells = [pick(cyclic, 1, e) for e in range(4)]
    along = lax.broadcasted_iota(jnp.int32, (8, LANES), 0) % 4
    sums = [jnp.zeros((8, LANES), jnp.float32) for _ in range(4)]
    for source in range(4):
        for d_z in range(4):
            value = cells[source]
            if d_z:
                value = pltpu.roll(value, LANES - 32 * d_z, 1)
            for d_x in range(4):
                moved = value
                if d_x:
                    moved = jnp.where(
                        along + d_x < 4, pltpu.roll(value, 8 - d_x, 0), pltpu.roll(value, 4 - d_x, 0)
                    )
                for e in range(4):
                    at = 8 * (((e * 4 + source) * 4 + d_z) * 4 + d_x)
                    sums[e] = sums[e] + matrix_ref[at : at + 8] * moved
    done = jnp.concatenate([pick(sums, -1, q) for q in range(4)], axis=0)
    for at in range(handlers):
        out_ref[at] = done


def regrid(parts, matrix, turn):
    handlers = parts.shape[0]
    return pl.pallas_call(
        functools.partial(regrid_kernel, handlers=handlers),
        out_shape=jax.ShapeDtypeStruct(parts.shape, jnp.float32),
        in_specs=[pl.BlockSpec(memory_space=pltpu.VMEM)] * 3,
        out_specs=pl.BlockSpec(memory_space=pltpu.VMEM),
        compiler_params=pltpu.CompilerParams(vmem_limit_bytes=VMEM),
        name="regrid",
    )(parts, matrix, turn)


def inverse_kernel(
    info, starts, u_ref, s_ref, a_hi, a_lo, b_hi, b_lo, cos_ref, sin_ref, x_hi, x_lo, *refs,
    length, planes, chunk, pieces, slots, handlers, batch
):
    out_refs = refs[:pieces]
    kbuf, gbuf, ybuf, image = refs[pieces:]
    step = pl.program_id(0)
    rows = length * planes
    part = length // pieces

    @pl.when(step == 0)
    def _():
        table = (x_hi[...], x_lo[...])

        def along_x(handler, carry):
            rows_at = pl.ds(pl.multiple_of(handler * slots, slots), slots)
            cos_b = jnp.concatenate([cos_ref[rows_at, :]] * 4, axis=0)
            sin_b = jnp.concatenate([sin_ref[rows_at, :]] * 4, axis=0)
            cells = dot_right(u_ref[handler].T, table)
            turned = cells * cos_b - pltpu.roll(cells, LANES // 2, 1) * sin_b
            gbuf[pl.ds(pl.multiple_of(handler * LANES, LANES), LANES), :] = turned
            return carry

        lax.fori_loop(0, handlers, along_x, 0)
        kbuf[...] = jnp.zeros_like(kbuf)

        def place(group, carry):
            for inner in range(8):
                block = group * 8 + inner
                here, after = window_masks(info[2, block], chunk, 4, planes)
                at = block // slots * (4 * slots) + block % slots
                cells = gbuf[pl.ds(at, 4, stride=slots), :]
                first = pl.ds(info[0, block], 4)
                kbuf[first, :] = kbuf[first, :] + jnp.where(here, cells, 0.0)
                second = pl.ds(info[1, block], 4)
                kbuf[second, :] = kbuf[second, :] + jnp.where(after, cells, 0.0)
            return carry

        lax.fori_loop(0, handlers * slots // 8, place, 0)
        right = (b_hi[...], b_lo[...])

        def along_z(at, carry):
            bands = []
            for inner in range(4):
                to = pl.multiple_of((at * 4 + inner) * length, length)
                tile = kbuf[pl.ds(to, length), :].T
                bands.append(jnp.concatenate([tile[:64], tile[64:]], axis=1))
            done = dot_right(jnp.concatenate(bands, axis=0), right)
            base = pl.multiple_of(at * 256, 256)
            ybuf[pl.ds(base, 256), :] = done[:, :length]
            ybuf[pl.ds(rows + base, 256), :] = done[:, length:]
            return carry

        lax.fori_loop(0, rows // 256, along_z, 0)

    left = (a_hi[...], a_lo[...])
    for pair in range(batch // 2):
        columns = []
        for inner in range(2):
            plane = step * batch + pair * 2 + inner
            columns.append(
                jnp.concatenate(
                    [ybuf[pl.ds(ri * rows + plane, length, stride=planes), :] for ri in range(2)],
                    axis=0,
                )
            )
        image[...] = dot_left(left, jnp.concatenate(columns, axis=1))
        for inner in range(2):
            at = pair * 2 + inner
            lanes = slice(inner * LANES, (inner + 1) * LANES)
            for piece in range(pieces):
                start = pl.multiple_of(starts[piece], part)
                i_re = image[pl.ds(start, part), lanes]
                i_im = image[pl.ds(length + start, part), lanes]
                s_re = s_ref[0, at, pl.ds(start, part), :]
                s_im = s_ref[1, at, pl.ds(start, part), :]
                out_refs[piece][0, at] = s_re * i_re + s_im * i_im
                out_refs[piece][1, at] = s_re * i_im - s_im * i_re


def inverse(info, starts, u, smap, tables, phases, shift, slots, pieces):
    planes, length = smap.shape[1], smap.shape[2]
    part = length // pieces
    batch = min(planes, 4)
    chunk = LANES // (2 * planes)
    handlers = info.shape[1] // slots
    rows = length * planes
    whole = lambda *shape: pl.BlockSpec(shape, lambda s: (0,) * len(shape))
    kernel = functools.partial(
        inverse_kernel, length=length, planes=planes, chunk=chunk, pieces=pieces,
        slots=slots, handlers=handlers, batch=batch,
    )
    return pl.pallas_call(
        kernel,
        grid=(planes // batch,),
        in_specs=[pl.BlockSpec(memory_space=pltpu.SMEM)] * 2
        + [whole(handlers, 32, LANES)]
        + [pl.BlockSpec((2, batch, length, length), lambda s: (0, s, 0, 0))]
        + [whole(2 * length, 2 * length)] * 4
        + [whole(handlers * slots, LANES)] * 2
        + [whole(32, LANES)] * 2,
        out_specs=[pl.BlockSpec((2, batch, part, length), lambda s: (0, s, 0, 0))] * pieces,
        out_shape=[jax.ShapeDtypeStruct((2, planes, part, length), jnp.float32)] * pieces,
        scratch_shapes=[
            pltpu.VMEM((length * (length // chunk), LANES), jnp.float32),
            pltpu.VMEM((handlers * LANES, LANES), jnp.float32),
            pltpu.VMEM((2 * rows, length), jnp.float32),
            pltpu.VMEM((2 * length, 2 * length), jnp.float32),
        ],
        compiler_params=pltpu.CompilerParams(vmem_limit_bytes=VMEM),
        name="inverse",
    )(info, starts, u, smap, *tables, *phases, *shift)


def sums_kernel(*refs, terms):
    term_refs = refs[:terms]
    p_ref, r_ref, normal_ref, out_ref = refs[terms:]
    shape = p_ref.shape

    def add(plane, held):
        held = list(held)
        for ri in range(2):
            normal = term_refs[0][ri, plane]
            for term in term_refs[1:]:
                normal = normal + term[ri, plane]
            normal_ref[ri, plane] = normal
            p = p_ref[ri, plane]
            r = r_ref[ri, plane]
            for at, product in enumerate((r * r, p * normal, r * normal, normal * normal)):
                held[at] = held[at] + jnp.sum(product.reshape(-1, 8, LANES), axis=0)
        return tuple(held)

    start = tuple(jnp.zeros((8, LANES), jnp.float32) for _ in range(4))
    held = lax.fori_loop(0, shape[1], add, start, unroll=4)
    lane = lax.broadcasted_iota(jnp.int32, out_ref.shape, 1)
    found = jnp.zeros(out_ref.shape, jnp.float32)
    for at in range(4):
        found = jnp.where(lane == at, jnp.sum(held[at]), found)
    out_ref[...] = found


def sums(terms, p, r, devices):
    return pl.pallas_call(
        functools.partial(sums_kernel, terms=len(terms)),
        in_specs=[pl.BlockSpec(memory_space=pltpu.VMEM)] * (len(terms) + 2),
        out_specs=[pl.BlockSpec(memory_space=pltpu.VMEM)] * 2,
        out_shape=[
            jax.ShapeDtypeStruct(p.shape, jnp.float32),
            jax.ShapeDtypeStruct((devices, LANES), jnp.float32),
        ],
        compiler_params=pltpu.CompilerParams(vmem_limit_bytes=VMEM // 2),
        name="sums",
    )(*terms, p, r)


def finish(total, x, r, p, normal):
    total = jnp.sum(total, axis=0)
    r_r, p_n, r_n, n_n = total[0], total[1], total[2], total[3]
    alpha = r_r / p_n
    beta = (r_r + alpha * (alpha * n_n - 2.0 * r_n)) / r_r
    next_r = r - alpha * normal
    return x + alpha * p, next_r, next_r + beta * p


def matrices_kernel(weights_ref, out_ref, held, *, slots):
    def one(block, carry):
        w_x = weights_ref[block, 0]
        w_y = weights_ref[block, 1]
        w_z = weights_ref[block, 2]
        twice = jnp.concatenate([w_x, w_x], axis=0)
        along_x = [twice * pltpu.roll(twice, (8 - d) % 8, 0) if d else twice * twice for d in range(4)]
        right = []
        for f in range(4):
            for d_z in range(4):
                other = (f + d_z) % 4
                along_z = w_z[f : f + 1] * w_z[other : other + 1]
                right += [along_x[d_x] * along_z for d_x in range(4)]
        left = jnp.concatenate([w_y * w_y[e : e + 1] for e in range(4)], axis=0)
        high, low = halves(jnp.concatenate(right, axis=0))
        done = dot_right(left, (high, low), ((1,), (1,)))
        for f in range(4):
            held[pl.ds(f * slots + block, 16, stride=LANES), :] = done[
                :, f * LANES : (f + 1) * LANES
            ]
        return carry

    lax.fori_loop(0, slots, one, 0, unroll=2)

    def turn(pair, carry):
        at = pl.ds(pl.multiple_of(pair * LANES, LANES), LANES)
        out_ref[at, :] = held[at, :].T
        return carry

    lax.fori_loop(0, 16, turn, 0, unroll=2)


def block_matrices(weights):
    slots = weights.shape[0]
    return pl.pallas_call(
        functools.partial(matrices_kernel, slots=slots),
        out_shape=jax.ShapeDtypeStruct((16 * LANES, LANES), jnp.float32),
        in_specs=[pl.BlockSpec(memory_space=pltpu.VMEM)],
        out_specs=pl.BlockSpec(memory_space=pltpu.VMEM),
        scratch_shapes=[pltpu.VMEM((16 * LANES, LANES), jnp.float32)],
        compiler_params=pltpu.CompilerParams(vmem_limit_bytes=VMEM // 2),
        name="matrices",
    )(weights)


def block_offsets(gathered, slots, ntile, capacity):
    owners = gathered[:, :slots]
    lists = gathered[:, slots:].reshape(ntile, 3, ntile, capacity)
    earlier = jnp.tril(jnp.ones((slots, slots), jnp.int32), -1)
    same = (owners[:, :, None] == owners[:, None, :]).astype(jnp.int32)
    ranks = jnp.sum(same * earlier[None], axis=2)
    wanted = owners * capacity + ranks
    lists = jnp.transpose(lists, (1, 2, 0, 3)).reshape(3, ntile, 1, ntile * capacity)
    hit = wanted[:, :, None] == jnp.arange(ntile * capacity, dtype=jnp.int32)
    found = jnp.sum(jnp.where(hit[None], lists, 0), axis=3)
    return found[0], found[1] + owners * (LANES // ntile), found[2]


def shards(image_p, image_x, image_r, sensitivity, kb_weights, block_owner, owner_list):
    ntile = lax.axis_size("tile")
    ncoil = lax.axis_size("coil")
    chips = ncoil // 2
    slots = kb_weights.shape[0]
    capacity = owner_list.shape[3]
    planes, length = image_p.shape[1], image_p.shape[3]
    part = image_p.shape[2]
    chunk = LANES // (2 * planes)
    tile = lax.axis_index("tile")
    coil = lax.axis_index("coil")
    chip, core = coil // 2, coil % 2

    mine = jnp.concatenate([block_owner, owner_list[:, 0].reshape(-1)])
    gathered = lax.all_to_all(
        jnp.broadcast_to(mine[None], (ntile, mine.shape[0])), "tile", 0, 0, tiled=True
    )

    def from_chip(values, by):
        pairs = [
            (a * 2 + k, (a - by) % chips * 2 + k) for a in range(chips) for k in range(2)
        ]
        return lax.ppermute(values, "coil", pairs)

    def to_chip(values, by):
        pairs = [
            (a * 2 + k, (a + by) % chips * 2 + k) for a in range(chips) for k in range(2)
        ]
        return lax.ppermute(values, "coil", pairs)

    def other_core(values):
        pairs = [(a * 2 + k, a * 2 + 1 - k) for a in range(chips) for k in range(2)]
        return lax.ppermute(values, "coil", pairs)

    p_same = [image_p] + [from_chip(image_p, by) for by in range(1, chips)]
    p_pieces = p_same + [other_core(piece) for piece in p_same]
    hops = jnp.arange(chips, dtype=jnp.int32)
    starts = jnp.concatenate(
        [((chip + hops) % chips * 2 + at) * part for at in (core, 1 - core)]
    )

    off_x, off_y, off_z = block_offsets(gathered, slots, ntile, capacity)
    band = off_y // chunk
    after = jnp.minimum(band + 1, length // chunk - 1)
    info = jnp.stack(
        [
            (band * length + off_z).reshape(-1),
            (after * length + off_z).reshape(-1),
            (off_y % chunk).reshape(-1),
        ]
    )
    lane = jnp.arange(LANES, dtype=jnp.int32)
    lane_ri = lane // (LANES // 2)
    lane_q = lane // planes % chunk
    lane_x = lane % planes + tile * planes
    unit = 2.0 * math.pi / length
    angle = unit * (off_x.reshape(-1, 1) * lane_x[None] % length).astype(jnp.float32)
    phases = (jnp.cos(angle), jnp.sin(angle) * jnp.where(lane_ri == 0, 1.0, -1.0)[None])
    row = jnp.arange(32, dtype=jnp.int32)[:, None]
    row_q, row_ri, row_i = row // 8, row // 4 % 2, row % 4
    angle = unit * (row_i * lane_x[None] % length).astype(jnp.float32)
    sine = jnp.where(row_ri == 0, 1.0, -1.0) * jnp.sin(angle)
    shift = jnp.where(row_ri == lane_ri[None], jnp.cos(angle), sine)
    shift = jnp.where(lane_q[None] % 4 == row_q, shift / math.sqrt(length), 0.0)
    shift_hi = lax.reduce_precision(shift, 8, 7)
    shift = (shift_hi.astype(jnp.bfloat16), (shift - shift_hi).astype(jnp.bfloat16))
    tables = fourier_tables(length)
    matrix = block_matrices(kb_weights)
    own_y = lax.dynamic_index_in_dim(off_y, tile, 0, keepdims=True) % 4
    turn = jnp.broadcast_to(jnp.tile(own_y, (1, 4)), (8, LANES))

    smap = sensitivity[0]
    partial = forward(info, starts, p_pieces, smap, tables, phases, shift, slots)
    parts = lax.all_to_all(partial, "tile", 0, 0, tiled=True)
    done = regrid(parts, matrix, turn)
    spread = lax.all_to_all(done, "tile", 0, 0, tiled=True)
    images = inverse(info, starts, spread, smap, tables, phases, shift, slots, ncoil)
    kept, sent = images[:chips], images[chips:]
    terms = [kept[0], other_core(sent[0])]
    for by in range(1, chips):
        terms.append(to_chip(kept[by] + other_core(sent[by]), by))
    normal, found = sums(terms, image_p, image_r, ncoil * ntile)
    total = lax.all_to_all(found, ("coil", "tile"), 0, 0, tiled=True)
    return finish(total, image_x, image_r, image_p, normal)


def solution(mesh):
    return jax.shard_map(
        shards,
        mesh=mesh,
        in_specs=(
            P(None, "tile", "coil", None),
            P(None, "tile", "coil", None),
            P(None, "tile", "coil", None),
            P("coil", None, "tile", None, None),
            P("tile", None, None, None),
            P("tile"),
            P(None, "tile", None, None),
        ),
        out_specs=(
            P(None, "tile", "coil", None),
            P(None, "tile", "coil", None),
            P(None, "tile", "coil", None),
        ),
        check_vma=False,
    )
```

```python
import functools
import math

import jax
import jax.numpy as jnp
import ml_dtypes
import numpy as np
from jax import lax
from jax.experimental import pallas as pl
from jax.experimental.pallas import tpu as pltpu
from jax.sharding import PartitionSpec as P

LANES = 128
VMEM = 24 * 1024 * 1024


def halves(values):
    high = values.astype(jnp.bfloat16)
    low = (values - high.astype(jnp.float32)).astype(jnp.bfloat16)
    return high, low


def dot_bf16(left, right, dims):
    return lax.dot_general(left, right, (dims, ((), ())), preferred_element_type=jnp.float32)


def dot_left(table, values, dims=((1,), (0,))):
    high, low = halves(values)
    return (
        dot_bf16(table[0], high, dims)
        + dot_bf16(table[0], low, dims)
        + dot_bf16(table[1], high, dims)
    )


def dot_right(values, table, dims=((1,), (0,))):
    high, low = halves(values)
    return (
        dot_bf16(high, table[0], dims)
        + dot_bf16(low, table[0], dims)
        + dot_bf16(high, table[1], dims)
    )


def fourier_tables(length):
    cells = np.arange(length)
    angle = 2.0 * math.pi / length * (cells[:, None] * cells[None, :] % length)
    cos_t = np.cos(angle) / math.sqrt(length)
    sin_t = np.sin(angle) / math.sqrt(length)
    found = []
    for sign in (1.0, -1.0):
        whole = np.block([[cos_t, -sign * sin_t], [sign * sin_t, cos_t]])
        high = whole.astype(ml_dtypes.bfloat16)
        low = (whole - high.astype(np.float64)).astype(ml_dtypes.bfloat16)
        found += [high, low]
    return jnp.asarray(np.stack(found))


def window_masks(first, chunk, rows, planes):
    lane = lax.broadcasted_iota(jnp.int32, (rows, LANES), 1)
    past = lane // planes % chunk - first
    here = jnp.logical_and(past >= 0, past < 4)
    after = jnp.logical_and(past + chunk >= 0, past + chunk < 4)
    return here, after


def call(kernel, outs, scratch, operands, smem, flops, name):
    specs = [pl.BlockSpec(memory_space=pltpu.SMEM)] * smem
    specs += [pl.BlockSpec(memory_space=pltpu.VMEM)] * (len(operands) - smem)
    moved = sum(math.prod(a.shape) * a.dtype.itemsize for a in operands)
    return pl.pallas_call(
        kernel,
        out_shape=[jax.ShapeDtypeStruct(shape, jnp.float32) for shape in outs],
        in_specs=specs,
        out_specs=[pl.BlockSpec(memory_space=pltpu.VMEM)] * len(outs),
        scratch_shapes=[pltpu.VMEM(shape, jnp.float32) for shape in scratch],
        compiler_params=pltpu.CompilerParams(vmem_limit_bytes=VMEM),
        cost_estimate=pl.CostEstimate(flops=flops, bytes_accessed=moved, transcendentals=0),
        name=name,
    )(*operands)


def coil_z_kernel(starts, *refs, quarters, planes, part, length):
    count = len(quarters)
    p_refs = refs[:count]
    s_ref, table_ref = refs[count : count + 2]
    outs = refs[count + 2 :]
    table = (table_ref[0], table_ref[1])
    batch = min(planes, 256 // part)
    for piece in range(count):
        rows = pl.ds(pl.multiple_of(starts[quarters[piece]], part), part)
        for base in range(0, planes, batch):
            bands = []
            for plane in range(base, base + batch):
                s_re = s_ref[0, plane, rows, :]
                s_im = s_ref[1, plane, rows, :]
                p_re = p_refs[piece][0, plane]
                p_im = p_refs[piece][1, plane]
                bands.append(
                    jnp.concatenate([s_re * p_re - s_im * p_im, s_re * p_im + s_im * p_re], axis=1)
                )
            done = dot_right(jnp.concatenate(bands, axis=0), table)
            for ri in range(2):
                half = done[:, ri * length : (ri + 1) * length]
                outs[piece][ri, base : base + batch] = half.reshape(batch, part, length)


def coil_z(starts, pieces, quarters, smap, tables):
    _, planes, part, length = pieces[0].shape
    count = len(pieces)
    kernel = functools.partial(
        coil_z_kernel, quarters=quarters, planes=planes, part=part, length=length
    )
    flops = count * planes * part * 24 * length * length
    return call(
        kernel, [pieces[0].shape] * count, [], [starts, *pieces, smap, tables], 1, flops, "coil_z"
    )


def along_y_kernel(starts, *refs, pieces, planes, part, length, chunk):
    t_refs = refs[:pieces]
    table_ref, out_ref, natural, ybuf = refs[pieces:]
    rows = length * planes
    table = (table_ref[2], table_ref[3])
    for piece in range(pieces):
        at = pl.ds(pl.multiple_of(starts[piece], part), part)
        for plane in range(planes):
            for ri in range(2):
                natural[ri, plane, at, :] = t_refs[piece][ri, plane]
    for pair in range(planes // 2):
        columns = [
            jnp.concatenate([natural[0, plane], natural[1, plane]], axis=0)
            for plane in (2 * pair, 2 * pair + 1)
        ]
        done = dot_left(table, jnp.concatenate(columns, axis=1))
        for inner in range(2):
            for ri in range(2):
                ybuf[pl.ds(ri * rows + 2 * pair + inner, length, stride=planes), :] = done[
                    ri * length : (ri + 1) * length, inner * LANES : (inner + 1) * LANES
                ]
    for band in range(length // chunk):
        re = ybuf[band * 64 : (band + 1) * 64, :]
        im = ybuf[rows + band * 64 : rows + (band + 1) * 64, :]
        out_ref[band * length : (band + 1) * length, :] = jnp.concatenate([re, im], axis=0).T


def along_y(starts, pieces, tables, chunk):
    _, planes, part, length = pieces[0].shape
    kernel = functools.partial(
        along_y_kernel, pieces=len(pieces), planes=planes, part=part, length=length, chunk=chunk
    )
    return call(
        kernel,
        [(length * (length // chunk), LANES)],
        [(2, planes, length, length), (2 * length * planes, length)],
        [starts, *pieces, tables],
        1,
        24 * planes * length**3,
        "along_y",
    )[0]


def cut_kernel(info, place, k_ref, cos_ref, sin_ref, shift_ref, *refs, planes, chunk, slots, handlers):
    outs = refs[:handlers]
    gbuf = refs[handlers]

    def cut(group, carry):
        for inner in range(8):
            block = group * 8 + inner
            here, after = window_masks(info[2, block], chunk, 4, planes)
            first = k_ref[pl.ds(info[0, block], 4), :]
            second = k_ref[pl.ds(info[1, block], 4), :]
            cells = jnp.where(here, first, jnp.where(after, second, 0.0))
            to = block // slots * (4 * slots) + block % slots
            gbuf[pl.ds(to, 4, stride=slots), :] = cells
        return carry

    lax.fori_loop(0, handlers * slots // 8, cut, 0)
    table = halves(shift_ref[...])
    for hop in range(handlers):
        handler = place[0] ^ hop
        at = pl.ds(pl.multiple_of(handler * slots, slots), slots)
        cos_b = jnp.concatenate([cos_ref[at, :]] * 4, axis=0)
        sin_b = jnp.concatenate([sin_ref[at, :]] * 4, axis=0)
        cells = gbuf[pl.ds(pl.multiple_of(handler * LANES, LANES), LANES), :]
        turned = cells * cos_b + pltpu.roll(cells, LANES // 2, 1) * sin_b
        outs[hop][...] = dot_left(table, turned, ((1,), (1,)))


def cut_boxes(info, place, grid, phases, shift, planes, chunk, slots):
    handlers = info.shape[1] // slots
    kernel = functools.partial(
        cut_kernel, planes=planes, chunk=chunk, slots=slots, handlers=handlers
    )
    return call(
        kernel,
        [(32, LANES)] * handlers,
        [(handlers * LANES, LANES)],
        [info, place, grid, *phases, shift],
        2,
        10**8,
        "cut_boxes",
    )


def regrid_kernel(*refs, handlers):
    part_refs = refs[:handlers]
    matrix_ref, turn_ref, out_ref = refs[handlers:]
    total = part_refs[0][...]
    for part in part_refs[1:]:
        total = total + part[...]
    turn = turn_ref[...]
    cyclic = [total[8 * q : 8 * q + 8] for q in range(4)]

    def pick(values, sign, at):
        found = values[at]
        for by in range(1, 4):
            found = jnp.where(turn == by, values[(at + sign * by) % 4], found)
        return found

    cells = [pick(cyclic, 1, e) for e in range(4)]
    along = lax.broadcasted_iota(jnp.int32, (8, LANES), 0) % 4
    sums = [jnp.zeros((8, LANES), jnp.float32) for _ in range(4)]
    for source in range(4):
        for d_z in range(4):
            value = cells[source]
            if d_z:
                value = pltpu.roll(value, LANES - 32 * d_z, 1)
            for d_x in range(4):
                moved = value
                if d_x:
                    moved = jnp.where(
                        along + d_x < 4, pltpu.roll(value, 8 - d_x, 0), pltpu.roll(value, 4 - d_x, 0)
                    )
                for e in range(4):
                    at = 8 * (((e * 4 + source) * 4 + d_z) * 4 + d_x)
                    sums[e] = sums[e] + matrix_ref[at : at + 8] * moved
    out_ref[...] = jnp.concatenate([pick(sums, -1, q) for q in range(4)], axis=0)


def regrid(parts, matrix, turn):
    return call(
        functools.partial(regrid_kernel, handlers=len(parts)),
        [parts[0].shape],
        [],
        [*parts, matrix, turn],
        0,
        10**7,
        "regrid",
    )[0]


def place_kernel(info, place, cos_ref, sin_ref, shift_ref, *refs, planes, chunk, slots, handlers):
    u_refs = refs[:handlers]
    out_ref, gbuf = refs[handlers:]
    table = halves(shift_ref[...])
    for hop in range(handlers):
        handler = place[0] ^ hop
        at = pl.ds(pl.multiple_of(handler * slots, slots), slots)
        cos_b = jnp.concatenate([cos_ref[at, :]] * 4, axis=0)
        sin_b = jnp.concatenate([sin_ref[at, :]] * 4, axis=0)
        cells = dot_right(u_refs[hop][...].T, table)
        turned = cells * cos_b - pltpu.roll(cells, LANES // 2, 1) * sin_b
        gbuf[pl.ds(pl.multiple_of(handler * LANES, LANES), LANES), :] = turned
    out_ref[...] = jnp.zeros_like(out_ref)

    def put(group, carry):
        for inner in range(8):
            block = group * 8 + inner
            here, after = window_masks(info[2, block], chunk, 4, planes)
            at = block // slots * (4 * slots) + block % slots
            cells = gbuf[pl.ds(at, 4, stride=slots), :]
            first = pl.ds(info[0, block], 4)
            out_ref[first, :] = out_ref[first, :] + jnp.where(here, cells, 0.0)
            second = pl.ds(info[1, block], 4)
            out_ref[second, :] = out_ref[second, :] + jnp.where(after, cells, 0.0)
        return carry

    lax.fori_loop(0, handlers * slots // 8, put, 0)


def place_boxes(info, place, spread, phases, shift, planes, chunk, slots, length):
    handlers = len(spread)
    kernel = functools.partial(
        place_kernel, planes=planes, chunk=chunk, slots=slots, handlers=handlers
    )
    return call(
        kernel,
        [(length * (length // chunk), LANES)],
        [(handlers * LANES, LANES)],
        [info, place, *phases, shift, *spread],
        2,
        10**8,
        "place_boxes",
    )[0]


def back_y_kernel(k_ref, table_ref, out_ref, ybuf, *, planes, length, chunk):
    rows = length * planes
    for band in range(length // chunk):
        tile = k_ref[band * length : (band + 1) * length, :].T
        ybuf[band * 64 : (band + 1) * 64, :] = tile[:64]
        ybuf[rows + band * 64 : rows + (band + 1) * 64, :] = tile[64:]
    table = (table_ref[0], table_ref[1])
    for pair in range(planes // 2):
        columns = [
            jnp.concatenate(
                [ybuf[pl.ds(ri * rows + plane, length, stride=planes), :] for ri in range(2)],
                axis=0,
            )
            for plane in (2 * pair, 2 * pair + 1)
        ]
        done = dot_left(table, jnp.concatenate(columns, axis=1))
        for inner in range(2):
            for ri in range(2):
                out_ref[ri, 2 * pair + inner] = done[
                    ri * length : (ri + 1) * length, inner * LANES : (inner + 1) * LANES
                ]


def back_y(grid, tables, planes, length, chunk):
    kernel = functools.partial(back_y_kernel, planes=planes, length=length, chunk=chunk)
    return call(
        kernel,
        [(2, planes, length, length)],
        [(2 * length * planes, length)],
        [grid, tables],
        0,
        24 * planes * length**3,
        "back_y",
    )[0]


def back_z_kernel(starts, w_ref, s_ref, table_ref, *outs, pieces, planes, part, length):
    table = (table_ref[2], table_ref[3])
    batch = min(planes, 256 // part)
    for at, piece in enumerate(pieces):
        rows = pl.ds(pl.multiple_of(starts[piece], part), part)
        for base in range(0, planes, batch):
            bands = [
                jnp.concatenate([w_ref[0, plane, rows, :], w_ref[1, plane, rows, :]], axis=1)
                for plane in range(base, base + batch)
            ]
            done = dot_right(jnp.concatenate(bands, axis=0), table)
            i_re = done[:, :length].reshape(batch, part, length)
            i_im = done[:, length:].reshape(batch, part, length)
            s_re = s_ref[0, base : base + batch, rows, :]
            s_im = s_ref[1, base : base + batch, rows, :]
            outs[at][0, base : base + batch] = s_re * i_re + s_im * i_im
            outs[at][1, base : base + batch] = s_re * i_im - s_im * i_re


def back_z(starts, image, smap, tables, pieces, part):
    _, planes, length, _ = smap.shape
    kernel = functools.partial(
        back_z_kernel, pieces=pieces, planes=planes, part=part, length=length
    )
    flops = len(pieces) * planes * part * 24 * length * length
    return call(
        kernel,
        [(2, planes, part, length)] * len(pieces),
        [],
        [starts, image, smap, tables],
        1,
        flops,
        "back_z",
    )


def sums_kernel(*refs, terms):
    term_refs = refs[:terms]
    p_ref, r_ref, normal_ref, out_ref = refs[terms:]
    shape = p_ref.shape

    def add(plane, held):
        held = list(held)
        for ri in range(2):
            normal = term_refs[0][ri, plane]
            for term in term_refs[1:]:
                normal = normal + term[ri, plane]
            normal_ref[ri, plane] = normal
            p = p_ref[ri, plane]
            r = r_ref[ri, plane]
            for at, product in enumerate((r * r, p * normal, r * normal, normal * normal)):
                held[at] = held[at] + jnp.sum(product.reshape(-1, 8, LANES), axis=0)
        return tuple(held)

    start = tuple(jnp.zeros((8, LANES), jnp.float32) for _ in range(4))
    held = lax.fori_loop(0, shape[1], add, start, unroll=4)
    lane = lax.broadcasted_iota(jnp.int32, out_ref.shape, 1)
    found = jnp.zeros(out_ref.shape, jnp.float32)
    for at in range(4):
        found = jnp.where(lane == at, jnp.sum(held[at]), found)
    out_ref[...] = found


def sums(terms, p, r):
    kernel = functools.partial(sums_kernel, terms=len(terms))
    return call(kernel, [p.shape, (8, LANES)], [], [*terms, p, r], 0, 10**7, "sums")


def finish_kernel(total_ref, x_ref, r_ref, p_ref, normal_ref, x_out, r_out, p_out):
    total = total_ref[0:1, :]
    r_r, p_n, r_n, n_n = (total[:, at : at + 1] for at in range(4))
    alpha = r_r / p_n
    beta = (r_r + alpha * (alpha * n_n - 2.0 * r_n)) / r_r
    for plane in range(x_ref.shape[1]):
        for ri in range(2):
            p = p_ref[ri, plane]
            next_r = r_ref[ri, plane] - alpha * normal_ref[ri, plane]
            x_out[ri, plane] = x_ref[ri, plane] + alpha * p
            r_out[ri, plane] = next_r
            p_out[ri, plane] = next_r + beta * p


def finish(total, x, r, p, normal):
    return call(finish_kernel, [x.shape] * 3, [], [total, x, r, p, normal], 0, 10**7, "finish")


def matrices_kernel(weights_ref, out_ref, held, *, slots):
    def one(block, carry):
        w_x = weights_ref[block, 0]
        w_y = weights_ref[block, 1]
        w_z = weights_ref[block, 2]
        twice = jnp.concatenate([w_x, w_x], axis=0)
        along_x = [twice * pltpu.roll(twice, (8 - d) % 8, 0) if d else twice * twice for d in range(4)]
        right = []
        for f in range(4):
            for d_z in range(4):
                other = (f + d_z) % 4
                along_z = w_z[f : f + 1] * w_z[other : other + 1]
                right += [along_x[d_x] * along_z for d_x in range(4)]
        left = jnp.concatenate([w_y * w_y[e : e + 1] for e in range(4)], axis=0)
        high, low = halves(jnp.concatenate(right, axis=0))
        done = dot_right(left, (high, low), ((1,), (1,)))
        for f in range(4):
            held[pl.ds(f * slots + block, 16, stride=LANES), :] = done[
                :, f * LANES : (f + 1) * LANES
            ]
        return carry

    lax.fori_loop(0, slots, one, 0, unroll=2)

    def turn(pair, carry):
        at = pl.ds(pl.multiple_of(pair * LANES, LANES), LANES)
        out_ref[at, :] = held[at, :].T
        return carry

    lax.fori_loop(0, 16, turn, 0, unroll=2)


def block_matrices(weights):
    slots = weights.shape[0]
    return pl.pallas_call(
        functools.partial(matrices_kernel, slots=slots),
        out_shape=jax.ShapeDtypeStruct((16 * LANES, LANES), jnp.float32),
        in_specs=[pl.BlockSpec(memory_space=pltpu.VMEM)],
        out_specs=pl.BlockSpec(memory_space=pltpu.VMEM),
        scratch_shapes=[pltpu.VMEM((16 * LANES, LANES), jnp.float32)],
        compiler_params=pltpu.CompilerParams(vmem_limit_bytes=VMEM),
        name="matrices",
    )(weights)


def block_offsets(gathered, slots, ntile, capacity):
    owners = gathered[:, :slots]
    lists = gathered[:, slots:].reshape(ntile, 3, ntile, capacity)
    earlier = jnp.tril(jnp.ones((slots, slots), jnp.int32), -1)
    same = (owners[:, :, None] == owners[:, None, :]).astype(jnp.int32)
    ranks = jnp.sum(same * earlier[None], axis=2)
    wanted = owners * capacity + ranks
    lists = jnp.transpose(lists, (1, 2, 0, 3)).reshape(3, ntile, 1, ntile * capacity)
    hit = wanted[:, :, None] == jnp.arange(ntile * capacity, dtype=jnp.int32)
    found = jnp.sum(jnp.where(hit[None], lists, 0), axis=3)
    return found[0], found[1] + owners * (LANES // ntile), found[2]


def shards(image_p, image_x, image_r, sensitivity, kb_weights, block_owner, owner_list):
    ntile = lax.axis_size("tile")
    ncoil = lax.axis_size("coil")
    chips = ncoil // 2
    slots = kb_weights.shape[0]
    capacity = owner_list.shape[3]
    planes, length = image_p.shape[1], image_p.shape[3]
    part = image_p.shape[2]
    chunk = LANES // (2 * planes)
    tile = lax.axis_index("tile")
    coil = lax.axis_index("coil")
    chip, core = coil // 2, coil % 2

    mine = jnp.concatenate([block_owner, owner_list[:, 0].reshape(-1)])
    gathered = lax.all_to_all(
        jnp.broadcast_to(mine[None], (ntile, mine.shape[0])), "tile", 0, 0, tiled=True
    )

    def from_chip(values, by):
        pairs = [
            (a * 2 + k, (a - by) % chips * 2 + k) for a in range(chips) for k in range(2)
        ]
        return lax.ppermute(values, "coil", pairs)

    def to_chip(values, by):
        pairs = [
            (a * 2 + k, (a + by) % chips * 2 + k) for a in range(chips) for k in range(2)
        ]
        return lax.ppermute(values, "coil", pairs)

    def other_core(values):
        pairs = [(a * 2 + k, a * 2 + 1 - k) for a in range(chips) for k in range(2)]
        return lax.ppermute(values, "coil", pairs)

    p_same = [image_p] + [from_chip(image_p, by) for by in range(1, chips)]
    p_pieces = p_same + [other_core(piece) for piece in p_same]
    hops = jnp.arange(chips, dtype=jnp.int32)
    starts = jnp.concatenate(
        [((chip + hops) % chips * 2 + at) * part for at in (core, 1 - core)]
    )

    off_x, off_y, off_z = block_offsets(gathered, slots, ntile, capacity)
    band = off_y // chunk
    after = jnp.minimum(band + 1, length // chunk - 1)
    info = jnp.stack(
        [
            (band * length + off_z).reshape(-1),
            (after * length + off_z).reshape(-1),
            (off_y % chunk).reshape(-1),
        ]
    )
    lane = jnp.arange(LANES, dtype=jnp.int32)
    lane_ri = lane // (LANES // 2)
    lane_q = lane // planes % chunk
    lane_x = lane % planes + tile * planes
    unit = 2.0 * math.pi / length
    angle = unit * (off_x.reshape(-1, 1) * lane_x[None] % length).astype(jnp.float32)
    phases = (jnp.cos(angle), jnp.sin(angle) * jnp.where(lane_ri == 0, 1.0, -1.0)[None])
    row = jnp.arange(32, dtype=jnp.int32)[:, None]
    row_q, row_ri, row_i = row // 8, row // 4 % 2, row % 4
    angle = unit * (row_i * lane_x[None] % length).astype(jnp.float32)
    sine = jnp.where(row_ri == 0, 1.0, -1.0) * jnp.sin(angle)
    shift = jnp.where(row_ri == lane_ri[None], jnp.cos(angle), sine)
    shift = jnp.where(lane_q[None] % 4 == row_q, shift / math.sqrt(length), 0.0)
    tables = fourier_tables(length)
    matrix = block_matrices(kb_weights)
    own_y = lax.dynamic_index_in_dim(off_y, tile, 0, keepdims=True) % 4
    turn = jnp.broadcast_to(jnp.tile(own_y, (1, 4)), (8, LANES))
    place = tile[None]

    def over_tile(values, hop):
        return lax.ppermute(values, "tile", [(t, t ^ hop) for t in range(ntile)])

    smap = sensitivity[0]
    near = coil_z(starts, [p_pieces[0], p_pieces[chips]], [0, chips], smap, tables)
    far = coil_z(starts, p_pieces[1:chips], list(range(1, chips)), smap, tables)
    last = coil_z(starts, p_pieces[chips + 1 :], list(range(chips + 1, ncoil)), smap, tables)
    bands = [near[0], *far, near[1], *last]
    bands[-1], matrix, turn = lax.optimization_barrier((bands[-1], matrix, turn))
    grid = along_y(starts, bands, tables, chunk)
    partial = cut_boxes(info, place, grid, phases, shift, planes, chunk, slots)
    parts = [partial[0]] + [over_tile(partial[hop], hop) for hop in range(1, ntile)]
    done = regrid(parts, matrix, turn)
    spread = [done] + [over_tile(done, hop) for hop in range(1, ntile)]
    grid = place_boxes(info, place, spread, phases, shift, planes, chunk, slots, length)
    image = back_y(grid, tables, planes, length, chunk)
    away = [at for at in range(ncoil) if at % chips]
    made = back_z(starts, image, smap, tables, away, part)
    terms = [
        to_chip(made[by - 1] + other_core(made[chips - 1 + by - 1]), by) for by in range(1, chips)
    ]
    kept, sent = back_z(starts, image, smap, tables, [0, chips], part)
    terms += [kept, other_core(sent)]
    normal, total = sums(terms, image_p, image_r)
    for axis, size in (("coil", ncoil), ("tile", ntile)):
        hop = 1
        while hop < size:
            total = total + lax.ppermute(total, axis, [(t, t ^ hop) for t in range(size)])
            hop *= 2
    return tuple(finish(total, image_x, image_r, image_p, normal))


def solution(mesh):
    return jax.shard_map(
        shards,
        mesh=mesh,
        in_specs=(
            P(None, "tile", "coil", None),
            P(None, "tile", "coil", None),
            P(None, "tile", "coil", None),
            P("coil", None, "tile", None, None),
            P("tile", None, None, None),
            P("tile"),
            P(None, "tile", None, None),
        ),
        out_specs=(
            P(None, "tile", "coil", None),
            P(None, "tile", "coil", None),
            P(None, "tile", "coil", None),
        ),
        check_vma=False,
    )
```

```python
import functools
import math

import jax
import jax.numpy as jnp
import ml_dtypes
import numpy as np
from jax import lax
from jax.experimental import pallas as pl
from jax.experimental.pallas import tpu as pltpu
from jax.sharding import PartitionSpec as P

LANES = 128
VMEM = 24 * 1024 * 1024


def halves(values):
    high = values.astype(jnp.bfloat16)
    low = (values - high.astype(jnp.float32)).astype(jnp.bfloat16)
    return high, low


def dot_bf16(left, right, dims):
    return lax.dot_general(left, right, (dims, ((), ())), preferred_element_type=jnp.float32)


def dot_left(table, values, dims=((1,), (0,))):
    high, low = halves(values)
    return (
        dot_bf16(table[0], high, dims)
        + dot_bf16(table[0], low, dims)
        + dot_bf16(table[1], high, dims)
    )


def dot_right(values, table, dims=((1,), (0,))):
    high, low = halves(values)
    return (
        dot_bf16(high, table[0], dims)
        + dot_bf16(low, table[0], dims)
        + dot_bf16(high, table[1], dims)
    )


def fourier_tables(length):
    cells = np.arange(length)
    angle = 2.0 * math.pi / length * (cells[:, None] * cells[None, :] % length)
    cos_t = np.cos(angle) / math.sqrt(length)
    sin_t = np.sin(angle) / math.sqrt(length)
    found = []
    for sign in (1.0, -1.0):
        whole = np.block([[cos_t, -sign * sin_t], [sign * sin_t, cos_t]])
        high = whole.astype(ml_dtypes.bfloat16)
        low = (whole - high.astype(np.float64)).astype(ml_dtypes.bfloat16)
        found += [high, low]
    return jnp.asarray(np.stack(found))


def band_of_lane(planes, chunk):
    return lax.broadcasted_iota(jnp.int32, (4, LANES), 1) // planes % chunk


def in_window(band, first, chunk):
    past = band - first
    if chunk == 4:
        here = past >= 0
        return here, jnp.logical_not(here)
    here = jnp.logical_and(past >= 0, past < 4)
    return here, past < 4 - chunk


def call(kernel, outs, scratch, operands, smem, flops, name):
    specs = [pl.BlockSpec(memory_space=pltpu.SMEM)] * smem
    specs += [pl.BlockSpec(memory_space=pltpu.VMEM)] * (len(operands) - smem)
    moved = sum(math.prod(a.shape) * a.dtype.itemsize for a in operands)
    return pl.pallas_call(
        kernel,
        out_shape=[jax.ShapeDtypeStruct(shape, jnp.float32) for shape in outs],
        in_specs=specs,
        out_specs=[pl.BlockSpec(memory_space=pltpu.VMEM)] * len(outs),
        scratch_shapes=[pltpu.VMEM(shape, jnp.float32) for shape in scratch],
        compiler_params=pltpu.CompilerParams(vmem_limit_bytes=VMEM),
        cost_estimate=pl.CostEstimate(flops=flops, bytes_accessed=moved, transcendentals=0),
        name=name,
    )(*operands)


def coil_z_kernel(starts, *refs, quarters, planes, part, length):
    count = len(quarters)
    p_refs = refs[:count]
    s_ref, table_ref = refs[count : count + 2]
    outs = refs[count + 2 :]
    table = (table_ref[0], table_ref[1])
    batch = min(planes, 256 // part)
    for piece in range(count):
        rows = pl.ds(pl.multiple_of(starts[quarters[piece]], part), part)
        for base in range(0, planes, batch):
            bands = []
            for plane in range(base, base + batch):
                s_re = s_ref[0, plane, rows, :]
                s_im = s_ref[1, plane, rows, :]
                p_re = p_refs[piece][0, plane]
                p_im = p_refs[piece][1, plane]
                bands.append(
                    jnp.concatenate([s_re * p_re - s_im * p_im, s_re * p_im + s_im * p_re], axis=1)
                )
            done = dot_right(jnp.concatenate(bands, axis=0), table)
            for ri in range(2):
                half = done[:, ri * length : (ri + 1) * length]
                outs[piece][ri, base : base + batch] = half.reshape(batch, part, length)


def coil_z(starts, pieces, quarters, smap, tables):
    _, planes, part, length = pieces[0].shape
    count = len(pieces)
    kernel = functools.partial(
        coil_z_kernel, quarters=quarters, planes=planes, part=part, length=length
    )
    flops = count * planes * part * 24 * length * length
    return call(
        kernel, [pieces[0].shape] * count, [], [starts, *pieces, smap, tables], 1, flops, "coil_z"
    )


def along_y_kernel(starts, *refs, pieces, planes, part, length, chunk):
    t_refs = refs[:pieces]
    table_ref, out_ref, natural, ybuf = refs[pieces:]
    rows = length * planes
    table = (table_ref[2], table_ref[3])
    for piece in range(pieces):
        at = pl.ds(pl.multiple_of(starts[piece], part), part)
        for plane in range(planes):
            for ri in range(2):
                natural[ri, plane, at, :] = t_refs[piece][ri, plane]
    for pair in range(planes // 2):
        columns = [
            jnp.concatenate([natural[0, plane], natural[1, plane]], axis=0)
            for plane in (2 * pair, 2 * pair + 1)
        ]
        done = dot_left(table, jnp.concatenate(columns, axis=1))
        for inner in range(2):
            for ri in range(2):
                ybuf[pl.ds(ri * rows + 2 * pair + inner, length, stride=planes), :] = done[
                    ri * length : (ri + 1) * length, inner * LANES : (inner + 1) * LANES
                ]
    for band in range(length // chunk):
        re = ybuf[band * 64 : (band + 1) * 64, :]
        im = ybuf[rows + band * 64 : rows + (band + 1) * 64, :]
        out_ref[band * length : (band + 1) * length, :] = jnp.concatenate([re, im], axis=0).T


def along_y(starts, pieces, tables, chunk):
    _, planes, part, length = pieces[0].shape
    kernel = functools.partial(
        along_y_kernel, pieces=len(pieces), planes=planes, part=part, length=length, chunk=chunk
    )
    return call(
        kernel,
        [(length * (length // chunk + 1), LANES)],
        [(2, planes, length, length), (2 * length * planes, length)],
        [starts, *pieces, tables],
        1,
        24 * planes * length**3,
        "along_y",
    )[0]


def cut_kernel(info, k_ref, cos_ref, sin_ref, shift_ref, out_ref, gbuf, *, planes, chunk, slots):
    handlers = out_ref.shape[0]
    band = band_of_lane(planes, chunk)

    def cut(group, carry):
        for inner in range(8):
            block = group * 8 + inner
            here, after = in_window(band, info[1, block], chunk)
            first = k_ref[pl.ds(info[0, block], 4), :]
            second = k_ref[pl.ds(info[0, block] + LANES, 4), :]
            if chunk > 4:
                second = jnp.where(after, second, 0.0)
            to = block // slots * (4 * slots) + block % slots
            gbuf[pl.ds(to, 4, stride=slots), :] = jnp.where(here, first, second)
        return carry

    lax.fori_loop(0, handlers * slots // 8, cut, 0)
    table = halves(shift_ref[...])
    for handler in range(handlers):
        cos_b = jnp.concatenate([cos_ref[handler * slots : (handler + 1) * slots, :]] * 4, axis=0)
        sin_b = jnp.concatenate([sin_ref[handler * slots : (handler + 1) * slots, :]] * 4, axis=0)
        cells = gbuf[handler * LANES : (handler + 1) * LANES, :]
        turned = cells * cos_b + pltpu.roll(cells, LANES // 2, 1) * sin_b
        out_ref[handler] = dot_left(table, turned, ((1,), (1,)))


def cut_boxes(info, grid, phases, shift, planes, chunk, slots):
    handlers = info.shape[1] // slots
    return call(
        functools.partial(cut_kernel, planes=planes, chunk=chunk, slots=slots),
        [(handlers, 32, LANES)],
        [(handlers * LANES, LANES)],
        [info, grid, *phases, shift],
        1,
        10**8,
        "cut_boxes",
    )[0]


def regrid_kernel(parts_ref, matrix_ref, turn_ref, out_ref):
    total = parts_ref[0]
    for at in range(1, parts_ref.shape[0]):
        total = total + parts_ref[at]
    turn = turn_ref[...]
    cyclic = [total[8 * q : 8 * q + 8] for q in range(4)]

    def pick(values, sign, at):
        found = values[at]
        for by in range(1, 4):
            found = jnp.where(turn == by, values[(at + sign * by) % 4], found)
        return found

    cells = [pick(cyclic, 1, e) for e in range(4)]
    along = lax.broadcasted_iota(jnp.int32, (8, LANES), 0) % 4
    sums = [jnp.zeros((8, LANES), jnp.float32) for _ in range(4)]
    for source in range(4):
        for d_z in range(4):
            value = cells[source]
            if d_z:
                value = pltpu.roll(value, LANES - 32 * d_z, 1)
            for d_x in range(4):
                moved = value
                if d_x:
                    moved = jnp.where(
                        along + d_x < 4, pltpu.roll(value, 8 - d_x, 0), pltpu.roll(value, 4 - d_x, 0)
                    )
                for e in range(4):
                    at = 8 * (((e * 4 + source) * 4 + d_z) * 4 + d_x)
                    sums[e] = sums[e] + matrix_ref[at : at + 8] * moved
    done = jnp.concatenate([pick(sums, -1, q) for q in range(4)], axis=0)
    for at in range(out_ref.shape[0]):
        out_ref[at] = done


def regrid(parts, matrix, turn, copies):
    return call(
        regrid_kernel,
        [(copies,) + parts.shape[1:]],
        [],
        [parts, matrix, turn],
        0,
        10**7,
        "regrid",
    )[0]


def place_kernel(
    info, chip, u_ref, cos_ref, sin_ref, shift_ref, *refs, planes, chunk, slots, chips, handlers
):
    outs, gbufs = refs[:chips], refs[chips:]
    table = halves(shift_ref[...])
    for handler in range(handlers):
        cos_b = jnp.concatenate([cos_ref[handler * slots : (handler + 1) * slots, :]] * 4, axis=0)
        sin_b = jnp.concatenate([sin_ref[handler * slots : (handler + 1) * slots, :]] * 4, axis=0)
        for hop in range(chips):
            cells = dot_right(u_ref[chip[hop] * handlers + handler].T, table)
            turned = cells * cos_b - pltpu.roll(cells, LANES // 2, 1) * sin_b
            gbufs[hop][handler * LANES : (handler + 1) * LANES, :] = turned
    for out in outs:
        out[...] = jnp.zeros_like(out)
    band = band_of_lane(planes, chunk)

    def put(group, carry):
        for inner in range(8):
            block = group * 8 + inner
            here, after = in_window(band, info[1, block], chunk)
            at = pl.ds(block // slots * (4 * slots) + block % slots, 4, stride=slots)
            first = pl.ds(info[0, block], 4)
            second = pl.ds(info[0, block] + LANES, 4)
            for hop in range(chips):
                cells = gbufs[hop][at, :]
                old_first = outs[hop][first, :]
                old_second = outs[hop][second, :]
                outs[hop][first, :] = old_first + jnp.where(here, cells, 0.0)
                outs[hop][second, :] = old_second + jnp.where(after, cells, 0.0)
        return carry

    lax.fori_loop(0, handlers * slots // 8, put, 0)


def place_boxes(info, chip_order, spread, phases, shift, planes, chunk, slots, length):
    handlers = info.shape[1] // slots
    chips = spread.shape[0] // handlers
    kernel = functools.partial(
        place_kernel, planes=planes, chunk=chunk, slots=slots, chips=chips, handlers=handlers
    )
    return call(
        kernel,
        [(length * (length // chunk + 1), LANES)] * chips,
        [(handlers * LANES, LANES)] * chips,
        [info, chip_order, spread, *phases, shift],
        2,
        10**8,
        "place_boxes",
    )


def back_y_kernel(chip, *refs, chips, planes, length, chunk):
    k_refs = refs[:chips]
    table_ref = refs[chips]
    outs, ybuf = refs[chips + 1 : -1], refs[-1]
    rows = length * planes
    own = length // chips
    table = []
    for half in range(2):
        parts = [
            table_ref[half, pl.ds(pl.multiple_of(ri * length + chip[0] * own, own), own), :]
            for ri in range(2)
        ]
        table.append(jnp.concatenate(parts, axis=0))
    for hop in range(chips):
        for band in range(length // chunk):
            tile = k_refs[hop][band * length : (band + 1) * length, :].T
            ybuf[hop, band * 64 : (band + 1) * 64, :] = tile[:64]
            ybuf[hop, rows + band * 64 : rows + (band + 1) * 64, :] = tile[64:]
        for pair in range(planes // 2):
            columns = [
                jnp.concatenate(
                    [
                        ybuf[hop, pl.ds(ri * rows + plane, length, stride=planes), :]
                        for ri in range(2)
                    ],
                    axis=0,
                )
                for plane in (2 * pair, 2 * pair + 1)
            ]
            done = dot_left(table, jnp.concatenate(columns, axis=1))
            for inner in range(2):
                for ri in range(2):
                    outs[hop][ri, 2 * pair + inner] = done[
                        ri * own : (ri + 1) * own, inner * LANES : (inner + 1) * LANES
                    ]


def back_y(chip_order, grids, tables, planes, length, chunk):
    chips = len(grids)
    kernel = functools.partial(
        back_y_kernel, chips=chips, planes=planes, length=length, chunk=chunk
    )
    return call(
        kernel,
        [(2, planes, length // chips, length)] * chips,
        [(chips, 2 * length * planes, length)],
        [chip_order, *grids, tables],
        1,
        24 * planes * length**3,
        "back_y",
    )


def back_z_kernel(place, *refs, chips, planes, part, length):
    w_refs = refs[:chips]
    s_refs = refs[chips : 2 * chips]
    table_ref, out_ref = refs[2 * chips :]
    table = (table_ref[2], table_ref[3])
    batch = min(planes, 256 // part)
    rows = pl.ds(pl.multiple_of(place[1] * part, part), part)
    for base in range(0, planes, batch):
        total_re, total_im = 0.0, 0.0
        for hop in range(chips):
            bands = [
                jnp.concatenate([w_refs[hop][ri, plane, rows, :] for ri in range(2)], axis=1)
                for plane in range(base, base + batch)
            ]
            done = dot_right(jnp.concatenate(bands, axis=0), table)
            i_re = done[:, :length].reshape(batch, part, length)
            i_im = done[:, length:].reshape(batch, part, length)
            s_rows = rows if hop else pl.ds(pl.multiple_of(place[0] * part, part), part)
            s_re = s_refs[hop][0, base : base + batch, s_rows, :]
            s_im = s_refs[hop][1, base : base + batch, s_rows, :]
            total_re = total_re + (s_re * i_re + s_im * i_im)
            total_im = total_im + (s_re * i_im - s_im * i_re)
        out_ref[0, base : base + batch] = total_re
        out_ref[1, base : base + batch] = total_im


def back_z(place, images, maps, tables, part):
    _, planes, _, length = images[0].shape
    chips = len(images)
    kernel = functools.partial(
        back_z_kernel, chips=chips, planes=planes, part=part, length=length
    )
    return call(
        kernel,
        [(2, planes, part, length)],
        [],
        [place, *images, *maps, tables],
        1,
        chips * planes * part * 24 * length * length,
        "back_z",
    )[0]


def sums_kernel(*refs, terms):
    term_refs = refs[:terms]
    p_ref, r_ref, normal_ref, out_ref = refs[terms:]
    shape = p_ref.shape

    def add(plane, held):
        held = list(held)
        for ri in range(2):
            normal = term_refs[0][ri, plane]
            for term in term_refs[1:]:
                normal = normal + term[ri, plane]
            normal_ref[ri, plane] = normal
            p = p_ref[ri, plane]
            r = r_ref[ri, plane]
            for at, product in enumerate((r * r, p * normal, r * normal, normal * normal)):
                held[at] = held[at] + jnp.sum(product.reshape(-1, 8, LANES), axis=0)
        return tuple(held)

    start = tuple(jnp.zeros((8, LANES), jnp.float32) for _ in range(4))
    held = lax.fori_loop(0, shape[1], add, start, unroll=4)
    lane = lax.broadcasted_iota(jnp.int32, out_ref.shape, 1)
    found = jnp.zeros(out_ref.shape, jnp.float32)
    for at in range(4):
        found = jnp.where(lane == at, jnp.sum(held[at]), found)
    out_ref[...] = found


def sums(terms, p, r, devices):
    kernel = functools.partial(sums_kernel, terms=len(terms))
    return call(kernel, [p.shape, (devices, LANES)], [], [*terms, p, r], 0, 10**7, "sums")


def finish_kernel(total_ref, x_ref, r_ref, p_ref, normal_ref, x_out, r_out, p_out):
    total = jnp.sum(total_ref[...], axis=0, keepdims=True)
    r_r, p_n, r_n, n_n = (total[:, at : at + 1] for at in range(4))
    alpha = r_r / p_n
    beta = (r_r + alpha * (alpha * n_n - 2.0 * r_n)) / r_r
    for plane in range(x_ref.shape[1]):
        for ri in range(2):
            p = p_ref[ri, plane]
            next_r = r_ref[ri, plane] - alpha * normal_ref[ri, plane]
            x_out[ri, plane] = x_ref[ri, plane] + alpha * p
            r_out[ri, plane] = next_r
            p_out[ri, plane] = next_r + beta * p


def finish(total, x, r, p, normal):
    return call(finish_kernel, [x.shape] * 3, [], [total, x, r, p, normal], 0, 10**7, "finish")


def matrices_kernel(weights_ref, out_ref, held, *, slots):
    def one(block, carry):
        w_x = weights_ref[block, 0]
        w_y = weights_ref[block, 1]
        w_z = weights_ref[block, 2]
        twice = jnp.concatenate([w_x, w_x], axis=0)
        rolled = [twice] + [pltpu.roll(twice, 8 - d, 0) for d in range(1, 4)]
        low = lax.broadcasted_iota(jnp.int32, (8, LANES), 0) < 4
        along_x = [twice * jnp.where(low, rolled[d], rolled[d + 1]) for d in (0, 2)]
        right = []
        for f in range(4):
            for d_z in range(4):
                other = (f + d_z) % 4
                along_z = w_z[f : f + 1] * w_z[other : other + 1]
                right += [along * along_z for along in along_x]
        left = jnp.concatenate([w_y * w_y[e : e + 1] for e in range(4)], axis=0)
        done = dot_right(left, halves(jnp.concatenate(right, axis=0)), ((1,), (1,)))
        for f in range(4):
            lanes = done[:, f // 2 * LANES : (f // 2 + 1) * LANES]
            if f % 2:
                lanes = pltpu.roll(lanes, LANES // 2, 1)
            held[pl.ds(f * slots + block, 16, stride=LANES), :] = lanes
        return carry

    lax.fori_loop(0, slots, one, 0, unroll=4)

    def turn(pair, carry):
        at = pl.ds(pl.multiple_of(pair * LANES, LANES), LANES)
        rows = held[at, :].T
        for group in range(16):
            four = rows[4 * group : 4 * group + 4]
            out_ref[pl.ds(pl.multiple_of(pair * LANES + 8 * group, 8), 8), :] = jnp.concatenate(
                [four, four], axis=0
            )
        return carry

    lax.fori_loop(0, 16, turn, 0, unroll=2)


def block_matrices(weights):
    slots = weights.shape[0]
    return pl.pallas_call(
        functools.partial(matrices_kernel, slots=slots),
        out_shape=jax.ShapeDtypeStruct((16 * LANES, LANES), jnp.float32),
        in_specs=[pl.BlockSpec(memory_space=pltpu.VMEM)],
        out_specs=pl.BlockSpec(memory_space=pltpu.VMEM),
        scratch_shapes=[pltpu.VMEM((16 * LANES, LANES), jnp.float32)],
        compiler_params=pltpu.CompilerParams(vmem_limit_bytes=VMEM),
        name="matrices",
    )(weights)


def block_offsets(gathered, slots, ntile, capacity):
    owners = gathered[:, :slots]
    lists = gathered[:, slots:].reshape(ntile, 3, ntile, capacity)
    earlier = jnp.tril(jnp.ones((slots, slots), jnp.int32), -1)
    same = (owners[:, :, None] == owners[:, None, :]).astype(jnp.int32)
    ranks = jnp.sum(same * earlier[None], axis=2)
    wanted = owners * capacity + ranks
    lists = jnp.transpose(lists, (1, 2, 0, 3)).reshape(3, ntile, 1, ntile * capacity)
    hit = wanted[:, :, None] == jnp.arange(ntile * capacity, dtype=jnp.int32)
    found = jnp.sum(jnp.where(hit[None], lists, 0), axis=3)
    return found[0], found[1] + owners * (LANES // ntile), found[2]


def shards(image_p, image_x, image_r, sensitivity, kb_weights, block_owner, owner_list):
    ntile = lax.axis_size("tile")
    ncoil = lax.axis_size("coil")
    chips = ncoil // 2
    slots = kb_weights.shape[0]
    capacity = owner_list.shape[3]
    planes, length = image_p.shape[1], image_p.shape[3]
    part = image_p.shape[2]
    chunk = LANES // (2 * planes)
    tile = lax.axis_index("tile")
    coil = lax.axis_index("coil")
    chip, core = coil // 2, coil % 2
    smap = sensitivity[0]
    tables = fourier_tables(length)

    def from_chip(values, by):
        pairs = [
            (a * 2 + k, (a - by) % chips * 2 + k) for a in range(chips) for k in range(2)
        ]
        return lax.ppermute(values, "coil", pairs)

    def other_core(values):
        pairs = [(a * 2 + k, a * 2 + 1 - k) for a in range(chips) for k in range(2)]
        return lax.ppermute(values, "coil", pairs)

    hops = jnp.arange(chips, dtype=jnp.int32)
    chip_order = (chip + hops) % chips
    starts = jnp.concatenate([(chip_order * 2 + at) * part for at in (core, 1 - core)])

    p_same = [image_p] + [from_chip(image_p, by) for by in range(1, chips)]
    p_other = [other_core(piece) for piece in p_same]
    mine = jnp.concatenate([block_owner, owner_list[:, 0].reshape(-1)])
    gathered = lax.all_to_all(
        jnp.broadcast_to(mine[None], (ntile, mine.shape[0])), "tile", 0, 0, tiled=True
    )
    near = coil_z(starts, [p_same[0], p_other[0]], [0, chips], smap, tables)
    far = coil_z(starts, p_same[1:], list(range(1, chips)), smap, tables)
    last = coil_z(starts, p_other[1:], list(range(chips + 1, ncoil)), smap, tables)

    late_map, _ = lax.optimization_barrier((smap, tuple(p_same[1:])))
    maps = [smap]
    for by in range(1, chips):
        rows = (chip - by) % chips * (2 * part)
        maps.append(from_chip(lax.dynamic_slice_in_dim(late_map, rows, 2 * part, 2), by))

    off_x, off_y, off_z = block_offsets(gathered, slots, ntile, capacity)
    info = jnp.stack(
        [(off_y // chunk * length + off_z).reshape(-1), (off_y % chunk).reshape(-1)]
    )
    lane = jnp.arange(LANES, dtype=jnp.int32)
    lane_ri = lane // (LANES // 2)
    lane_q = lane // planes % chunk
    lane_x = lane % planes + tile * planes
    unit = 2.0 * math.pi / length
    angle = unit * (off_x.reshape(-1, 1) * lane_x[None] % length).astype(jnp.float32)
    phases = (jnp.cos(angle), jnp.sin(angle) * jnp.where(lane_ri == 0, 1.0, -1.0)[None])
    row = jnp.arange(32, dtype=jnp.int32)[:, None]
    row_q, row_ri, row_i = row // 8, row // 4 % 2, row % 4
    angle = unit * (row_i * lane_x[None] % length).astype(jnp.float32)
    sine = jnp.where(row_ri == 0, 1.0, -1.0) * jnp.sin(angle)
    shift = jnp.where(row_ri == lane_ri[None], jnp.cos(angle), sine)
    shift = jnp.where(lane_q[None] % 4 == row_q, shift / math.sqrt(length), 0.0)
    own_y = lax.dynamic_index_in_dim(off_y, tile, 0, keepdims=True) % 4
    turn = jnp.broadcast_to(jnp.tile(own_y, (1, 4)), (8, LANES))

    bands = [near[0], *far, near[1], *last]
    bands[0], turn = lax.optimization_barrier((bands[0], turn))
    grid = along_y(starts, bands, tables, chunk)
    partial = cut_boxes(info, grid, phases, shift, planes, chunk, slots)
    partial, weights = lax.optimization_barrier((partial, kb_weights))
    parts = lax.all_to_all(partial, "tile", 0, 0, tiled=True)
    done = regrid(parts, block_matrices(weights), turn, chips * ntile)
    groups = [
        [at * ntile + t for at in range(ncoil) if at % 2 == k for t in range(ntile)]
        for k in range(2)
    ]
    spread = lax.all_to_all(
        done, ("coil", "tile"), 0, 0, axis_index_groups=groups, tiled=True
    )
    grids = place_boxes(info, chip_order, spread, phases, shift, planes, chunk, slots, length)
    images = back_y(chip_order, grids, tables, planes, length, chunk)
    halves_of = [jnp.stack([chip * 2 + at, at]) for at in (1 - core, core)]
    sent = back_z(halves_of[0], images, maps, tables, part)
    kept = back_z(halves_of[1], images, maps, tables, part)
    normal, found = sums([kept, other_core(sent)], image_p, image_r, ncoil * ntile)
    total = lax.all_to_all(found, ("coil", "tile"), 0, 0, tiled=True)
    return tuple(finish(total, image_x, image_r, image_p, normal))


def solution(mesh):
    return jax.shard_map(
        shards,
        mesh=mesh,
        in_specs=(
            P(None, "tile", "coil", None),
            P(None, "tile", "coil", None),
            P(None, "tile", "coil", None),
            P("coil", None, "tile", None, None),
            P("tile", None, None, None),
            P("tile"),
            P(None, "tile", None, None),
        ),
        out_specs=(
            P(None, "tile", "coil", None),
            P(None, "tile", "coil", None),
            P(None, "tile", "coil", None),
        ),
        check_vma=False,
    )
```

```python
import functools
import math

import jax
import jax.numpy as jnp
import ml_dtypes
import numpy as np
from jax import lax
from jax.experimental import pallas as pl
from jax.experimental.pallas import tpu as pltpu
from jax.sharding import PartitionSpec as P

LANES = 128
VMEM = 24 * 1024 * 1024


def halves(values):
    high = values.astype(jnp.bfloat16)
    low = (values - high.astype(jnp.float32)).astype(jnp.bfloat16)
    return high, low


def dot_bf16(left, right, dims):
    return lax.dot_general(left, right, (dims, ((), ())), preferred_element_type=jnp.float32)


def dot_left(table, values, dims=((1,), (0,))):
    high, low = halves(values)
    return (
        dot_bf16(table[0], high, dims)
        + dot_bf16(table[0], low, dims)
        + dot_bf16(table[1], high, dims)
    )


def dot_right(values, table, dims=((1,), (0,))):
    high, low = halves(values)
    return (
        dot_bf16(high, table[0], dims)
        + dot_bf16(low, table[0], dims)
        + dot_bf16(high, table[1], dims)
    )


def fourier_tables(length):
    cells = np.arange(length)
    angle = 2.0 * math.pi / length * (cells[:, None] * cells[None, :] % length)
    cos_t = np.cos(angle) / math.sqrt(length)
    sin_t = np.sin(angle) / math.sqrt(length)
    found = []
    for sign in (1.0, -1.0):
        whole = np.block([[cos_t, -sign * sin_t], [sign * sin_t, cos_t]])
        high = whole.astype(ml_dtypes.bfloat16)
        low = (whole - high.astype(np.float64)).astype(ml_dtypes.bfloat16)
        found += [high, low]
    return jnp.asarray(np.stack(found))


def band_of_lane(planes, chunk):
    return lax.broadcasted_iota(jnp.int32, (4, LANES), 1) // planes % chunk


def in_window(band, first, chunk):
    past = band - first
    if chunk == 4:
        here = past >= 0
        return here, jnp.logical_not(here)
    here = jnp.logical_and(past >= 0, past < 4)
    return here, past < 4 - chunk


def call(kernel, outs, scratch, operands, smem, flops, name, hbm=(), limit=VMEM):
    specs = [pl.BlockSpec(memory_space=pltpu.SMEM)] * smem
    specs += [pl.BlockSpec(memory_space=pltpu.VMEM)] * (len(operands) - smem)
    for at in hbm:
        specs[at] = pl.BlockSpec(memory_space=pltpu.HBM)
    moved = sum(math.prod(a.shape) * a.dtype.itemsize for a in operands)
    return pl.pallas_call(
        kernel,
        out_shape=[jax.ShapeDtypeStruct(shape, jnp.float32) for shape in outs],
        in_specs=specs,
        out_specs=[pl.BlockSpec(memory_space=pltpu.VMEM)] * len(outs),
        scratch_shapes=[
            pltpu.VMEM(shape, jnp.float32) if isinstance(shape, tuple) else shape
            for shape in scratch
        ],
        compiler_params=pltpu.CompilerParams(vmem_limit_bytes=limit),
        cost_estimate=pl.CostEstimate(flops=flops, bytes_accessed=moved, transcendentals=0),
        name=name,
    )(*operands)


def z_of_coil(p_ref, s_ref, out_ref, rows, table):
    _, planes, part, length = p_ref.shape
    batch = min(planes, 256 // part)
    for base in range(0, planes, batch):
        bands = []
        for plane in range(base, base + batch):
            s_re = s_ref[0, plane, rows, :]
            s_im = s_ref[1, plane, rows, :]
            p_re = p_ref[0, plane]
            p_im = p_ref[1, plane]
            bands.append(
                jnp.concatenate([s_re * p_re - s_im * p_im, s_re * p_im + s_im * p_re], axis=1)
            )
        done = dot_right(jnp.concatenate(bands, axis=0), table)
        for ri in range(2):
            half = done[:, ri * length : (ri + 1) * length]
            out_ref[ri, base : base + batch] = half.reshape(batch, part, length)


def quarter(starts, at, part):
    return pl.ds(pl.multiple_of(starts[at], part), part)


def coil_z_kernel(starts, *refs, quarters, sends):
    count = len(quarters)
    p_refs = refs[:count]
    s_ref, table_ref = refs[count : count + 2]
    outs = refs[count + 2 :]
    part = p_refs[0].shape[2]
    table = (table_ref[0], table_ref[1])
    for at in range(count):
        z_of_coil(p_refs[at], s_ref, outs[at], quarter(starts, quarters[at], part), table)
    chips = sends + 1
    for by in range(1, chips):
        hop = chips - by
        for half in range(2):
            rows = quarter(starts, half * chips + hop, part)
            to = quarter(starts, 2 * chips + half, part)
            for ri in range(2):
                outs[count + by - 1][ri, :, to, :] = s_ref[ri, :, rows, :]


def coil_z(starts, pieces, quarters, smap, tables, sends=0):
    _, planes, part, length = pieces[0].shape
    count = len(pieces)
    return call(
        functools.partial(coil_z_kernel, quarters=quarters, sends=sends),
        [pieces[0].shape] * count + [(2, planes, 2 * part, length)] * sends,
        [],
        [starts, *pieces, smap, tables],
        1,
        count * planes * part * 24 * length * length,
        "coil_z",
    )


def cut_boxes(info, grid, cos_ref, sin_ref, shift_ref, out_ref, gbuf, planes, chunk, slots):
    handlers = out_ref.shape[0]
    band = band_of_lane(planes, chunk)

    def cut(handler, carry):
        base = pl.multiple_of(handler * LANES, LANES)
        for slot in range(slots):
            block = handler * slots + slot
            here, after = in_window(band, info[1, block], chunk)
            first = grid[pl.ds(info[0, block], 4), :]
            second = grid[pl.ds(info[0, block] + LANES, 4), :]
            if chunk > 4:
                second = jnp.where(after, second, 0.0)
            gbuf[pl.ds(base + slot, 4, stride=slots), :] = jnp.where(here, first, second)
        return carry

    lax.fori_loop(0, handlers, cut, 0)
    high, low = halves(shift_ref[...])
    table = jnp.concatenate(
        [
            jnp.concatenate([high, high], axis=1),
            jnp.concatenate([low, jnp.zeros_like(low)], axis=1),
        ],
        axis=0,
    )
    for handler in range(handlers):
        rows = slice(handler * slots, (handler + 1) * slots)
        cos_b = jnp.concatenate([cos_ref[rows, :]] * 4, axis=0)
        sin_b = jnp.concatenate([sin_ref[rows, :]] * 4, axis=0)
        cells = gbuf[handler * LANES : (handler + 1) * LANES, :]
        turned = cells * cos_b + pltpu.roll(cells, LANES // 2, 1) * sin_b
        both = dot_bf16(table, jnp.concatenate(halves(turned), axis=1), ((1,), (1,)))
        out_ref[handler] = both[:32] + both[32:]


def forward_kernel(info, starts, *refs, done, pieces, planes, part, length, chunk, slots):
    t_refs = refs[:done]
    p_refs = refs[done:pieces]
    s_ref, table_ref, cos_ref, sin_ref, shift_ref = refs[pieces : pieces + 5]
    out_ref, natural, ybuf, grid, gbuf, late = refs[pieces + 5 :]
    rows = length * planes
    table = (table_ref[0], table_ref[1])
    for at in range(done, pieces):
        z_of_coil(p_refs[at - done], s_ref, late.at[at - done], quarter(starts, at, part), table)
    for at in range(pieces):
        to = quarter(starts, at, part)
        source = t_refs[at] if at < done else late.at[at - done]
        for ri in range(2):
            natural[ri, :, to, :] = source[ri]
    table = (table_ref[2], table_ref[3])
    for pair in range(planes // 2):
        columns = [
            jnp.concatenate([natural[0, plane], natural[1, plane]], axis=0)
            for plane in (2 * pair, 2 * pair + 1)
        ]
        both = dot_left(table, jnp.concatenate(columns, axis=1))
        for inner in range(2):
            for ri in range(2):
                ybuf[pl.ds(ri * rows + 2 * pair + inner, length, stride=planes), :] = both[
                    ri * length : (ri + 1) * length, inner * LANES : (inner + 1) * LANES
                ]
    for band in range(length // chunk):
        re = ybuf[band * 64 : (band + 1) * 64, :]
        im = ybuf[rows + band * 64 : rows + (band + 1) * 64, :]
        grid[band * length : (band + 1) * length, :] = jnp.concatenate([re, im], axis=0).T
    cut_boxes(info, grid, cos_ref, sin_ref, shift_ref, out_ref, gbuf, planes, chunk, slots)


def forward(info, starts, done, rest, smap, tables, phases, shift, chunk, slots):
    _, planes, part, length = done[0].shape
    pieces = len(done) + len(rest)
    handlers = info.shape[1] // slots
    kernel = functools.partial(
        forward_kernel, done=len(done), pieces=pieces, planes=planes, part=part, length=length,
        chunk=chunk, slots=slots,
    )
    return call(
        kernel,
        [(handlers, 32, LANES)],
        [
            (2, planes, length, length),
            (2 * length * planes, length),
            (length * (length // chunk + 1), LANES),
            (handlers * LANES, LANES),
            (len(rest), 2, planes, part, length),
        ],
        [info, starts, *done, *rest, smap, tables, *phases, shift],
        2,
        48 * planes * length**3,
        "forward",
    )[0]


def regrid_kernel(parts_ref, matrix_ref, out_ref, held, done_sem):
    total = parts_ref[0]
    for at in range(1, parts_ref.shape[0]):
        total = total + parts_ref[at]
    along = lax.broadcasted_iota(jnp.int32, (8, LANES), 0) % 4
    sums = [jnp.zeros((8, LANES), jnp.float32) for _ in range(4)]
    for source in range(4):
        for d_z in range(4):
            value = total[8 * source : 8 * source + 8]
            if d_z:
                value = pltpu.roll(value, LANES - 32 * d_z, 1)
            for d_x in range(4):
                moved = value
                if d_x:
                    moved = jnp.where(
                        along + d_x < 4, pltpu.roll(value, 8 - d_x, 0), pltpu.roll(value, 4 - d_x, 0)
                    )
                for e in range(4):
                    at = 8 * (((e * 4 + source) * 4 + d_z) * 4 + d_x)
                    sums[e] = sums[e] + matrix_ref[at : at + 8] * moved
    done = jnp.concatenate(sums, axis=0)
    for at in range(held.shape[0]):
        held[at] = done
    copy = pltpu.make_async_copy(held, out_ref, done_sem)
    copy.start()
    copy.wait()


def regrid(parts, matrix, copies):
    shape = (copies,) + parts.shape[1:]
    return pl.pallas_call(
        regrid_kernel,
        out_shape=jax.ShapeDtypeStruct(shape, jnp.float32),
        in_specs=[pl.BlockSpec(memory_space=pltpu.VMEM)] * 2,
        out_specs=pl.BlockSpec(memory_space=pltpu.HBM),
        scratch_shapes=[pltpu.VMEM(shape, jnp.float32), pltpu.SemaphoreType.DMA],
        compiler_params=pltpu.CompilerParams(vmem_limit_bytes=VMEM // 2),
        cost_estimate=pl.CostEstimate(flops=10**7, bytes_accessed=10**6, transcendentals=0),
        name="regrid",
    )(parts, matrix)


def place_boxes(info, chip, u_ref, cos_ref, sin_ref, shift_ref, outs, gbufs, planes, chunk, slots):
    chips = len(outs)
    handlers = u_ref.shape[0] // chips
    high, low = halves(shift_ref[...])
    table = jnp.concatenate([high, high, low, jnp.zeros_like(low)], axis=0)
    for handler in range(handlers):
        rows = slice(handler * slots, (handler + 1) * slots)
        cos_b = jnp.concatenate([cos_ref[rows, :]] * 4, axis=0)
        sin_b = jnp.concatenate([sin_ref[rows, :]] * 4, axis=0)
        for hop in range(chips):
            u_hi, u_lo = (
                half.astype(jnp.float32) for half in halves(u_ref[chip[hop] * handlers + handler])
            )
            stack = jnp.concatenate([u_hi, u_lo, u_hi, jnp.zeros_like(u_hi)], axis=0)
            cells = dot_bf16(stack.T.astype(jnp.bfloat16), table, ((1,), (0,)))
            turned = cells * cos_b - pltpu.roll(cells, LANES // 2, 1) * sin_b
            gbufs[hop][handler * LANES : (handler + 1) * LANES, :] = turned
    for out in outs:
        out[...] = jnp.zeros_like(out)
    band = band_of_lane(planes, chunk)

    def put(handler, carry):
        base = pl.multiple_of(handler * LANES, LANES)
        for slot in range(slots):
            block = handler * slots + slot
            here, after = in_window(band, info[1, block], chunk)
            first = pl.ds(info[0, block], 4)
            second = pl.ds(info[0, block] + LANES, 4)
            for hop in range(chips):
                cells = gbufs[hop][pl.ds(base + slot, 4, stride=slots), :]
                old_first = outs[hop][first, :]
                old_second = outs[hop][second, :]
                outs[hop][first, :] = old_first + jnp.where(here, cells, 0.0)
                outs[hop][second, :] = old_second + jnp.where(after, cells, 0.0)
        return carry

    lax.fori_loop(0, handlers, put, 0)


def inverse_kernel(
    info, chip, quarters, u_ref, cos_ref, sin_ref, shift_ref, s_ref, table_ref, *refs,
    planes, part, length, chunk, slots, chips
):
    far_maps = refs[: chips - 1]
    outs = refs[chips - 1 : chips + 1]
    refs = refs[chips + 1 :]
    grids, gbufs, refs = refs[:chips], refs[chips : 2 * chips], refs[2 * chips :]
    ybuf, images, maps, sems = refs
    copies = [
        pltpu.make_async_copy(far_maps[at], maps.at[at], sems.at[at]) for at in range(chips - 1)
    ]
    for copy in copies:
        copy.start()
    place_boxes(info, chip, u_ref, cos_ref, sin_ref, shift_ref, grids, gbufs, planes, chunk, slots)
    rows = length * planes
    own = length // chips
    table = []
    for half in range(2):
        bands = [
            table_ref[half, pl.ds(pl.multiple_of(ri * length + chip[0] * own, own), own), :]
            for ri in range(2)
        ]
        table.append(jnp.concatenate(bands, axis=0))
    for hop in range(chips):
        for band in range(length // chunk):
            tile = grids[hop][band * length : (band + 1) * length, :].T
            ybuf[hop, band * 64 : (band + 1) * 64, :] = tile[:64]
            ybuf[hop, rows + band * 64 : rows + (band + 1) * 64, :] = tile[64:]
        for pair in range(planes // 2):
            columns = [
                jnp.concatenate(
                    [
                        ybuf[hop, pl.ds(ri * rows + plane, length, stride=planes), :]
                        for ri in range(2)
                    ],
                    axis=0,
                )
                for plane in (2 * pair, 2 * pair + 1)
            ]
            done = dot_left(table, jnp.concatenate(columns, axis=1))
            for inner in range(2):
                for ri in range(2):
                    images[hop, ri, 2 * pair + inner] = done[
                        ri * own : (ri + 1) * own, inner * LANES : (inner + 1) * LANES
                    ]
    for copy in copies:
        copy.wait()
    table = (table_ref[2], table_ref[3])
    batch = min(planes, 256 // part)
    for at in range(2):
        local = pl.ds(pl.multiple_of(quarters[2 + at], part), part)
        whole = pl.ds(pl.multiple_of(quarters[at], part), part)
        for base in range(0, planes, batch):
            total_re, total_im = 0.0, 0.0
            for hop in range(chips):
                bands = [
                    jnp.concatenate([images[hop, ri, plane, local, :] for ri in range(2)], axis=1)
                    for plane in range(base, base + batch)
                ]
                done = dot_right(jnp.concatenate(bands, axis=0), table)
                i_re = done[:, :length].reshape(batch, part, length)
                i_im = done[:, length:].reshape(batch, part, length)
                if hop:
                    s_re = maps[hop - 1, 0, base : base + batch, local, :]
                    s_im = maps[hop - 1, 1, base : base + batch, local, :]
                else:
                    s_re = s_ref[0, base : base + batch, whole, :]
                    s_im = s_ref[1, base : base + batch, whole, :]
                total_re = total_re + (s_re * i_re + s_im * i_im)
                total_im = total_im + (s_re * i_im - s_im * i_re)
            outs[at][0, base : base + batch] = total_re
            outs[at][1, base : base + batch] = total_im


def inverse(info, chip_order, quarters, spread, phases, shift, smap, tables, far_maps, part, chunk, slots):
    _, planes, length, _ = smap.shape
    chips = len(far_maps) + 1
    handlers = info.shape[1] // slots
    rows = length * (length // chunk + 1)
    kernel = functools.partial(
        inverse_kernel, planes=planes, part=part, length=length, chunk=chunk, slots=slots,
        chips=chips,
    )
    return call(
        kernel,
        [(2, planes, part, length)] * 2,
        [(rows, LANES)] * chips
        + [(handlers * LANES, LANES)] * chips
        + [
            (chips, 2 * length * planes, length),
            (chips, 2, planes, 2 * part, length),
            (chips - 1, 2, planes, 2 * part, length),
            pltpu.SemaphoreType.DMA((chips - 1,)),
        ],
        [info, chip_order, quarters, spread, *phases, shift, smap, tables, *far_maps],
        3,
        48 * planes * length**3,
        "inverse",
        hbm=range(9, 9 + chips - 1),
    )


def sums_kernel(*refs, terms):
    term_refs = refs[:terms]
    p_ref, r_ref, normal_ref, out_ref = refs[terms:]
    shape = p_ref.shape

    def add(plane, held):
        held = list(held)
        for ri in range(2):
            normal = term_refs[0][ri, plane]
            for term in term_refs[1:]:
                normal = normal + term[ri, plane]
            normal_ref[ri, plane] = normal
            p = p_ref[ri, plane]
            r = r_ref[ri, plane]
            for at, product in enumerate((r * r, p * normal, r * normal, normal * normal)):
                held[at] = held[at] + jnp.sum(product.reshape(-1, 8, LANES), axis=0)
        return tuple(held)

    start = tuple(jnp.zeros((8, LANES), jnp.float32) for _ in range(4))
    held = lax.fori_loop(0, shape[1], add, start, unroll=4)
    lane = lax.broadcasted_iota(jnp.int32, out_ref.shape, 1)
    found = jnp.zeros(out_ref.shape, jnp.float32)
    for at in range(4):
        found = jnp.where(lane == at, jnp.sum(held[at]), found)
    out_ref[...] = found


def sums(terms, p, r, devices):
    kernel = functools.partial(sums_kernel, terms=len(terms))
    return call(kernel, [p.shape, (devices, LANES)], [], [*terms, p, r], 0, 10**7, "sums")


def finish_kernel(total_ref, x_ref, r_ref, p_ref, normal_ref, x_out, r_out, p_out):
    total = jnp.sum(total_ref[...], axis=0, keepdims=True)
    r_r, p_n, r_n, n_n = (total[:, at : at + 1] for at in range(4))
    alpha = r_r / p_n
    beta = (r_r + alpha * (alpha * n_n - 2.0 * r_n)) / r_r
    for plane in range(x_ref.shape[1]):
        for ri in range(2):
            p = p_ref[ri, plane]
            next_r = r_ref[ri, plane] - alpha * normal_ref[ri, plane]
            x_out[ri, plane] = x_ref[ri, plane] + alpha * p
            r_out[ri, plane] = next_r
            p_out[ri, plane] = next_r + beta * p


def finish(total, x, r, p, normal):
    return call(finish_kernel, [x.shape] * 3, [], [total, x, r, p, normal], 0, 10**7, "finish")


def matrices_kernel(info, tile, weights_ref, out_ref, held, *, slots):
    def one(block, carry):
        w_x = weights_ref[block, 0]
        w_y = weights_ref[block, 1]
        w_z = weights_ref[block, 2]
        twice = jnp.concatenate([w_x, w_x], axis=0)
        rolled = [twice] + [pltpu.roll(twice, 8 - d, 0) for d in range(1, 4)]
        low = lax.broadcasted_iota(jnp.int32, (8, LANES), 0) < 4
        along_x = [twice * jnp.where(low, rolled[d], rolled[d + 1]) for d in (0, 2)]
        right = []
        for f in range(4):
            for d_z in range(4):
                other = (f + d_z) % 4
                along_z = w_z[f : f + 1] * w_z[other : other + 1]
                right += [along * along_z for along in along_x]
        turned = pltpu.roll(
            jnp.concatenate([w_y, w_y], axis=0), info[1, tile[0] * slots + block] % 4, 0
        )[:4]
        left = jnp.concatenate([turned * turned[e : e + 1] for e in range(4)], axis=0)
        done = dot_right(left, halves(jnp.concatenate(right, axis=0)), ((1,), (1,)))
        for f in range(4):
            lanes = done[:, f // 2 * LANES : (f // 2 + 1) * LANES]
            if f % 2:
                lanes = pltpu.roll(lanes, LANES // 2, 1)
            held[pl.ds(f * slots + block, 16, stride=LANES), :] = lanes
        return carry

    lax.fori_loop(0, slots, one, 0, unroll=4)

    def turn(pair, carry):
        at = pl.ds(pl.multiple_of(pair * LANES, LANES), LANES)
        rows = held[at, :].T
        for group in range(16):
            four = rows[4 * group : 4 * group + 4]
            out_ref[pl.ds(pl.multiple_of(pair * LANES + 8 * group, 8), 8), :] = jnp.concatenate(
                [four, four], axis=0
            )
        return carry

    lax.fori_loop(0, 16, turn, 0, unroll=2)


def block_matrices(info, tile, weights):
    slots = weights.shape[0]
    return call(
        functools.partial(matrices_kernel, slots=slots),
        [(16 * LANES, LANES)],
        [(16 * LANES, LANES)],
        [info, tile, weights],
        2,
        10**9,
        "matrices",
    )[0]


def block_offsets(gathered, slots, ntile, capacity):
    owners = gathered[:, :slots]
    lists = gathered[:, slots:].reshape(ntile, 3, ntile, capacity)
    earlier = jnp.tril(jnp.ones((slots, slots), jnp.int32), -1)
    same = (owners[:, :, None] == owners[:, None, :]).astype(jnp.int32)
    ranks = jnp.sum(same * earlier[None], axis=2)
    wanted = owners * capacity + ranks
    lists = jnp.transpose(lists, (1, 2, 0, 3)).reshape(3, ntile, 1, ntile * capacity)
    hit = wanted[:, :, None] == jnp.arange(ntile * capacity, dtype=jnp.int32)
    found = jnp.sum(jnp.where(hit[None], lists, 0), axis=3)
    return found[0], found[1] + owners * (LANES // ntile), found[2]


def shards(image_p, image_x, image_r, sensitivity, kb_weights, block_owner, owner_list):
    ntile = lax.axis_size("tile")
    ncoil = lax.axis_size("coil")
    chips = ncoil // 2
    slots = kb_weights.shape[0]
    capacity = owner_list.shape[3]
    planes, length = image_p.shape[1], image_p.shape[3]
    part = image_p.shape[2]
    chunk = LANES // (2 * planes)
    tile = lax.axis_index("tile")
    coil = lax.axis_index("coil")
    chip, core = coil // 2, coil % 2
    smap = sensitivity[0]
    tables = fourier_tables(length)

    def from_chip(values, by):
        pairs = [
            (a * 2 + k, (a - by) % chips * 2 + k) for a in range(chips) for k in range(2)
        ]
        return lax.ppermute(values, "coil", pairs)

    def other_core(values):
        pairs = [(a * 2 + k, a * 2 + 1 - k) for a in range(chips) for k in range(2)]
        return lax.ppermute(values, "coil", pairs)

    hops = jnp.arange(chips, dtype=jnp.int32)
    chip_order = (chip + hops) % chips
    starts = jnp.concatenate(
        [(chip_order * 2 + at) * part for at in (core, 1 - core)]
        + [jnp.stack([core * part, (1 - core) * part])]
    )

    p_same = [image_p] + [from_chip(image_p, by) for by in range(1, chips)]
    p_other = [other_core(piece) for piece in p_same]
    mine = jnp.concatenate([block_owner, owner_list[:, 0].reshape(-1)])
    gathered = lax.all_to_all(
        jnp.broadcast_to(mine[None], (ntile, mine.shape[0])), "tile", 0, 0, tiled=True
    )
    near = coil_z(starts, [p_same[0], p_other[0]], [0, chips], smap, tables)
    far = coil_z(starts, p_same[1:], list(range(1, chips)), smap, tables, chips - 1)
    far_maps = [from_chip(rows, by) for by, rows in enumerate(far[chips - 1 :], 1)]
    gathered, near = lax.optimization_barrier((gathered, near))

    off_x, off_y, off_z = block_offsets(gathered, slots, ntile, capacity)
    info = jnp.stack(
        [(off_y // chunk * length + off_z).reshape(-1), (off_y % chunk).reshape(-1)]
    )
    lane = jnp.arange(LANES, dtype=jnp.int32)
    lane_ri = lane // (LANES // 2)
    lane_q = lane // planes % chunk
    lane_x = lane % planes + tile * planes
    unit = 2.0 * math.pi / length
    angle = unit * (off_x.reshape(-1, 1) * lane_x[None] % length).astype(jnp.float32)
    phases = (jnp.cos(angle), jnp.sin(angle) * jnp.where(lane_ri == 0, 1.0, -1.0)[None])
    row = jnp.arange(32, dtype=jnp.int32)[:, None]
    row_q, row_ri, row_i = row // 8, row // 4 % 2, row % 4
    angle = unit * (row_i * lane_x[None] % length).astype(jnp.float32)
    sine = jnp.where(row_ri == 0, 1.0, -1.0) * jnp.sin(angle)
    shift = jnp.where(row_ri == lane_ri[None], jnp.cos(angle), sine)
    shift = jnp.where(lane_q[None] % 4 == row_q, shift / math.sqrt(length), 0.0)
    done = [near[0], *far[: chips - 1], near[1]]
    partial = forward(
        info, starts[: 2 * chips], done, p_other[1:], smap, tables, phases, shift, chunk, slots
    )
    partial, weights = lax.optimization_barrier((partial, kb_weights))
    parts = lax.all_to_all(partial, "tile", 0, 0, tiled=True)
    done = regrid(parts, block_matrices(info, tile[None], weights), chips * ntile)
    groups = [
        [at * ntile + t for at in range(ncoil) if at % 2 == k for t in range(ntile)]
        for k in range(2)
    ]
    spread = lax.all_to_all(
        done, ("coil", "tile"), 0, 0, axis_index_groups=groups, tiled=True
    )
    quarters = jnp.stack([chip * 2 + 1 - core, chip * 2 + core, 1 - core, core]) * part
    sent, kept = inverse(
        info, chip_order, quarters, spread, phases, shift, smap, tables, far_maps, part, chunk,
        slots,
    )
    normal, found = sums([kept, other_core(sent)], image_p, image_r, ncoil * ntile)
    total = lax.all_to_all(found, ("coil", "tile"), 0, 0, tiled=True)
    return tuple(finish(total, image_x, image_r, image_p, normal))


def solution(mesh):
    return jax.shard_map(
        shards,
        mesh=mesh,
        in_specs=(
            P(None, "tile", "coil", None),
            P(None, "tile", "coil", None),
            P(None, "tile", "coil", None),
            P("coil", None, "tile", None, None),
            P("tile", None, None, None),
            P("tile"),
            P(None, "tile", None, None),
        ),
        out_specs=(
            P(None, "tile", "coil", None),
            P(None, "tile", "coil", None),
            P(None, "tile", "coil", None),
        ),
        check_vma=False,
    )
```

```python
import functools
import math

import jax
import jax.numpy as jnp
import ml_dtypes
import numpy as np
from jax import lax
from jax.experimental import pallas as pl
from jax.experimental.pallas import tpu as pltpu
from jax.sharding import PartitionSpec as P

LANES = 128
VMEM = 24 * 1024 * 1024


def halves(values):
    high = values.astype(jnp.bfloat16)
    low = (values - high.astype(jnp.float32)).astype(jnp.bfloat16)
    return high, low


def dot_bf16(left, right, dims):
    return lax.dot_general(left, right, (dims, ((), ())), preferred_element_type=jnp.float32)


def dot_left(table, values, dims=((1,), (0,))):
    high, low = halves(values)
    return (
        dot_bf16(table[0], high, dims)
        + dot_bf16(table[0], low, dims)
        + dot_bf16(table[1], high, dims)
    )


def dot_right(values, table, dims=((1,), (0,))):
    high, low = halves(values)
    return (
        dot_bf16(high, table[0], dims)
        + dot_bf16(low, table[0], dims)
        + dot_bf16(high, table[1], dims)
    )


def fourier_tables(length):
    cells = np.arange(length)
    angle = 2.0 * math.pi / length * (cells[:, None] * cells[None, :] % length)
    cos_t = np.cos(angle) / math.sqrt(length)
    sin_t = np.sin(angle) / math.sqrt(length)
    found = []
    for sign in (1.0, -1.0):
        whole = np.block([[cos_t, -sign * sin_t], [sign * sin_t, cos_t]])
        high = whole.astype(ml_dtypes.bfloat16)
        low = (whole - high.astype(np.float64)).astype(ml_dtypes.bfloat16)
        found += [high, low]
    return jnp.asarray(np.stack(found))


def band_of_lane(planes, chunk):
    return lax.broadcasted_iota(jnp.int32, (4, LANES), 1) // planes % chunk


def in_window(band, first, chunk):
    past = band - first
    if chunk == 4:
        here = past >= 0
        return here, jnp.logical_not(here)
    here = jnp.logical_and(past >= 0, past < 4)
    return here, past < 4 - chunk


def call(kernel, outs, scratch, operands, flops, name, hbm=(), hbm_outs=()):
    here = pl.BlockSpec(memory_space=pltpu.VMEM)
    there = pl.BlockSpec(memory_space=pltpu.HBM)
    moved = sum(math.prod(a.shape) * a.dtype.itemsize for a in operands)
    return pl.pallas_call(
        kernel,
        out_shape=[jax.ShapeDtypeStruct(shape, jnp.float32) for shape in outs],
        in_specs=[there if at in hbm else here for at in range(len(operands))],
        out_specs=[there if at in hbm_outs else here for at in range(len(outs))],
        scratch_shapes=[
            pltpu.VMEM(shape, jnp.float32) if isinstance(shape, tuple) else shape
            for shape in scratch
        ],
        compiler_params=pltpu.CompilerParams(vmem_limit_bytes=VMEM),
        cost_estimate=pl.CostEstimate(flops=flops, bytes_accessed=moved, transcendentals=0),
        name=name,
    )(*operands)


def started(pairs, sems):
    copies = [
        pltpu.make_async_copy(source, to, sems.at[at]) for at, (source, to) in enumerate(pairs)
    ]
    for copy in copies:
        copy.start()
    return copies


def place_on_coil():
    coil = lax.axis_index("coil")
    return coil // 2, coil % 2


def quarters_of(chips, part):
    chip, core = place_on_coil()
    return [
        pl.multiple_of(((chip + hop) % chips * 2 + at) * part, part)
        for at in (core, 1 - core)
        for hop in range(chips)
    ]


def map_rows_kernel(s_ref, *refs, chips):
    outs, sems = refs[:-1], refs[-1]
    chip, _ = place_on_coil()
    own = s_ref.shape[2] // chips
    pairs = [
        (s_ref.at[:, :, pl.ds(pl.multiple_of((chip + chips - by) % chips * own, own), own), :], out)
        for by, out in enumerate(outs, 1)
    ]
    for copy in started(pairs, sems):
        copy.wait()


def map_rows(smap, chips):
    _, planes, length, _ = smap.shape
    return call(
        functools.partial(map_rows_kernel, chips=chips),
        [(2, planes, length // chips, length)] * (chips - 1),
        [pltpu.SemaphoreType.DMA((chips - 1,))],
        [smap],
        0,
        "map_rows",
        hbm=[0],
        hbm_outs=range(chips - 1),
    )


def cut_boxes(info, grid, cos_ref, sin_ref, shift_ref, out_ref, gbuf, planes, chunk, slots):
    handlers = out_ref.shape[0]
    band = band_of_lane(planes, chunk)

    def cut(handler, carry):
        base = pl.multiple_of(handler * LANES, LANES)
        for slot in range(slots):
            block = handler * slots + slot
            here, after = in_window(band, info[1, block], chunk)
            first = grid[pl.ds(info[0, block], 4), :]
            second = grid[pl.ds(info[0, block] + LANES, 4), :]
            if chunk > 4:
                second = jnp.where(after, second, 0.0)
            gbuf[pl.ds(base + slot, 4, stride=slots), :] = jnp.where(here, first, second)
        return carry

    lax.fori_loop(0, handlers, cut, 0)
    high, low = halves(shift_ref[...])
    table = jnp.concatenate(
        [
            jnp.concatenate([high, high], axis=1),
            jnp.concatenate([low, jnp.zeros_like(low)], axis=1),
        ],
        axis=0,
    )
    for handler in range(handlers):
        rows = slice(handler * slots, (handler + 1) * slots)
        cos_b = jnp.concatenate([cos_ref[rows, :]] * 4, axis=0)
        sin_b = jnp.concatenate([sin_ref[rows, :]] * 4, axis=0)
        cells = gbuf[handler * LANES : (handler + 1) * LANES, :]
        turned = cells * cos_b + pltpu.roll(cells, LANES // 2, 1) * sin_b
        both = dot_bf16(table, jnp.concatenate(halves(turned), axis=1), ((1,), (1,)))
        out_ref[handler] = both[:32] + both[32:]


def forward_kernel(*refs, pieces, chunk, slots):
    p_hbm = refs[:pieces]
    s_hbm, table_hbm, info_hbm, cos_hbm, sin_hbm, shift_hbm, out_ref = refs[pieces : pieces + 7]
    pbuf, sbuf, tables, info, cos_ref, sin_ref, shift_ref = refs[pieces + 7 : pieces + 14]
    natural, ybuf, grid, gbuf, sems = refs[pieces + 14 :]
    _, planes, part, length = p_hbm[0].shape
    rows = length * planes
    starts = quarters_of(pieces // 2, part)
    order = [0, pieces // 2]
    order += [at for at in range(pieces) if at not in order]
    first = [(table_hbm.at[0:2], tables.at[0:2])]
    for at in order:
        first += [(p_hbm[at], pbuf.at[at]), (s_hbm.at[:, :, pl.ds(starts[at], part), :], sbuf.at[at])]
    last = [
        (table_hbm.at[2:4], tables.at[2:4]),
        (info_hbm, info),
        (cos_hbm, cos_ref),
        (sin_hbm, sin_ref),
        (shift_hbm, shift_ref),
    ]
    copies = started(first + last, sems)
    copies[0].wait()
    batch = min(planes, 256 // part)
    table = (tables[0], tables[1])
    for turn, at in enumerate(order):
        copies[1 + 2 * turn].wait()
        copies[2 + 2 * turn].wait()
        for base in range(0, planes, batch):
            bands = []
            for plane in range(base, base + batch):
                s_re = sbuf[at, 0, plane]
                s_im = sbuf[at, 1, plane]
                p_re = pbuf[at, 0, plane]
                p_im = pbuf[at, 1, plane]
                bands.append(
                    jnp.concatenate([s_re * p_re - s_im * p_im, s_re * p_im + s_im * p_re], axis=1)
                )
            done = dot_right(jnp.concatenate(bands, axis=0), table)
            for ri in range(2):
                half = done[:, ri * length : (ri + 1) * length]
                natural[ri, base : base + batch, pl.ds(starts[at], part), :] = half.reshape(
                    batch, part, length
                )
    for copy in copies[1 + 2 * pieces :]:
        copy.wait()
    table = (tables[2], tables[3])
    for pair in range(planes // 2):
        columns = [
            jnp.concatenate([natural[0, plane], natural[1, plane]], axis=0)
            for plane in (2 * pair, 2 * pair + 1)
        ]
        both = dot_left(table, jnp.concatenate(columns, axis=1))
        for inner in range(2):
            for ri in range(2):
                ybuf[pl.ds(ri * rows + 2 * pair + inner, length, stride=planes), :] = both[
                    ri * length : (ri + 1) * length, inner * LANES : (inner + 1) * LANES
                ]
    for band in range(length // chunk):
        re = ybuf[band * 64 : (band + 1) * 64, :]
        im = ybuf[rows + band * 64 : rows + (band + 1) * 64, :]
        grid[band * length : (band + 1) * length, :] = jnp.concatenate([re, im], axis=0).T
    cut_boxes(info, grid, cos_ref, sin_ref, shift_ref, out_ref, gbuf, planes, chunk, slots)


def forward(pieces, smap, tables, info, phases, shift, chunk, slots):
    _, planes, part, length = pieces[0].shape
    count = len(pieces)
    blocks = info.shape[1]
    operands = [*pieces, smap, tables, info, *phases, shift]
    return call(
        functools.partial(forward_kernel, pieces=count, chunk=chunk, slots=slots),
        [(blocks // slots, 32, LANES)],
        [
            (count, 2, planes, part, length),
            (count, 2, planes, part, length),
            pltpu.VMEM(tables.shape, tables.dtype),
            pltpu.SMEM(info.shape, info.dtype),
            (blocks, LANES),
            (blocks, LANES),
            shift.shape,
            (2, planes, length, length),
            (2 * length * planes, length),
            (length * (length // chunk + 1), LANES),
            (blocks * 4, LANES),
            pltpu.SemaphoreType.DMA((2 * count + 6,)),
        ],
        operands,
        48 * planes * length**3,
        "forward",
        hbm=range(len(operands)),
    )[0]


def regrid_kernel(parts_ref, matrix_ref, out_ref, held, done_sem):
    total = parts_ref[0]
    for at in range(1, parts_ref.shape[0]):
        total = total + parts_ref[at]
    along = lax.broadcasted_iota(jnp.int32, (8, LANES), 0) % 4
    sums = [jnp.zeros((8, LANES), jnp.float32) for _ in range(4)]
    for source in range(4):
        for d_z in range(4):
            value = total[8 * source : 8 * source + 8]
            if d_z:
                value = pltpu.roll(value, LANES - 32 * d_z, 1)
            for d_x in range(4):
                moved = value
                if d_x:
                    moved = jnp.where(
                        along + d_x < 4, pltpu.roll(value, 8 - d_x, 0), pltpu.roll(value, 4 - d_x, 0)
                    )
                for e in range(4):
                    at = 8 * (((e * 4 + source) * 4 + d_z) * 4 + d_x)
                    sums[e] = sums[e] + matrix_ref[at : at + 8] * moved
    done = jnp.concatenate(sums, axis=0)
    for at in range(held.shape[0]):
        held[at] = done
    copy = pltpu.make_async_copy(held, out_ref, done_sem)
    copy.start()
    copy.wait()


def regrid(parts, matrix, copies):
    shape = (copies,) + parts.shape[1:]
    return call(
        regrid_kernel,
        [shape],
        [shape, pltpu.SemaphoreType.DMA],
        [parts, matrix],
        10**7,
        "regrid",
        hbm_outs=[0],
    )[0]


def place_boxes(info, chip, u_ref, cos_ref, sin_ref, shift_ref, outs, gbufs, planes, chunk, slots):
    chips = len(outs)
    handlers = u_ref.shape[0] // chips
    high, low = halves(shift_ref[...])
    table = jnp.concatenate([high, high, low, jnp.zeros_like(low)], axis=0)
    for handler in range(handlers):
        rows = slice(handler * slots, (handler + 1) * slots)
        cos_b = jnp.concatenate([cos_ref[rows, :]] * 4, axis=0)
        sin_b = jnp.concatenate([sin_ref[rows, :]] * 4, axis=0)
        for hop in range(chips):
            u_hi, u_lo = (
                half.astype(jnp.float32) for half in halves(u_ref[(chip + hop) % chips * handlers + handler])
            )
            stack = jnp.concatenate([u_hi, u_lo, u_hi, jnp.zeros_like(u_hi)], axis=0)
            cells = dot_bf16(stack.T.astype(jnp.bfloat16), table, ((1,), (0,)))
            turned = cells * cos_b - pltpu.roll(cells, LANES // 2, 1) * sin_b
            gbufs[hop][handler * LANES : (handler + 1) * LANES, :] = turned
    band = band_of_lane(planes, chunk)

    def put(handler, carry):
        base = pl.multiple_of(handler * LANES, LANES)
        for slot in range(slots):
            block = handler * slots + slot
            here, after = in_window(band, info[1, block], chunk)
            first = pl.ds(info[0, block], 4)
            second = pl.ds(info[0, block] + LANES, 4)
            for hop in range(chips):
                cells = gbufs[hop][pl.ds(base + slot, 4, stride=slots), :]
                old_first = outs[hop][first, :]
                old_second = outs[hop][second, :]
                outs[hop][first, :] = old_first + jnp.where(here, cells, 0.0)
                outs[hop][second, :] = old_second + jnp.where(after, cells, 0.0)
        return carry

    lax.fori_loop(0, handlers, put, 0)


def inverse_kernel(*refs, part, length, chunk, slots, chips):
    u_ref, info_hbm, cos_hbm, sin_hbm, shift_hbm, table_hbm, s_hbm = refs[:7]
    far_maps = refs[7 : 6 + chips]
    outs = refs[6 + chips : 8 + chips]
    refs = refs[8 + chips :]
    grids, gbufs, refs = refs[:chips], refs[chips : 2 * chips], refs[2 * chips :]
    info, cos_ref, sin_ref, shift_ref, table_ref, ybuf, images, maps, sems = refs
    planes = s_hbm.shape[1]
    rows = length * planes
    own = length // chips
    chip, core = place_on_coil()
    own_rows = pl.multiple_of(chip * own, own)
    pairs = [
        (info_hbm, info),
        (cos_hbm, cos_ref),
        (sin_hbm, sin_ref),
        (shift_hbm, shift_ref),
        (table_hbm, table_ref),
        (s_hbm.at[:, :, pl.ds(own_rows, own), :], maps.at[0]),
    ]
    pairs += [(far_map, maps.at[at]) for at, far_map in enumerate(far_maps, 1)]
    copies = started(pairs, sems)
    for grid in grids:
        grid[...] = jnp.zeros_like(grid)
    for copy in copies[:4]:
        copy.wait()
    place_boxes(info, chip, u_ref, cos_ref, sin_ref, shift_ref, grids, gbufs, planes, chunk, slots)
    for copy in copies[4:]:
        copy.wait()
    table = []
    for half in range(2):
        bands = [
            table_ref[half, pl.ds(pl.multiple_of(ri * length + own_rows, own), own), :]
            for ri in range(2)
        ]
        table.append(jnp.concatenate(bands, axis=0))
    for hop in range(chips):
        for band in range(length // chunk):
            tile = grids[hop][band * length : (band + 1) * length, :].T
            ybuf[hop, band * 64 : (band + 1) * 64, :] = tile[:64]
            ybuf[hop, rows + band * 64 : rows + (band + 1) * 64, :] = tile[64:]
        for pair in range(planes // 2):
            columns = [
                jnp.concatenate(
                    [
                        ybuf[hop, pl.ds(ri * rows + plane, length, stride=planes), :]
                        for ri in range(2)
                    ],
                    axis=0,
                )
                for plane in (2 * pair, 2 * pair + 1)
            ]
            done = dot_left(table, jnp.concatenate(columns, axis=1))
            for inner in range(2):
                for ri in range(2):
                    images[hop, ri, 2 * pair + inner] = done[
                        ri * own : (ri + 1) * own, inner * LANES : (inner + 1) * LANES
                    ]
    table = (table_ref[2], table_ref[3])
    batch = min(planes, 256 // part)
    for at, half in enumerate((1 - core, core)):
        local = pl.ds(pl.multiple_of(half * part, part), part)
        for base in range(0, planes, batch):
            total_re, total_im = 0.0, 0.0
            for hop in range(chips):
                bands = [
                    jnp.concatenate([images[hop, ri, plane, local, :] for ri in range(2)], axis=1)
                    for plane in range(base, base + batch)
                ]
                done = dot_right(jnp.concatenate(bands, axis=0), table)
                i_re = done[:, :length].reshape(batch, part, length)
                i_im = done[:, length:].reshape(batch, part, length)
                s_re = maps[hop, 0, base : base + batch, local, :]
                s_im = maps[hop, 1, base : base + batch, local, :]
                total_re = total_re + (s_re * i_re + s_im * i_im)
                total_im = total_im + (s_re * i_im - s_im * i_re)
            outs[at][0, base : base + batch] = total_re
            outs[at][1, base : base + batch] = total_im


def inverse(spread, info, phases, shift, tables, smap, far_maps, part, chunk, slots):
    _, planes, length, _ = smap.shape
    chips = len(far_maps) + 1
    blocks = info.shape[1]
    rows = length * (length // chunk + 1)
    own = (chips, 2, planes, 2 * part, length)
    operands = [spread, info, *phases, shift, tables, smap, *far_maps]
    return call(
        functools.partial(
            inverse_kernel, part=part, length=length, chunk=chunk, slots=slots, chips=chips
        ),
        [(2, planes, part, length)] * 2,
        [(rows, LANES)] * chips
        + [(blocks * 4, LANES)] * chips
        + [
            pltpu.SMEM(info.shape, info.dtype),
            (blocks, LANES),
            (blocks, LANES),
            shift.shape,
            pltpu.VMEM(tables.shape, tables.dtype),
            (chips, 2 * length * planes, length),
            own,
            own,
            pltpu.SemaphoreType.DMA((5 + chips,)),
        ],
        operands,
        48 * planes * length**3,
        "inverse",
        hbm=range(1, len(operands)),
    )


def sums_kernel(*refs, terms):
    term_refs = refs[:terms]
    p_ref, r_ref, normal_ref, out_ref = refs[terms:]
    shape = p_ref.shape

    def add(plane, held):
        held = list(held)
        for ri in range(2):
            normal = term_refs[0][ri, plane]
            for term in term_refs[1:]:
                normal = normal + term[ri, plane]
            normal_ref[ri, plane] = normal
            p = p_ref[ri, plane]
            r = r_ref[ri, plane]
            for at, product in enumerate((r * r, p * normal, r * normal, normal * normal)):
                held[at] = held[at] + jnp.sum(product.reshape(-1, 8, LANES), axis=0)
        return tuple(held)

    start = tuple(jnp.zeros((8, LANES), jnp.float32) for _ in range(4))
    held = lax.fori_loop(0, shape[1], add, start, unroll=4)
    lane = lax.broadcasted_iota(jnp.int32, out_ref.shape, 1)
    found = jnp.zeros(out_ref.shape, jnp.float32)
    for at in range(4):
        found = jnp.where(lane == at, jnp.sum(held[at]), found)
    out_ref[...] = found


def sums(terms, p, r, devices):
    kernel = functools.partial(sums_kernel, terms=len(terms))
    return call(kernel, [p.shape, (devices, LANES)], [], [*terms, p, r], 10**7, "sums")


def finish_kernel(total_ref, x_ref, r_ref, p_ref, normal_ref, x_out, r_out, p_out):
    total = jnp.sum(total_ref[...], axis=0, keepdims=True)
    r_r, p_n, r_n, n_n = (total[:, at : at + 1] for at in range(4))
    alpha = r_r / p_n
    beta = (r_r + alpha * (alpha * n_n - 2.0 * r_n)) / r_r
    for plane in range(x_ref.shape[1]):
        for ri in range(2):
            p = p_ref[ri, plane]
            next_r = r_ref[ri, plane] - alpha * normal_ref[ri, plane]
            x_out[ri, plane] = x_ref[ri, plane] + alpha * p
            r_out[ri, plane] = next_r
            p_out[ri, plane] = next_r + beta * p


def finish(total, x, r, p, normal):
    return call(finish_kernel, [x.shape] * 3, [], [total, x, r, p, normal], 10**7, "finish")


def matrices_kernel(info_hbm, weights_ref, out_ref, held, info, sem, *, slots):
    base = lax.axis_index("tile") * slots
    copy = pltpu.make_async_copy(info_hbm, info, sem)
    copy.start()
    copy.wait()

    def one(block, carry):
        w_x = weights_ref[block, 0]
        w_y = weights_ref[block, 1]
        w_z = weights_ref[block, 2]
        twice = jnp.concatenate([w_x, w_x], axis=0)
        rolled = [twice] + [pltpu.roll(twice, 8 - d, 0) for d in range(1, 4)]
        low = lax.broadcasted_iota(jnp.int32, (8, LANES), 0) < 4
        along_x = [twice * jnp.where(low, rolled[d], rolled[d + 1]) for d in (0, 2)]
        right = []
        for f in range(4):
            for d_z in range(4):
                other = (f + d_z) % 4
                along_z = w_z[f : f + 1] * w_z[other : other + 1]
                right += [along * along_z for along in along_x]
        turned = pltpu.roll(
            jnp.concatenate([w_y, w_y], axis=0), info[1, base + block] % 4, 0
        )[:4]
        left = jnp.concatenate([turned * turned[e : e + 1] for e in range(4)], axis=0)
        done = dot_right(left, halves(jnp.concatenate(right, axis=0)), ((1,), (1,)))
        for f in range(4):
            lanes = done[:, f // 2 * LANES : (f // 2 + 1) * LANES]
            if f % 2:
                lanes = pltpu.roll(lanes, LANES // 2, 1)
            held[pl.ds(f * slots + block, 16, stride=LANES), :] = lanes
        return carry

    lax.fori_loop(0, slots, one, 0, unroll=4)

    def turn(pair, carry):
        at = pl.ds(pl.multiple_of(pair * LANES, LANES), LANES)
        rows = held[at, :].T
        for group in range(16):
            four = rows[4 * group : 4 * group + 4]
            out_ref[pl.ds(pl.multiple_of(pair * LANES + 8 * group, 8), 8), :] = jnp.concatenate(
                [four, four], axis=0
            )
        return carry

    lax.fori_loop(0, 16, turn, 0, unroll=2)


def block_matrices(info, weights):
    return call(
        functools.partial(matrices_kernel, slots=weights.shape[0]),
        [(16 * LANES, LANES)],
        [(16 * LANES, LANES), pltpu.SMEM(info.shape, info.dtype), pltpu.SemaphoreType.DMA],
        [info, weights],
        10**9,
        "matrices",
        hbm=[0],
    )[0]


def block_offsets(gathered, slots, ntile, capacity):
    owners = gathered[:, :slots]
    lists = gathered[:, slots:].reshape(ntile, 3, ntile, capacity)
    earlier = jnp.tril(jnp.ones((slots, slots), jnp.int32), -1)
    same = (owners[:, :, None] == owners[:, None, :]).astype(jnp.int32)
    ranks = jnp.sum(same * earlier[None], axis=2)
    wanted = owners * capacity + ranks
    lists = jnp.transpose(lists, (1, 2, 0, 3)).reshape(3, ntile, 1, ntile * capacity)
    hit = wanted[:, :, None] == jnp.arange(ntile * capacity, dtype=jnp.int32)
    found = jnp.sum(jnp.where(hit[None], lists, 0), axis=3)
    return found[0], found[1] + owners * (LANES // ntile), found[2]


def shards(image_p, image_x, image_r, sensitivity, kb_weights, block_owner, owner_list):
    ntile = lax.axis_size("tile")
    ncoil = lax.axis_size("coil")
    chips = ncoil // 2
    slots = kb_weights.shape[0]
    capacity = owner_list.shape[3]
    planes, length = image_p.shape[1], image_p.shape[3]
    part = image_p.shape[2]
    chunk = LANES // (2 * planes)
    tile = lax.axis_index("tile")
    smap = sensitivity[0]
    tables = fourier_tables(length)

    def from_chip(values, by):
        pairs = [
            (a * 2 + k, (a - by) % chips * 2 + k) for a in range(chips) for k in range(2)
        ]
        return lax.ppermute(values, "coil", pairs)

    def other_core(values):
        pairs = [(a * 2 + k, a * 2 + 1 - k) for a in range(chips) for k in range(2)]
        return lax.ppermute(values, "coil", pairs)

    p_same = [image_p] + [from_chip(image_p, by) for by in range(1, chips)]
    p_other = [other_core(piece) for piece in p_same]
    mine = jnp.concatenate([block_owner, owner_list[:, 0].reshape(-1)])
    gathered = lax.all_to_all(
        jnp.broadcast_to(mine[None], (ntile, mine.shape[0])), "tile", 0, 0, tiled=True
    )
    far_rows = map_rows(smap, chips)
    far_rows, p_same[1:] = lax.optimization_barrier((far_rows, p_same[1:]))
    far_maps = [from_chip(rows, by) for by, rows in enumerate(far_rows, 1)]

    off_x, off_y, off_z = block_offsets(gathered, slots, ntile, capacity)
    info = jnp.stack(
        [(off_y // chunk * length + off_z).reshape(-1), (off_y % chunk).reshape(-1)]
    )
    lane = jnp.arange(LANES, dtype=jnp.int32)
    lane_ri = lane // (LANES // 2)
    lane_q = lane // planes % chunk
    lane_x = lane % planes + tile * planes
    unit = 2.0 * math.pi / length
    angle = unit * (off_x.reshape(-1, 1) * lane_x[None] % length).astype(jnp.float32)
    phases = (jnp.cos(angle), jnp.sin(angle) * jnp.where(lane_ri == 0, 1.0, -1.0)[None])
    row = jnp.arange(32, dtype=jnp.int32)[:, None]
    row_q, row_ri, row_i = row // 8, row // 4 % 2, row % 4
    angle = unit * (row_i * lane_x[None] % length).astype(jnp.float32)
    sine = jnp.where(row_ri == 0, 1.0, -1.0) * jnp.sin(angle)
    shift = jnp.where(row_ri == lane_ri[None], jnp.cos(angle), sine)
    shift = jnp.where(lane_q[None] % 4 == row_q, shift / math.sqrt(length), 0.0)
    partial = forward(p_same + p_other, smap, tables, info, phases, shift, chunk, slots)
    partial, weights = lax.optimization_barrier((partial, kb_weights))
    parts = lax.all_to_all(partial, "tile", 0, 0, tiled=True)
    done = regrid(parts, block_matrices(info, weights), chips * ntile)
    groups = [
        [at * ntile + t for at in range(ncoil) if at % 2 == k for t in range(ntile)]
        for k in range(2)
    ]
    spread = lax.all_to_all(
        done, ("coil", "tile"), 0, 0, axis_index_groups=groups, tiled=True
    )
    sent, kept = inverse(
        spread, info, phases, shift, tables, smap, far_maps, part, chunk, slots
    )
    normal, found = sums([kept, other_core(sent)], image_p, image_r, ncoil * ntile)
    total = lax.all_to_all(found, ("coil", "tile"), 0, 0, tiled=True)
    return tuple(finish(total, image_x, image_r, image_p, normal))


def solution(mesh):
    return jax.shard_map(
        shards,
        mesh=mesh,
        in_specs=(
            P(None, "tile", "coil", None),
            P(None, "tile", "coil", None),
            P(None, "tile", "coil", None),
            P("coil", None, "tile", None, None),
            P("tile", None, None, None),
            P("tile"),
            P(None, "tile", None, None),
        ),
        out_specs=(
            P(None, "tile", "coil", None),
            P(None, "tile", "coil", None),
            P(None, "tile", "coil", None),
        ),
        check_vma=False,
    )
```

```python
import functools
import math

import jax
import jax.numpy as jnp
import ml_dtypes
import numpy as np
from jax import lax
from jax.experimental import pallas as pl
from jax.experimental.pallas import tpu as pltpu
from jax.sharding import PartitionSpec as P

LANES = 128
VMEM = 60 * 1024 * 1024
SMALL = 16 * 1024 * 1024


def halves(values):
    high = values.astype(jnp.bfloat16)
    low = (values - high.astype(jnp.float32)).astype(jnp.bfloat16)
    return high, low


def dot_bf16(left, right, dims):
    return lax.dot_general(left, right, (dims, ((), ())), preferred_element_type=jnp.float32)


def dot_left(table, values, dims=((1,), (0,))):
    high, low = halves(values)
    return (
        dot_bf16(table[0], high, dims)
        + dot_bf16(table[0], low, dims)
        + dot_bf16(table[1], high, dims)
    )


def dot_right(values, table, dims=((1,), (0,))):
    high, low = halves(values)
    return (
        dot_bf16(high, table[0], dims)
        + dot_bf16(low, table[0], dims)
        + dot_bf16(high, table[1], dims)
    )


def fourier_tables(length):
    cells = np.arange(length)
    angle = 2.0 * math.pi / length * (cells[:, None] * cells[None, :] % length)
    cos_t = np.cos(angle) / math.sqrt(length)
    sin_t = np.sin(angle) / math.sqrt(length)
    found = []
    for sign in (1.0, -1.0):
        whole = np.block([[cos_t, -sign * sin_t], [sign * sin_t, cos_t]])
        high = whole.astype(ml_dtypes.bfloat16)
        low = (whole - high.astype(np.float64)).astype(ml_dtypes.bfloat16)
        found += [high, low]
    return jnp.asarray(np.stack(found))


def band_of_lane(planes, chunk):
    return lax.broadcasted_iota(jnp.int32, (4, LANES), 1) // planes % chunk


def in_window(band, first, chunk):
    past = band - first
    if chunk == 4:
        here = past >= 0
        return here, jnp.logical_not(here)
    here = jnp.logical_and(past >= 0, past < 4)
    return here, past < 4 - chunk


def call(kernel, outs, scratch, operands, flops, name, hbm=(), hbm_outs=(), limit=VMEM):
    here = pl.BlockSpec(memory_space=pltpu.VMEM)
    there = pl.BlockSpec(memory_space=pltpu.HBM)
    moved = sum(math.prod(a.shape) * a.dtype.itemsize for a in operands)
    return pl.pallas_call(
        kernel,
        out_shape=[jax.ShapeDtypeStruct(shape, jnp.float32) for shape in outs],
        in_specs=[there if at in hbm else here for at in range(len(operands))],
        out_specs=[there if at in hbm_outs else here for at in range(len(outs))],
        scratch_shapes=[
            pltpu.VMEM(shape, jnp.float32) if isinstance(shape, tuple) else shape
            for shape in scratch
        ],
        compiler_params=pltpu.CompilerParams(vmem_limit_bytes=limit),
        cost_estimate=pl.CostEstimate(flops=flops, bytes_accessed=moved, transcendentals=0),
        name=name,
    )(*operands)


def started(pairs, sems):
    copies = [
        pltpu.make_async_copy(source, to, sems.at[at]) for at, (source, to) in enumerate(pairs)
    ]
    for copy in copies:
        copy.start()
    return copies


def place_on_coil():
    coil = lax.axis_index("coil")
    return coil // 2, coil % 2


def quarters_of(chips, part):
    chip, core = place_on_coil()
    return [
        pl.multiple_of(((chip + hop) % chips * 2 + at) * part, part)
        for at in (core, 1 - core)
        for hop in range(chips)
    ]


def map_rows_kernel(s_ref, *refs, chips):
    outs, sems = refs[:-1], refs[-1]
    chip, _ = place_on_coil()
    own = s_ref.shape[2] // chips
    pairs = [
        (s_ref.at[:, :, pl.ds(pl.multiple_of((chip + chips - by) % chips * own, own), own), :], out)
        for by, out in enumerate(outs, 1)
    ]
    for copy in started(pairs, sems):
        copy.wait()


def map_rows(smap, chips):
    _, planes, length, _ = smap.shape
    return call(
        functools.partial(map_rows_kernel, chips=chips),
        [(2, planes, length // chips, length)] * (chips - 1),
        [pltpu.SemaphoreType.DMA((chips - 1,))],
        [smap],
        0,
        "map_rows",
        hbm=[0],
        hbm_outs=range(chips - 1),
    )


def cut_boxes(info, grid, cos_ref, sin_ref, shift_ref, out_ref, gbuf, planes, chunk, slots):
    handlers = out_ref.shape[0]
    band = band_of_lane(planes, chunk)

    def cut(handler, carry):
        base = pl.multiple_of(handler * LANES, LANES)
        for slot in range(slots):
            block = handler * slots + slot
            here, after = in_window(band, info[1, block], chunk)
            first = grid[pl.ds(info[0, block], 4), :]
            second = grid[pl.ds(info[0, block] + LANES, 4), :]
            if chunk > 4:
                second = jnp.where(after, second, 0.0)
            gbuf[pl.ds(base + slot, 4, stride=slots), :] = jnp.where(here, first, second)
        return carry

    lax.fori_loop(0, handlers, cut, 0)
    high, low = halves(shift_ref[...])
    table = jnp.concatenate(
        [
            jnp.concatenate([high, high], axis=1),
            jnp.concatenate([low, jnp.zeros_like(low)], axis=1),
        ],
        axis=0,
    )
    for handler in range(handlers):
        rows = slice(handler * slots, (handler + 1) * slots)
        cos_b = jnp.concatenate([cos_ref[rows, :]] * 4, axis=0)
        sin_b = jnp.concatenate([sin_ref[rows, :]] * 4, axis=0)
        cells = gbuf[handler * LANES : (handler + 1) * LANES, :]
        turned = cells * cos_b + pltpu.roll(cells, LANES // 2, 1) * sin_b
        both = dot_bf16(table, jnp.concatenate(halves(turned), axis=1), ((1,), (1,)))
        out_ref[handler] = both[:32] + both[32:]


def forward_kernel(*refs, pieces, chunk, slots):
    p_hbm = refs[:pieces]
    s_hbm, table_hbm, info_hbm, cos_hbm, sin_hbm, shift_hbm, out_ref = refs[pieces : pieces + 7]
    pbuf, sbuf, tables, info, cos_ref, sin_ref, shift_ref = refs[pieces + 7 : pieces + 14]
    natural, ybuf, grid, gbuf, sems = refs[pieces + 14 :]
    _, planes, part, length = p_hbm[0].shape
    rows = length * planes
    starts = quarters_of(pieces // 2, part)
    order = [0, pieces // 2]
    order += [at for at in range(pieces) if at not in order]
    first = [(table_hbm.at[0:2], tables.at[0:2])]
    for at in order:
        first += [(p_hbm[at], pbuf.at[at]), (s_hbm.at[:, :, pl.ds(starts[at], part), :], sbuf.at[at])]
    last = [
        (table_hbm.at[2:4], tables.at[2:4]),
        (info_hbm, info),
        (cos_hbm, cos_ref),
        (sin_hbm, sin_ref),
        (shift_hbm, shift_ref),
    ]
    copies = started(first + last, sems)
    copies[0].wait()
    batch = min(planes, 256 // part)
    table = (tables[0], tables[1])
    for turn, at in enumerate(order):
        copies[1 + 2 * turn].wait()
        copies[2 + 2 * turn].wait()
        for base in range(0, planes, batch):
            bands = []
            for plane in range(base, base + batch):
                s_re = sbuf[at, 0, plane]
                s_im = sbuf[at, 1, plane]
                p_re = pbuf[at, 0, plane]
                p_im = pbuf[at, 1, plane]
                bands.append(
                    jnp.concatenate([s_re * p_re - s_im * p_im, s_re * p_im + s_im * p_re], axis=1)
                )
            done = dot_right(jnp.concatenate(bands, axis=0), table)
            for ri in range(2):
                half = done[:, ri * length : (ri + 1) * length]
                natural[ri, base : base + batch, pl.ds(starts[at], part), :] = half.reshape(
                    batch, part, length
                )
    for copy in copies[1 + 2 * pieces :]:
        copy.wait()
    table = (tables[2], tables[3])
    for pair in range(planes // 2):
        columns = [
            jnp.concatenate([natural[0, plane], natural[1, plane]], axis=0)
            for plane in (2 * pair, 2 * pair + 1)
        ]
        both = dot_left(table, jnp.concatenate(columns, axis=1))
        for inner in range(2):
            for ri in range(2):
                ybuf[pl.ds(ri * rows + 2 * pair + inner, length, stride=planes), :] = both[
                    ri * length : (ri + 1) * length, inner * LANES : (inner + 1) * LANES
                ]
    for band in range(length // chunk):
        re = ybuf[band * 64 : (band + 1) * 64, :]
        im = ybuf[rows + band * 64 : rows + (band + 1) * 64, :]
        grid[band * length : (band + 1) * length, :] = jnp.concatenate([re, im], axis=0).T
    cut_boxes(info, grid, cos_ref, sin_ref, shift_ref, out_ref, gbuf, planes, chunk, slots)


def forward(pieces, smap, tables, info, phases, shift, chunk, slots):
    _, planes, part, length = pieces[0].shape
    count = len(pieces)
    blocks = info.shape[1]
    operands = [*pieces, smap, tables, info, *phases, shift]
    return call(
        functools.partial(forward_kernel, pieces=count, chunk=chunk, slots=slots),
        [(blocks // slots, 32, LANES)],
        [
            (count, 2, planes, part, length),
            (count, 2, planes, part, length),
            pltpu.VMEM(tables.shape, tables.dtype),
            pltpu.SMEM(info.shape, info.dtype),
            (blocks, LANES),
            (blocks, LANES),
            shift.shape,
            (2, planes, length, length),
            (2 * length * planes, length),
            (length * (length // chunk + 1), LANES),
            (blocks * 4, LANES),
            pltpu.SemaphoreType.DMA((2 * count + 6,)),
        ],
        operands,
        48 * planes * length**3,
        "forward",
        hbm=range(len(operands)),
    )[0]


def regrid_kernel(parts_hbm, matrix_hbm, out_ref, parts_ref, matrix_ref, held, sems):
    copies = started([(parts_hbm, parts_ref), (matrix_hbm, matrix_ref)], sems)
    for copy in copies:
        copy.wait()
    total = parts_ref[0]
    for at in range(1, parts_ref.shape[0]):
        total = total + parts_ref[at]
    along = lax.broadcasted_iota(jnp.int32, (8, LANES), 0) % 4
    sums = [jnp.zeros((8, LANES), jnp.float32) for _ in range(4)]
    for source in range(4):
        for d_z in range(4):
            value = total[8 * source : 8 * source + 8]
            if d_z:
                value = pltpu.roll(value, LANES - 32 * d_z, 1)
            for d_x in range(4):
                moved = value
                if d_x:
                    moved = jnp.where(
                        along + d_x < 4, pltpu.roll(value, 8 - d_x, 0), pltpu.roll(value, 4 - d_x, 0)
                    )
                for e in range(4):
                    at = 8 * (((e * 4 + source) * 4 + d_z) * 4 + d_x)
                    sums[e] = sums[e] + matrix_ref[at : at + 8] * moved
    done = jnp.concatenate(sums, axis=0)
    for at in range(held.shape[0]):
        held[at] = done
    for copy in started([(held, out_ref)], sems):
        copy.wait()


def regrid(parts, matrix, copies):
    shape = (copies,) + parts.shape[1:]
    return call(
        regrid_kernel,
        [shape],
        [parts.shape, matrix.shape, shape, pltpu.SemaphoreType.DMA((2,))],
        [parts, matrix],
        10**7,
        "regrid",
        hbm=[0, 1],
        hbm_outs=[0],
    )[0]


def place_boxes(info, chip, u_ref, cos_ref, sin_ref, shift_ref, outs, gbufs, planes, chunk, slots):
    chips = len(outs)
    handlers = u_ref.shape[0] // chips
    high, low = halves(shift_ref[...])
    table = jnp.concatenate([high, high, low, jnp.zeros_like(low)], axis=0)
    for handler in range(handlers):
        rows = slice(handler * slots, (handler + 1) * slots)
        cos_b = jnp.concatenate([cos_ref[rows, :]] * 4, axis=0)
        sin_b = jnp.concatenate([sin_ref[rows, :]] * 4, axis=0)
        for hop in range(chips):
            u_hi, u_lo = (
                half.astype(jnp.float32) for half in halves(u_ref[(chip + hop) % chips * handlers + handler])
            )
            stack = jnp.concatenate([u_hi, u_lo, u_hi, jnp.zeros_like(u_hi)], axis=0)
            cells = dot_bf16(stack.T.astype(jnp.bfloat16), table, ((1,), (0,)))
            turned = cells * cos_b - pltpu.roll(cells, LANES // 2, 1) * sin_b
            gbufs[hop][handler * LANES : (handler + 1) * LANES, :] = turned
    band = band_of_lane(planes, chunk)

    def put(handler, carry):
        base = pl.multiple_of(handler * LANES, LANES)
        for slot in range(slots):
            block = handler * slots + slot
            here, after = in_window(band, info[1, block], chunk)
            first = pl.ds(info[0, block], 4)
            second = pl.ds(info[0, block] + LANES, 4)
            for hop in range(chips):
                cells = gbufs[hop][pl.ds(base + slot, 4, stride=slots), :]
                old_first = outs[hop][first, :]
                old_second = outs[hop][second, :]
                outs[hop][first, :] = old_first + jnp.where(here, cells, 0.0)
                outs[hop][second, :] = old_second + jnp.where(after, cells, 0.0)
        return carry

    lax.fori_loop(0, handlers, put, 0)


def inverse_kernel(*refs, part, length, chunk, slots, chips):
    u_ref, info_hbm, cos_hbm, sin_hbm, shift_hbm, table_hbm, s_hbm = refs[:7]
    far_maps = refs[7 : 6 + chips]
    outs = refs[6 + chips : 8 + chips]
    refs = refs[8 + chips :]
    grids, gbufs, refs = refs[:chips], refs[chips : 2 * chips], refs[2 * chips :]
    info, cos_ref, sin_ref, shift_ref, table_ref, ybuf, images, maps, sems = refs
    planes = s_hbm.shape[1]
    rows = length * planes
    own = length // chips
    chip, core = place_on_coil()
    own_rows = pl.multiple_of(chip * own, own)
    pairs = [
        (info_hbm, info),
        (cos_hbm, cos_ref),
        (sin_hbm, sin_ref),
        (shift_hbm, shift_ref),
        (table_hbm, table_ref),
        (s_hbm.at[:, :, pl.ds(own_rows, own), :], maps.at[0]),
    ]
    pairs += [(far_map, maps.at[at]) for at, far_map in enumerate(far_maps, 1)]
    copies = started(pairs, sems)
    for grid in grids:
        grid[...] = jnp.zeros_like(grid)
    for copy in copies[:4]:
        copy.wait()
    place_boxes(info, chip, u_ref, cos_ref, sin_ref, shift_ref, grids, gbufs, planes, chunk, slots)
    for copy in copies[4:]:
        copy.wait()
    table = []
    for half in range(2):
        bands = [
            table_ref[half, pl.ds(pl.multiple_of(ri * length + own_rows, own), own), :]
            for ri in range(2)
        ]
        table.append(jnp.concatenate(bands, axis=0))
    for hop in range(chips):
        for band in range(length // chunk):
            tile = grids[hop][band * length : (band + 1) * length, :].T
            ybuf[hop, band * 64 : (band + 1) * 64, :] = tile[:64]
            ybuf[hop, rows + band * 64 : rows + (band + 1) * 64, :] = tile[64:]
        for pair in range(planes // 2):
            columns = [
                jnp.concatenate(
                    [
                        ybuf[hop, pl.ds(ri * rows + plane, length, stride=planes), :]
                        for ri in range(2)
                    ],
                    axis=0,
                )
                for plane in (2 * pair, 2 * pair + 1)
            ]
            done = dot_left(table, jnp.concatenate(columns, axis=1))
            for inner in range(2):
                for ri in range(2):
                    images[hop, ri, 2 * pair + inner] = done[
                        ri * own : (ri + 1) * own, inner * LANES : (inner + 1) * LANES
                    ]
    table = (table_ref[2], table_ref[3])
    batch = min(planes, 256 // part)
    for at, half in enumerate((1 - core, core)):
        local = pl.ds(pl.multiple_of(half * part, part), part)
        for base in range(0, planes, batch):
            total_re, total_im = 0.0, 0.0
            for hop in range(chips):
                bands = [
                    jnp.concatenate([images[hop, ri, plane, local, :] for ri in range(2)], axis=1)
                    for plane in range(base, base + batch)
                ]
                done = dot_right(jnp.concatenate(bands, axis=0), table)
                i_re = done[:, :length].reshape(batch, part, length)
                i_im = done[:, length:].reshape(batch, part, length)
                s_re = maps[hop, 0, base : base + batch, local, :]
                s_im = maps[hop, 1, base : base + batch, local, :]
                total_re = total_re + (s_re * i_re + s_im * i_im)
                total_im = total_im + (s_re * i_im - s_im * i_re)
            outs[at][0, base : base + batch] = total_re
            outs[at][1, base : base + batch] = total_im


def inverse(spread, info, phases, shift, tables, smap, far_maps, part, chunk, slots):
    _, planes, length, _ = smap.shape
    chips = len(far_maps) + 1
    blocks = info.shape[1]
    rows = length * (length // chunk + 1)
    own = (chips, 2, planes, 2 * part, length)
    operands = [spread, info, *phases, shift, tables, smap, *far_maps]
    return call(
        functools.partial(
            inverse_kernel, part=part, length=length, chunk=chunk, slots=slots, chips=chips
        ),
        [(2, planes, part, length)] * 2,
        [(rows, LANES)] * chips
        + [(blocks * 4, LANES)] * chips
        + [
            pltpu.SMEM(info.shape, info.dtype),
            (blocks, LANES),
            (blocks, LANES),
            shift.shape,
            pltpu.VMEM(tables.shape, tables.dtype),
            (chips, 2 * length * planes, length),
            own,
            own,
            pltpu.SemaphoreType.DMA((5 + chips,)),
        ],
        operands,
        48 * planes * length**3,
        "inverse",
        hbm=range(1, len(operands)),
    )


def sums_kernel(*refs, terms):
    term_refs = refs[:terms]
    p_ref, r_ref, normal_ref, out_ref = refs[terms:]
    shape = p_ref.shape

    def add(plane, held):
        held = list(held)
        for ri in range(2):
            normal = term_refs[0][ri, plane]
            for term in term_refs[1:]:
                normal = normal + term[ri, plane]
            normal_ref[ri, plane] = normal
            p = p_ref[ri, plane]
            r = r_ref[ri, plane]
            for at, product in enumerate((r * r, p * normal, r * normal, normal * normal)):
                held[at] = held[at] + jnp.sum(product.reshape(-1, 8, LANES), axis=0)
        return tuple(held)

    start = tuple(jnp.zeros((8, LANES), jnp.float32) for _ in range(4))
    held = lax.fori_loop(0, shape[1], add, start, unroll=4)
    lane = lax.broadcasted_iota(jnp.int32, out_ref.shape, 1)
    found = jnp.zeros(out_ref.shape, jnp.float32)
    for at in range(4):
        found = jnp.where(lane == at, jnp.sum(held[at]), found)
    out_ref[...] = found


def sums(terms, p, r, devices):
    kernel = functools.partial(sums_kernel, terms=len(terms))
    return call(kernel, [p.shape, (devices, LANES)], [], [*terms, p, r], 10**7, "sums", limit=SMALL)


def finish_kernel(total_ref, x_ref, r_ref, p_ref, normal_ref, x_out, r_out, p_out):
    total = jnp.sum(total_ref[...], axis=0, keepdims=True)
    r_r, p_n, r_n, n_n = (total[:, at : at + 1] for at in range(4))
    alpha = r_r / p_n
    beta = (r_r + alpha * (alpha * n_n - 2.0 * r_n)) / r_r
    for plane in range(x_ref.shape[1]):
        for ri in range(2):
            p = p_ref[ri, plane]
            next_r = r_ref[ri, plane] - alpha * normal_ref[ri, plane]
            x_out[ri, plane] = x_ref[ri, plane] + alpha * p
            r_out[ri, plane] = next_r
            p_out[ri, plane] = next_r + beta * p


def finish(total, x, r, p, normal):
    return call(finish_kernel, [x.shape] * 3, [], [total, x, r, p, normal], 10**7, "finish", limit=SMALL)


def matrices_kernel(info_hbm, weights_ref, out_ref, held, info, sem, *, slots):
    base = lax.axis_index("tile") * slots
    copy = pltpu.make_async_copy(info_hbm, info, sem)
    copy.start()
    copy.wait()

    def one(block, carry):
        w_x = weights_ref[block, 0]
        w_y = weights_ref[block, 1]
        w_z = weights_ref[block, 2]
        twice = jnp.concatenate([w_x, w_x], axis=0)
        rolled = [twice] + [pltpu.roll(twice, 8 - d, 0) for d in range(1, 4)]
        low = lax.broadcasted_iota(jnp.int32, (8, LANES), 0) < 4
        along_x = [twice * jnp.where(low, rolled[d], rolled[d + 1]) for d in (0, 2)]
        right = []
        for f in range(4):
            for d_z in range(4):
                other = (f + d_z) % 4
                along_z = w_z[f : f + 1] * w_z[other : other + 1]
                right += [along * along_z for along in along_x]
        turned = pltpu.roll(
            jnp.concatenate([w_y, w_y], axis=0), info[1, base + block] % 4, 0
        )[:4]
        left = jnp.concatenate([turned * turned[e : e + 1] for e in range(4)], axis=0)
        done = dot_right(left, halves(jnp.concatenate(right, axis=0)), ((1,), (1,)))
        for f in range(4):
            lanes = done[:, f // 2 * LANES : (f // 2 + 1) * LANES]
            if f % 2:
                lanes = pltpu.roll(lanes, LANES // 2, 1)
            held[pl.ds(f * slots + block, 16, stride=LANES), :] = lanes
        return carry

    lax.fori_loop(0, slots, one, 0, unroll=4)

    def turn(pair, carry):
        at = pl.ds(pl.multiple_of(pair * LANES, LANES), LANES)
        rows = held[at, :].T
        for group in range(16):
            four = rows[4 * group : 4 * group + 4]
            out_ref[pl.ds(pl.multiple_of(pair * LANES + 8 * group, 8), 8), :] = jnp.concatenate(
                [four, four], axis=0
            )
        return carry

    lax.fori_loop(0, 16, turn, 0, unroll=2)


def block_matrices(info, weights):
    return call(
        functools.partial(matrices_kernel, slots=weights.shape[0]),
        [(16 * LANES, LANES)],
        [(16 * LANES, LANES), pltpu.SMEM(info.shape, info.dtype), pltpu.SemaphoreType.DMA],
        [info, weights],
        10**9,
        "matrices",
        hbm=[0],
    )[0]


def block_offsets(gathered, slots, ntile, capacity):
    owners = gathered[:, :slots]
    lists = gathered[:, slots:].reshape(ntile, 3, ntile, capacity)
    earlier = jnp.tril(jnp.ones((slots, slots), jnp.int32), -1)
    same = (owners[:, :, None] == owners[:, None, :]).astype(jnp.int32)
    ranks = jnp.sum(same * earlier[None], axis=2)
    wanted = owners * capacity + ranks
    lists = jnp.transpose(lists, (1, 2, 0, 3)).reshape(3, ntile, 1, ntile * capacity)
    hit = wanted[:, :, None] == jnp.arange(ntile * capacity, dtype=jnp.int32)
    found = jnp.sum(jnp.where(hit[None], lists, 0), axis=3)
    return found[0], found[1] + owners * (LANES // ntile), found[2]


def shards(image_p, image_x, image_r, sensitivity, kb_weights, block_owner, owner_list):
    ntile = lax.axis_size("tile")
    ncoil = lax.axis_size("coil")
    chips = ncoil // 2
    slots = kb_weights.shape[0]
    capacity = owner_list.shape[3]
    planes, length = image_p.shape[1], image_p.shape[3]
    part = image_p.shape[2]
    chunk = LANES // (2 * planes)
    tile = lax.axis_index("tile")
    smap = sensitivity[0]
    tables = fourier_tables(length)

    def from_chip(values, by):
        pairs = [
            (a * 2 + k, (a - by) % chips * 2 + k) for a in range(chips) for k in range(2)
        ]
        return lax.ppermute(values, "coil", pairs)

    def other_core(values):
        pairs = [(a * 2 + k, a * 2 + 1 - k) for a in range(chips) for k in range(2)]
        return lax.ppermute(values, "coil", pairs)

    p_same = [image_p] + [from_chip(image_p, by) for by in range(1, chips)]
    p_other = [other_core(piece) for piece in p_same]
    mine = jnp.concatenate([block_owner, owner_list[:, 0].reshape(-1)])
    gathered = lax.all_gather(mine, "tile")
    far_rows = map_rows(smap, chips)
    far_rows, p_same[1:] = lax.optimization_barrier((far_rows, p_same[1:]))
    far_maps = [from_chip(rows, by) for by, rows in enumerate(far_rows, 1)]

    off_x, off_y, off_z = block_offsets(gathered, slots, ntile, capacity)
    info = jnp.stack(
        [(off_y // chunk * length + off_z).reshape(-1), (off_y % chunk).reshape(-1)]
    )
    lane = jnp.arange(LANES, dtype=jnp.int32)
    lane_ri = lane // (LANES // 2)
    lane_q = lane // planes % chunk
    lane_x = lane % planes + tile * planes
    unit = 2.0 * math.pi / length
    angle = unit * (off_x.reshape(-1, 1) * lane_x[None] % length).astype(jnp.float32)
    phases = (jnp.cos(angle), jnp.sin(angle) * jnp.where(lane_ri == 0, 1.0, -1.0)[None])
    row = jnp.arange(32, dtype=jnp.int32)[:, None]
    row_q, row_ri, row_i = row // 8, row // 4 % 2, row % 4
    angle = unit * (row_i * lane_x[None] % length).astype(jnp.float32)
    sine = jnp.where(row_ri == 0, 1.0, -1.0) * jnp.sin(angle)
    shift = jnp.where(row_ri == lane_ri[None], jnp.cos(angle), sine)
    shift = jnp.where(lane_q[None] % 4 == row_q, shift / math.sqrt(length), 0.0)
    partial = forward(p_same + p_other, smap, tables, info, phases, shift, chunk, slots)
    partial, weights = lax.optimization_barrier((partial, kb_weights))
    parts = lax.all_to_all(partial, "tile", 0, 0, tiled=True)
    done = regrid(parts, block_matrices(info, weights), chips * ntile)
    groups = [
        [at * ntile + t for at in range(ncoil) if at % 2 == k for t in range(ntile)]
        for k in range(2)
    ]
    spread = lax.all_to_all(
        done, ("coil", "tile"), 0, 0, axis_index_groups=groups, tiled=True
    )
    sent, kept = inverse(
        spread, info, phases, shift, tables, smap, far_maps, part, chunk, slots
    )
    normal, found = sums([kept, other_core(sent)], image_p, image_r, ncoil * ntile)
    total = lax.all_to_all(found, ("coil", "tile"), 0, 0, tiled=True)
    return tuple(finish(total, image_x, image_r, image_p, normal))


def solution(mesh):
    return jax.shard_map(
        shards,
        mesh=mesh,
        in_specs=(
            P(None, "tile", "coil", None),
            P(None, "tile", "coil", None),
            P(None, "tile", "coil", None),
            P("coil", None, "tile", None, None),
            P("tile", None, None, None),
            P("tile"),
            P(None, "tile", None, None),
        ),
        out_specs=(
            P(None, "tile", "coil", None),
            P(None, "tile", "coil", None),
            P(None, "tile", "coil", None),
        ),
        check_vma=False,
    )
```

```python
import functools
import math

import jax
import jax.numpy as jnp
import ml_dtypes
import numpy as np
from jax import lax
from jax.experimental import pallas as pl
from jax.experimental.pallas import tpu as pltpu
from jax.sharding import PartitionSpec as P

LANES = 128
VMEM = 24 * 1024 * 1024


def halves(values):
    high = values.astype(jnp.bfloat16)
    low = (values - high.astype(jnp.float32)).astype(jnp.bfloat16)
    return high, low


def dot_bf16(left, right, dims):
    return lax.dot_general(left, right, (dims, ((), ())), preferred_element_type=jnp.float32)


def dot_left(table, values, dims=((1,), (0,))):
    high, low = halves(values)
    return (
        dot_bf16(table[0], high, dims)
        + dot_bf16(table[0], low, dims)
        + dot_bf16(table[1], high, dims)
    )


def dot_right(values, table, dims=((1,), (0,))):
    high, low = halves(values)
    return (
        dot_bf16(high, table[0], dims)
        + dot_bf16(low, table[0], dims)
        + dot_bf16(high, table[1], dims)
    )


def fourier_tables(length):
    cells = np.arange(length)
    angle = 2.0 * math.pi / length * (cells[:, None] * cells[None, :] % length)
    cos_t = np.cos(angle) / math.sqrt(length)
    sin_t = np.sin(angle) / math.sqrt(length)
    found = []
    for sign in (1.0, -1.0):
        whole = np.block([[cos_t, -sign * sin_t], [sign * sin_t, cos_t]])
        high = whole.astype(ml_dtypes.bfloat16)
        low = (whole - high.astype(np.float64)).astype(ml_dtypes.bfloat16)
        found += [high, low]
    return jnp.asarray(np.stack(found))


def band_of_lane(planes, chunk):
    return lax.broadcasted_iota(jnp.int32, (4, LANES), 1) // planes % chunk


def in_window(band, first, chunk):
    past = band - first
    if chunk == 4:
        here = past >= 0
        return here, jnp.logical_not(here)
    here = jnp.logical_and(past >= 0, past < 4)
    return here, past < 4 - chunk


def call(kernel, outs, scratch, operands, flops, name, hbm=(), hbm_outs=(), vmem=(), fixed=()):
    operands = list(operands)
    for listed, space in ((fixed, pltpu.HBM), (vmem, pltpu.VMEM)):
        for at in listed:
            operands[at] = pltpu.with_memory_space_constraint(operands[at], space)
    here = pl.BlockSpec(memory_space=pltpu.VMEM)
    there = pl.BlockSpec(memory_space=pltpu.HBM)
    moved = sum(math.prod(a.shape) * a.dtype.itemsize for a in operands)
    return pl.pallas_call(
        kernel,
        out_shape=[jax.ShapeDtypeStruct(shape, jnp.float32) for shape in outs],
        in_specs=[there if at in hbm else here for at in range(len(operands))],
        out_specs=[there if at in hbm_outs else here for at in range(len(outs))],
        scratch_shapes=[
            pltpu.VMEM(shape, jnp.float32) if isinstance(shape, tuple) else shape
            for shape in scratch
        ],
        compiler_params=pltpu.CompilerParams(vmem_limit_bytes=VMEM),
        cost_estimate=pl.CostEstimate(flops=flops, bytes_accessed=moved, transcendentals=0),
        name=name,
    )(*operands)


def started(pairs, sems):
    copies = [
        pltpu.make_async_copy(source, to, sems.at[at]) for at, (source, to) in enumerate(pairs)
    ]
    for copy in copies:
        copy.start()
    return copies


def place_on_coil():
    coil = lax.axis_index("coil")
    return coil // 2, coil % 2


def quarters_of(chips, part):
    chip, core = place_on_coil()
    return [
        pl.multiple_of(((chip + hop) % chips * 2 + at) * part, part)
        for at in (core, 1 - core)
        for hop in range(chips)
    ]


def map_rows_kernel(s_ref, *refs, chips):
    outs, (held, sems) = refs[:-2], refs[-2:]
    chip, _ = place_on_coil()
    own = s_ref.shape[2] // chips
    for by in range(1, chips):
        rows = pl.ds(pl.multiple_of((chip + chips - by) % chips * own, own), own)
        for copy in started([(s_ref.at[:, :, rows, :], held)], sems):
            copy.wait()
        for copy in started([(held, outs[by - 1])], sems):
            copy.wait()


def map_rows(smap, chips):
    _, planes, length, _ = smap.shape
    shape = (2, planes, length // chips, length)
    return call(
        functools.partial(map_rows_kernel, chips=chips),
        [shape] * (chips - 1),
        [shape, pltpu.SemaphoreType.DMA((1,))],
        [smap],
        0,
        "map_rows",
        hbm=[0],
        fixed=[0],
        hbm_outs=range(chips - 1),
    )


def message_kernel(owner_ref, list_ref, out_ref):
    _, _, ntile, capacity = list_ref.shape
    out_ref[...] = jnp.zeros_like(out_ref)
    slots = owner_ref.shape[1]
    for to in range(ntile):
        for axis in range(3):
            out_ref[to, :, axis * capacity : (axis + 1) * capacity] = list_ref[axis, 0]
        out_ref[to, 0:1, 3 * capacity : 3 * capacity + slots] = owner_ref[...]


def message(block_owner, owner_list):
    ntile = owner_list.shape[2]
    return pl.pallas_call(
        message_kernel,
        out_shape=jax.ShapeDtypeStruct((ntile, ntile, LANES), jnp.int32),
        in_specs=[pl.BlockSpec(memory_space=pltpu.VMEM)] * 2,
        out_specs=pl.BlockSpec(memory_space=pltpu.VMEM),
        name="message",
    )(block_owner[None], owner_list)


def cut_boxes(info, grid, cos_ref, sin_ref, shift_ref, out_ref, gbuf, planes, chunk, slots):
    handlers = out_ref.shape[0]
    band = band_of_lane(planes, chunk)

    def cut(handler, carry):
        base = pl.multiple_of(handler * LANES, LANES)
        for slot in range(slots):
            block = handler * slots + slot
            here, after = in_window(band, info[1, block], chunk)
            first = grid[pl.ds(info[0, block], 4), :]
            second = grid[pl.ds(info[0, block] + LANES, 4), :]
            if chunk > 4:
                second = jnp.where(after, second, 0.0)
            gbuf[pl.ds(base + slot, 4, stride=slots), :] = jnp.where(here, first, second)
        return carry

    lax.fori_loop(0, handlers, cut, 0)
    high, low = halves(shift_ref[...])
    table = jnp.concatenate(
        [
            jnp.concatenate([high, high], axis=1),
            jnp.concatenate([low, jnp.zeros_like(low)], axis=1),
        ],
        axis=0,
    )
    for handler in range(handlers):
        rows = slice(handler * slots, (handler + 1) * slots)
        cos_b = jnp.concatenate([cos_ref[rows, :]] * 4, axis=0)
        sin_b = jnp.concatenate([sin_ref[rows, :]] * 4, axis=0)
        cells = gbuf[handler * LANES : (handler + 1) * LANES, :]
        turned = cells * cos_b + pltpu.roll(cells, LANES // 2, 1) * sin_b
        both = dot_bf16(table, jnp.concatenate(halves(turned), axis=1), ((1,), (1,)))
        out_ref[handler] = both[:32] + both[32:]


def forward_kernel(*refs, pieces, chunk, slots):
    p_hbm = refs[:pieces]
    s_hbm, table_hbm, info_hbm, cos_hbm, sin_hbm, shift_hbm, out_ref = refs[pieces : pieces + 7]
    pbuf, sbuf, tables, info, cos_ref, sin_ref, shift_ref = refs[pieces + 7 : pieces + 14]
    natural, ybuf, grid, gbuf, sems = refs[pieces + 14 :]
    _, planes, part, length = p_hbm[0].shape
    rows = length * planes
    starts = quarters_of(pieces // 2, part)
    order = [0, pieces // 2]
    order += [at for at in range(pieces) if at not in order]
    first = [(table_hbm.at[0:2], tables.at[0:2])]
    for at in order:
        first += [(p_hbm[at], pbuf.at[at]), (s_hbm.at[:, :, pl.ds(starts[at], part), :], sbuf.at[at])]
    last = [
        (table_hbm.at[2:4], tables.at[2:4]),
        (info_hbm, info),
        (cos_hbm, cos_ref),
        (sin_hbm, sin_ref),
        (shift_hbm, shift_ref),
    ]
    copies = started(first + last, sems)
    copies[0].wait()
    batch = min(planes, 256 // part)
    table = (tables[0], tables[1])
    for turn, at in enumerate(order):
        copies[1 + 2 * turn].wait()
        copies[2 + 2 * turn].wait()
        for base in range(0, planes, batch):
            bands = []
            for plane in range(base, base + batch):
                s_re = sbuf[at, 0, plane]
                s_im = sbuf[at, 1, plane]
                p_re = pbuf[at, 0, plane]
                p_im = pbuf[at, 1, plane]
                bands.append(
                    jnp.concatenate([s_re * p_re - s_im * p_im, s_re * p_im + s_im * p_re], axis=1)
                )
            done = dot_right(jnp.concatenate(bands, axis=0), table)
            for ri in range(2):
                half = done[:, ri * length : (ri + 1) * length]
                natural[ri, base : base + batch, pl.ds(starts[at], part), :] = half.reshape(
                    batch, part, length
                )
    for copy in copies[1 + 2 * pieces :]:
        copy.wait()
    table = (tables[2], tables[3])
    for pair in range(planes // 2):
        columns = [
            jnp.concatenate([natural[0, plane], natural[1, plane]], axis=0)
            for plane in (2 * pair, 2 * pair + 1)
        ]
        both = dot_left(table, jnp.concatenate(columns, axis=1))
        for inner in range(2):
            for ri in range(2):
                ybuf[pl.ds(ri * rows + 2 * pair + inner, length, stride=planes), :] = both[
                    ri * length : (ri + 1) * length, inner * LANES : (inner + 1) * LANES
                ]
    for band in range(length // chunk):
        re = ybuf[band * 64 : (band + 1) * 64, :]
        im = ybuf[rows + band * 64 : rows + (band + 1) * 64, :]
        grid[band * length : (band + 1) * length, :] = jnp.concatenate([re, im], axis=0).T
    cut_boxes(info, grid, cos_ref, sin_ref, shift_ref, out_ref, gbuf, planes, chunk, slots)


def forward(pieces, smap, tables, info, phases, shift, chunk, slots):
    _, planes, part, length = pieces[0].shape
    count = len(pieces)
    blocks = info.shape[1]
    operands = [*pieces, smap, tables, info, *phases, shift]
    return call(
        functools.partial(forward_kernel, pieces=count, chunk=chunk, slots=slots),
        [(blocks // slots, 32, LANES)],
        [
            (count, 2, planes, part, length),
            (count, 2, planes, part, length),
            pltpu.VMEM(tables.shape, tables.dtype),
            pltpu.SMEM(info.shape, info.dtype),
            (blocks, LANES),
            (blocks, LANES),
            shift.shape,
            (2, planes, length, length),
            (2 * length * planes, length),
            (length * (length // chunk + 1), LANES),
            (blocks * 4, LANES),
            pltpu.SemaphoreType.DMA((2 * count + 6,)),
        ],
        operands,
        48 * planes * length**3,
        "forward",
        hbm=range(len(operands)),
        fixed=range(count, len(operands)),
    )[0]


def regrid_kernel(parts_ref, matrix_ref, out_ref, held, done_sem):
    total = parts_ref[0]
    for at in range(1, parts_ref.shape[0]):
        total = total + parts_ref[at]
    along = lax.broadcasted_iota(jnp.int32, (8, LANES), 0) % 4
    sums = [jnp.zeros((8, LANES), jnp.float32) for _ in range(4)]
    for source in range(4):
        for d_z in range(4):
            value = total[8 * source : 8 * source + 8]
            if d_z:
                value = pltpu.roll(value, LANES - 32 * d_z, 1)
            for d_x in range(4):
                moved = value
                if d_x:
                    moved = jnp.where(
                        along + d_x < 4, pltpu.roll(value, 8 - d_x, 0), pltpu.roll(value, 4 - d_x, 0)
                    )
                for e in range(4):
                    at = 8 * (((e * 4 + source) * 4 + d_z) * 4 + d_x)
                    sums[e] = sums[e] + matrix_ref[at : at + 8] * moved
    done = jnp.concatenate(sums, axis=0)
    for at in range(held.shape[0]):
        held[at] = done
    copy = pltpu.make_async_copy(held, out_ref, done_sem)
    copy.start()
    copy.wait()


def regrid(parts, matrix, copies):
    shape = (copies,) + parts.shape[1:]
    return call(
        regrid_kernel,
        [shape],
        [shape, pltpu.SemaphoreType.DMA],
        [parts, matrix],
        10**7,
        "regrid",
        hbm_outs=[0],
        vmem=[1],
    )[0]


def place_boxes(info, chip, u_ref, cos_ref, sin_ref, shift_ref, outs, gbufs, planes, chunk, slots):
    chips = len(outs)
    handlers = u_ref.shape[0] // chips
    high, low = halves(shift_ref[...])
    table = jnp.concatenate([high, high, low, jnp.zeros_like(low)], axis=0)
    for handler in range(handlers):
        rows = slice(handler * slots, (handler + 1) * slots)
        cos_b = jnp.concatenate([cos_ref[rows, :]] * 4, axis=0)
        sin_b = jnp.concatenate([sin_ref[rows, :]] * 4, axis=0)
        for hop in range(chips):
            u_hi, u_lo = (
                half.astype(jnp.float32) for half in halves(u_ref[(chip + hop) % chips * handlers + handler])
            )
            stack = jnp.concatenate([u_hi, u_lo, u_hi, jnp.zeros_like(u_hi)], axis=0)
            cells = dot_bf16(stack.T.astype(jnp.bfloat16), table, ((1,), (0,)))
            turned = cells * cos_b - pltpu.roll(cells, LANES // 2, 1) * sin_b
            gbufs[hop][handler * LANES : (handler + 1) * LANES, :] = turned
    band = band_of_lane(planes, chunk)

    def put(handler, carry):
        base = pl.multiple_of(handler * LANES, LANES)
        for slot in range(slots):
            block = handler * slots + slot
            here, after = in_window(band, info[1, block], chunk)
            first = pl.ds(info[0, block], 4)
            second = pl.ds(info[0, block] + LANES, 4)
            for hop in range(chips):
                cells = gbufs[hop][pl.ds(base + slot, 4, stride=slots), :]
                old_first = outs[hop][first, :]
                old_second = outs[hop][second, :]
                outs[hop][first, :] = old_first + jnp.where(here, cells, 0.0)
                outs[hop][second, :] = old_second + jnp.where(after, cells, 0.0)
        return carry

    lax.fori_loop(0, handlers, put, 0)


def inverse_kernel(*refs, part, length, chunk, slots, chips):
    u_ref, info_hbm, cos_hbm, sin_hbm, shift_hbm, table_hbm, s_hbm = refs[:7]
    far_maps = refs[7 : 6 + chips]
    outs = refs[6 + chips : 8 + chips]
    refs = refs[8 + chips :]
    grids, gbufs, refs = refs[:chips], refs[chips : 2 * chips], refs[2 * chips :]
    info, cos_ref, sin_ref, shift_ref, table_ref, ybuf, images, maps, sems = refs
    planes = s_hbm.shape[1]
    rows = length * planes
    own = length // chips
    chip, core = place_on_coil()
    own_rows = pl.multiple_of(chip * own, own)
    pairs = [
        (info_hbm, info),
        (cos_hbm, cos_ref),
        (sin_hbm, sin_ref),
        (shift_hbm, shift_ref),
        (table_hbm, table_ref),
        (s_hbm.at[:, :, pl.ds(own_rows, own), :], maps.at[0]),
    ]
    pairs += [(far_map, maps.at[at]) for at, far_map in enumerate(far_maps, 1)]
    copies = started(pairs, sems)
    for grid in grids:
        grid[...] = jnp.zeros_like(grid)
    for copy in copies[:4]:
        copy.wait()
    place_boxes(info, chip, u_ref, cos_ref, sin_ref, shift_ref, grids, gbufs, planes, chunk, slots)
    for copy in copies[4:]:
        copy.wait()
    table = []
    for half in range(2):
        bands = [
            table_ref[half, pl.ds(pl.multiple_of(ri * length + own_rows, own), own), :]
            for ri in range(2)
        ]
        table.append(jnp.concatenate(bands, axis=0))
    for hop in range(chips):
        for band in range(length // chunk):
            tile = grids[hop][band * length : (band + 1) * length, :].T
            ybuf[hop, band * 64 : (band + 1) * 64, :] = tile[:64]
            ybuf[hop, rows + band * 64 : rows + (band + 1) * 64, :] = tile[64:]
        for pair in range(planes // 2):
            columns = [
                jnp.concatenate(
                    [
                        ybuf[hop, pl.ds(ri * rows + plane, length, stride=planes), :]
                        for ri in range(2)
                    ],
                    axis=0,
                )
                for plane in (2 * pair, 2 * pair + 1)
            ]
            done = dot_left(table, jnp.concatenate(columns, axis=1))
            for inner in range(2):
                for ri in range(2):
                    images[hop, ri, 2 * pair + inner] = done[
                        ri * own : (ri + 1) * own, inner * LANES : (inner + 1) * LANES
                    ]
    table = (table_ref[2], table_ref[3])
    batch = min(planes, 256 // part)
    for at, half in enumerate((1 - core, core)):
        local = pl.ds(pl.multiple_of(half * part, part), part)
        for base in range(0, planes, batch):
            total_re, total_im = 0.0, 0.0
            for hop in range(chips):
                bands = [
                    jnp.concatenate([images[hop, ri, plane, local, :] for ri in range(2)], axis=1)
                    for plane in range(base, base + batch)
                ]
                done = dot_right(jnp.concatenate(bands, axis=0), table)
                i_re = done[:, :length].reshape(batch, part, length)
                i_im = done[:, length:].reshape(batch, part, length)
                s_re = maps[hop, 0, base : base + batch, local, :]
                s_im = maps[hop, 1, base : base + batch, local, :]
                total_re = total_re + (s_re * i_re + s_im * i_im)
                total_im = total_im + (s_re * i_im - s_im * i_re)
            outs[at][0, base : base + batch] = total_re
            outs[at][1, base : base + batch] = total_im


def inverse(spread, info, phases, shift, tables, smap, far_maps, part, chunk, slots):
    _, planes, length, _ = smap.shape
    chips = len(far_maps) + 1
    blocks = info.shape[1]
    rows = length * (length // chunk + 1)
    own = (chips, 2, planes, 2 * part, length)
    operands = [spread, info, *phases, shift, tables, smap, *far_maps]
    return call(
        functools.partial(
            inverse_kernel, part=part, length=length, chunk=chunk, slots=slots, chips=chips
        ),
        [(2, planes, part, length)] * 2,
        [(rows, LANES)] * chips
        + [(blocks * 4, LANES)] * chips
        + [
            pltpu.SMEM(info.shape, info.dtype),
            (blocks, LANES),
            (blocks, LANES),
            shift.shape,
            pltpu.VMEM(tables.shape, tables.dtype),
            (chips, 2 * length * planes, length),
            own,
            own,
            pltpu.SemaphoreType.DMA((5 + chips,)),
        ],
        operands,
        48 * planes * length**3,
        "inverse",
        hbm=range(1, len(operands)),
        fixed=range(1, 7),
    )


def sums_kernel(*refs, terms):
    term_refs = refs[:terms]
    p_ref, r_ref, normal_ref, out_ref = refs[terms:]
    shape = p_ref.shape

    def add(plane, held):
        held = list(held)
        for ri in range(2):
            normal = term_refs[0][ri, plane]
            for term in term_refs[1:]:
                normal = normal + term[ri, plane]
            normal_ref[ri, plane] = normal
            p = p_ref[ri, plane]
            r = r_ref[ri, plane]
            for at, product in enumerate((r * r, p * normal, r * normal, normal * normal)):
                held[at] = held[at] + jnp.sum(product.reshape(-1, 8, LANES), axis=0)
        return tuple(held)

    start = tuple(jnp.zeros((8, LANES), jnp.float32) for _ in range(4))
    held = lax.fori_loop(0, shape[1], add, start, unroll=4)
    lane = lax.broadcasted_iota(jnp.int32, out_ref.shape, 1)
    found = jnp.zeros(out_ref.shape, jnp.float32)
    for at in range(4):
        found = jnp.where(lane == at, jnp.sum(held[at]), found)
    out_ref[...] = found


def sums(terms, p, r, devices):
    kernel = functools.partial(sums_kernel, terms=len(terms))
    return call(kernel, [p.shape, (devices, LANES)], [], [*terms, p, r], 10**7, "sums")


def finish_kernel(total_ref, x_ref, r_ref, p_ref, normal_ref, x_out, r_out, p_out):
    total = jnp.sum(total_ref[...], axis=0, keepdims=True)
    r_r, p_n, r_n, n_n = (total[:, at : at + 1] for at in range(4))
    alpha = r_r / p_n
    beta = (r_r + alpha * (alpha * n_n - 2.0 * r_n)) / r_r
    for plane in range(x_ref.shape[1]):
        for ri in range(2):
            p = p_ref[ri, plane]
            next_r = r_ref[ri, plane] - alpha * normal_ref[ri, plane]
            x_out[ri, plane] = x_ref[ri, plane] + alpha * p
            r_out[ri, plane] = next_r
            p_out[ri, plane] = next_r + beta * p


def finish(total, x, r, p, normal):
    return call(finish_kernel, [x.shape] * 3, [], [total, x, r, p, normal], 10**7, "finish")


def matrices_kernel(info_hbm, weights_ref, out_ref, held, info, sem, *, slots):
    base = lax.axis_index("tile") * slots
    copy = pltpu.make_async_copy(info_hbm, info, sem)
    copy.start()
    copy.wait()

    def one(block, carry):
        w_x = weights_ref[block, 0]
        w_y = weights_ref[block, 1]
        w_z = weights_ref[block, 2]
        twice = jnp.concatenate([w_x, w_x], axis=0)
        rolled = [twice] + [pltpu.roll(twice, 8 - d, 0) for d in range(1, 4)]
        low = lax.broadcasted_iota(jnp.int32, (8, LANES), 0) < 4
        along_x = [twice * jnp.where(low, rolled[d], rolled[d + 1]) for d in (0, 2)]
        right = []
        for f in range(4):
            for d_z in range(4):
                other = (f + d_z) % 4
                along_z = w_z[f : f + 1] * w_z[other : other + 1]
                right += [along * along_z for along in along_x]
        turned = pltpu.roll(
            jnp.concatenate([w_y, w_y], axis=0), info[1, base + block] % 4, 0
        )[:4]
        left = jnp.concatenate([turned * turned[e : e + 1] for e in range(4)], axis=0)
        done = dot_right(left, halves(jnp.concatenate(right, axis=0)), ((1,), (1,)))
        for f in range(4):
            lanes = done[:, f // 2 * LANES : (f // 2 + 1) * LANES]
            if f % 2:
                lanes = pltpu.roll(lanes, LANES // 2, 1)
            held[pl.ds(f * slots + block, 16, stride=LANES), :] = lanes
        return carry

    lax.fori_loop(0, slots, one, 0, unroll=4)

    def turn(pair, carry):
        at = pl.ds(pl.multiple_of(pair * LANES, LANES), LANES)
        rows = held[at, :].T
        for group in range(16):
            four = rows[4 * group : 4 * group + 4]
            out_ref[pl.ds(pl.multiple_of(pair * LANES + 8 * group, 8), 8), :] = jnp.concatenate(
                [four, four], axis=0
            )
        return carry

    lax.fori_loop(0, 16, turn, 0, unroll=2)


def block_matrices(info, weights):
    return call(
        functools.partial(matrices_kernel, slots=weights.shape[0]),
        [(16 * LANES, LANES)],
        [(16 * LANES, LANES), pltpu.SMEM(info.shape, info.dtype), pltpu.SemaphoreType.DMA],
        [info, weights],
        10**9,
        "matrices",
        hbm=[0],
    )[0]


def block_offsets(gathered, slots, ntile, capacity):
    owners = gathered[:, 0, 3 * capacity : 3 * capacity + slots]
    lists = gathered[:, :, : 3 * capacity].reshape(ntile, ntile, 3, capacity)
    earlier = jnp.tril(jnp.ones((slots, slots), jnp.int32), -1)
    same = (owners[:, :, None] == owners[:, None, :]).astype(jnp.int32)
    ranks = jnp.sum(same * earlier[None], axis=2)
    wanted = owners * capacity + ranks
    lists = jnp.transpose(lists, (2, 1, 0, 3)).reshape(3, ntile, 1, ntile * capacity)
    hit = wanted[:, :, None] == jnp.arange(ntile * capacity, dtype=jnp.int32)
    found = jnp.sum(jnp.where(hit[None], lists, 0), axis=3)
    return found[0], found[1] + owners * (LANES // ntile), found[2]


def shards(image_p, image_x, image_r, sensitivity, kb_weights, block_owner, owner_list):
    ntile = lax.axis_size("tile")
    ncoil = lax.axis_size("coil")
    chips = ncoil // 2
    slots = kb_weights.shape[0]
    capacity = owner_list.shape[3]
    planes, length = image_p.shape[1], image_p.shape[3]
    part = image_p.shape[2]
    chunk = LANES // (2 * planes)
    tile = lax.axis_index("tile")
    smap = sensitivity[0]
    tables = fourier_tables(length)

    def from_chip(values, by):
        pairs = [
            (a * 2 + k, (a - by) % chips * 2 + k) for a in range(chips) for k in range(2)
        ]
        return lax.ppermute(values, "coil", pairs)

    def other_core(values):
        pairs = [(a * 2 + k, a * 2 + 1 - k) for a in range(chips) for k in range(2)]
        return lax.ppermute(values, "coil", pairs)

    p_same = [image_p] + [from_chip(image_p, by) for by in range(1, chips)]
    p_other = [other_core(piece) for piece in p_same]
    gathered = lax.all_to_all(message(block_owner, owner_list), "tile", 0, 0, tiled=True)
    gathered, _ = lax.optimization_barrier((gathered, p_same[1:]))
    far_rows = map_rows(smap, chips)
    far_rows, _ = lax.optimization_barrier((far_rows, p_same[1:]))
    far_maps = [from_chip(rows, by) for by, rows in enumerate(far_rows, 1)]

    off_x, off_y, off_z = block_offsets(gathered, slots, ntile, capacity)
    info = jnp.stack(
        [(off_y // chunk * length + off_z).reshape(-1), (off_y % chunk).reshape(-1)]
    )
    lane = jnp.arange(LANES, dtype=jnp.int32)
    lane_ri = lane // (LANES // 2)
    lane_q = lane // planes % chunk
    lane_x = lane % planes + tile * planes
    unit = 2.0 * math.pi / length
    angle = unit * (off_x.reshape(-1, 1) * lane_x[None] % length).astype(jnp.float32)
    phases = (jnp.cos(angle), jnp.sin(angle) * jnp.where(lane_ri == 0, 1.0, -1.0)[None])
    row = jnp.arange(32, dtype=jnp.int32)[:, None]
    row_q, row_ri, row_i = row // 8, row // 4 % 2, row % 4
    angle = unit * (row_i * lane_x[None] % length).astype(jnp.float32)
    sine = jnp.where(row_ri == 0, 1.0, -1.0) * jnp.sin(angle)
    shift = jnp.where(row_ri == lane_ri[None], jnp.cos(angle), sine)
    shift = jnp.where(lane_q[None] % 4 == row_q, shift / math.sqrt(length), 0.0)
    partial = forward(p_same + p_other, smap, tables, info, phases, shift, chunk, slots)
    partial, weights = lax.optimization_barrier((partial, kb_weights))
    parts = lax.all_to_all(partial, "tile", 0, 0, tiled=True)
    done = regrid(parts, block_matrices(info, weights), chips * ntile)
    groups = [
        [at * ntile + t for at in range(ncoil) if at % 2 == k for t in range(ntile)]
        for k in range(2)
    ]
    spread = lax.all_to_all(
        done, ("coil", "tile"), 0, 0, axis_index_groups=groups, tiled=True
    )
    sent, kept = inverse(
        spread, info, phases, shift, tables, smap, far_maps, part, chunk, slots
    )
    normal, found = sums([kept, other_core(sent)], image_p, image_r, ncoil * ntile)
    total = lax.all_to_all(found, ("coil", "tile"), 0, 0, tiled=True)
    return tuple(finish(total, image_x, image_r, image_p, normal))


def solution(mesh):
    return jax.shard_map(
        shards,
        mesh=mesh,
        in_specs=(
            P(None, "tile", "coil", None),
            P(None, "tile", "coil", None),
            P(None, "tile", "coil", None),
            P("coil", None, "tile", None, None),
            P("tile", None, None, None),
            P("tile"),
            P(None, "tile", None, None),
        ),
        out_specs=(
            P(None, "tile", "coil", None),
            P(None, "tile", "coil", None),
            P(None, "tile", "coil", None),
        ),
        check_vma=False,
    )
```

```python
import functools
import math

import jax
import jax.numpy as jnp
import ml_dtypes
import numpy as np
from jax import lax
from jax.experimental import pallas as pl
from jax.experimental.pallas import tpu as pltpu
from jax.sharding import PartitionSpec as P

LANES = 128
VMEM = 24 * 1024 * 1024


def halves(values):
    high = values.astype(jnp.bfloat16)
    low = (values - high.astype(jnp.float32)).astype(jnp.bfloat16)
    return high, low


def dot_bf16(left, right, dims):
    return lax.dot_general(left, right, (dims, ((), ())), preferred_element_type=jnp.float32)


def dot_left(table, values, dims=((1,), (0,))):
    high, low = halves(values)
    return (
        dot_bf16(table[0], high, dims)
        + dot_bf16(table[0], low, dims)
        + dot_bf16(table[1], high, dims)
    )


def dot_right(values, table, dims=((1,), (0,))):
    high, low = halves(values)
    return (
        dot_bf16(high, table[0], dims)
        + dot_bf16(low, table[0], dims)
        + dot_bf16(high, table[1], dims)
    )


def fourier_tables(length):
    cells = np.arange(length)
    angle = 2.0 * math.pi / length * (cells[:, None] * cells[None, :] % length)
    cos_t = np.cos(angle) / math.sqrt(length)
    sin_t = np.sin(angle) / math.sqrt(length)
    found = []
    for sign in (1.0, -1.0):
        whole = np.block([[cos_t, -sign * sin_t], [sign * sin_t, cos_t]])
        high = whole.astype(ml_dtypes.bfloat16)
        low = (whole - high.astype(np.float64)).astype(ml_dtypes.bfloat16)
        found += [high, low]
    return jnp.asarray(np.stack(found))


def band_of_lane(planes, chunk):
    return lax.broadcasted_iota(jnp.int32, (4, LANES), 1) // planes % chunk


def in_window(band, first, chunk):
    past = band - first
    if chunk == 4:
        here = past >= 0
        return here, jnp.logical_not(here)
    here = jnp.logical_and(past >= 0, past < 4)
    return here, past < 4 - chunk


def call(kernel, outs, scratch, operands, flops, name, hbm=(), hbm_outs=(), vmem=(), fixed=()):
    operands = list(operands)
    for listed, space in ((fixed, pltpu.HBM), (vmem, pltpu.VMEM)):
        for at in listed:
            operands[at] = pltpu.with_memory_space_constraint(operands[at], space)
    here = pl.BlockSpec(memory_space=pltpu.VMEM)
    there = pl.BlockSpec(memory_space=pltpu.HBM)
    moved = sum(math.prod(a.shape) * a.dtype.itemsize for a in operands)
    return pl.pallas_call(
        kernel,
        out_shape=[
            jax.ShapeDtypeStruct(shape, jnp.float32) if isinstance(shape, tuple) else shape
            for shape in outs
        ],
        in_specs=[there if at in hbm else here for at in range(len(operands))],
        out_specs=[there if at in hbm_outs else here for at in range(len(outs))],
        scratch_shapes=[
            pltpu.VMEM(shape, jnp.float32) if isinstance(shape, tuple) else shape
            for shape in scratch
        ],
        compiler_params=pltpu.CompilerParams(vmem_limit_bytes=VMEM),
        cost_estimate=pl.CostEstimate(flops=flops, bytes_accessed=moved, transcendentals=0),
        name=name,
    )(*operands)


def started(pairs, sems):
    copies = [
        pltpu.make_async_copy(source, to, sems.at[at]) for at, (source, to) in enumerate(pairs)
    ]
    for copy in copies:
        copy.start()
    return copies


def place_on_coil():
    coil = lax.axis_index("coil")
    return coil // 2, coil % 2


def quarters_of(chips, part):
    chip, core = place_on_coil()
    return [
        pl.multiple_of(((chip + hop) % chips * 2 + at) * part, part)
        for at in (core, 1 - core)
        for hop in range(chips)
    ]


def z_of_coil(p_ref, s_ref, half, table, out_ref, rows):
    _, planes, part, length = p_ref.shape
    batch = min(planes, 256 // part)
    from_rows = pl.ds(pl.multiple_of(half * part, part), part)
    for base in range(0, planes, batch):
        bands = []
        for plane in range(base, base + batch):
            s_re = s_ref[0, plane, from_rows, :]
            s_im = s_ref[1, plane, from_rows, :]
            p_re = p_ref[0, plane]
            p_im = p_ref[1, plane]
            bands.append(
                jnp.concatenate([s_re * p_re - s_im * p_im, s_re * p_im + s_im * p_re], axis=1)
            )
        done = dot_right(jnp.concatenate(bands, axis=0), table)
        for ri in range(2):
            found = done[:, ri * length : (ri + 1) * length]
            out_ref[ri, base : base + batch, rows, :] = found.reshape(batch, part, length)


def near_kernel(p_own, p_other, s_hbm, table_hbm, *refs, chips):
    maps, (out_ref, tables, sems) = refs[:chips], refs[chips:]
    chip, core = place_on_coil()
    part = p_own.shape[2]
    own = 2 * part
    pairs = [(table_hbm, tables)]
    for hop in range(chips):
        rows = pl.ds(pl.multiple_of((chip + hop) % chips * own, own), own)
        pairs.append((s_hbm.at[:, :, rows, :], maps[hop]))
    copies = started(pairs, sems)
    copies[0].wait()
    copies[1].wait()
    table = (tables[0], tables[1])
    for half, p_ref in ((core, p_own), (1 - core, p_other)):
        rows = pl.ds(pl.multiple_of(half * part, part), part)
        z_of_coil(p_ref, maps[0], half, table, out_ref, rows)
    for copy in copies[2:]:
        copy.wait()


def near(p_own, p_other, smap, tables, chips):
    _, planes, part, length = p_own.shape
    shape = (2, planes, 2 * part, length)
    *maps, done, held = call(
        functools.partial(near_kernel, chips=chips),
        [shape] * (chips + 1) + [jax.ShapeDtypeStruct(tables.shape, tables.dtype)],
        [pltpu.SemaphoreType.DMA((chips + 1,))],
        [p_own, p_other, smap, tables],
        48 * planes * part * length * length,
        "near",
        hbm=[2, 3],
        fixed=[2],
    )
    return maps, done, held


def message_kernel(owner_ref, list_ref, out_ref):
    _, _, ntile, capacity = list_ref.shape
    out_ref[...] = jnp.zeros_like(out_ref)
    slots = owner_ref.shape[1]
    for to in range(ntile):
        for axis in range(3):
            out_ref[to, :, axis * capacity : (axis + 1) * capacity] = list_ref[axis, 0]
        out_ref[to, 0:1, 3 * capacity : 3 * capacity + slots] = owner_ref[...]


def message(block_owner, owner_list):
    ntile = owner_list.shape[2]
    return pl.pallas_call(
        message_kernel,
        out_shape=jax.ShapeDtypeStruct((ntile, ntile, LANES), jnp.int32),
        in_specs=[pl.BlockSpec(memory_space=pltpu.VMEM)] * 2,
        out_specs=pl.BlockSpec(memory_space=pltpu.VMEM),
        name="message",
    )(block_owner[None], owner_list)


def cut_boxes(info, grid, turns_ref, shift_ref, out_ref, gbuf, planes, chunk, slots):
    handlers = out_ref.shape[0]
    band = band_of_lane(planes, chunk)

    def cut(handler, carry):
        base = pl.multiple_of(handler * LANES, LANES)
        for slot in range(slots):
            block = handler * slots + slot
            here, after = in_window(band, info[1, block], chunk)
            first = grid[pl.ds(info[0, block], 4), :]
            second = grid[pl.ds(info[0, block] + LANES, 4), :]
            if chunk > 4:
                second = jnp.where(after, second, 0.0)
            cells = jnp.where(here, first, second)
            turn = pl.ds(info[2, block], 1)
            cells = cells * turns_ref[0, turn, :] + pltpu.roll(cells, LANES // 2, 1) * turns_ref[
                1, turn, :
            ]
            gbuf[pl.ds(base + slot, 4, stride=slots), :] = cells
        return carry

    lax.fori_loop(0, handlers, cut, 0)
    high, low = halves(shift_ref[...])
    table = jnp.concatenate(
        [
            jnp.concatenate([high, high], axis=1),
            jnp.concatenate([low, jnp.zeros_like(low)], axis=1),
        ],
        axis=0,
    )
    for handler in range(handlers):
        cells = gbuf[handler * LANES : (handler + 1) * LANES, :]
        both = dot_bf16(table, jnp.concatenate(halves(cells), axis=1), ((1,), (1,)))
        out_ref[handler] = both[:32] + both[32:]


def forward_kernel(near_ref, *refs, chips, chunk, slots):
    far = chips - 1
    p_refs = refs[: 2 * far]
    maps = refs[2 * far : 3 * far]
    tables, turns_ref, shift_ref, info_hbm, out_ref = refs[3 * far : 3 * far + 5]
    info, natural, ybuf, grid, gbuf, sems = refs[3 * far + 5 :]
    _, planes, own, length = near_ref.shape
    rows = length * planes
    chip, core = place_on_coil()
    (copy,) = started([(info_hbm, info)], sems)
    table = (tables[0], tables[1])
    starts = quarters_of(chips, own // 2)
    for hop in range(1, chips):
        for at, half in enumerate((core, 1 - core)):
            to = pl.ds(starts[at * chips + hop], own // 2)
            z_of_coil(p_refs[at * far + hop - 1], maps[hop - 1], half, table, natural, to)
    for ri in range(2):
        natural[ri, :, pl.ds(pl.multiple_of(chip * own, own), own), :] = near_ref[ri]
    table = (tables[2], tables[3])
    for pair in range(planes // 2):
        columns = [
            jnp.concatenate([natural[0, plane], natural[1, plane]], axis=0)
            for plane in (2 * pair, 2 * pair + 1)
        ]
        both = dot_left(table, jnp.concatenate(columns, axis=1))
        for inner in range(2):
            for ri in range(2):
                ybuf[pl.ds(ri * rows + 2 * pair + inner, length, stride=planes), :] = both[
                    ri * length : (ri + 1) * length, inner * LANES : (inner + 1) * LANES
                ]
    for band in range(length // chunk):
        re = ybuf[band * 64 : (band + 1) * 64, :]
        im = ybuf[rows + band * 64 : rows + (band + 1) * 64, :]
        grid[band * length : (band + 1) * length, :] = jnp.concatenate([re, im], axis=0).T
    copy.wait()
    cut_boxes(info, grid, turns_ref, shift_ref, out_ref, gbuf, planes, chunk, slots)


def forward(done, pieces, maps, tables, turns, shift, info, chunk, slots):
    _, planes, own, length = done.shape
    blocks = info.shape[1]
    chips = len(maps) + 1
    operands = [done, *pieces, *maps, tables, turns, shift, info]
    count = len(operands)
    return call(
        functools.partial(forward_kernel, chips=chips, chunk=chunk, slots=slots),
        [(blocks // slots, 32, LANES)],
        [
            pltpu.SMEM(info.shape, info.dtype),
            (2, planes, length, length),
            (2 * length * planes, length),
            (length * (length // chunk + 1), LANES),
            (blocks * 4, LANES),
            pltpu.SemaphoreType.DMA((1,)),
        ],
        operands,
        48 * planes * length**3,
        "forward",
        hbm=[count - 1],
        fixed=[count - 1],
        vmem=[0, *range(count - 3 - chips, count - 1)],
    )[0]


def regrid_kernel(parts_ref, matrix_ref, out_ref, held, done_sem):
    total = parts_ref[0]
    for at in range(1, parts_ref.shape[0]):
        total = total + parts_ref[at]
    along = lax.broadcasted_iota(jnp.int32, (8, LANES), 0) % 4
    sums = [jnp.zeros((8, LANES), jnp.float32) for _ in range(4)]
    for source in range(4):
        for d_z in range(4):
            value = total[8 * source : 8 * source + 8]
            if d_z:
                value = pltpu.roll(value, LANES - 32 * d_z, 1)
            for d_x in range(4):
                moved = value
                if d_x:
                    moved = jnp.where(
                        along + d_x < 4, pltpu.roll(value, 8 - d_x, 0), pltpu.roll(value, 4 - d_x, 0)
                    )
                for e in range(4):
                    at = 8 * (((e * 4 + source) * 4 + d_z) * 4 + d_x)
                    sums[e] = sums[e] + matrix_ref[at : at + 8] * moved
    done = jnp.concatenate(sums, axis=0)
    for at in range(held.shape[0]):
        held[at] = done
    copy = pltpu.make_async_copy(held, out_ref, done_sem)
    copy.start()
    copy.wait()


def regrid(parts, matrix, copies):
    shape = (copies,) + parts.shape[1:]
    return call(
        regrid_kernel,
        [shape],
        [shape, pltpu.SemaphoreType.DMA],
        [parts, matrix],
        10**7,
        "regrid",
        hbm_outs=[0],
        vmem=[1],
    )[0]


def place_boxes(info, chip, u_ref, turns_ref, shift_ref, outs, gbufs, planes, chunk, slots):
    chips = len(outs)
    handlers = u_ref.shape[0] // chips
    high, low = halves(shift_ref[...])
    table = jnp.concatenate([high, high, low, jnp.zeros_like(low)], axis=0)
    for handler in range(handlers):
        for hop in range(chips):
            u_hi, u_lo = (
                half.astype(jnp.float32)
                for half in halves(u_ref[(chip + hop) % chips * handlers + handler])
            )
            stack = jnp.concatenate([u_hi, u_lo, u_hi, jnp.zeros_like(u_hi)], axis=0)
            gbufs[hop][handler * LANES : (handler + 1) * LANES, :] = dot_bf16(
                stack.T.astype(jnp.bfloat16), table, ((1,), (0,))
            )
    band = band_of_lane(planes, chunk)

    def put(handler, carry):
        base = pl.multiple_of(handler * LANES, LANES)
        for slot in range(slots):
            block = handler * slots + slot
            here, after = in_window(band, info[1, block], chunk)
            first = pl.ds(info[0, block], 4)
            second = pl.ds(info[0, block] + LANES, 4)
            turn = pl.ds(info[2, block], 1)
            cos_b, sin_b = turns_ref[0, turn, :], turns_ref[1, turn, :]
            for hop in range(chips):
                cells = gbufs[hop][pl.ds(base + slot, 4, stride=slots), :]
                cells = cells * cos_b - pltpu.roll(cells, LANES // 2, 1) * sin_b
                old_first = outs[hop][first, :]
                old_second = outs[hop][second, :]
                outs[hop][first, :] = old_first + jnp.where(here, cells, 0.0)
                outs[hop][second, :] = old_second + jnp.where(after, cells, 0.0)
        return carry

    lax.fori_loop(0, handlers, put, 0)


def inverse_kernel(*refs, part, length, chunk, slots, chips):
    u_ref, table_ref, turns_ref, shift_ref, own_map, info_hbm = refs[:6]
    far_maps = refs[6 : 5 + chips]
    outs = refs[5 + chips : 7 + chips]
    refs = refs[7 + chips :]
    grids, gbufs, refs = refs[:chips], refs[chips : 2 * chips], refs[2 * chips :]
    info, ybuf, images, maps, sems = refs
    planes = own_map.shape[1]
    rows = length * planes
    own = length // chips
    chip, core = place_on_coil()
    own_rows = pl.multiple_of(chip * own, own)
    copies = started(
        [(info_hbm, info)] + [(far_map, maps.at[at]) for at, far_map in enumerate(far_maps)], sems
    )
    for grid in grids:
        grid[...] = jnp.zeros_like(grid)
    copies[0].wait()
    place_boxes(info, chip, u_ref, turns_ref, shift_ref, grids, gbufs, planes, chunk, slots)
    for copy in copies[1:]:
        copy.wait()
    table = []
    for half in range(2):
        bands = [
            table_ref[half, pl.ds(pl.multiple_of(ri * length + own_rows, own), own), :]
            for ri in range(2)
        ]
        table.append(jnp.concatenate(bands, axis=0))
    for hop in range(chips):
        for band in range(length // chunk):
            tile = grids[hop][band * length : (band + 1) * length, :].T
            ybuf[hop, band * 64 : (band + 1) * 64, :] = tile[:64]
            ybuf[hop, rows + band * 64 : rows + (band + 1) * 64, :] = tile[64:]
        for pair in range(planes // 2):
            columns = [
                jnp.concatenate(
                    [
                        ybuf[hop, pl.ds(ri * rows + plane, length, stride=planes), :]
                        for ri in range(2)
                    ],
                    axis=0,
                )
                for plane in (2 * pair, 2 * pair + 1)
            ]
            done = dot_left(table, jnp.concatenate(columns, axis=1))
            for inner in range(2):
                for ri in range(2):
                    images[hop, ri, 2 * pair + inner] = done[
                        ri * own : (ri + 1) * own, inner * LANES : (inner + 1) * LANES
                    ]
    table = (table_ref[2], table_ref[3])
    batch = min(planes, 256 // part)
    for at, half in enumerate((1 - core, core)):
        local = pl.ds(pl.multiple_of(half * part, part), part)
        for base in range(0, planes, batch):
            total_re, total_im = 0.0, 0.0
            for hop in range(chips):
                bands = [
                    jnp.concatenate([images[hop, ri, plane, local, :] for ri in range(2)], axis=1)
                    for plane in range(base, base + batch)
                ]
                done = dot_right(jnp.concatenate(bands, axis=0), table)
                i_re = done[:, :length].reshape(batch, part, length)
                i_im = done[:, length:].reshape(batch, part, length)
                s_map = maps.at[hop - 1] if hop else own_map
                s_re = s_map[0, base : base + batch, local, :]
                s_im = s_map[1, base : base + batch, local, :]
                total_re = total_re + (s_re * i_re + s_im * i_im)
                total_im = total_im + (s_re * i_im - s_im * i_re)
            outs[at][0, base : base + batch] = total_re
            outs[at][1, base : base + batch] = total_im


def inverse(spread, tables, turns, shift, own_map, info, far_maps, part, chunk, slots):
    _, planes, own, length = own_map.shape
    chips = len(far_maps) + 1
    blocks = info.shape[1]
    rows = length * (length // chunk + 1)
    return call(
        functools.partial(
            inverse_kernel, part=part, length=length, chunk=chunk, slots=slots, chips=chips
        ),
        [(2, planes, part, length)] * 2,
        [(rows, LANES)] * chips
        + [(blocks * 4, LANES)] * chips
        + [
            pltpu.SMEM(info.shape, info.dtype),
            (chips, 2 * length * planes, length),
            (chips, 2, planes, own, length),
            (chips - 1, 2, planes, own, length),
            pltpu.SemaphoreType.DMA((chips,)),
        ],
        [spread, tables, turns, shift, own_map, info, *far_maps],
        48 * planes * length**3,
        "inverse",
        hbm=range(5, 5 + chips),
        fixed=[5],
        vmem=[1, 2, 3, 4],
    )


def sums_kernel(*refs, terms):
    term_refs = refs[:terms]
    p_ref, r_ref, normal_ref, out_ref = refs[terms:]
    shape = p_ref.shape

    def add(plane, held):
        held = list(held)
        for ri in range(2):
            normal = term_refs[0][ri, plane]
            for term in term_refs[1:]:
                normal = normal + term[ri, plane]
            normal_ref[ri, plane] = normal
            p = p_ref[ri, plane]
            r = r_ref[ri, plane]
            for at, product in enumerate((r * r, p * normal, r * normal, normal * normal)):
                held[at] = held[at] + jnp.sum(product.reshape(-1, 8, LANES), axis=0)
        return tuple(held)

    start = tuple(jnp.zeros((8, LANES), jnp.float32) for _ in range(4))
    held = lax.fori_loop(0, shape[1], add, start, unroll=4)
    lane = lax.broadcasted_iota(jnp.int32, out_ref.shape, 1)
    found = jnp.zeros(out_ref.shape, jnp.float32)
    for at in range(4):
        found = jnp.where(lane == at, jnp.sum(held[at]), found)
    out_ref[...] = found


def sums(terms, p, r, devices):
    kernel = functools.partial(sums_kernel, terms=len(terms))
    return call(kernel, [p.shape, (devices, LANES)], [], [*terms, p, r], 10**7, "sums")


def finish_kernel(total_ref, x_ref, r_ref, p_ref, normal_ref, *refs):
    outs, held, sems = refs[:3], refs[3:6], refs[6]
    total = jnp.sum(total_ref[...], axis=0, keepdims=True)
    r_r, p_n, r_n, n_n = (total[:, at : at + 1] for at in range(4))
    alpha = r_r / p_n
    beta = (r_r + alpha * (alpha * n_n - 2.0 * r_n)) / r_r
    planes = x_ref.shape[1]
    batch = min(planes, 4)
    copies = []
    for base in range(0, planes, batch):
        some = slice(base, base + batch)
        for plane in range(base, base + batch):
            for ri in range(2):
                p = p_ref[ri, plane]
                next_r = r_ref[ri, plane] - alpha * normal_ref[ri, plane]
                held[0][ri, plane] = x_ref[ri, plane] + alpha * p
                held[1][ri, plane] = next_r
                held[2][ri, plane] = next_r + beta * p
        copies += started(
            [(held[at].at[:, some], outs[at].at[:, some]) for at in range(3)], sems.at[base // batch]
        )
    for copy in copies:
        copy.wait()


def finish(total, x, r, p, normal):
    chunks = x.shape[1] // min(x.shape[1], 4)
    return call(
        finish_kernel,
        [x.shape] * 3,
        [x.shape] * 3 + [pltpu.SemaphoreType.DMA((chunks, 3))],
        [total, x, r, p, normal],
        10**7,
        "finish",
        hbm_outs=range(3),
    )


def matrices_kernel(info_hbm, weights_ref, out_ref, held, info, sem, *, slots):
    base = lax.axis_index("tile") * slots
    copy = pltpu.make_async_copy(info_hbm, info, sem)
    copy.start()
    copy.wait()

    def one(block, carry):
        w_x = weights_ref[block, 0]
        w_y = weights_ref[block, 1]
        w_z = weights_ref[block, 2]
        twice = jnp.concatenate([w_x, w_x], axis=0)
        rolled = [twice] + [pltpu.roll(twice, 8 - d, 0) for d in range(1, 4)]
        low = lax.broadcasted_iota(jnp.int32, (8, LANES), 0) < 4
        along_x = [twice * jnp.where(low, rolled[d], rolled[d + 1]) for d in (0, 2)]
        right = []
        for f in range(4):
            for d_z in range(3):
                other = (f + d_z) % 4
                along_z = w_z[f : f + 1] * w_z[other : other + 1]
                right += [along * along_z for along in along_x]
        turned = pltpu.roll(
            jnp.concatenate([w_y, w_y], axis=0), info[1, base + block] % 4, 0
        )[:4]
        left = jnp.concatenate([turned * turned[e : e + 1] for e in range(4)], axis=0)
        high, low = halves(jnp.concatenate(right, axis=0))
        left = halves(left)
        both = dot_bf16(jnp.concatenate(left, axis=0), high, ((1,), (1,)))
        done = both[:16] + both[16:] + dot_bf16(left[0], low, ((1,), (1,)))
        for f in range(4):
            held[pl.ds(f * slots + block, 16, stride=LANES), :] = jnp.concatenate(
                [done[:, 48 * f : 48 * f + 48], jnp.zeros((16, LANES - 48), jnp.float32)], axis=1
            )
        return carry

    lax.fori_loop(0, slots, one, 0, unroll=4)

    def turn(pair, carry):
        at = pl.ds(pl.multiple_of(pair * LANES, LANES), LANES)
        rows = held[at, :].T
        last = pltpu.roll(rows[16:32], slots, 1)
        for group in range(16):
            source = rows if group < 12 else last
            first = 4 * group if group < 12 else 4 * group - 48
            four = source[first : first + 4]
            out_ref[pl.ds(pl.multiple_of(pair * LANES + 8 * group, 8), 8), :] = jnp.concatenate(
                [four, four], axis=0
            )
        return carry

    lax.fori_loop(0, 16, turn, 0, unroll=2)


def block_matrices(info, weights):
    return call(
        functools.partial(matrices_kernel, slots=weights.shape[0]),
        [(16 * LANES, LANES)],
        [(16 * LANES, LANES), pltpu.SMEM(info.shape, info.dtype), pltpu.SemaphoreType.DMA],
        [info, weights],
        10**9,
        "matrices",
        hbm=[0],
    )[0]


def block_offsets(gathered, slots, ntile, capacity):
    owners = gathered[:, 0, 3 * capacity : 3 * capacity + slots]
    lists = gathered[:, :, : 3 * capacity].reshape(ntile, ntile, 3, capacity)
    earlier = jnp.tril(jnp.ones((slots, slots), jnp.int32), -1)
    same = (owners[:, :, None] == owners[:, None, :]).astype(jnp.int32)
    ranks = jnp.sum(same * earlier[None], axis=2)
    wanted = owners * capacity + ranks
    lists = jnp.transpose(lists, (2, 1, 0, 3)).reshape(3, ntile, 1, ntile * capacity)
    hit = wanted[:, :, None] == jnp.arange(ntile * capacity, dtype=jnp.int32)
    found = jnp.sum(jnp.where(hit[None], lists, 0), axis=3)
    return found[0], found[1] + owners * (LANES // ntile), found[2]


def shards(image_p, image_x, image_r, sensitivity, kb_weights, block_owner, owner_list):
    ntile = lax.axis_size("tile")
    ncoil = lax.axis_size("coil")
    chips = ncoil // 2
    slots = kb_weights.shape[0]
    capacity = owner_list.shape[3]
    planes, length = image_p.shape[1], image_p.shape[3]
    part = image_p.shape[2]
    chunk = LANES // (2 * planes)
    tile = lax.axis_index("tile")
    smap = sensitivity[0]
    tables = fourier_tables(length)

    def from_chip(values, by):
        pairs = [
            (a * 2 + k, (a - by) % chips * 2 + k) for a in range(chips) for k in range(2)
        ]
        return lax.ppermute(values, "coil", pairs)

    def other_core(values):
        pairs = [(a * 2 + k, a * 2 + 1 - k) for a in range(chips) for k in range(2)]
        return lax.ppermute(values, "coil", pairs)

    p_same = [image_p] + [from_chip(image_p, by) for by in range(1, chips)]
    p_other = [other_core(image_p)]
    gathered = lax.all_to_all(message(block_owner, owner_list), "tile", 0, 0, tiled=True)
    maps, done, held = near(p_same[0], p_other[0], smap, tables, chips)
    off_x, off_y, off_z = block_offsets(gathered, slots, ntile, capacity)
    info = jnp.stack(
        [
            (off_y // chunk * length + off_z).reshape(-1),
            (off_y % chunk).reshape(-1),
            off_x.reshape(-1),
        ]
    )
    lane = jnp.arange(LANES, dtype=jnp.int32)
    lane_ri = lane // (LANES // 2)
    lane_q = lane // planes % chunk
    lane_x = lane % planes + tile * planes
    unit = 2.0 * math.pi / length
    offset = jnp.arange(length, dtype=jnp.int32)[:, None]
    angle = unit * (offset * lane_x[None] % length).astype(jnp.float32)
    turns = jnp.stack(
        [jnp.cos(angle), jnp.sin(angle) * jnp.where(lane_ri == 0, 1.0, -1.0)[None]]
    )
    row = jnp.arange(32, dtype=jnp.int32)[:, None]
    row_q, row_ri, row_i = row // 8, row // 4 % 2, row % 4
    angle = unit * (row_i * lane_x[None] % length).astype(jnp.float32)
    sine = jnp.where(row_ri == 0, 1.0, -1.0) * jnp.sin(angle)
    shift = jnp.where(row_ri == lane_ri[None], jnp.cos(angle), sine)
    shift = jnp.where(lane_q[None] % 4 == row_q, shift / math.sqrt(length), 0.0)
    p_far, done, info = lax.optimization_barrier((p_same[1:], done, info))
    p_other += [other_core(piece) for piece in p_far]
    far_rows, _ = lax.optimization_barrier((maps[1:], p_other[1:]))
    far_maps = [from_chip(far_rows[chips - by - 1], by) for by in range(1, chips)]
    partial = forward(
        done, p_same[1:] + p_other[1:], maps[1:], held, turns, shift, info, chunk, slots
    )
    partial, weights = lax.optimization_barrier((partial, kb_weights))
    parts = lax.all_to_all(partial, "tile", 0, 0, tiled=True)
    done = regrid(parts, block_matrices(info, weights), chips * ntile)
    groups = [
        [at * ntile + t for at in range(ncoil) if at % 2 == k for t in range(ntile)]
        for k in range(2)
    ]
    spread = lax.all_to_all(
        done, ("coil", "tile"), 0, 0, axis_index_groups=groups, tiled=True
    )
    sent, kept = inverse(
        spread, held, turns, shift, maps[0], info, far_maps, part, chunk, slots
    )
    normal, found = sums([kept, other_core(sent)], image_p, image_r, ncoil * ntile)
    total = lax.all_to_all(found, ("coil", "tile"), 0, 0, tiled=True)
    return tuple(finish(total, image_x, image_r, image_p, normal))


def solution(mesh):
    return jax.shard_map(
        shards,
        mesh=mesh,
        in_specs=(
            P(None, "tile", "coil", None),
            P(None, "tile", "coil", None),
            P(None, "tile", "coil", None),
            P("coil", None, "tile", None, None),
            P("tile", None, None, None),
            P("tile"),
            P(None, "tile", None, None),
        ),
        out_specs=(
            P(None, "tile", "coil", None),
            P(None, "tile", "coil", None),
            P(None, "tile", "coil", None),
        ),
        check_vma=False,
    )
```

```python
import functools
import math

import jax
import jax.numpy as jnp
import ml_dtypes
import numpy as np
from jax import lax
from jax.experimental import pallas as pl
from jax.experimental.pallas import tpu as pltpu
from jax.sharding import PartitionSpec as P

LANES = 128
VMEM = 24 * 1024 * 1024


def halves(values):
    high = values.astype(jnp.bfloat16)
    low = (values - high.astype(jnp.float32)).astype(jnp.bfloat16)
    return high, low


def dot_bf16(left, right, dims):
    return lax.dot_general(left, right, (dims, ((), ())), preferred_element_type=jnp.float32)


def dot_left(table, values, dims=((1,), (0,))):
    high, low = halves(values)
    return (
        dot_bf16(table[0], high, dims)
        + dot_bf16(table[0], low, dims)
        + dot_bf16(table[1], high, dims)
    )


def dot_right(values, table, dims=((1,), (0,))):
    high, low = halves(values)
    return (
        dot_bf16(high, table[0], dims)
        + dot_bf16(low, table[0], dims)
        + dot_bf16(high, table[1], dims)
    )


def fourier_tables(length):
    cells = np.arange(length)
    angle = 2.0 * math.pi / length * (cells[:, None] * cells[None, :] % length)
    cos_t = np.cos(angle) / math.sqrt(length)
    sin_t = np.sin(angle) / math.sqrt(length)
    found = []
    for sign in (1.0, -1.0):
        whole = np.block([[cos_t, -sign * sin_t], [sign * sin_t, cos_t]])
        high = whole.astype(ml_dtypes.bfloat16)
        low = (whole - high.astype(np.float64)).astype(ml_dtypes.bfloat16)
        found += [high, low]
    return jnp.asarray(np.stack(found))


def band_of_lane(planes, chunk):
    return lax.broadcasted_iota(jnp.int32, (4, LANES), 1) // planes % chunk


def in_window(band, first, chunk):
    past = band - first
    if chunk == 4:
        here = past >= 0
        return here, jnp.logical_not(here)
    here = jnp.logical_and(past >= 0, past < 4)
    return here, past < 4 - chunk


def call(kernel, outs, scratch, operands, flops, name, hbm=(), hbm_outs=(), vmem=(), fixed=()):
    operands = list(operands)
    for listed, space in ((fixed, pltpu.HBM), (vmem, pltpu.VMEM)):
        for at in listed:
            operands[at] = pltpu.with_memory_space_constraint(operands[at], space)
    here = pl.BlockSpec(memory_space=pltpu.VMEM)
    there = pl.BlockSpec(memory_space=pltpu.HBM)
    moved = sum(math.prod(a.shape) * a.dtype.itemsize for a in operands)
    return pl.pallas_call(
        kernel,
        out_shape=[
            jax.ShapeDtypeStruct(shape, jnp.float32) if isinstance(shape, tuple) else shape
            for shape in outs
        ],
        in_specs=[there if at in hbm else here for at in range(len(operands))],
        out_specs=[there if at in hbm_outs else here for at in range(len(outs))],
        scratch_shapes=[
            pltpu.VMEM(shape, jnp.float32) if isinstance(shape, tuple) else shape
            for shape in scratch
        ],
        compiler_params=pltpu.CompilerParams(vmem_limit_bytes=VMEM),
        cost_estimate=pl.CostEstimate(flops=flops, bytes_accessed=moved, transcendentals=0),
        name=name,
    )(*operands)


def started(pairs, sems):
    copies = [
        pltpu.make_async_copy(source, to, sems.at[at]) for at, (source, to) in enumerate(pairs)
    ]
    for copy in copies:
        copy.start()
    return copies


def place_on_coil():
    coil = lax.axis_index("coil")
    return coil // 2, coil % 2


def quarters_of(chips, part):
    chip, core = place_on_coil()
    return [
        pl.multiple_of(((chip + hop) % chips * 2 + at) * part, part)
        for at in (core, 1 - core)
        for hop in range(chips)
    ]


def z_of_coil(p_ref, s_ref, half, table, out_ref, rows):
    _, planes, part, length = p_ref.shape
    batch = min(planes, 256 // part)
    from_rows = pl.ds(pl.multiple_of(half * part, part), part)
    for base in range(0, planes, batch):
        bands = []
        for plane in range(base, base + batch):
            s_re = s_ref[0, plane, from_rows, :]
            s_im = s_ref[1, plane, from_rows, :]
            p_re = p_ref[0, plane]
            p_im = p_ref[1, plane]
            bands.append(
                jnp.concatenate([s_re * p_re - s_im * p_im, s_re * p_im + s_im * p_re], axis=1)
            )
        done = dot_right(jnp.concatenate(bands, axis=0), table)
        for ri in range(2):
            found = done[:, ri * length : (ri + 1) * length]
            out_ref[ri, base : base + batch, rows, :] = found.reshape(batch, part, length)


def near_kernel(p_hbm, p_other, s_hbm, table_hbm, *refs, chips):
    maps, (out_ref, p_own, tables, sems) = refs[:chips], refs[chips:]
    chip, core = place_on_coil()
    part = p_own.shape[2]
    own = 2 * part
    pairs = [(table_hbm.at[0:2], tables), (p_hbm, p_own)]
    for hop in range(chips):
        rows = pl.ds(pl.multiple_of((chip + hop) % chips * own, own), own)
        pairs.append((s_hbm.at[:, :, rows, :], maps[hop]))
    copies = started(pairs, sems)
    for copy in copies[:3]:
        copy.wait()
    table = (tables[0], tables[1])
    for half, p_ref in ((core, p_own), (1 - core, p_other)):
        rows = pl.ds(pl.multiple_of(half * part, part), part)
        z_of_coil(p_ref, maps[0], half, table, out_ref, rows)
    for copy in copies[3:]:
        copy.wait()


def near(p_own, p_other, smap, tables, chips):
    _, planes, part, length = p_own.shape
    shape = (2, planes, 2 * part, length)
    *maps, done = call(
        functools.partial(near_kernel, chips=chips),
        [shape] * (chips + 1),
        [
            p_own.shape,
            pltpu.VMEM((2,) + tables.shape[1:], tables.dtype),
            pltpu.SemaphoreType.DMA((chips + 2,)),
        ],
        [p_own, p_other, smap, tables],
        48 * planes * part * length * length,
        "near",
        hbm=[0, 2, 3],
        fixed=[0, 2, 3],
    )
    return maps, done


def message_kernel(owner_ref, list_ref, out_ref):
    _, _, ntile, capacity = list_ref.shape
    out_ref[...] = jnp.zeros_like(out_ref)
    slots = owner_ref.shape[1]
    for to in range(ntile):
        for axis in range(3):
            out_ref[to, :, axis * capacity : (axis + 1) * capacity] = list_ref[axis, 0]
        out_ref[to, 0:1, 3 * capacity : 3 * capacity + slots] = owner_ref[...]


def message(block_owner, owner_list):
    ntile = owner_list.shape[2]
    return pl.pallas_call(
        message_kernel,
        out_shape=jax.ShapeDtypeStruct((ntile, ntile, LANES), jnp.int32),
        in_specs=[pl.BlockSpec(memory_space=pltpu.VMEM)] * 2,
        out_specs=pl.BlockSpec(memory_space=pltpu.VMEM),
        name="message",
    )(block_owner[None], owner_list)


def cut_boxes(info, grid, turns_ref, shift_ref, out_ref, gbuf, planes, chunk, slots):
    handlers = out_ref.shape[0]
    band = band_of_lane(planes, chunk)

    def cut(handler, carry):
        base = pl.multiple_of(handler * LANES, LANES)
        for slot in range(slots):
            block = handler * slots + slot
            here, after = in_window(band, info[1, block], chunk)
            first = grid[pl.ds(info[0, block], 4), :]
            second = grid[pl.ds(info[0, block] + LANES, 4), :]
            if chunk > 4:
                second = jnp.where(after, second, 0.0)
            cells = jnp.where(here, first, second)
            turn = pl.ds(info[2, block], 1)
            cells = cells * turns_ref[0, turn, :] + pltpu.roll(cells, LANES // 2, 1) * turns_ref[
                1, turn, :
            ]
            gbuf[pl.ds(base + slot, 4, stride=slots), :] = cells
        return carry

    lax.fori_loop(0, handlers, cut, 0)
    high, low = halves(shift_ref[...])
    table = jnp.concatenate(
        [
            jnp.concatenate([high, high], axis=1),
            jnp.concatenate([low, jnp.zeros_like(low)], axis=1),
        ],
        axis=0,
    )
    for handler in range(handlers):
        cells = gbuf[handler * LANES : (handler + 1) * LANES, :]
        both = dot_bf16(table, jnp.concatenate(halves(cells), axis=1), ((1,), (1,)))
        out_ref[handler] = both[:32] + both[32:]


def forward_kernel(near_ref, *refs, chips, chunk, slots):
    far = chips - 1
    p_refs = refs[: 2 * far]
    maps = refs[2 * far : 3 * far]
    table_hbm, turns_hbm, shift_hbm, info_hbm, out_ref = refs[3 * far : 3 * far + 5]
    tables, turns_ref, shift_ref, info, natural, ybuf, grid, gbuf, sems = refs[3 * far + 5 :]
    _, planes, own, length = near_ref.shape
    rows = length * planes
    chip, core = place_on_coil()
    copies = started(
        [
            (table_hbm.at[0:2], tables.at[0:2]),
            (table_hbm.at[2:4], tables.at[2:4]),
            (info_hbm, info),
            (turns_hbm, turns_ref),
            (shift_hbm, shift_ref),
        ],
        sems,
    )
    starts = quarters_of(chips, own // 2)
    for ri in range(2):
        natural[ri, :, pl.ds(pl.multiple_of(chip * own, own), own), :] = near_ref[ri]
    copies[0].wait()
    table = (tables[0], tables[1])
    for hop in range(1, chips):
        for at, half in enumerate((core, 1 - core)):
            to = pl.ds(starts[at * chips + hop], own // 2)
            z_of_coil(p_refs[at * far + hop - 1], maps[hop - 1], half, table, natural, to)
    copies[1].wait()
    table = (tables[2], tables[3])
    for pair in range(planes // 2):
        columns = [
            jnp.concatenate([natural[0, plane], natural[1, plane]], axis=0)
            for plane in (2 * pair, 2 * pair + 1)
        ]
        both = dot_left(table, jnp.concatenate(columns, axis=1))
        for inner in range(2):
            for ri in range(2):
                ybuf[pl.ds(ri * rows + 2 * pair + inner, length, stride=planes), :] = both[
                    ri * length : (ri + 1) * length, inner * LANES : (inner + 1) * LANES
                ]
    for band in range(length // chunk):
        re = ybuf[band * 64 : (band + 1) * 64, :]
        im = ybuf[rows + band * 64 : rows + (band + 1) * 64, :]
        grid[band * length : (band + 1) * length, :] = jnp.concatenate([re, im], axis=0).T
    for copy in copies[2:]:
        copy.wait()
    cut_boxes(info, grid, turns_ref, shift_ref, out_ref, gbuf, planes, chunk, slots)


def forward(done, pieces, maps, tables, turns, shift, info, chunk, slots):
    _, planes, own, length = done.shape
    blocks = info.shape[1]
    chips = len(maps) + 1
    operands = [done, *pieces, *maps, tables, turns, shift, info]
    count = len(operands)
    return call(
        functools.partial(forward_kernel, chips=chips, chunk=chunk, slots=slots),
        [(blocks // slots, 32, LANES)],
        [
            pltpu.VMEM(tables.shape, tables.dtype),
            turns.shape,
            shift.shape,
            pltpu.SMEM(info.shape, info.dtype),
            (2, planes, length, length),
            (2 * length * planes, length),
            (length * (length // chunk + 1), LANES),
            (blocks * 4, LANES),
            pltpu.SemaphoreType.DMA((5,)),
        ],
        operands,
        48 * planes * length**3,
        "forward",
        hbm=range(count - 4, count),
        fixed=range(count - 4, count),
        vmem=[0, *range(count - 3 - chips, count - 4)],
    )[0]


def regrid_kernel(parts_ref, matrix_ref, out_ref, held, done_sem):
    total = parts_ref[0]
    for at in range(1, parts_ref.shape[0]):
        total = total + parts_ref[at]
    along = lax.broadcasted_iota(jnp.int32, (8, LANES), 0) % 4
    sums = [jnp.zeros((8, LANES), jnp.float32) for _ in range(4)]
    for source in range(4):
        for d_z in range(4):
            value = total[8 * source : 8 * source + 8]
            if d_z:
                value = pltpu.roll(value, LANES - 32 * d_z, 1)
            for d_x in range(4):
                moved = value
                if d_x:
                    moved = jnp.where(
                        along + d_x < 4, pltpu.roll(value, 8 - d_x, 0), pltpu.roll(value, 4 - d_x, 0)
                    )
                for e in range(4):
                    at = 8 * (((e * 4 + source) * 4 + d_z) * 4 + d_x)
                    sums[e] = sums[e] + matrix_ref[at : at + 8] * moved
    done = jnp.concatenate(sums, axis=0)
    for at in range(held.shape[0]):
        held[at] = done
    copy = pltpu.make_async_copy(held, out_ref, done_sem)
    copy.start()
    copy.wait()


def regrid(parts, matrix, copies):
    shape = (copies,) + parts.shape[1:]
    return call(
        regrid_kernel,
        [shape],
        [shape, pltpu.SemaphoreType.DMA],
        [parts, matrix],
        10**7,
        "regrid",
        hbm_outs=[0],
        vmem=[1],
    )[0]


def place_boxes(info, chip, u_ref, turns_ref, shift_ref, outs, gbufs, planes, chunk, slots):
    chips = len(outs)
    handlers = u_ref.shape[0] // chips
    high, low = halves(shift_ref[...])
    table = jnp.concatenate([high, high, low, jnp.zeros_like(low)], axis=0)
    for handler in range(handlers):
        for hop in range(chips):
            u_hi, u_lo = (
                half.astype(jnp.float32)
                for half in halves(u_ref[(chip + hop) % chips * handlers + handler])
            )
            stack = jnp.concatenate([u_hi, u_lo, u_hi, jnp.zeros_like(u_hi)], axis=0)
            gbufs[hop][handler * LANES : (handler + 1) * LANES, :] = dot_bf16(
                stack.T.astype(jnp.bfloat16), table, ((1,), (0,))
            )
    band = band_of_lane(planes, chunk)

    def put(handler, carry):
        base = pl.multiple_of(handler * LANES, LANES)
        for slot in range(slots):
            block = handler * slots + slot
            here, after = in_window(band, info[1, block], chunk)
            first = pl.ds(info[0, block], 4)
            second = pl.ds(info[0, block] + LANES, 4)
            turn = pl.ds(info[2, block], 1)
            cos_b, sin_b = turns_ref[0, turn, :], turns_ref[1, turn, :]
            for hop in range(chips):
                cells = gbufs[hop][pl.ds(base + slot, 4, stride=slots), :]
                cells = cells * cos_b - pltpu.roll(cells, LANES // 2, 1) * sin_b
                old_first = outs[hop][first, :]
                old_second = outs[hop][second, :]
                outs[hop][first, :] = old_first + jnp.where(here, cells, 0.0)
                outs[hop][second, :] = old_second + jnp.where(after, cells, 0.0)
        return carry

    lax.fori_loop(0, handlers, put, 0)


def inverse_kernel(*refs, part, length, chunk, slots, chips):
    u_ref, own_map, table_hbm, turns_hbm, shift_hbm, info_hbm = refs[:6]
    far_maps = refs[6 : 5 + chips]
    outs = refs[5 + chips : 7 + chips]
    refs = refs[7 + chips :]
    grids, gbufs, refs = refs[:chips], refs[chips : 2 * chips], refs[2 * chips :]
    table_ref, turns_ref, shift_ref, info, ybuf, images, maps, sems = refs
    planes = own_map.shape[1]
    rows = length * planes
    own = length // chips
    chip, core = place_on_coil()
    own_rows = pl.multiple_of(chip * own, own)
    pairs = [
        (shift_hbm, shift_ref),
        (info_hbm, info),
        (turns_hbm, turns_ref),
        (table_hbm, table_ref),
    ]
    pairs += [(far_map, maps.at[at]) for at, far_map in enumerate(far_maps)]
    copies = started(pairs, sems)
    for grid in grids:
        grid[...] = jnp.zeros_like(grid)
    for copy in copies[:3]:
        copy.wait()
    place_boxes(info, chip, u_ref, turns_ref, shift_ref, grids, gbufs, planes, chunk, slots)
    for copy in copies[3:]:
        copy.wait()
    table = []
    for half in range(2):
        bands = [
            table_ref[half, pl.ds(pl.multiple_of(ri * length + own_rows, own), own), :]
            for ri in range(2)
        ]
        table.append(jnp.concatenate(bands, axis=0))
    for hop in range(chips):
        for band in range(length // chunk):
            tile = grids[hop][band * length : (band + 1) * length, :].T
            ybuf[hop, band * 64 : (band + 1) * 64, :] = tile[:64]
            ybuf[hop, rows + band * 64 : rows + (band + 1) * 64, :] = tile[64:]
        for pair in range(planes // 2):
            columns = [
                jnp.concatenate(
                    [
                        ybuf[hop, pl.ds(ri * rows + plane, length, stride=planes), :]
                        for ri in range(2)
                    ],
                    axis=0,
                )
                for plane in (2 * pair, 2 * pair + 1)
            ]
            done = dot_left(table, jnp.concatenate(columns, axis=1))
            for inner in range(2):
                for ri in range(2):
                    images[hop, ri, 2 * pair + inner] = done[
                        ri * own : (ri + 1) * own, inner * LANES : (inner + 1) * LANES
                    ]
    table = (table_ref[2], table_ref[3])
    batch = min(planes, 256 // part)
    for at, half in enumerate((1 - core, core)):
        local = pl.ds(pl.multiple_of(half * part, part), part)
        for base in range(0, planes, batch):
            total_re, total_im = 0.0, 0.0
            for hop in range(chips):
                bands = [
                    jnp.concatenate([images[hop, ri, plane, local, :] for ri in range(2)], axis=1)
                    for plane in range(base, base + batch)
                ]
                done = dot_right(jnp.concatenate(bands, axis=0), table)
                i_re = done[:, :length].reshape(batch, part, length)
                i_im = done[:, length:].reshape(batch, part, length)
                s_map = maps.at[hop - 1] if hop else own_map
                s_re = s_map[0, base : base + batch, local, :]
                s_im = s_map[1, base : base + batch, local, :]
                total_re = total_re + (s_re * i_re + s_im * i_im)
                total_im = total_im + (s_re * i_im - s_im * i_re)
            outs[at][0, base : base + batch] = total_re
            outs[at][1, base : base + batch] = total_im


def inverse(spread, tables, turns, shift, own_map, info, far_maps, part, chunk, slots):
    _, planes, own, length = own_map.shape
    chips = len(far_maps) + 1
    blocks = info.shape[1]
    rows = length * (length // chunk + 1)
    return call(
        functools.partial(
            inverse_kernel, part=part, length=length, chunk=chunk, slots=slots, chips=chips
        ),
        [(2, planes, part, length)] * 2,
        [(rows, LANES)] * chips
        + [(blocks * 4, LANES)] * chips
        + [
            pltpu.VMEM(tables.shape, tables.dtype),
            turns.shape,
            shift.shape,
            pltpu.SMEM(info.shape, info.dtype),
            (chips, 2 * length * planes, length),
            (chips, 2, planes, own, length),
            (chips - 1, 2, planes, own, length),
            pltpu.SemaphoreType.DMA((3 + chips,)),
        ],
        [spread, own_map, tables, turns, shift, info, *far_maps],
        48 * planes * length**3,
        "inverse",
        hbm=range(2, 5 + chips),
        fixed=[2, 3, 4, 5],
        vmem=[1],
    )


def sums_kernel(*refs, terms):
    term_refs = refs[:terms]
    p_ref, r_ref, normal_ref, out_ref = refs[terms:]
    shape = p_ref.shape

    def add(plane, held):
        held = list(held)
        for ri in range(2):
            normal = term_refs[0][ri, plane]
            for term in term_refs[1:]:
                normal = normal + term[ri, plane]
            normal_ref[ri, plane] = normal
            p = p_ref[ri, plane]
            r = r_ref[ri, plane]
            for at, product in enumerate((r * r, p * normal, r * normal, normal * normal)):
                held[at] = held[at] + jnp.sum(product.reshape(-1, 8, LANES), axis=0)
        return tuple(held)

    start = tuple(jnp.zeros((8, LANES), jnp.float32) for _ in range(4))
    held = lax.fori_loop(0, shape[1], add, start, unroll=4)
    lane = lax.broadcasted_iota(jnp.int32, out_ref.shape, 1)
    found = jnp.zeros(out_ref.shape, jnp.float32)
    for at in range(4):
        found = jnp.where(lane == at, jnp.sum(held[at]), found)
    out_ref[...] = found


def sums(terms, p, r, devices):
    kernel = functools.partial(sums_kernel, terms=len(terms))
    return call(kernel, [p.shape, (devices, LANES)], [], [*terms, p, r], 10**7, "sums")


def finish_kernel(total_ref, x_ref, r_ref, p_ref, normal_ref, *refs):
    outs, held, sems = refs[:3], refs[3:6], refs[6]
    total = jnp.sum(total_ref[...], axis=0, keepdims=True)
    r_r, p_n, r_n, n_n = (total[:, at : at + 1] for at in range(4))
    alpha = r_r / p_n
    beta = (r_r + alpha * (alpha * n_n - 2.0 * r_n)) / r_r
    planes = x_ref.shape[1]
    batch = min(planes, 4)
    copies = []
    for base in range(0, planes, batch):
        some = slice(base, base + batch)
        for plane in range(base, base + batch):
            for ri in range(2):
                p = p_ref[ri, plane]
                next_r = r_ref[ri, plane] - alpha * normal_ref[ri, plane]
                held[0][ri, plane] = x_ref[ri, plane] + alpha * p
                held[1][ri, plane] = next_r
                held[2][ri, plane] = next_r + beta * p
        copies += started(
            [(held[at].at[:, some], outs[at].at[:, some]) for at in range(3)], sems.at[base // batch]
        )
    for copy in copies:
        copy.wait()


def finish(total, x, r, p, normal):
    chunks = x.shape[1] // min(x.shape[1], 4)
    return call(
        finish_kernel,
        [x.shape] * 3,
        [x.shape] * 3 + [pltpu.SemaphoreType.DMA((chunks, 3))],
        [total, x, r, p, normal],
        10**7,
        "finish",
        hbm_outs=range(3),
    )


def matrices_kernel(info_hbm, weights_ref, out_ref, held, info, sem, *, slots):
    base = lax.axis_index("tile") * slots
    copy = pltpu.make_async_copy(info_hbm, info, sem)
    copy.start()
    copy.wait()

    def one(block, carry):
        w_x = weights_ref[block, 0]
        w_y = weights_ref[block, 1]
        w_z = weights_ref[block, 2]
        twice = jnp.concatenate([w_x, w_x], axis=0)
        rolled = [twice] + [pltpu.roll(twice, 8 - d, 0) for d in range(1, 4)]
        low = lax.broadcasted_iota(jnp.int32, (8, LANES), 0) < 4
        along_x = [twice * jnp.where(low, rolled[d], rolled[d + 1]) for d in (0, 2)]
        right = []
        for f in range(4):
            for d_z in range(4):
                other = (f + d_z) % 4
                along_z = w_z[f : f + 1] * w_z[other : other + 1]
                right += [along * along_z for along in along_x]
        turned = pltpu.roll(
            jnp.concatenate([w_y, w_y], axis=0), info[1, base + block] % 4, 0
        )[:4]
        left = jnp.concatenate([turned * turned[e : e + 1] for e in range(4)], axis=0)
        high, low = halves(jnp.concatenate(right, axis=0))
        left = halves(left)
        both = dot_bf16(jnp.concatenate(left, axis=0), high, ((1,), (1,)))
        done = both[:16] + both[16:] + dot_bf16(left[0], low, ((1,), (1,)))
        for f in range(4):
            lanes = done[:, f // 2 * LANES : (f // 2 + 1) * LANES]
            if f % 2:
                lanes = pltpu.roll(lanes, LANES // 2, 1)
            held[pl.ds(f * slots + block, 16, stride=LANES), :] = lanes
        return carry

    lax.fori_loop(0, slots, one, 0, unroll=4)

    def turn(pair, carry):
        at = pl.ds(pl.multiple_of(pair * LANES, LANES), LANES)
        rows = held[at, :].T
        for group in range(16):
            four = rows[4 * group : 4 * group + 4]
            out_ref[pl.ds(pl.multiple_of(pair * LANES + 8 * group, 8), 8), :] = jnp.concatenate(
                [four, four], axis=0
            )
        return carry

    lax.fori_loop(0, 16, turn, 0, unroll=2)


def block_matrices(info, weights):
    return call(
        functools.partial(matrices_kernel, slots=weights.shape[0]),
        [(16 * LANES, LANES)],
        [(16 * LANES, LANES), pltpu.SMEM(info.shape, info.dtype), pltpu.SemaphoreType.DMA],
        [info, weights],
        10**9,
        "matrices",
        hbm=[0],
    )[0]


def block_offsets(gathered, slots, ntile, capacity):
    owners = gathered[:, 0, 3 * capacity : 3 * capacity + slots]
    lists = gathered[:, :, : 3 * capacity].reshape(ntile, ntile, 3, capacity)
    earlier = jnp.tril(jnp.ones((slots, slots), jnp.int32), -1)
    same = (owners[:, :, None] == owners[:, None, :]).astype(jnp.int32)
    ranks = jnp.sum(same * earlier[None], axis=2)
    wanted = owners * capacity + ranks
    lists = jnp.transpose(lists, (2, 1, 0, 3)).reshape(3, ntile, 1, ntile * capacity)
    hit = wanted[:, :, None] == jnp.arange(ntile * capacity, dtype=jnp.int32)
    found = jnp.sum(jnp.where(hit[None], lists, 0), axis=3)
    return found[0], found[1] + owners * (LANES // ntile), found[2]


def shards(image_p, image_x, image_r, sensitivity, kb_weights, block_owner, owner_list):
    ntile = lax.axis_size("tile")
    ncoil = lax.axis_size("coil")
    chips = ncoil // 2
    slots = kb_weights.shape[0]
    capacity = owner_list.shape[3]
    planes, length = image_p.shape[1], image_p.shape[3]
    part = image_p.shape[2]
    chunk = LANES // (2 * planes)
    tile = lax.axis_index("tile")
    smap = sensitivity[0]
    tables = fourier_tables(length)

    def from_chip(values, by):
        pairs = [
            (a * 2 + k, (a - by) % chips * 2 + k) for a in range(chips) for k in range(2)
        ]
        return lax.ppermute(values, "coil", pairs)

    def other_core(values):
        pairs = [(a * 2 + k, a * 2 + 1 - k) for a in range(chips) for k in range(2)]
        return lax.ppermute(values, "coil", pairs)

    p_same = [image_p] + [from_chip(image_p, by) for by in range(1, chips)]
    p_other = [other_core(image_p)]
    maps, done = near(p_same[0], p_other[0], smap, tables, chips)
    sent, done = lax.optimization_barrier((message(block_owner, owner_list), done))
    gathered = lax.all_to_all(sent, "tile", 0, 0, tiled=True)
    off_x, off_y, off_z = block_offsets(gathered, slots, ntile, capacity)
    info = jnp.stack(
        [
            (off_y // chunk * length + off_z).reshape(-1),
            (off_y % chunk).reshape(-1),
            off_x.reshape(-1),
        ]
    )
    lane = jnp.arange(LANES, dtype=jnp.int32)
    lane_ri = lane // (LANES // 2)
    lane_q = lane // planes % chunk
    lane_x = lane % planes + tile * planes
    unit = 2.0 * math.pi / length
    offset = jnp.arange(length, dtype=jnp.int32)[:, None]
    angle = unit * (offset * lane_x[None] % length).astype(jnp.float32)
    turns = jnp.stack(
        [jnp.cos(angle), jnp.sin(angle) * jnp.where(lane_ri == 0, 1.0, -1.0)[None]]
    )
    row = jnp.arange(32, dtype=jnp.int32)[:, None]
    row_q, row_ri, row_i = row // 8, row // 4 % 2, row % 4
    angle = unit * (row_i * lane_x[None] % length).astype(jnp.float32)
    sine = jnp.where(row_ri == 0, 1.0, -1.0) * jnp.sin(angle)
    shift = jnp.where(row_ri == lane_ri[None], jnp.cos(angle), sine)
    shift = jnp.where(lane_q[None] % 4 == row_q, shift / math.sqrt(length), 0.0)
    p_far, done, info = lax.optimization_barrier((p_same[1:], done, info))
    p_other += [other_core(piece) for piece in p_far]
    far_rows, _ = lax.optimization_barrier((maps[1:], p_other[1:]))
    far_maps = [from_chip(far_rows[chips - by - 1], by) for by in range(1, chips)]
    partial = forward(
        done, p_same[1:] + p_other[1:], maps[1:], tables, turns, shift, info, chunk, slots
    )
    partial, weights = lax.optimization_barrier((partial, kb_weights))
    parts = lax.all_to_all(partial, "tile", 0, 0, tiled=True)
    done = regrid(parts, block_matrices(info, weights), chips * ntile)
    groups = [
        [at * ntile + t for at in range(ncoil) if at % 2 == k for t in range(ntile)]
        for k in range(2)
    ]
    spread = lax.all_to_all(
        done, ("coil", "tile"), 0, 0, axis_index_groups=groups, tiled=True
    )
    sent, kept = inverse(
        spread, tables, turns, shift, maps[0], info, far_maps, part, chunk, slots
    )
    normal, found = sums([kept, other_core(sent)], image_p, image_r, ncoil * ntile)
    total = lax.all_to_all(found, ("coil", "tile"), 0, 0, tiled=True)
    return tuple(finish(total, image_x, image_r, image_p, normal))


def solution(mesh):
    return jax.shard_map(
        shards,
        mesh=mesh,
        in_specs=(
            P(None, "tile", "coil", None),
            P(None, "tile", "coil", None),
            P(None, "tile", "coil", None),
            P("coil", None, "tile", None, None),
            P("tile", None, None, None),
            P("tile"),
            P(None, "tile", None, None),
        ),
        out_specs=(
            P(None, "tile", "coil", None),
            P(None, "tile", "coil", None),
            P(None, "tile", "coil", None),
        ),
        check_vma=False,
    )
```

```python
import functools
import math

import jax
import jax.numpy as jnp
import ml_dtypes
import numpy as np
from jax import lax
from jax.experimental import pallas as pl
from jax.experimental.pallas import tpu as pltpu
from jax.sharding import PartitionSpec as P

LANES = 128
VMEM = 24 * 1024 * 1024


def halves(values):
    high = values.astype(jnp.bfloat16)
    low = (values - high.astype(jnp.float32)).astype(jnp.bfloat16)
    return high, low


def dot_bf16(left, right, dims):
    return lax.dot_general(left, right, (dims, ((), ())), preferred_element_type=jnp.float32)


def dot_left(table, values, dims=((1,), (0,))):
    high, low = halves(values)
    return (
        dot_bf16(table[0], high, dims)
        + dot_bf16(table[0], low, dims)
        + dot_bf16(table[1], high, dims)
    )


def dot_right(values, table, dims=((1,), (0,))):
    high, low = halves(values)
    return (
        dot_bf16(high, table[0], dims)
        + dot_bf16(low, table[0], dims)
        + dot_bf16(high, table[1], dims)
    )


def fourier_tables(length):
    cells = np.arange(length)
    angle = 2.0 * math.pi / length * (cells[:, None] * cells[None, :] % length)
    cos_t = np.cos(angle) / math.sqrt(length)
    sin_t = np.sin(angle) / math.sqrt(length)
    found = []
    for sign in (1.0, -1.0):
        whole = np.block([[cos_t, -sign * sin_t], [sign * sin_t, cos_t]])
        high = whole.astype(ml_dtypes.bfloat16)
        low = (whole - high.astype(np.float64)).astype(ml_dtypes.bfloat16)
        found += [high, low]
    return jnp.asarray(np.stack(found))


def band_of_lane(planes, chunk):
    return lax.broadcasted_iota(jnp.int32, (4, LANES), 1) // planes % chunk


def in_window(band, first, chunk):
    past = band - first
    if chunk == 4:
        here = past >= 0
        return here, jnp.logical_not(here)
    here = jnp.logical_and(past >= 0, past < 4)
    return here, past < 4 - chunk


def call(kernel, outs, scratch, operands, flops, name, hbm=(), hbm_outs=(), vmem=(), fixed=()):
    operands = list(operands)
    for listed, space in ((fixed, pltpu.HBM), (vmem, pltpu.VMEM)):
        for at in listed:
            operands[at] = pltpu.with_memory_space_constraint(operands[at], space)
    here = pl.BlockSpec(memory_space=pltpu.VMEM)
    there = pl.BlockSpec(memory_space=pltpu.HBM)
    moved = sum(math.prod(a.shape) * a.dtype.itemsize for a in operands)
    return pl.pallas_call(
        kernel,
        out_shape=[
            pltpu.HBM(shape, jnp.float32)
            if at in hbm_outs
            else jax.ShapeDtypeStruct(shape, jnp.float32)
            for at, shape in enumerate(outs)
        ],
        in_specs=[there if at in hbm else here for at in range(len(operands))],
        out_specs=[there if at in hbm_outs else here for at in range(len(outs))],
        scratch_shapes=[
            pltpu.VMEM(shape, jnp.float32) if isinstance(shape, tuple) else shape
            for shape in scratch
        ],
        compiler_params=pltpu.CompilerParams(vmem_limit_bytes=VMEM),
        cost_estimate=pl.CostEstimate(flops=flops, bytes_accessed=moved, transcendentals=0),
        name=name,
    )(*operands)


def started(pairs, sems):
    copies = [
        pltpu.make_async_copy(source, to, sems.at[at]) for at, (source, to) in enumerate(pairs)
    ]
    for copy in copies:
        copy.start()
    return copies


def place_on_coil():
    coil = lax.axis_index("coil")
    return coil // 2, coil % 2


def quarters_of(chips, part):
    chip, core = place_on_coil()
    return [
        pl.multiple_of(((chip + hop) % chips * 2 + at) * part, part)
        for at in (core, 1 - core)
        for hop in range(chips)
    ]


def z_of_coil(p_ref, s_ref, half, table, out_ref, rows):
    _, planes, part, length = p_ref.shape
    batch = min(planes, 256 // part)
    from_rows = pl.ds(pl.multiple_of(half * part, part), part)
    for base in range(0, planes, batch):
        bands = []
        for plane in range(base, base + batch):
            s_re = s_ref[0, plane, from_rows, :]
            s_im = s_ref[1, plane, from_rows, :]
            p_re = p_ref[0, plane]
            p_im = p_ref[1, plane]
            bands.append(
                jnp.concatenate([s_re * p_re - s_im * p_im, s_re * p_im + s_im * p_re], axis=1)
            )
        done = dot_right(jnp.concatenate(bands, axis=0), table)
        for ri in range(2):
            found = done[:, ri * length : (ri + 1) * length]
            out_ref[ri, base : base + batch, rows, :] = found.reshape(batch, part, length)


def near_kernel(p_hbm, s_hbm, table_hbm, *refs, chips):
    sends, out_ref = refs[: chips - 1], refs[chips - 1]
    p_own, s_own, tables, done, sems, out_sems, *held = refs[chips:]
    chip, core = place_on_coil()
    part = p_own.shape[2]
    own = 2 * part
    quarter = pl.multiple_of((chip * 2 + core) * part, part)
    pairs = [
        (table_hbm.at[0:2], tables),
        (p_hbm, p_own),
        (s_hbm.at[:, :, pl.ds(quarter, part), :], s_own),
    ]
    for by in range(1, chips):
        rows = pl.ds(pl.multiple_of((chip + chips - by) % chips * own, own), own)
        pairs.append((s_hbm.at[:, :, rows, :], held[by - 1]))
    copies = started(pairs, sems)
    for copy in copies[:3]:
        copy.wait()
    z_of_coil(p_own, s_own, 0, (tables[0], tables[1]), done, slice(0, part))
    for copy in copies[3:]:
        copy.wait()
    pairs = [(done, out_ref)] + list(zip(held, sends))
    for copy in started(pairs, out_sems):
        copy.wait()


def near(p_own, smap, tables, chips):
    _, planes, part, length = p_own.shape
    shape = (2, planes, 2 * part, length)
    *sends, done = call(
        functools.partial(near_kernel, chips=chips),
        [shape] * (chips - 1) + [p_own.shape],
        [
            p_own.shape,
            p_own.shape,
            pltpu.VMEM((2,) + tables.shape[1:], tables.dtype),
            p_own.shape,
            pltpu.SemaphoreType.DMA((chips + 2,)),
            pltpu.SemaphoreType.DMA((chips,)),
        ]
        + [shape] * (chips - 1),
        [p_own, smap, tables],
        24 * planes * part * length * length,
        "near",
        hbm=[0, 1, 2],
        fixed=[0, 1, 2],
        hbm_outs=range(chips),
    )
    return sends, done


def message_kernel(owner_ref, list_ref, out_ref):
    _, _, ntile, capacity = list_ref.shape
    out_ref[...] = jnp.zeros_like(out_ref)
    slots = owner_ref.shape[1]
    for to in range(ntile):
        for axis in range(3):
            out_ref[to, :, axis * capacity : (axis + 1) * capacity] = list_ref[axis, 0]
        out_ref[to, 0:1, 3 * capacity : 3 * capacity + slots] = owner_ref[...]


def message(block_owner, owner_list):
    ntile = owner_list.shape[2]
    return pl.pallas_call(
        message_kernel,
        out_shape=jax.ShapeDtypeStruct((ntile, ntile, LANES), jnp.int32),
        in_specs=[pl.BlockSpec(memory_space=pltpu.VMEM)] * 2,
        out_specs=pl.BlockSpec(memory_space=pltpu.VMEM),
        name="message",
    )(block_owner[None], owner_list)


def cut_boxes(info, grid, turns_ref, shift_ref, out_ref, gbuf, planes, chunk, slots):
    handlers = out_ref.shape[0]
    band = band_of_lane(planes, chunk)

    def cut(handler, carry):
        base = pl.multiple_of(handler * LANES, LANES)
        for slot in range(slots):
            block = handler * slots + slot
            here, after = in_window(band, info[1, block], chunk)
            first = grid[pl.ds(info[0, block], 4), :]
            second = grid[pl.ds(info[0, block] + LANES, 4), :]
            if chunk > 4:
                second = jnp.where(after, second, 0.0)
            cells = jnp.where(here, first, second)
            turn = pl.ds(info[2, block], 1)
            cells = cells * turns_ref[0, turn, :] + pltpu.roll(cells, LANES // 2, 1) * turns_ref[
                1, turn, :
            ]
            gbuf[pl.ds(base + slot, 4, stride=slots), :] = cells
        return carry

    lax.fori_loop(0, handlers, cut, 0)
    high, low = halves(shift_ref[...])
    table = jnp.concatenate(
        [
            jnp.concatenate([high, high], axis=1),
            jnp.concatenate([low, jnp.zeros_like(low)], axis=1),
        ],
        axis=0,
    )
    for handler in range(handlers):
        cells = gbuf[handler * LANES : (handler + 1) * LANES, :]
        both = dot_bf16(table, jnp.concatenate(halves(cells), axis=1), ((1,), (1,)))
        out_ref[handler] = both[:32] + both[32:]


def forward_kernel(*refs, chips, chunk, slots):
    pieces = 2 * chips - 1
    p_hbm = refs[:pieces]
    near_hbm, s_hbm, table_hbm, turns_hbm, shift_hbm, info_hbm, out_ref = refs[pieces : pieces + 7]
    pbuf, sbuf, tables, turns_ref, shift_ref, info = refs[pieces + 7 : pieces + 13]
    natural, ybuf, grid, gbuf, sems = refs[pieces + 13 :]
    _, planes, part, length = near_hbm.shape
    rows = length * planes
    starts = quarters_of(chips, part)
    order = [chips] + [at for at in range(1, 2 * chips) if at != chips]
    pairs = [(table_hbm.at[0:2], tables.at[0:2]), (table_hbm.at[2:4], tables.at[2:4])]
    for turn, at in enumerate(order):
        pairs.append((s_hbm.at[:, :, pl.ds(starts[at], part), :], sbuf.at[turn]))
        pairs.append((p_hbm[turn], pbuf.at[turn]))
    pairs += [
        (near_hbm, natural.at[:, :, pl.ds(starts[0], part), :]),
        (info_hbm, info),
        (turns_hbm, turns_ref),
        (shift_hbm, shift_ref),
    ]
    copies = started(pairs, sems)
    copies[0].wait()
    table = (tables[0], tables[1])
    for turn, at in enumerate(order):
        copies[2 + 2 * turn].wait()
        copies[3 + 2 * turn].wait()
        z_of_coil(pbuf.at[turn], sbuf.at[turn], 0, table, natural, pl.ds(starts[at], part))
    copies[2 + 2 * pieces].wait()
    copies[1].wait()
    table = (tables[2], tables[3])
    for pair in range(planes // 2):
        columns = [
            jnp.concatenate([natural[0, plane], natural[1, plane]], axis=0)
            for plane in (2 * pair, 2 * pair + 1)
        ]
        both = dot_left(table, jnp.concatenate(columns, axis=1))
        for inner in range(2):
            for ri in range(2):
                ybuf[pl.ds(ri * rows + 2 * pair + inner, length, stride=planes), :] = both[
                    ri * length : (ri + 1) * length, inner * LANES : (inner + 1) * LANES
                ]
    for band in range(length // chunk):
        re = ybuf[band * 64 : (band + 1) * 64, :]
        im = ybuf[rows + band * 64 : rows + (band + 1) * 64, :]
        grid[band * length : (band + 1) * length, :] = jnp.concatenate([re, im], axis=0).T
    for copy in copies[3 + 2 * pieces :]:
        copy.wait()
    cut_boxes(info, grid, turns_ref, shift_ref, out_ref, gbuf, planes, chunk, slots)


def forward(pieces, done, smap, tables, turns, shift, info, chunk, slots):
    _, planes, part, length = done.shape
    blocks = info.shape[1]
    count = len(pieces)
    operands = [*pieces, done, smap, tables, turns, shift, info]
    return call(
        functools.partial(forward_kernel, chips=(count + 1) // 2, chunk=chunk, slots=slots),
        [(blocks // slots, 32, LANES)],
        [
            (count, 2, planes, part, length),
            (count, 2, planes, part, length),
            pltpu.VMEM(tables.shape, tables.dtype),
            turns.shape,
            shift.shape,
            pltpu.SMEM(info.shape, info.dtype),
            (2, planes, length, length),
            (2 * length * planes, length),
            (length * (length // chunk + 1), LANES),
            (blocks * 4, LANES),
            pltpu.SemaphoreType.DMA((2 * count + 6,)),
        ],
        operands,
        48 * planes * length**3,
        "forward",
        hbm=range(len(operands)),
        fixed=range(count, len(operands)),
    )[0]


def regrid_kernel(parts_ref, matrix_ref, out_ref, held, done_sem):
    total = parts_ref[0]
    for at in range(1, parts_ref.shape[0]):
        total = total + parts_ref[at]
    along = lax.broadcasted_iota(jnp.int32, (8, LANES), 0) % 4
    sums = [jnp.zeros((8, LANES), jnp.float32) for _ in range(4)]
    for source in range(4):
        for d_z in range(4):
            value = total[8 * source : 8 * source + 8]
            if d_z:
                value = pltpu.roll(value, LANES - 32 * d_z, 1)
            for d_x in range(4):
                moved = value
                if d_x:
                    moved = jnp.where(
                        along + d_x < 4, pltpu.roll(value, 8 - d_x, 0), pltpu.roll(value, 4 - d_x, 0)
                    )
                for e in range(4):
                    at = 8 * (((e * 4 + source) * 4 + d_z) * 4 + d_x)
                    sums[e] = sums[e] + matrix_ref[at : at + 8] * moved
    done = jnp.concatenate(sums, axis=0)
    for at in range(held.shape[0]):
        held[at] = done
    copy = pltpu.make_async_copy(held, out_ref, done_sem)
    copy.start()
    copy.wait()


def regrid(parts, matrix, copies):
    shape = (copies,) + parts.shape[1:]
    return call(
        regrid_kernel,
        [shape],
        [shape, pltpu.SemaphoreType.DMA],
        [parts, matrix],
        10**7,
        "regrid",
        hbm_outs=[0],
        vmem=[1],
    )[0]


def place_boxes(info, chip, u_ref, turns_ref, shift_ref, outs, gbufs, planes, chunk, slots):
    chips = len(outs)
    handlers = u_ref.shape[0] // chips
    high, low = halves(shift_ref[...])
    table = jnp.concatenate([high, high, low, jnp.zeros_like(low)], axis=0)
    for handler in range(handlers):
        for hop in range(chips):
            u_hi, u_lo = (
                half.astype(jnp.float32)
                for half in halves(u_ref[(chip + hop) % chips * handlers + handler])
            )
            stack = jnp.concatenate([u_hi, u_lo, u_hi, jnp.zeros_like(u_hi)], axis=0)
            gbufs[hop][handler * LANES : (handler + 1) * LANES, :] = dot_bf16(
                stack.T.astype(jnp.bfloat16), table, ((1,), (0,))
            )
    band = band_of_lane(planes, chunk)

    def put(handler, carry):
        base = pl.multiple_of(handler * LANES, LANES)
        for slot in range(slots):
            block = handler * slots + slot
            here, after = in_window(band, info[1, block], chunk)
            first = pl.ds(info[0, block], 4)
            second = pl.ds(info[0, block] + LANES, 4)
            turn = pl.ds(info[2, block], 1)
            cos_b, sin_b = turns_ref[0, turn, :], turns_ref[1, turn, :]
            for hop in range(chips):
                cells = gbufs[hop][pl.ds(base + slot, 4, stride=slots), :]
                cells = cells * cos_b - pltpu.roll(cells, LANES // 2, 1) * sin_b
                old_first = outs[hop][first, :]
                old_second = outs[hop][second, :]
                outs[hop][first, :] = old_first + jnp.where(here, cells, 0.0)
                outs[hop][second, :] = old_second + jnp.where(after, cells, 0.0)
        return carry

    lax.fori_loop(0, handlers, put, 0)


def inverse_kernel(*refs, part, length, chunk, slots, chips):
    u_ref, s_hbm, table_hbm, turns_hbm, shift_hbm, info_hbm = refs[:6]
    far_maps = refs[6 : 5 + chips]
    outs = refs[5 + chips : 7 + chips]
    refs = refs[7 + chips :]
    grids, gbufs, refs = refs[:chips], refs[chips : 2 * chips], refs[2 * chips :]
    table_ref, turns_ref, shift_ref, info, ybuf, images, maps, sems = refs
    planes = s_hbm.shape[1]
    rows = length * planes
    own = length // chips
    chip, core = place_on_coil()
    own_rows = pl.multiple_of(chip * own, own)
    pairs = [
        (shift_hbm, shift_ref),
        (info_hbm, info),
        (turns_hbm, turns_ref),
        (table_hbm, table_ref),
        (s_hbm.at[:, :, pl.ds(own_rows, own), :], maps.at[0]),
    ]
    pairs += [(far_map, maps.at[at]) for at, far_map in enumerate(far_maps, 1)]
    copies = started(pairs, sems)
    for grid in grids:
        grid[...] = jnp.zeros_like(grid)
    for copy in copies[:3]:
        copy.wait()
    place_boxes(info, chip, u_ref, turns_ref, shift_ref, grids, gbufs, planes, chunk, slots)
    for copy in copies[3:]:
        copy.wait()
    table = []
    for half in range(2):
        bands = [
            table_ref[half, pl.ds(pl.multiple_of(ri * length + own_rows, own), own), :]
            for ri in range(2)
        ]
        table.append(jnp.concatenate(bands, axis=0))
    for hop in range(chips):
        for band in range(length // chunk):
            tile = grids[hop][band * length : (band + 1) * length, :].T
            ybuf[hop, band * 64 : (band + 1) * 64, :] = tile[:64]
            ybuf[hop, rows + band * 64 : rows + (band + 1) * 64, :] = tile[64:]
        for pair in range(planes // 2):
            columns = [
                jnp.concatenate(
                    [
                        ybuf[hop, pl.ds(ri * rows + plane, length, stride=planes), :]
                        for ri in range(2)
                    ],
                    axis=0,
                )
                for plane in (2 * pair, 2 * pair + 1)
            ]
            done = dot_left(table, jnp.concatenate(columns, axis=1))
            for inner in range(2):
                for ri in range(2):
                    images[hop, ri, 2 * pair + inner] = done[
                        ri * own : (ri + 1) * own, inner * LANES : (inner + 1) * LANES
                    ]
    table = (table_ref[2], table_ref[3])
    batch = min(planes, 256 // part)
    for at, half in enumerate((1 - core, core)):
        local = pl.ds(pl.multiple_of(half * part, part), part)
        for base in range(0, planes, batch):
            total_re, total_im = 0.0, 0.0
            for hop in range(chips):
                bands = [
                    jnp.concatenate([images[hop, ri, plane, local, :] for ri in range(2)], axis=1)
                    for plane in range(base, base + batch)
                ]
                done = dot_right(jnp.concatenate(bands, axis=0), table)
                i_re = done[:, :length].reshape(batch, part, length)
                i_im = done[:, length:].reshape(batch, part, length)
                s_re = maps[hop, 0, base : base + batch, local, :]
                s_im = maps[hop, 1, base : base + batch, local, :]
                total_re = total_re + (s_re * i_re + s_im * i_im)
                total_im = total_im + (s_re * i_im - s_im * i_re)
            outs[at][0, base : base + batch] = total_re
            outs[at][1, base : base + batch] = total_im


def inverse(spread, tables, turns, shift, smap, info, far_maps, part, chunk, slots):
    _, planes, length, _ = smap.shape
    chips = len(far_maps) + 1
    own = 2 * part
    blocks = info.shape[1]
    rows = length * (length // chunk + 1)
    return call(
        functools.partial(
            inverse_kernel, part=part, length=length, chunk=chunk, slots=slots, chips=chips
        ),
        [(2, planes, part, length)] * 2,
        [(rows, LANES)] * chips
        + [(blocks * 4, LANES)] * chips
        + [
            pltpu.VMEM(tables.shape, tables.dtype),
            turns.shape,
            shift.shape,
            pltpu.SMEM(info.shape, info.dtype),
            (chips, 2 * length * planes, length),
            (chips, 2, planes, own, length),
            (chips, 2, planes, own, length),
            pltpu.SemaphoreType.DMA((4 + chips,)),
        ],
        [spread, smap, tables, turns, shift, info, *far_maps],
        48 * planes * length**3,
        "inverse",
        hbm=range(1, 5 + chips),
        fixed=[1, 2, 3, 4, 5],
    )


def sums_kernel(*refs, terms):
    term_refs = refs[:terms]
    p_ref, r_ref, normal_ref, out_ref = refs[terms:]
    shape = p_ref.shape

    def add(plane, held):
        held = list(held)
        for ri in range(2):
            normal = term_refs[0][ri, plane]
            for term in term_refs[1:]:
                normal = normal + term[ri, plane]
            normal_ref[ri, plane] = normal
            p = p_ref[ri, plane]
            r = r_ref[ri, plane]
            for at, product in enumerate((r * r, p * normal, r * normal, normal * normal)):
                held[at] = held[at] + jnp.sum(product.reshape(-1, 8, LANES), axis=0)
        return tuple(held)

    start = tuple(jnp.zeros((8, LANES), jnp.float32) for _ in range(4))
    held = lax.fori_loop(0, shape[1], add, start, unroll=4)
    lane = lax.broadcasted_iota(jnp.int32, out_ref.shape, 1)
    found = jnp.zeros(out_ref.shape, jnp.float32)
    for at in range(4):
        found = jnp.where(lane == at, jnp.sum(held[at]), found)
    out_ref[...] = found


def sums(terms, p, r, devices):
    kernel = functools.partial(sums_kernel, terms=len(terms))
    return call(kernel, [p.shape, (devices, LANES)], [], [*terms, p, r], 10**7, "sums")


def finish_kernel(total_ref, x_ref, r_ref, p_ref, normal_ref, x_out, r_out, p_out):
    total = jnp.sum(total_ref[...], axis=0, keepdims=True)
    r_r, p_n, r_n, n_n = (total[:, at : at + 1] for at in range(4))
    alpha = r_r / p_n
    beta = (r_r + alpha * (alpha * n_n - 2.0 * r_n)) / r_r
    for plane in range(x_ref.shape[1]):
        for ri in range(2):
            p = p_ref[ri, plane]
            next_r = r_ref[ri, plane] - alpha * normal_ref[ri, plane]
            x_out[ri, plane] = x_ref[ri, plane] + alpha * p
            r_out[ri, plane] = next_r
            p_out[ri, plane] = next_r + beta * p


def finish(total, x, r, p, normal):
    return call(finish_kernel, [x.shape] * 3, [], [total, x, r, p, normal], 10**7, "finish")


def outer_rows(info, weights_ref, held, first, count, slots):
    base = lax.axis_index("tile") * slots

    def one(at, carry):
        block = first + at
        w_x = weights_ref[block, 0]
        w_y = weights_ref[block, 1]
        w_z = weights_ref[block, 2]
        twice = jnp.concatenate([w_x, w_x], axis=0)
        rolled = [twice] + [pltpu.roll(twice, 8 - d, 0) for d in range(1, 4)]
        low = lax.broadcasted_iota(jnp.int32, (8, LANES), 0) < 4
        along_x = [twice * jnp.where(low, rolled[d], rolled[d + 1]) for d in (0, 2)]
        right = []
        for f in range(4):
            for d_z in range(4):
                other = (f + d_z) % 4
                along_z = w_z[f : f + 1] * w_z[other : other + 1]
                right += [along * along_z for along in along_x]
        turned = pltpu.roll(
            jnp.concatenate([w_y, w_y], axis=0), info[1, base + block] % 4, 0
        )[:4]
        left = halves(jnp.concatenate([turned * turned[e : e + 1] for e in range(4)], axis=0))
        high, low = halves(jnp.concatenate(right, axis=0))
        both = dot_bf16(jnp.concatenate(left, axis=0), high, ((1,), (1,)))
        done = both[:16] + both[16:] + dot_bf16(left[0], low, ((1,), (1,)))
        for f in range(4):
            lanes = done[:, f // 2 * LANES : (f // 2 + 1) * LANES]
            if f % 2:
                lanes = pltpu.roll(lanes, LANES // 2, 1)
            held[pl.ds(f * count + at, 16, stride=4 * count), :] = lanes
        return carry

    lax.fori_loop(0, count, one, 0, unroll=4)


def matrices_first_kernel(info_hbm, weights_ref, out_ref, held, info, sem, *, slots):
    for copy in started([(info_hbm, info)], sem):
        copy.wait()
    outer_rows(info, weights_ref, held, 0, slots // 2, slots)
    for copy in started([(held, out_ref)], sem):
        copy.wait()


def matrices_last_kernel(info_hbm, first_hbm, weights_ref, out_ref, held, other, info, sems, *, slots):
    count = slots // 2
    copies = started([(info_hbm, info), (first_hbm, other)], sems)
    copies[0].wait()
    outer_rows(info, weights_ref, held, count, count, slots)
    copies[1].wait()

    def turn(pair, carry):
        at = pl.ds(pl.multiple_of(pair * 4 * count, 4 * count), 4 * count)
        ahead, behind = other[at, :], held[at, :]
        rows = []
        for f in range(4):
            rows += [ahead[f * count : (f + 1) * count], behind[f * count : (f + 1) * count]]
        rows = jnp.concatenate(rows, axis=0).T
        for group in range(16):
            four = rows[4 * group : 4 * group + 4]
            out_ref[pl.ds(pl.multiple_of(pair * LANES + 8 * group, 8), 8), :] = jnp.concatenate(
                [four, four], axis=0
            )
        return carry

    lax.fori_loop(0, 16, turn, 0, unroll=2)


def matrices_first(info, weights):
    shape = (8 * LANES, LANES)
    return call(
        functools.partial(matrices_first_kernel, slots=weights.shape[0]),
        [shape],
        [shape, pltpu.SMEM(info.shape, info.dtype), pltpu.SemaphoreType.DMA((1,))],
        [info, weights],
        10**9,
        "matrices_first",
        hbm=[0],
        fixed=[0],
        hbm_outs=[0],
    )[0]


def matrices_last(info, first, weights):
    return call(
        functools.partial(matrices_last_kernel, slots=weights.shape[0]),
        [(16 * LANES, LANES)],
        [
            first.shape,
            first.shape,
            pltpu.SMEM(info.shape, info.dtype),
            pltpu.SemaphoreType.DMA((2,)),
        ],
        [info, first, weights],
        10**9,
        "matrices_last",
        hbm=[0, 1],
        fixed=[0, 1],
    )[0]


def block_offsets(gathered, slots, ntile, capacity):
    owners = gathered[:, 0, 3 * capacity : 3 * capacity + slots]
    lists = gathered[:, :, : 3 * capacity].reshape(ntile, ntile, 3, capacity)
    earlier = jnp.tril(jnp.ones((slots, slots), jnp.int32), -1)
    same = (owners[:, :, None] == owners[:, None, :]).astype(jnp.int32)
    ranks = jnp.sum(same * earlier[None], axis=2)
    wanted = owners * capacity + ranks
    lists = jnp.transpose(lists, (2, 1, 0, 3)).reshape(3, ntile, 1, ntile * capacity)
    hit = wanted[:, :, None] == jnp.arange(ntile * capacity, dtype=jnp.int32)
    found = jnp.sum(jnp.where(hit[None], lists, 0), axis=3)
    return found[0], found[1] + owners * (LANES // ntile), found[2]


def shards(image_p, image_x, image_r, sensitivity, kb_weights, block_owner, owner_list):
    ntile = lax.axis_size("tile")
    ncoil = lax.axis_size("coil")
    chips = ncoil // 2
    slots = kb_weights.shape[0]
    capacity = owner_list.shape[3]
    planes, length = image_p.shape[1], image_p.shape[3]
    part = image_p.shape[2]
    chunk = LANES // (2 * planes)
    tile = lax.axis_index("tile")
    smap = sensitivity[0]
    tables = fourier_tables(length)

    def from_chip(values, by):
        pairs = [
            (a * 2 + k, (a - by) % chips * 2 + k) for a in range(chips) for k in range(2)
        ]
        return lax.ppermute(values, "coil", pairs)

    def other_core(values):
        pairs = [(a * 2 + k, a * 2 + 1 - k) for a in range(chips) for k in range(2)]
        return lax.ppermute(values, "coil", pairs)

    p_same = [image_p] + [from_chip(image_p, by) for by in range(1, chips)]
    p_other = [other_core(image_p)]
    gathered = lax.all_to_all(message(block_owner, owner_list), "tile", 0, 0, tiled=True)
    sends, done = near(image_p, smap, tables, chips)
    off_x, off_y, off_z = block_offsets(gathered, slots, ntile, capacity)
    info = jnp.stack(
        [
            (off_y // chunk * length + off_z).reshape(-1),
            (off_y % chunk).reshape(-1),
            off_x.reshape(-1),
        ]
    )
    lane = jnp.arange(LANES, dtype=jnp.int32)
    lane_ri = lane // (LANES // 2)
    lane_q = lane // planes % chunk
    lane_x = lane % planes + tile * planes
    unit = 2.0 * math.pi / length
    offset = jnp.arange(length, dtype=jnp.int32)[:, None]
    angle = unit * (offset * lane_x[None] % length).astype(jnp.float32)
    turns = jnp.stack(
        [jnp.cos(angle), jnp.sin(angle) * jnp.where(lane_ri == 0, 1.0, -1.0)[None]]
    )
    row = jnp.arange(32, dtype=jnp.int32)[:, None]
    row_q, row_ri, row_i = row // 8, row // 4 % 2, row % 4
    angle = unit * (row_i * lane_x[None] % length).astype(jnp.float32)
    sine = jnp.where(row_ri == 0, 1.0, -1.0) * jnp.sin(angle)
    shift = jnp.where(row_ri == lane_ri[None], jnp.cos(angle), sine)
    shift = jnp.where(lane_q[None] % 4 == row_q, shift / math.sqrt(length), 0.0)
    first = matrices_first(info, kb_weights)
    p_far, sends, done, info, first, turns, shift = lax.optimization_barrier(
        (p_same[1:], sends, done, info, first, turns, shift)
    )
    far_maps = [from_chip(rows, by) for by, rows in enumerate(sends, 1)]
    p_other += [other_core(piece) for piece in p_far]
    partial = forward(
        [p_other[0], *p_far, *p_other[1:]], done, smap, tables, turns, shift, info, chunk, slots
    )
    partial, weights = lax.optimization_barrier((partial, kb_weights))
    parts = lax.all_to_all(partial, "tile", 0, 0, tiled=True)
    done = regrid(parts, matrices_last(info, first, weights), chips * ntile)
    groups = [
        [at * ntile + t for at in range(ncoil) if at % 2 == k for t in range(ntile)]
        for k in range(2)
    ]
    spread = lax.all_to_all(
        done, ("coil", "tile"), 0, 0, axis_index_groups=groups, tiled=True
    )
    sent, kept = inverse(
        spread, tables, turns, shift, smap, info, far_maps, part, chunk, slots
    )
    normal, found = sums([kept, other_core(sent)], image_p, image_r, ncoil * ntile)
    total = lax.all_to_all(found, ("coil", "tile"), 0, 0, tiled=True)
    return tuple(finish(total, image_x, image_r, image_p, normal))


def solution(mesh):
    return jax.shard_map(
        shards,
        mesh=mesh,
        in_specs=(
            P(None, "tile", "coil", None),
            P(None, "tile", "coil", None),
            P(None, "tile", "coil", None),
            P("coil", None, "tile", None, None),
            P("tile", None, None, None),
            P("tile"),
            P(None, "tile", None, None),
        ),
        out_specs=(
            P(None, "tile", "coil", None),
            P(None, "tile", "coil", None),
            P(None, "tile", "coil", None),
        ),
        check_vma=False,
    )
```

```python
import functools
import math

import jax
import jax.numpy as jnp
import ml_dtypes
import numpy as np
from jax import lax
from jax.experimental import pallas as pl
from jax.experimental.pallas import tpu as pltpu
from jax.sharding import PartitionSpec as P

LANES = 128
VMEM = 24 * 1024 * 1024


def halves(values):
    high = values.astype(jnp.bfloat16)
    low = (values - high.astype(jnp.float32)).astype(jnp.bfloat16)
    return high, low


def dot_bf16(left, right, dims):
    return lax.dot_general(left, right, (dims, ((), ())), preferred_element_type=jnp.float32)


def dot_left(table, values, dims=((1,), (0,))):
    high, low = halves(values)
    return (
        dot_bf16(table[0], high, dims)
        + dot_bf16(table[0], low, dims)
        + dot_bf16(table[1], high, dims)
    )


def dot_right(values, table, dims=((1,), (0,))):
    high, low = halves(values)
    return (
        dot_bf16(high, table[0], dims)
        + dot_bf16(low, table[0], dims)
        + dot_bf16(high, table[1], dims)
    )


def fourier_tables(length):
    cells = np.arange(length)
    angle = 2.0 * math.pi / length * (cells[:, None] * cells[None, :] % length)
    cos_t = np.cos(angle) / math.sqrt(length)
    sin_t = np.sin(angle) / math.sqrt(length)
    found = []
    for sign in (1.0, -1.0):
        whole = np.block([[cos_t, -sign * sin_t], [sign * sin_t, cos_t]])
        high = whole.astype(ml_dtypes.bfloat16)
        low = (whole - high.astype(np.float64)).astype(ml_dtypes.bfloat16)
        found += [high, low]
    return jnp.asarray(np.stack(found))


def band_of_lane(planes, chunk):
    return lax.broadcasted_iota(jnp.int32, (4, LANES), 1) // planes % chunk


def in_window(band, first, chunk):
    past = band - first
    if chunk == 4:
        here = past >= 0
        return here, jnp.logical_not(here)
    here = jnp.logical_and(past >= 0, past < 4)
    return here, past < 4 - chunk


def call(kernel, outs, scratch, operands, flops, name, hbm=(), hbm_outs=(), vmem=(), fixed=()):
    operands = list(operands)
    for listed, space in ((fixed, pltpu.HBM), (vmem, pltpu.VMEM)):
        for at in listed:
            operands[at] = pltpu.with_memory_space_constraint(operands[at], space)
    here = pl.BlockSpec(memory_space=pltpu.VMEM)
    there = pl.BlockSpec(memory_space=pltpu.HBM)
    moved = sum(math.prod(a.shape) * a.dtype.itemsize for a in operands)
    return pl.pallas_call(
        kernel,
        out_shape=[
            pltpu.HBM(shape, jnp.float32)
            if at in hbm_outs
            else jax.ShapeDtypeStruct(shape, jnp.float32)
            for at, shape in enumerate(outs)
        ],
        in_specs=[there if at in hbm else here for at in range(len(operands))],
        out_specs=[there if at in hbm_outs else here for at in range(len(outs))],
        scratch_shapes=[
            pltpu.VMEM(shape, jnp.float32) if isinstance(shape, tuple) else shape
            for shape in scratch
        ],
        compiler_params=pltpu.CompilerParams(vmem_limit_bytes=VMEM),
        cost_estimate=pl.CostEstimate(flops=flops, bytes_accessed=moved, transcendentals=0),
        name=name,
    )(*operands)


def started(pairs, sems):
    copies = [
        pltpu.make_async_copy(source, to, sems.at[at]) for at, (source, to) in enumerate(pairs)
    ]
    for copy in copies:
        copy.start()
    return copies


def place_on_coil():
    coil = lax.axis_index("coil")
    return coil // 2, coil % 2


def quarters_of(chips, part):
    chip, core = place_on_coil()
    return [
        pl.multiple_of(((chip + hop) % chips * 2 + at) * part, part)
        for at in (core, 1 - core)
        for hop in range(chips)
    ]


def map_rows_kernel(s_ref, *refs, chips):
    outs, (held, sems) = refs[:-2], refs[-2:]
    chip, _ = place_on_coil()
    own = s_ref.shape[2] // chips
    for by in range(1, chips):
        rows = pl.ds(pl.multiple_of((chip + chips - by) % chips * own, own), own)
        for copy in started([(s_ref.at[:, :, rows, :], held)], sems):
            copy.wait()
        for copy in started([(held, outs[by - 1])], sems):
            copy.wait()


def map_rows(smap, chips):
    _, planes, length, _ = smap.shape
    shape = (2, planes, length // chips, length)
    return call(
        functools.partial(map_rows_kernel, chips=chips),
        [shape] * (chips - 1),
        [shape, pltpu.SemaphoreType.DMA((1,))],
        [smap],
        0,
        "map_rows",
        hbm=[0],
        fixed=[0],
        hbm_outs=range(chips - 1),
    )


def message_kernel(owner_ref, list_ref, out_ref):
    _, _, ntile, capacity = list_ref.shape
    out_ref[...] = jnp.zeros_like(out_ref)
    slots = owner_ref.shape[1]
    for to in range(ntile):
        for axis in range(3):
            out_ref[to, :, axis * capacity : (axis + 1) * capacity] = list_ref[axis, 0]
        out_ref[to, 0:1, 3 * capacity : 3 * capacity + slots] = owner_ref[...]


def message(block_owner, owner_list):
    ntile = owner_list.shape[2]
    return pl.pallas_call(
        message_kernel,
        out_shape=jax.ShapeDtypeStruct((ntile, ntile, LANES), jnp.int32),
        in_specs=[pl.BlockSpec(memory_space=pltpu.VMEM)] * 2,
        out_specs=pl.BlockSpec(memory_space=pltpu.VMEM),
        name="message",
    )(block_owner[None], owner_list)


def cut_boxes(info, grid, cos_ref, sin_ref, shift_ref, out_ref, gbuf, planes, chunk, slots):
    handlers = out_ref.shape[0]
    band = band_of_lane(planes, chunk)

    def cut(handler, carry):
        base = pl.multiple_of(handler * LANES, LANES)
        for slot in range(slots):
            block = handler * slots + slot
            here, after = in_window(band, info[1, block], chunk)
            first = grid[pl.ds(info[0, block], 4), :]
            second = grid[pl.ds(info[0, block] + LANES, 4), :]
            if chunk > 4:
                second = jnp.where(after, second, 0.0)
            gbuf[pl.ds(base + slot, 4, stride=slots), :] = jnp.where(here, first, second)
        return carry

    lax.fori_loop(0, handlers, cut, 0)
    high, low = halves(shift_ref[...])
    table = jnp.concatenate(
        [
            jnp.concatenate([high, high], axis=1),
            jnp.concatenate([low, jnp.zeros_like(low)], axis=1),
        ],
        axis=0,
    )
    for handler in range(handlers):
        rows = slice(handler * slots, (handler + 1) * slots)
        cos_b = jnp.concatenate([cos_ref[rows, :]] * 4, axis=0)
        sin_b = jnp.concatenate([sin_ref[rows, :]] * 4, axis=0)
        cells = gbuf[handler * LANES : (handler + 1) * LANES, :]
        turned = cells * cos_b + pltpu.roll(cells, LANES // 2, 1) * sin_b
        both = dot_bf16(table, jnp.concatenate(halves(turned), axis=1), ((1,), (1,)))
        out_ref[handler] = both[:32] + both[32:]


def forward_kernel(*refs, pieces, chunk, slots):
    p_hbm = refs[:pieces]
    s_hbm, table_hbm, info_hbm, cos_hbm, sin_hbm, shift_hbm, out_ref = refs[pieces : pieces + 7]
    pbuf, sbuf, tables, info, cos_ref, sin_ref, shift_ref = refs[pieces + 7 : pieces + 14]
    natural, ybuf, grid, gbuf, sems = refs[pieces + 14 :]
    _, planes, part, length = p_hbm[0].shape
    rows = length * planes
    starts = quarters_of(pieces // 2, part)
    order = [0, pieces // 2]
    order += [at for at in range(pieces) if at not in order]
    first = [(table_hbm.at[0:2], tables.at[0:2])]
    for at in order:
        first += [(p_hbm[at], pbuf.at[at]), (s_hbm.at[:, :, pl.ds(starts[at], part), :], sbuf.at[at])]
    last = [
        (table_hbm.at[2:4], tables.at[2:4]),
        (info_hbm, info),
        (cos_hbm, cos_ref),
        (sin_hbm, sin_ref),
        (shift_hbm, shift_ref),
    ]
    copies = started(first + last, sems)
    copies[0].wait()
    batch = min(planes, 256 // part)
    table = (tables[0], tables[1])
    for turn, at in enumerate(order):
        copies[1 + 2 * turn].wait()
        copies[2 + 2 * turn].wait()
        for base in range(0, planes, batch):
            bands = []
            for plane in range(base, base + batch):
                s_re = sbuf[at, 0, plane]
                s_im = sbuf[at, 1, plane]
                p_re = pbuf[at, 0, plane]
                p_im = pbuf[at, 1, plane]
                bands.append(
                    jnp.concatenate([s_re * p_re - s_im * p_im, s_re * p_im + s_im * p_re], axis=1)
                )
            done = dot_right(jnp.concatenate(bands, axis=0), table)
            for ri in range(2):
                half = done[:, ri * length : (ri + 1) * length]
                natural[ri, base : base + batch, pl.ds(starts[at], part), :] = half.reshape(
                    batch, part, length
                )
    for copy in copies[1 + 2 * pieces :]:
        copy.wait()
    table = (tables[2], tables[3])
    for pair in range(planes // 2):
        columns = [
            jnp.concatenate([natural[0, plane], natural[1, plane]], axis=0)
            for plane in (2 * pair, 2 * pair + 1)
        ]
        both = dot_left(table, jnp.concatenate(columns, axis=1))
        for inner in range(2):
            for ri in range(2):
                ybuf[pl.ds(ri * rows + 2 * pair + inner, length, stride=planes), :] = both[
                    ri * length : (ri + 1) * length, inner * LANES : (inner + 1) * LANES
                ]
    for band in range(length // chunk):
        re = ybuf[band * 64 : (band + 1) * 64, :]
        im = ybuf[rows + band * 64 : rows + (band + 1) * 64, :]
        grid[band * length : (band + 1) * length, :] = jnp.concatenate([re, im], axis=0).T
    cut_boxes(info, grid, cos_ref, sin_ref, shift_ref, out_ref, gbuf, planes, chunk, slots)


def forward(pieces, smap, tables, info, phases, shift, chunk, slots):
    _, planes, part, length = pieces[0].shape
    count = len(pieces)
    blocks = info.shape[1]
    operands = [*pieces, smap, tables, info, *phases, shift]
    return call(
        functools.partial(forward_kernel, pieces=count, chunk=chunk, slots=slots),
        [(blocks // slots, 32, LANES)],
        [
            (count, 2, planes, part, length),
            (count, 2, planes, part, length),
            pltpu.VMEM(tables.shape, tables.dtype),
            pltpu.SMEM(info.shape, info.dtype),
            (blocks, LANES),
            (blocks, LANES),
            shift.shape,
            (2, planes, length, length),
            (2 * length * planes, length),
            (length * (length // chunk + 1), LANES),
            (blocks * 4, LANES),
            pltpu.SemaphoreType.DMA((2 * count + 6,)),
        ],
        operands,
        48 * planes * length**3,
        "forward",
        hbm=range(len(operands)),
        fixed=range(count, len(operands)),
    )[0]


def regrid_kernel(parts_ref, matrix_ref, out_ref, held, done_sem):
    total = parts_ref[0]
    for at in range(1, parts_ref.shape[0]):
        total = total + parts_ref[at]
    along = lax.broadcasted_iota(jnp.int32, (8, LANES), 0) % 4
    sums = [jnp.zeros((8, LANES), jnp.float32) for _ in range(4)]
    for source in range(4):
        for d_z in range(4):
            value = total[8 * source : 8 * source + 8]
            if d_z:
                value = pltpu.roll(value, LANES - 32 * d_z, 1)
            for d_x in range(4):
                moved = value
                if d_x:
                    moved = jnp.where(
                        along + d_x < 4, pltpu.roll(value, 8 - d_x, 0), pltpu.roll(value, 4 - d_x, 0)
                    )
                for e in range(4):
                    at = 8 * (((e * 4 + source) * 4 + d_z) * 4 + d_x)
                    sums[e] = sums[e] + matrix_ref[at : at + 8] * moved
    done = jnp.concatenate(sums, axis=0)
    for at in range(held.shape[0]):
        held[at] = done
    copy = pltpu.make_async_copy(held, out_ref, done_sem)
    copy.start()
    copy.wait()


def regrid(parts, matrix, copies):
    shape = (copies,) + parts.shape[1:]
    return call(
        regrid_kernel,
        [shape],
        [shape, pltpu.SemaphoreType.DMA],
        [parts, matrix],
        10**7,
        "regrid",
        hbm_outs=[0],
        vmem=[1],
    )[0]


def place_boxes(info, chip, u_ref, cos_ref, sin_ref, shift_ref, outs, gbufs, planes, chunk, slots):
    chips = len(outs)
    handlers = u_ref.shape[0] // chips
    high, low = halves(shift_ref[...])
    table = jnp.concatenate([high, high, low, jnp.zeros_like(low)], axis=0)
    for handler in range(handlers):
        rows = slice(handler * slots, (handler + 1) * slots)
        cos_b = jnp.concatenate([cos_ref[rows, :]] * 4, axis=0)
        sin_b = jnp.concatenate([sin_ref[rows, :]] * 4, axis=0)
        for hop in range(chips):
            u_hi, u_lo = (
                half.astype(jnp.float32) for half in halves(u_ref[(chip + hop) % chips * handlers + handler])
            )
            stack = jnp.concatenate([u_hi, u_lo, u_hi, jnp.zeros_like(u_hi)], axis=0)
            cells = dot_bf16(stack.T.astype(jnp.bfloat16), table, ((1,), (0,)))
            turned = cells * cos_b - pltpu.roll(cells, LANES // 2, 1) * sin_b
            gbufs[hop][handler * LANES : (handler + 1) * LANES, :] = turned
    band = band_of_lane(planes, chunk)

    def put(handler, carry):
        base = pl.multiple_of(handler * LANES, LANES)
        for slot in range(slots):
            block = handler * slots + slot
            here, after = in_window(band, info[1, block], chunk)
            first = pl.ds(info[0, block], 4)
            second = pl.ds(info[0, block] + LANES, 4)
            for hop in range(chips):
                cells = gbufs[hop][pl.ds(base + slot, 4, stride=slots), :]
                old_first = outs[hop][first, :]
                old_second = outs[hop][second, :]
                outs[hop][first, :] = old_first + jnp.where(here, cells, 0.0)
                outs[hop][second, :] = old_second + jnp.where(after, cells, 0.0)
        return carry

    lax.fori_loop(0, handlers, put, 0)


def inverse_kernel(*refs, part, length, chunk, slots, chips):
    u_ref, info_hbm, cos_hbm, sin_hbm, shift_hbm, table_hbm, s_hbm = refs[:7]
    far_maps = refs[7 : 6 + chips]
    outs = refs[6 + chips : 8 + chips]
    refs = refs[8 + chips :]
    grids, gbufs, refs = refs[:chips], refs[chips : 2 * chips], refs[2 * chips :]
    info, cos_ref, sin_ref, shift_ref, table_ref, ybuf, images, maps, sems = refs
    planes = s_hbm.shape[1]
    rows = length * planes
    own = length // chips
    chip, core = place_on_coil()
    own_rows = pl.multiple_of(chip * own, own)
    pairs = [
        (info_hbm, info),
        (cos_hbm, cos_ref),
        (sin_hbm, sin_ref),
        (shift_hbm, shift_ref),
        (table_hbm, table_ref),
        (s_hbm.at[:, :, pl.ds(own_rows, own), :], maps.at[0]),
    ]
    pairs += [(far_map, maps.at[at]) for at, far_map in enumerate(far_maps, 1)]
    copies = started(pairs, sems)
    for grid in grids:
        grid[...] = jnp.zeros_like(grid)
    for copy in copies[:4]:
        copy.wait()
    place_boxes(info, chip, u_ref, cos_ref, sin_ref, shift_ref, grids, gbufs, planes, chunk, slots)
    for copy in copies[4:]:
        copy.wait()
    table = []
    for half in range(2):
        bands = [
            table_ref[half, pl.ds(pl.multiple_of(ri * length + own_rows, own), own), :]
            for ri in range(2)
        ]
        table.append(jnp.concatenate(bands, axis=0))
    for hop in range(chips):
        for band in range(length // chunk):
            tile = grids[hop][band * length : (band + 1) * length, :].T
            ybuf[hop, band * 64 : (band + 1) * 64, :] = tile[:64]
            ybuf[hop, rows + band * 64 : rows + (band + 1) * 64, :] = tile[64:]
        for pair in range(planes // 2):
            columns = [
                jnp.concatenate(
                    [
                        ybuf[hop, pl.ds(ri * rows + plane, length, stride=planes), :]
                        for ri in range(2)
                    ],
                    axis=0,
                )
                for plane in (2 * pair, 2 * pair + 1)
            ]
            done = dot_left(table, jnp.concatenate(columns, axis=1))
            for inner in range(2):
                for ri in range(2):
                    images[hop, ri, 2 * pair + inner] = done[
                        ri * own : (ri + 1) * own, inner * LANES : (inner + 1) * LANES
                    ]
    table = (table_ref[2], table_ref[3])
    batch = min(planes, 256 // part)
    for at, half in enumerate((1 - core, core)):
        local = pl.ds(pl.multiple_of(half * part, part), part)
        for base in range(0, planes, batch):
            total_re, total_im = 0.0, 0.0
            for hop in range(chips):
                bands = [
                    jnp.concatenate([images[hop, ri, plane, local, :] for ri in range(2)], axis=1)
                    for plane in range(base, base + batch)
                ]
                done = dot_right(jnp.concatenate(bands, axis=0), table)
                i_re = done[:, :length].reshape(batch, part, length)
                i_im = done[:, length:].reshape(batch, part, length)
                s_re = maps[hop, 0, base : base + batch, local, :]
                s_im = maps[hop, 1, base : base + batch, local, :]
                total_re = total_re + (s_re * i_re + s_im * i_im)
                total_im = total_im + (s_re * i_im - s_im * i_re)
            outs[at][0, base : base + batch] = total_re
            outs[at][1, base : base + batch] = total_im


def inverse(spread, info, phases, shift, tables, smap, far_maps, part, chunk, slots):
    _, planes, length, _ = smap.shape
    chips = len(far_maps) + 1
    blocks = info.shape[1]
    rows = length * (length // chunk + 1)
    own = (chips, 2, planes, 2 * part, length)
    operands = [spread, info, *phases, shift, tables, smap, *far_maps]
    return call(
        functools.partial(
            inverse_kernel, part=part, length=length, chunk=chunk, slots=slots, chips=chips
        ),
        [(2, planes, part, length)] * 2,
        [(rows, LANES)] * chips
        + [(blocks * 4, LANES)] * chips
        + [
            pltpu.SMEM(info.shape, info.dtype),
            (blocks, LANES),
            (blocks, LANES),
            shift.shape,
            pltpu.VMEM(tables.shape, tables.dtype),
            (chips, 2 * length * planes, length),
            own,
            own,
            pltpu.SemaphoreType.DMA((5 + chips,)),
        ],
        operands,
        48 * planes * length**3,
        "inverse",
        hbm=range(1, len(operands)),
        fixed=range(1, 7),
    )


def sums_kernel(*refs, terms):
    term_refs = refs[:terms]
    p_ref, r_ref, normal_ref, out_ref = refs[terms:]
    shape = p_ref.shape

    def add(plane, held):
        held = list(held)
        for ri in range(2):
            normal = term_refs[0][ri, plane]
            for term in term_refs[1:]:
                normal = normal + term[ri, plane]
            normal_ref[ri, plane] = normal
            p = p_ref[ri, plane]
            r = r_ref[ri, plane]
            for at, product in enumerate((r * r, p * normal, r * normal, normal * normal)):
                held[at] = held[at] + jnp.sum(product.reshape(-1, 8, LANES), axis=0)
        return tuple(held)

    start = tuple(jnp.zeros((8, LANES), jnp.float32) for _ in range(4))
    held = lax.fori_loop(0, shape[1], add, start, unroll=4)
    lane = lax.broadcasted_iota(jnp.int32, out_ref.shape, 1)
    found = jnp.zeros(out_ref.shape, jnp.float32)
    for at in range(4):
        found = jnp.where(lane == at, jnp.sum(held[at]), found)
    out_ref[...] = found


def sums(terms, p, r, devices):
    kernel = functools.partial(sums_kernel, terms=len(terms))
    return call(kernel, [p.shape, (devices, LANES)], [], [*terms, p, r], 10**7, "sums")


def finish_kernel(total_ref, x_ref, r_ref, p_ref, normal_ref, x_out, r_out, p_out):
    total = jnp.sum(total_ref[...], axis=0, keepdims=True)
    r_r, p_n, r_n, n_n = (total[:, at : at + 1] for at in range(4))
    alpha = r_r / p_n
    beta = (r_r + alpha * (alpha * n_n - 2.0 * r_n)) / r_r
    for plane in range(x_ref.shape[1]):
        for ri in range(2):
            p = p_ref[ri, plane]
            next_r = r_ref[ri, plane] - alpha * normal_ref[ri, plane]
            x_out[ri, plane] = x_ref[ri, plane] + alpha * p
            r_out[ri, plane] = next_r
            p_out[ri, plane] = next_r + beta * p


def finish(total, x, r, p, normal):
    return call(finish_kernel, [x.shape] * 3, [], [total, x, r, p, normal], 10**7, "finish")


def matrices_kernel(info_hbm, weights_ref, out_ref, held, info, sem, *, slots):
    base = lax.axis_index("tile") * slots
    copy = pltpu.make_async_copy(info_hbm, info, sem)
    copy.start()
    copy.wait()

    def one(block, carry):
        w_x = weights_ref[block, 0]
        w_y = weights_ref[block, 1]
        w_z = weights_ref[block, 2]
        twice = jnp.concatenate([w_x, w_x], axis=0)
        rolled = [twice] + [pltpu.roll(twice, 8 - d, 0) for d in range(1, 4)]
        low = lax.broadcasted_iota(jnp.int32, (8, LANES), 0) < 4
        along_x = [twice * jnp.where(low, rolled[d], rolled[d + 1]) for d in (0, 2)]
        right = []
        for f in range(4):
            for d_z in range(4):
                other = (f + d_z) % 4
                along_z = w_z[f : f + 1] * w_z[other : other + 1]
                right += [along * along_z for along in along_x]
        turned = pltpu.roll(
            jnp.concatenate([w_y, w_y], axis=0), info[1, base + block] % 4, 0
        )[:4]
        left = halves(jnp.concatenate([turned * turned[e : e + 1] for e in range(4)], axis=0))
        high, low = halves(jnp.concatenate(right, axis=0))
        both = dot_bf16(jnp.concatenate(left, axis=0), high, ((1,), (1,)))
        done = both[:16] + both[16:] + dot_bf16(left[0], low, ((1,), (1,)))
        for f in range(4):
            lanes = done[:, f // 2 * LANES : (f // 2 + 1) * LANES]
            if f % 2:
                lanes = pltpu.roll(lanes, LANES // 2, 1)
            held[pl.ds(f * slots + block, 16, stride=LANES), :] = lanes
        return carry

    lax.fori_loop(0, slots, one, 0, unroll=4)

    def turn(pair, carry):
        at = pl.ds(pl.multiple_of(pair * LANES, LANES), LANES)
        rows = held[at, :].T
        for group in range(16):
            four = rows[4 * group : 4 * group + 4]
            out_ref[pl.ds(pl.multiple_of(pair * LANES + 8 * group, 8), 8), :] = jnp.concatenate(
                [four, four], axis=0
            )
        return carry

    lax.fori_loop(0, 16, turn, 0, unroll=2)


def block_matrices(info, weights):
    return call(
        functools.partial(matrices_kernel, slots=weights.shape[0]),
        [(16 * LANES, LANES)],
        [(16 * LANES, LANES), pltpu.SMEM(info.shape, info.dtype), pltpu.SemaphoreType.DMA],
        [info, weights],
        10**9,
        "matrices",
        hbm=[0],
    )[0]


def block_offsets(gathered, slots, ntile, capacity):
    owners = gathered[:, 0, 3 * capacity : 3 * capacity + slots]
    lists = gathered[:, :, : 3 * capacity].reshape(ntile, ntile, 3, capacity)
    earlier = jnp.tril(jnp.ones((slots, slots), jnp.int32), -1)
    same = (owners[:, :, None] == owners[:, None, :]).astype(jnp.int32)
    ranks = jnp.sum(same * earlier[None], axis=2)
    wanted = owners * capacity + ranks
    lists = jnp.transpose(lists, (2, 1, 0, 3)).reshape(3, ntile, 1, ntile * capacity)
    hit = wanted[:, :, None] == jnp.arange(ntile * capacity, dtype=jnp.int32)
    found = jnp.sum(jnp.where(hit[None], lists, 0), axis=3)
    return found[0], found[1] + owners * (LANES // ntile), found[2]


def shards(image_p, image_x, image_r, sensitivity, kb_weights, block_owner, owner_list):
    ntile = lax.axis_size("tile")
    ncoil = lax.axis_size("coil")
    chips = ncoil // 2
    slots = kb_weights.shape[0]
    capacity = owner_list.shape[3]
    planes, length = image_p.shape[1], image_p.shape[3]
    part = image_p.shape[2]
    chunk = LANES // (2 * planes)
    tile = lax.axis_index("tile")
    smap = sensitivity[0]
    tables = fourier_tables(length)

    def from_chip(values, by):
        pairs = [
            (a * 2 + k, (a - by) % chips * 2 + k) for a in range(chips) for k in range(2)
        ]
        return lax.ppermute(values, "coil", pairs)

    def other_core(values):
        pairs = [(a * 2 + k, a * 2 + 1 - k) for a in range(chips) for k in range(2)]
        return lax.ppermute(values, "coil", pairs)

    p_same = [image_p] + [from_chip(image_p, by) for by in range(1, chips)]
    p_other = [other_core(image_p)]
    gathered = lax.all_to_all(message(block_owner, owner_list), "tile", 0, 0, tiled=True)
    far_rows = map_rows(smap, chips)
    off_x, off_y, off_z = block_offsets(gathered, slots, ntile, capacity)
    info = jnp.stack(
        [(off_y // chunk * length + off_z).reshape(-1), (off_y % chunk).reshape(-1)]
    )
    lane = jnp.arange(LANES, dtype=jnp.int32)
    lane_ri = lane // (LANES // 2)
    lane_q = lane // planes % chunk
    lane_x = lane % planes + tile * planes
    unit = 2.0 * math.pi / length
    angle = unit * (off_x.reshape(-1, 1) * lane_x[None] % length).astype(jnp.float32)
    phases = (jnp.cos(angle), jnp.sin(angle) * jnp.where(lane_ri == 0, 1.0, -1.0)[None])
    row = jnp.arange(32, dtype=jnp.int32)[:, None]
    row_q, row_ri, row_i = row // 8, row // 4 % 2, row % 4
    angle = unit * (row_i * lane_x[None] % length).astype(jnp.float32)
    sine = jnp.where(row_ri == 0, 1.0, -1.0) * jnp.sin(angle)
    shift = jnp.where(row_ri == lane_ri[None], jnp.cos(angle), sine)
    shift = jnp.where(lane_q[None] % 4 == row_q, shift / math.sqrt(length), 0.0)
    p_far, far_rows, info, phases, shift = lax.optimization_barrier(
        (p_same[1:], far_rows, info, phases, shift)
    )
    p_other += [other_core(piece) for piece in p_far]
    far_maps = [from_chip(rows, by) for by, rows in enumerate(far_rows, 1)]
    partial = forward([image_p, *p_far, *p_other], smap, tables, info, phases, shift, chunk, slots)
    partial, weights = lax.optimization_barrier((partial, kb_weights))
    parts = lax.all_to_all(partial, "tile", 0, 0, tiled=True)
    done = regrid(parts, block_matrices(info, weights), chips * ntile)
    groups = [
        [at * ntile + t for at in range(ncoil) if at % 2 == k for t in range(ntile)]
        for k in range(2)
    ]
    spread = lax.all_to_all(
        done, ("coil", "tile"), 0, 0, axis_index_groups=groups, tiled=True
    )
    sent, kept = inverse(
        spread, info, phases, shift, tables, smap, far_maps, part, chunk, slots
    )
    normal, found = sums([kept, other_core(sent)], image_p, image_r, ncoil * ntile)
    total = lax.all_to_all(found, ("coil", "tile"), 0, 0, tiled=True)
    return tuple(finish(total, image_x, image_r, image_p, normal))


def solution(mesh):
    return jax.shard_map(
        shards,
        mesh=mesh,
        in_specs=(
            P(None, "tile", "coil", None),
            P(None, "tile", "coil", None),
            P(None, "tile", "coil", None),
            P("coil", None, "tile", None, None),
            P("tile", None, None, None),
            P("tile"),
            P(None, "tile", None, None),
        ),
        out_specs=(
            P(None, "tile", "coil", None),
            P(None, "tile", "coil", None),
            P(None, "tile", "coil", None),
        ),
        check_vma=False,
    )
```

```python
import functools
import math

import jax
import jax.numpy as jnp
import ml_dtypes
import numpy as np
from jax import lax
from jax.experimental import pallas as pl
from jax.experimental.pallas import tpu as pltpu
from jax.sharding import PartitionSpec as P

LANES = 128
VMEM = 24 * 1024 * 1024


def halves(values):
    high = values.astype(jnp.bfloat16)
    low = (values - high.astype(jnp.float32)).astype(jnp.bfloat16)
    return high, low


def dot_bf16(left, right, dims):
    return lax.dot_general(left, right, (dims, ((), ())), preferred_element_type=jnp.float32)


def dot_left(table, values, dims=((1,), (0,))):
    high, low = halves(values)
    return (
        dot_bf16(table[0], high, dims)
        + dot_bf16(table[0], low, dims)
        + dot_bf16(table[1], high, dims)
    )


def dot_right(values, table, dims=((1,), (0,))):
    high, low = halves(values)
    return (
        dot_bf16(high, table[0], dims)
        + dot_bf16(low, table[0], dims)
        + dot_bf16(high, table[1], dims)
    )


def fourier_tables(length):
    cells = np.arange(length)
    angle = 2.0 * math.pi / length * (cells[:, None] * cells[None, :] % length)
    cos_t = np.cos(angle) / math.sqrt(length)
    sin_t = np.sin(angle) / math.sqrt(length)
    found = []
    for sign in (1.0, -1.0):
        whole = np.block([[cos_t, -sign * sin_t], [sign * sin_t, cos_t]])
        high = whole.astype(ml_dtypes.bfloat16)
        low = (whole - high.astype(np.float64)).astype(ml_dtypes.bfloat16)
        found += [high, low]
    return jnp.asarray(np.stack(found))


def band_of_lane(planes, chunk):
    return lax.broadcasted_iota(jnp.int32, (4, LANES), 1) // planes % chunk


def in_window(band, first, chunk):
    past = band - first
    if chunk == 4:
        here = past >= 0
        return here, jnp.logical_not(here)
    here = jnp.logical_and(past >= 0, past < 4)
    return here, past < 4 - chunk


def call(kernel, outs, scratch, operands, flops, name, hbm=(), hbm_outs=(), vmem=(), fixed=(), free=(), limit=VMEM):
    operands = list(operands)
    for listed, space in ((fixed, pltpu.HBM), (vmem, pltpu.VMEM)):
        for at in listed:
            operands[at] = pltpu.with_memory_space_constraint(operands[at], space)
    here = pl.BlockSpec(memory_space=pltpu.VMEM)
    there = pl.BlockSpec(memory_space=pltpu.HBM)
    moved = sum(math.prod(a.shape) * a.dtype.itemsize for a in operands)
    return pl.pallas_call(
        kernel,
        out_shape=[
            pltpu.HBM(shape, jnp.float32)
            if at in hbm_outs and at not in free
            else jax.ShapeDtypeStruct(shape, jnp.float32)
            for at, shape in enumerate(outs)
        ],
        in_specs=[there if at in hbm else here for at in range(len(operands))],
        out_specs=[there if at in hbm_outs else here for at in range(len(outs))],
        scratch_shapes=[
            pltpu.VMEM(shape, jnp.float32) if isinstance(shape, tuple) else shape
            for shape in scratch
        ],
        compiler_params=pltpu.CompilerParams(vmem_limit_bytes=limit),
        cost_estimate=pl.CostEstimate(flops=flops, bytes_accessed=moved, transcendentals=0),
        name=name,
    )(*operands)


def started(pairs, sems):
    copies = [
        pltpu.make_async_copy(source, to, sems.at[at]) for at, (source, to) in enumerate(pairs)
    ]
    for copy in copies:
        copy.start()
    return copies


def place_on_coil():
    coil = lax.axis_index("coil")
    return coil // 2, coil % 2


def quarters_of(chips, part):
    chip, core = place_on_coil()
    return [
        pl.multiple_of(((chip + hop) % chips * 2 + at) * part, part)
        for at in (core, 1 - core)
        for hop in range(chips)
    ]


def map_rows_kernel(s_ref, *refs, chips):
    outs, (held, sems) = refs[:-2], refs[-2:]
    chip, _ = place_on_coil()
    own = s_ref.shape[2] // chips
    for by in range(1, chips):
        rows = pl.ds(pl.multiple_of((chip + chips - by) % chips * own, own), own)
        for copy in started([(s_ref.at[:, :, rows, :], held)], sems):
            copy.wait()
        for copy in started([(held, outs[by - 1])], sems):
            copy.wait()


def map_rows(smap, chips):
    _, planes, length, _ = smap.shape
    shape = (2, planes, length // chips, length)
    return call(
        functools.partial(map_rows_kernel, chips=chips),
        [shape] * (chips - 1),
        [shape, pltpu.SemaphoreType.DMA((1,))],
        [smap],
        0,
        "map_rows",
        hbm=[0],
        fixed=[0],
        hbm_outs=range(chips - 1),
    )


def message_kernel(owner_ref, list_ref, out_ref):
    _, _, ntile, capacity = list_ref.shape
    out_ref[...] = jnp.zeros_like(out_ref)
    slots = owner_ref.shape[1]
    for to in range(ntile):
        for axis in range(3):
            out_ref[to, :, axis * capacity : (axis + 1) * capacity] = list_ref[axis, 0]
        out_ref[to, 0:1, 3 * capacity : 3 * capacity + slots] = owner_ref[...]


def message(block_owner, owner_list):
    ntile = owner_list.shape[2]
    return pl.pallas_call(
        message_kernel,
        out_shape=jax.ShapeDtypeStruct((ntile, ntile, LANES), jnp.int32),
        in_specs=[pl.BlockSpec(memory_space=pltpu.VMEM)] * 2,
        out_specs=pl.BlockSpec(memory_space=pltpu.VMEM),
        name="message",
    )(block_owner[None], owner_list)


def cut_boxes(info, grid, cos_ref, sin_ref, shift_ref, out_ref, gbuf, planes, chunk, slots):
    handlers = out_ref.shape[0]
    band = band_of_lane(planes, chunk)

    def cut(handler, carry):
        base = pl.multiple_of(handler * LANES, LANES)
        for slot in range(slots):
            block = handler * slots + slot
            here, after = in_window(band, info[1, block], chunk)
            first = grid[pl.ds(info[0, block], 4), :]
            second = grid[pl.ds(info[0, block] + LANES, 4), :]
            if chunk > 4:
                second = jnp.where(after, second, 0.0)
            gbuf[pl.ds(base + slot, 4, stride=slots), :] = jnp.where(here, first, second)
        return carry

    lax.fori_loop(0, handlers, cut, 0)
    high, low = halves(shift_ref[...])
    table = jnp.concatenate(
        [
            jnp.concatenate([high, high], axis=1),
            jnp.concatenate([low, jnp.zeros_like(low)], axis=1),
        ],
        axis=0,
    )
    for handler in range(handlers):
        rows = slice(handler * slots, (handler + 1) * slots)
        cos_b = jnp.concatenate([cos_ref[rows, :]] * 4, axis=0)
        sin_b = jnp.concatenate([sin_ref[rows, :]] * 4, axis=0)
        cells = gbuf[handler * LANES : (handler + 1) * LANES, :]
        turned = cells * cos_b + pltpu.roll(cells, LANES // 2, 1) * sin_b
        both = dot_bf16(table, jnp.concatenate(halves(turned), axis=1), ((1,), (1,)))
        out_ref[handler] = both[:32] + both[32:]


def forward_kernel(*refs, pieces, chunk, slots):
    p_hbm = refs[:pieces]
    s_hbm, table_hbm, info_hbm, cos_hbm, sin_hbm, shift_hbm, out_ref = refs[pieces : pieces + 7]
    pbuf, sbuf, tables, info, cos_ref, sin_ref, shift_ref = refs[pieces + 7 : pieces + 14]
    natural, ybuf, grid, gbuf, sems = refs[pieces + 14 :]
    _, planes, part, length = p_hbm[0].shape
    rows = length * planes
    starts = quarters_of(pieces // 2, part)
    order = [0, pieces // 2]
    order += [at for at in range(pieces) if at not in order]
    first = [(table_hbm.at[0:2], tables.at[0:2])]
    for at in order:
        first += [(p_hbm[at], pbuf.at[at]), (s_hbm.at[:, :, pl.ds(starts[at], part), :], sbuf.at[at])]
    last = [
        (table_hbm.at[2:4], tables.at[2:4]),
        (info_hbm, info),
        (cos_hbm, cos_ref),
        (sin_hbm, sin_ref),
        (shift_hbm, shift_ref),
    ]
    copies = started(first + last, sems)
    copies[0].wait()
    batch = min(planes, 256 // part)
    table = (tables[0], tables[1])
    for turn, at in enumerate(order):
        copies[1 + 2 * turn].wait()
        copies[2 + 2 * turn].wait()
        for base in range(0, planes, batch):
            bands = []
            for plane in range(base, base + batch):
                s_re = sbuf[at, 0, plane]
                s_im = sbuf[at, 1, plane]
                p_re = pbuf[at, 0, plane]
                p_im = pbuf[at, 1, plane]
                bands.append(
                    jnp.concatenate([s_re * p_re - s_im * p_im, s_re * p_im + s_im * p_re], axis=1)
                )
            done = dot_right(jnp.concatenate(bands, axis=0), table)
            for ri in range(2):
                half = done[:, ri * length : (ri + 1) * length]
                natural[ri, base : base + batch, pl.ds(starts[at], part), :] = half.reshape(
                    batch, part, length
                )
    for copy in copies[1 + 2 * pieces :]:
        copy.wait()
    table = (tables[2], tables[3])
    for pair in range(planes // 2):
        columns = [
            jnp.concatenate([natural[0, plane], natural[1, plane]], axis=0)
            for plane in (2 * pair, 2 * pair + 1)
        ]
        both = dot_left(table, jnp.concatenate(columns, axis=1))
        for inner in range(2):
            for ri in range(2):
                ybuf[pl.ds(ri * rows + 2 * pair + inner, length, stride=planes), :] = both[
                    ri * length : (ri + 1) * length, inner * LANES : (inner + 1) * LANES
                ]
    for band in range(length // chunk):
        re = ybuf[band * 64 : (band + 1) * 64, :]
        im = ybuf[rows + band * 64 : rows + (band + 1) * 64, :]
        grid[band * length : (band + 1) * length, :] = jnp.concatenate([re, im], axis=0).T
    cut_boxes(info, grid, cos_ref, sin_ref, shift_ref, out_ref, gbuf, planes, chunk, slots)


def forward(pieces, smap, tables, info, phases, shift, chunk, slots):
    _, planes, part, length = pieces[0].shape
    count = len(pieces)
    blocks = info.shape[1]
    operands = [*pieces, smap, tables, info, *phases, shift]
    return call(
        functools.partial(forward_kernel, pieces=count, chunk=chunk, slots=slots),
        [(blocks // slots, 32, LANES)],
        [
            (count, 2, planes, part, length),
            (count, 2, planes, part, length),
            pltpu.VMEM(tables.shape, tables.dtype),
            pltpu.SMEM(info.shape, info.dtype),
            (blocks, LANES),
            (blocks, LANES),
            shift.shape,
            (2, planes, length, length),
            (2 * length * planes, length),
            (length * (length // chunk + 1), LANES),
            (blocks * 4, LANES),
            pltpu.SemaphoreType.DMA((2 * count + 6,)),
        ],
        operands,
        48 * planes * length**3,
        "forward",
        hbm=range(len(operands)),
        fixed=range(count, len(operands)),
    )[0]


def regrid_kernel(parts_ref, matrix_ref, out_ref, held, done_sem):
    total = parts_ref[0]
    for at in range(1, parts_ref.shape[0]):
        total = total + parts_ref[at]
    along = lax.broadcasted_iota(jnp.int32, (8, LANES), 0) % 4
    sums = [jnp.zeros((8, LANES), jnp.float32) for _ in range(4)]
    for source in range(4):
        for d_z in range(4):
            value = total[8 * source : 8 * source + 8]
            if d_z:
                value = pltpu.roll(value, LANES - 32 * d_z, 1)
            for d_x in range(4):
                moved = value
                if d_x:
                    moved = jnp.where(
                        along + d_x < 4, pltpu.roll(value, 8 - d_x, 0), pltpu.roll(value, 4 - d_x, 0)
                    )
                for e in range(4):
                    at = 8 * (((e * 4 + source) * 4 + d_z) * 4 + d_x)
                    sums[e] = sums[e] + matrix_ref[at : at + 8] * moved
    done = jnp.concatenate(sums, axis=0)
    for at in range(held.shape[0]):
        held[at] = done
    copy = pltpu.make_async_copy(held, out_ref, done_sem)
    copy.start()
    copy.wait()


def regrid(parts, matrix, copies):
    shape = (copies,) + parts.shape[1:]
    return call(
        regrid_kernel,
        [shape],
        [shape, pltpu.SemaphoreType.DMA],
        [parts, matrix],
        10**7,
        "regrid",
        hbm_outs=[0],
        free=[0],
        vmem=[1],
    )[0]


def place_boxes(info, chip, u_ref, cos_ref, sin_ref, shift_ref, outs, gbufs, planes, chunk, slots):
    chips = len(gbufs)
    handlers = u_ref.shape[0] // chips
    high, low = halves(shift_ref[...])
    table = jnp.concatenate([high, high, low, jnp.zeros_like(low)], axis=0)
    for handler in range(handlers):
        rows = slice(handler * slots, (handler + 1) * slots)
        cos_b = jnp.concatenate([cos_ref[rows, :]] * 4, axis=0)
        sin_b = jnp.concatenate([sin_ref[rows, :]] * 4, axis=0)
        for hop in range(chips):
            u_hi, u_lo = (
                half.astype(jnp.float32) for half in halves(u_ref[(chip + hop) % chips * handlers + handler])
            )
            stack = jnp.concatenate([u_hi, u_lo, u_hi, jnp.zeros_like(u_hi)], axis=0)
            cells = dot_bf16(stack.T.astype(jnp.bfloat16), table, ((1,), (0,)))
            turned = cells * cos_b - pltpu.roll(cells, LANES // 2, 1) * sin_b
            gbufs[hop][handler * LANES : (handler + 1) * LANES, :] = turned
    band = band_of_lane(planes, chunk)

    def put(handler, carry):
        base = pl.multiple_of(handler * LANES, LANES)
        for slot in range(slots):
            block = handler * slots + slot
            here, after = in_window(band, info[1, block], chunk)
            first = pl.ds(info[0, block], 4)
            second = pl.ds(info[0, block] + LANES, 4)
            for hop in range(chips):
                out = outs[hop + slot % 2 * chips]
                cells = gbufs[hop][pl.ds(base + slot, 4, stride=slots), :]
                old_first = out[first, :]
                old_second = out[second, :]
                out[first, :] = old_first + jnp.where(here, cells, 0.0)
                out[second, :] = old_second + jnp.where(after, cells, 0.0)
        return carry

    lax.fori_loop(0, handlers, put, 0)


def inverse_kernel(*refs, part, length, chunk, slots, chips):
    u_ref, info_hbm, cos_hbm, sin_hbm, shift_hbm, table_hbm, s_hbm = refs[:7]
    far_maps = refs[7 : 6 + chips]
    outs = refs[6 + chips : 8 + chips]
    refs = refs[8 + chips :]
    grids, gbufs, refs = refs[: 2 * chips], refs[2 * chips : 3 * chips], refs[3 * chips :]
    info, cos_ref, sin_ref, shift_ref, table_ref, ybuf, images, maps, sems = refs
    planes = s_hbm.shape[1]
    rows = length * planes
    own = length // chips
    chip, core = place_on_coil()
    own_rows = pl.multiple_of(chip * own, own)
    pairs = [
        (info_hbm, info),
        (cos_hbm, cos_ref),
        (sin_hbm, sin_ref),
        (shift_hbm, shift_ref),
        (table_hbm, table_ref),
        (s_hbm.at[:, :, pl.ds(own_rows, own), :], maps.at[0]),
    ]
    pairs += [(far_map, maps.at[at]) for at, far_map in enumerate(far_maps, 1)]
    copies = started(pairs, sems)
    for grid in grids:
        grid[...] = jnp.zeros_like(grid)
    for copy in copies[:4]:
        copy.wait()
    place_boxes(info, chip, u_ref, cos_ref, sin_ref, shift_ref, grids, gbufs, planes, chunk, slots)
    for copy in copies[4:]:
        copy.wait()
    table = []
    for half in range(2):
        bands = [
            table_ref[half, pl.ds(pl.multiple_of(ri * length + own_rows, own), own), :]
            for ri in range(2)
        ]
        table.append(jnp.concatenate(bands, axis=0))
    for hop in range(chips):
        for band in range(length // chunk):
            at = slice(band * length, (band + 1) * length)
            tile = (grids[hop][at, :] + grids[hop + chips][at, :]).T
            ybuf[hop, band * 64 : (band + 1) * 64, :] = tile[:64]
            ybuf[hop, rows + band * 64 : rows + (band + 1) * 64, :] = tile[64:]
        for pair in range(planes // 2):
            columns = [
                jnp.concatenate(
                    [
                        ybuf[hop, pl.ds(ri * rows + plane, length, stride=planes), :]
                        for ri in range(2)
                    ],
                    axis=0,
                )
                for plane in (2 * pair, 2 * pair + 1)
            ]
            done = dot_left(table, jnp.concatenate(columns, axis=1))
            for inner in range(2):
                for ri in range(2):
                    images[hop, ri, 2 * pair + inner] = done[
                        ri * own : (ri + 1) * own, inner * LANES : (inner + 1) * LANES
                    ]
    table = (table_ref[2], table_ref[3])
    batch = min(planes, 256 // part)
    for at, half in enumerate((1 - core, core)):
        local = pl.ds(pl.multiple_of(half * part, part), part)
        for base in range(0, planes, batch):
            total_re, total_im = 0.0, 0.0
            for hop in range(chips):
                bands = [
                    jnp.concatenate([images[hop, ri, plane, local, :] for ri in range(2)], axis=1)
                    for plane in range(base, base + batch)
                ]
                done = dot_right(jnp.concatenate(bands, axis=0), table)
                i_re = done[:, :length].reshape(batch, part, length)
                i_im = done[:, length:].reshape(batch, part, length)
                s_re = maps[hop, 0, base : base + batch, local, :]
                s_im = maps[hop, 1, base : base + batch, local, :]
                total_re = total_re + (s_re * i_re + s_im * i_im)
                total_im = total_im + (s_re * i_im - s_im * i_re)
            outs[at][0, base : base + batch] = total_re
            outs[at][1, base : base + batch] = total_im


def inverse(spread, info, phases, shift, tables, smap, far_maps, part, chunk, slots):
    _, planes, length, _ = smap.shape
    chips = len(far_maps) + 1
    blocks = info.shape[1]
    rows = length * (length // chunk + 1)
    own = (chips, 2, planes, 2 * part, length)
    operands = [spread, info, *phases, shift, tables, smap, *far_maps]
    return call(
        functools.partial(
            inverse_kernel, part=part, length=length, chunk=chunk, slots=slots, chips=chips
        ),
        [(2, planes, part, length)] * 2,
        [(rows, LANES)] * (2 * chips)
        + [(blocks * 4, LANES)] * chips
        + [
            pltpu.SMEM(info.shape, info.dtype),
            (blocks, LANES),
            (blocks, LANES),
            shift.shape,
            pltpu.VMEM(tables.shape, tables.dtype),
            (chips, 2 * length * planes, length),
            own,
            own,
            pltpu.SemaphoreType.DMA((5 + chips,)),
        ],
        operands,
        48 * planes * length**3,
        "inverse",
        hbm=range(1, len(operands)),
        fixed=range(1, 7),
        limit=VMEM * max(1, chips // 2),
    )


def sums_kernel(*refs, terms):
    term_refs = refs[:terms]
    p_ref, r_ref, normal_ref, out_ref = refs[terms:]
    shape = p_ref.shape

    def add(plane, held):
        held = list(held)
        for ri in range(2):
            normal = term_refs[0][ri, plane]
            for term in term_refs[1:]:
                normal = normal + term[ri, plane]
            normal_ref[ri, plane] = normal
            p = p_ref[ri, plane]
            r = r_ref[ri, plane]
            for at, product in enumerate((r * r, p * normal, r * normal, normal * normal)):
                held[at] = held[at] + jnp.sum(product.reshape(-1, 8, LANES), axis=0)
        return tuple(held)

    start = tuple(jnp.zeros((8, LANES), jnp.float32) for _ in range(4))
    held = lax.fori_loop(0, shape[1], add, start, unroll=4)
    lane = lax.broadcasted_iota(jnp.int32, out_ref.shape, 1)
    found = jnp.zeros(out_ref.shape, jnp.float32)
    for at in range(4):
        found = jnp.where(lane == at, jnp.sum(held[at]), found)
    out_ref[...] = found


def sums(terms, p, r, devices):
    kernel = functools.partial(sums_kernel, terms=len(terms))
    return call(kernel, [p.shape, (devices, LANES)], [], [*terms, p, r], 10**7, "sums")


def finish_kernel(total_ref, x_ref, r_ref, p_ref, normal_ref, x_out, r_out, p_out):
    total = jnp.sum(total_ref[...], axis=0, keepdims=True)
    r_r, p_n, r_n, n_n = (total[:, at : at + 1] for at in range(4))
    alpha = r_r / p_n
    beta = (r_r + alpha * (alpha * n_n - 2.0 * r_n)) / r_r
    for plane in range(x_ref.shape[1]):
        for ri in range(2):
            p = p_ref[ri, plane]
            next_r = r_ref[ri, plane] - alpha * normal_ref[ri, plane]
            x_out[ri, plane] = x_ref[ri, plane] + alpha * p
            r_out[ri, plane] = next_r
            p_out[ri, plane] = next_r + beta * p


def finish(total, x, r, p, normal):
    return call(finish_kernel, [x.shape] * 3, [], [total, x, r, p, normal], 10**7, "finish")


def matrices_kernel(info_hbm, weights_ref, out_ref, held, info, sem, *, slots):
    base = lax.axis_index("tile") * slots
    copy = pltpu.make_async_copy(info_hbm, info, sem)
    copy.start()
    copy.wait()

    def one(block, carry):
        w_x = weights_ref[block, 0]
        w_y = weights_ref[block, 1]
        w_z = weights_ref[block, 2]
        twice = jnp.concatenate([w_x, w_x], axis=0)
        rolled = [twice] + [pltpu.roll(twice, 8 - d, 0) for d in range(1, 4)]
        low = lax.broadcasted_iota(jnp.int32, (8, LANES), 0) < 4
        along_x = [twice * jnp.where(low, rolled[d], rolled[d + 1]) for d in (0, 2)]
        right = []
        for f in range(4):
            for d_z in range(4):
                other = (f + d_z) % 4
                along_z = w_z[f : f + 1] * w_z[other : other + 1]
                right += [along * along_z for along in along_x]
        turned = pltpu.roll(
            jnp.concatenate([w_y, w_y], axis=0), info[1, base + block] % 4, 0
        )[:4]
        left = halves(jnp.concatenate([turned * turned[e : e + 1] for e in range(4)], axis=0))
        high, low = halves(jnp.concatenate(right, axis=0))
        both = dot_bf16(jnp.concatenate(left, axis=0), high, ((1,), (1,)))
        done = both[:16] + both[16:] + dot_bf16(left[0], low, ((1,), (1,)))
        for f in range(4):
            lanes = done[:, f // 2 * LANES : (f // 2 + 1) * LANES]
            if f % 2:
                lanes = pltpu.roll(lanes, LANES // 2, 1)
            held[pl.ds(f * slots + block, 16, stride=LANES), :] = lanes
        return carry

    lax.fori_loop(0, slots, one, 0, unroll=4)

    def turn(pair, carry):
        at = pl.ds(pl.multiple_of(pair * LANES, LANES), LANES)
        rows = held[at, :64].T
        for group in range(16):
            four = rows[4 * group : 4 * group + 4]
            out_ref[pl.ds(pl.multiple_of(pair * LANES + 8 * group, 8), 8), :] = jnp.concatenate(
                [four, four], axis=0
            )
        return carry

    lax.fori_loop(0, 16, turn, 0, unroll=2)


def block_matrices(info, weights):
    return call(
        functools.partial(matrices_kernel, slots=weights.shape[0]),
        [(16 * LANES, LANES)],
        [(16 * LANES, LANES), pltpu.SMEM(info.shape, info.dtype), pltpu.SemaphoreType.DMA],
        [info, weights],
        10**9,
        "matrices",
        hbm=[0],
    )[0]


def block_offsets(gathered, slots, ntile, capacity):
    owners = gathered[:, 0, 3 * capacity : 3 * capacity + slots]
    lists = gathered[:, :, : 3 * capacity].reshape(ntile, ntile, 3, capacity)
    earlier = jnp.tril(jnp.ones((slots, slots), jnp.int32), -1)
    same = (owners[:, :, None] == owners[:, None, :]).astype(jnp.int32)
    ranks = jnp.sum(same * earlier[None], axis=2)
    wanted = owners * capacity + ranks
    lists = jnp.transpose(lists, (2, 1, 0, 3)).reshape(3, ntile, 1, ntile * capacity)
    hit = wanted[:, :, None] == jnp.arange(ntile * capacity, dtype=jnp.int32)
    found = jnp.sum(jnp.where(hit[None], lists, 0), axis=3)
    return found[0], found[1] + owners * (LANES // ntile), found[2]


def shards(image_p, image_x, image_r, sensitivity, kb_weights, block_owner, owner_list):
    ntile = lax.axis_size("tile")
    ncoil = lax.axis_size("coil")
    chips = ncoil // 2
    slots = kb_weights.shape[0]
    capacity = owner_list.shape[3]
    planes, length = image_p.shape[1], image_p.shape[3]
    part = image_p.shape[2]
    chunk = LANES // (2 * planes)
    tile = lax.axis_index("tile")
    smap = sensitivity[0]
    tables = fourier_tables(length)

    def from_chip(values, by):
        pairs = [
            (a * 2 + k, (a - by) % chips * 2 + k) for a in range(chips) for k in range(2)
        ]
        return lax.ppermute(values, "coil", pairs)

    def other_core(values):
        pairs = [(a * 2 + k, a * 2 + 1 - k) for a in range(chips) for k in range(2)]
        return lax.ppermute(values, "coil", pairs)

    p_same = [image_p] + [from_chip(image_p, by) for by in range(1, chips)]
    p_other = [other_core(image_p)]
    gathered = lax.all_to_all(message(block_owner, owner_list), "tile", 0, 0, tiled=True)
    far_rows = map_rows(smap, chips)
    off_x, off_y, off_z = block_offsets(gathered, slots, ntile, capacity)
    info = jnp.stack(
        [(off_y // chunk * length + off_z).reshape(-1), (off_y % chunk).reshape(-1)]
    )
    lane = jnp.arange(LANES, dtype=jnp.int32)
    lane_ri = lane // (LANES // 2)
    lane_q = lane // planes % chunk
    lane_x = lane % planes + tile * planes
    unit = 2.0 * math.pi / length
    angle = unit * (off_x.reshape(-1, 1) * lane_x[None] % length).astype(jnp.float32)
    phases = (jnp.cos(angle), jnp.sin(angle) * jnp.where(lane_ri == 0, 1.0, -1.0)[None])
    row = jnp.arange(32, dtype=jnp.int32)[:, None]
    row_q, row_ri, row_i = row // 8, row // 4 % 2, row % 4
    angle = unit * (row_i * lane_x[None] % length).astype(jnp.float32)
    sine = jnp.where(row_ri == 0, 1.0, -1.0) * jnp.sin(angle)
    shift = jnp.where(row_ri == lane_ri[None], jnp.cos(angle), sine)
    shift = jnp.where(lane_q[None] % 4 == row_q, shift / math.sqrt(length), 0.0)
    p_far, far_rows, info, phases, shift = lax.optimization_barrier(
        (p_same[1:], far_rows, info, phases, shift)
    )
    p_other += [other_core(piece) for piece in p_far]
    far_maps = [from_chip(rows, by) for by, rows in enumerate(far_rows, 1)]
    partial = forward([image_p, *p_far, *p_other], smap, tables, info, phases, shift, chunk, slots)
    partial, weights = lax.optimization_barrier((partial, kb_weights))
    parts = lax.all_to_all(partial, "tile", 0, 0, tiled=True)
    done = regrid(parts, block_matrices(info, weights), chips * ntile)
    groups = [
        [at * ntile + t for at in range(ncoil) if at % 2 == k for t in range(ntile)]
        for k in range(2)
    ]
    spread = lax.all_to_all(
        done, ("coil", "tile"), 0, 0, axis_index_groups=groups, tiled=True
    )
    sent, kept = inverse(
        spread, info, phases, shift, tables, smap, far_maps, part, chunk, slots
    )
    normal, found = sums([kept, other_core(sent)], image_p, image_r, ncoil * ntile)
    total = lax.all_to_all(found, ("coil", "tile"), 0, 0, tiled=True)
    return tuple(finish(total, image_x, image_r, image_p, normal))


def solution(mesh):
    return jax.shard_map(
        shards,
        mesh=mesh,
        in_specs=(
            P(None, "tile", "coil", None),
            P(None, "tile", "coil", None),
            P(None, "tile", "coil", None),
            P("coil", None, "tile", None, None),
            P("tile", None, None, None),
            P("tile"),
            P(None, "tile", None, None),
        ),
        out_specs=(
            P(None, "tile", "coil", None),
            P(None, "tile", "coil", None),
            P(None, "tile", "coil", None),
        ),
        check_vma=False,
    )
```

```python
import functools
import math

import jax
import jax.numpy as jnp
import ml_dtypes
import numpy as np
from jax import lax
from jax.experimental import pallas as pl
from jax.experimental.pallas import tpu as pltpu
from jax.sharding import PartitionSpec as P

LANES = 128
VMEM = 24 * 1024 * 1024


def halves(values):
    high = values.astype(jnp.bfloat16)
    low = (values - high.astype(jnp.float32)).astype(jnp.bfloat16)
    return high, low


def dot_bf16(left, right, dims):
    return lax.dot_general(left, right, (dims, ((), ())), preferred_element_type=jnp.float32)


def dot_left(table, values, dims=((1,), (0,))):
    high, low = halves(values)
    rows = table.shape[0] // 2
    both = dot_bf16(table, high, dims)
    return both[:rows] + both[rows:] + dot_bf16(table[:rows], low, dims)


def dot_right(values, table, dims=((1,), (0,))):
    high, low = halves(values)
    rows = values.shape[0]
    both = dot_bf16(jnp.concatenate([high, low], axis=0), table[0], dims)
    return both[:rows] + both[rows:] + dot_bf16(high, table[1], dims)


def fourier_tables(length):
    cells = np.arange(length)
    angle = 2.0 * math.pi / length * (cells[:, None] * cells[None, :] % length)
    cos_t = np.cos(angle) / math.sqrt(length)
    sin_t = np.sin(angle) / math.sqrt(length)
    found = []
    for sign in (1.0, -1.0):
        whole = np.block([[cos_t, -sign * sin_t], [sign * sin_t, cos_t]])
        high = whole.astype(ml_dtypes.bfloat16)
        low = (whole - high.astype(np.float64)).astype(ml_dtypes.bfloat16)
        found += [high, low]
    return jnp.asarray(np.stack(found))


def band_of_lane(planes, chunk):
    return lax.broadcasted_iota(jnp.int32, (4, LANES), 1) // planes % chunk


def in_window(band, first, chunk):
    past = band - first
    if chunk == 4:
        here = past >= 0
        return here, jnp.logical_not(here)
    here = jnp.logical_and(past >= 0, past < 4)
    return here, past < 4 - chunk


def call(kernel, outs, scratch, operands, flops, name, hbm=(), hbm_outs=(), vmem=(), fixed=()):
    operands = list(operands)
    for listed, space in ((fixed, pltpu.HBM), (vmem, pltpu.VMEM)):
        for at in listed:
            operands[at] = pltpu.with_memory_space_constraint(operands[at], space)
    here = pl.BlockSpec(memory_space=pltpu.VMEM)
    there = pl.BlockSpec(memory_space=pltpu.HBM)
    moved = sum(math.prod(a.shape) * a.dtype.itemsize for a in operands)
    return pl.pallas_call(
        kernel,
        out_shape=[
            pltpu.HBM(shape, jnp.float32)
            if at in hbm_outs
            else jax.ShapeDtypeStruct(shape, jnp.float32)
            for at, shape in enumerate(outs)
        ],
        in_specs=[there if at in hbm else here for at in range(len(operands))],
        out_specs=[there if at in hbm_outs else here for at in range(len(outs))],
        scratch_shapes=[
            pltpu.VMEM(shape, jnp.float32) if isinstance(shape, tuple) else shape
            for shape in scratch
        ],
        compiler_params=pltpu.CompilerParams(vmem_limit_bytes=VMEM),
        cost_estimate=pl.CostEstimate(flops=flops, bytes_accessed=moved, transcendentals=0),
        name=name,
    )(*operands)


def started(pairs, sems):
    copies = [
        pltpu.make_async_copy(source, to, sems.at[at]) for at, (source, to) in enumerate(pairs)
    ]
    for copy in copies:
        copy.start()
    return copies


def place_on_coil():
    coil = lax.axis_index("coil")
    return coil // 2, coil % 2


def quarters_of(chips, part):
    chip, core = place_on_coil()
    return [
        pl.multiple_of(((chip + hop) % chips * 2 + at) * part, part)
        for at in (core, 1 - core)
        for hop in range(chips)
    ]


def map_rows_kernel(s_ref, *refs, chips):
    outs, (held, sems) = refs[:-2], refs[-2:]
    chip, _ = place_on_coil()
    own = s_ref.shape[2] // chips
    for by in range(1, chips):
        rows = pl.ds(pl.multiple_of((chip + chips - by) % chips * own, own), own)
        for copy in started([(s_ref.at[:, :, rows, :], held)], sems):
            copy.wait()
        for copy in started([(held, outs[by - 1])], sems):
            copy.wait()


def map_rows(smap, chips):
    _, planes, length, _ = smap.shape
    shape = (2, planes, length // chips, length)
    return call(
        functools.partial(map_rows_kernel, chips=chips),
        [shape] * (chips - 1),
        [shape, pltpu.SemaphoreType.DMA((1,))],
        [smap],
        0,
        "map_rows",
        hbm=[0],
        fixed=[0],
        hbm_outs=range(chips - 1),
    )


def message_kernel(owner_ref, list_ref, out_ref):
    _, _, ntile, capacity = list_ref.shape
    out_ref[...] = jnp.zeros_like(out_ref)
    slots = owner_ref.shape[1]
    for to in range(ntile):
        for axis in range(3):
            out_ref[to, :, axis * capacity : (axis + 1) * capacity] = list_ref[axis, 0]
        out_ref[to, 0:1, 3 * capacity : 3 * capacity + slots] = owner_ref[...]


def message(block_owner, owner_list):
    ntile = owner_list.shape[2]
    return pl.pallas_call(
        message_kernel,
        out_shape=jax.ShapeDtypeStruct((ntile, ntile, LANES), jnp.int32),
        in_specs=[pl.BlockSpec(memory_space=pltpu.VMEM)] * 2,
        out_specs=pl.BlockSpec(memory_space=pltpu.VMEM),
        name="message",
    )(block_owner[None], owner_list)


def cut_boxes(info, grid, cos_ref, sin_ref, shift_ref, out_ref, gbuf, planes, chunk, slots):
    handlers = out_ref.shape[0]
    band = band_of_lane(planes, chunk)

    def cut(handler, carry):
        base = pl.multiple_of(handler * LANES, LANES)
        for slot in range(slots):
            block = handler * slots + slot
            here, after = in_window(band, info[1, block], chunk)
            first = grid[pl.ds(info[0, block], 4), :]
            second = grid[pl.ds(info[0, block] + LANES, 4), :]
            if chunk > 4:
                second = jnp.where(after, second, 0.0)
            gbuf[pl.ds(base + slot, 4, stride=slots), :] = jnp.where(here, first, second)
        return carry

    lax.fori_loop(0, handlers, cut, 0)
    high, low = halves(shift_ref[...])
    table = jnp.concatenate(
        [
            jnp.concatenate([high, high], axis=1),
            jnp.concatenate([low, jnp.zeros_like(low)], axis=1),
        ],
        axis=0,
    )
    for handler in range(handlers):
        rows = slice(handler * slots, (handler + 1) * slots)
        cos_b = jnp.concatenate([cos_ref[rows, :]] * 4, axis=0)
        sin_b = jnp.concatenate([sin_ref[rows, :]] * 4, axis=0)
        cells = gbuf[handler * LANES : (handler + 1) * LANES, :]
        turned = cells * cos_b + pltpu.roll(cells, LANES // 2, 1) * sin_b
        both = dot_bf16(table, jnp.concatenate(halves(turned), axis=1), ((1,), (1,)))
        out_ref[handler] = both[:32] + both[32:]


def forward_kernel(*refs, pieces, chunk, slots):
    p_refs = refs[:pieces]
    s_hbm, table_hbm, info_hbm, cos_hbm, sin_hbm, shift_hbm, out_ref = refs[pieces : pieces + 7]
    sbuf, tables, info, cos_ref, sin_ref, shift_ref = refs[pieces + 7 : pieces + 13]
    natural, ybuf, grid, gbuf, sems = refs[pieces + 13 :]
    _, planes, part, length = p_refs[0].shape
    rows = length * planes
    starts = quarters_of(pieces // 2, part)
    order = [0, pieces // 2]
    order += [at for at in range(pieces) if at not in order]
    pairs = [(table_hbm.at[0:2], tables.at[0:2])]
    pairs += [(s_hbm.at[:, :, pl.ds(starts[at], part), :], sbuf.at[at]) for at in order]
    pairs += [
        (table_hbm.at[2:4], tables.at[2:4]),
        (info_hbm, info),
        (cos_hbm, cos_ref),
        (sin_hbm, sin_ref),
        (shift_hbm, shift_ref),
    ]
    copies = started(pairs, sems)
    copies[0].wait()
    table = (tables[0], tables[1])
    for turn, at in enumerate(order):
        copies[1 + turn].wait()
        bands = []
        for plane in range(planes):
            s_re = sbuf[at, 0, plane]
            s_im = sbuf[at, 1, plane]
            p_re = p_refs[at][0, plane]
            p_im = p_refs[at][1, plane]
            bands.append(
                jnp.concatenate([s_re * p_re - s_im * p_im, s_re * p_im + s_im * p_re], axis=1)
            )
        done = dot_right(jnp.concatenate(bands, axis=0), table)
        for ri in range(2):
            half = done[:, ri * length : (ri + 1) * length]
            natural[ri, :, pl.ds(starts[at], part), :] = half.reshape(planes, part, length)
    for copy in copies[1 + pieces :]:
        copy.wait()
    table = jnp.concatenate([tables[2], tables[3]], axis=0)
    for pair in range(planes // 2):
        columns = [
            jnp.concatenate([natural[0, plane], natural[1, plane]], axis=0)
            for plane in (2 * pair, 2 * pair + 1)
        ]
        both = dot_left(table, jnp.concatenate(columns, axis=1))
        for inner in range(2):
            for ri in range(2):
                ybuf[pl.ds(ri * rows + 2 * pair + inner, length, stride=planes), :] = both[
                    ri * length : (ri + 1) * length, inner * LANES : (inner + 1) * LANES
                ]
    for band in range(length // chunk):
        re = ybuf[band * 64 : (band + 1) * 64, :]
        im = ybuf[rows + band * 64 : rows + (band + 1) * 64, :]
        grid[band * length : (band + 1) * length, :] = jnp.concatenate([re, im], axis=0).T
    cut_boxes(info, grid, cos_ref, sin_ref, shift_ref, out_ref, gbuf, planes, chunk, slots)


def forward(pieces, smap, tables, info, phases, shift, chunk, slots):
    _, planes, part, length = pieces[0].shape
    count = len(pieces)
    blocks = info.shape[1]
    operands = [*pieces, smap, tables, info, *phases, shift]
    return call(
        functools.partial(forward_kernel, pieces=count, chunk=chunk, slots=slots),
        [(blocks // slots, 32, LANES)],
        [
            (count, 2, planes, part, length),
            pltpu.VMEM(tables.shape, tables.dtype),
            pltpu.SMEM(info.shape, info.dtype),
            (blocks, LANES),
            (blocks, LANES),
            shift.shape,
            (2, planes, length, length),
            (2 * length * planes, length),
            (length * (length // chunk + 1), LANES),
            (blocks * 4, LANES),
            pltpu.SemaphoreType.DMA((count + 6,)),
        ],
        operands,
        48 * planes * length**3,
        "forward",
        hbm=range(count, len(operands)),
        fixed=range(count, len(operands)),
    )[0]


def regrid_kernel(parts_ref, matrix_ref, out_ref, held, done_sem):
    total = parts_ref[0]
    for at in range(1, parts_ref.shape[0]):
        total = total + parts_ref[at]
    along = lax.broadcasted_iota(jnp.int32, (8, LANES), 0) % 4
    sums = [jnp.zeros((8, LANES), jnp.float32) for _ in range(4)]
    for source in range(4):
        for d_z in range(4):
            value = total[8 * source : 8 * source + 8]
            if d_z:
                value = pltpu.roll(value, LANES - 32 * d_z, 1)
            for d_x in range(4):
                moved = value
                if d_x:
                    moved = jnp.where(
                        along + d_x < 4, pltpu.roll(value, 8 - d_x, 0), pltpu.roll(value, 4 - d_x, 0)
                    )
                for e in range(4):
                    at = 8 * (((e * 4 + source) * 4 + d_z) * 4 + d_x)
                    sums[e] = sums[e] + matrix_ref[at : at + 8] * moved
    done = jnp.concatenate(sums, axis=0)
    for at in range(held.shape[0]):
        held[at] = done
    copy = pltpu.make_async_copy(held, out_ref, done_sem)
    copy.start()
    copy.wait()


def regrid(parts, matrix, copies):
    shape = (copies,) + parts.shape[1:]
    return call(
        regrid_kernel,
        [shape],
        [shape, pltpu.SemaphoreType.DMA],
        [parts, matrix],
        10**7,
        "regrid",
        hbm_outs=[0],
        vmem=[1],
    )[0]


def place_boxes(info, chip, u_ref, cos_ref, sin_ref, shift_ref, outs, gbufs, planes, chunk, slots):
    chips = len(outs)
    handlers = u_ref.shape[0] // chips
    high, low = halves(shift_ref[...])
    table = jnp.concatenate([high, high, low, jnp.zeros_like(low)], axis=0)
    for hop in range(chips):
        stacks = []
        for handler in range(handlers):
            u_hi, u_lo = (
                half.astype(jnp.float32)
                for half in halves(u_ref[(chip + hop) % chips * handlers + handler])
            )
            stack = jnp.concatenate([u_hi, u_lo, u_hi, jnp.zeros_like(u_hi)], axis=0)
            stacks.append(stack.T.astype(jnp.bfloat16))
        cells = dot_bf16(jnp.concatenate(stacks, axis=0), table, ((1,), (0,)))
        for handler in range(handlers):
            rows = slice(handler * slots, (handler + 1) * slots)
            cos_b = jnp.concatenate([cos_ref[rows, :]] * 4, axis=0)
            sin_b = jnp.concatenate([sin_ref[rows, :]] * 4, axis=0)
            own = cells[handler * LANES : (handler + 1) * LANES]
            gbufs[hop][handler * LANES : (handler + 1) * LANES, :] = (
                own * cos_b - pltpu.roll(own, LANES // 2, 1) * sin_b
            )
    band = band_of_lane(planes, chunk)

    def put(handler, carry):
        base = pl.multiple_of(handler * LANES, LANES)
        for slot in range(slots):
            block = handler * slots + slot
            here, after = in_window(band, info[1, block], chunk)
            first = pl.ds(info[0, block], 4)
            second = pl.ds(info[0, block] + LANES, 4)
            for hop in range(chips):
                cells = gbufs[hop][pl.ds(base + slot, 4, stride=slots), :]
                old_first = outs[hop][first, :]
                old_second = outs[hop][second, :]
                outs[hop][first, :] = old_first + jnp.where(here, cells, 0.0)
                outs[hop][second, :] = old_second + jnp.where(after, cells, 0.0)
        return carry

    lax.fori_loop(0, handlers, put, 0)


def inverse_kernel(*refs, part, length, chunk, slots, chips):
    u_ref, info_hbm, cos_hbm, sin_hbm, shift_hbm, table_hbm, s_hbm = refs[:7]
    far_maps = refs[7 : 6 + chips]
    outs = refs[6 + chips : 8 + chips]
    refs = refs[8 + chips :]
    grids, gbufs, refs = refs[:chips], refs[chips : 2 * chips], refs[2 * chips :]
    info, cos_ref, sin_ref, shift_ref, table_ref, ybuf, images, maps, sems = refs
    planes = s_hbm.shape[1]
    rows = length * planes
    own = length // chips
    chip, core = place_on_coil()
    own_rows = pl.multiple_of(chip * own, own)
    pairs = [
        (info_hbm, info),
        (cos_hbm, cos_ref),
        (sin_hbm, sin_ref),
        (shift_hbm, shift_ref),
        (table_hbm, table_ref),
        (s_hbm.at[:, :, pl.ds(own_rows, own), :], maps.at[0]),
    ]
    pairs += [(far_map, maps.at[at]) for at, far_map in enumerate(far_maps, 1)]
    copies = started(pairs, sems)
    for grid in grids:
        grid[...] = jnp.zeros_like(grid)
    for copy in copies[:4]:
        copy.wait()
    place_boxes(info, chip, u_ref, cos_ref, sin_ref, shift_ref, grids, gbufs, planes, chunk, slots)
    for copy in copies[4:]:
        copy.wait()
    table = jnp.concatenate(
        [
            table_ref[half, pl.ds(pl.multiple_of(ri * length + own_rows, own), own), :]
            for half in range(2)
            for ri in range(2)
        ],
        axis=0,
    )
    for hop in range(chips):
        for band in range(length // chunk):
            tile = grids[hop][band * length : (band + 1) * length, :].T
            ybuf[hop, band * 64 : (band + 1) * 64, :] = tile[:64]
            ybuf[hop, rows + band * 64 : rows + (band + 1) * 64, :] = tile[64:]
        for pair in range(planes // 2):
            columns = [
                jnp.concatenate(
                    [
                        ybuf[hop, pl.ds(ri * rows + plane, length, stride=planes), :]
                        for ri in range(2)
                    ],
                    axis=0,
                )
                for plane in (2 * pair, 2 * pair + 1)
            ]
            done = dot_left(table, jnp.concatenate(columns, axis=1))
            for inner in range(2):
                for ri in range(2):
                    images[hop, ri, 2 * pair + inner] = done[
                        ri * own : (ri + 1) * own, inner * LANES : (inner + 1) * LANES
                    ]
    table = (table_ref[2], table_ref[3])
    for at, half in enumerate((1 - core, core)):
        local = pl.ds(pl.multiple_of(half * part, part), part)
        total_re, total_im = 0.0, 0.0
        for hop in range(chips):
            bands = [
                jnp.concatenate([images[hop, ri, plane, local, :] for ri in range(2)], axis=1)
                for plane in range(planes)
            ]
            done = dot_right(jnp.concatenate(bands, axis=0), table)
            i_re = done[:, :length].reshape(planes, part, length)
            i_im = done[:, length:].reshape(planes, part, length)
            s_re = maps[hop, 0, :, local, :]
            s_im = maps[hop, 1, :, local, :]
            total_re = total_re + (s_re * i_re + s_im * i_im)
            total_im = total_im + (s_re * i_im - s_im * i_re)
        outs[at][0] = total_re
        outs[at][1] = total_im


def inverse(spread, info, phases, shift, tables, smap, far_maps, part, chunk, slots):
    _, planes, length, _ = smap.shape
    chips = len(far_maps) + 1
    blocks = info.shape[1]
    rows = length * (length // chunk + 1)
    own = (chips, 2, planes, 2 * part, length)
    operands = [spread, info, *phases, shift, tables, smap, *far_maps]
    return call(
        functools.partial(
            inverse_kernel, part=part, length=length, chunk=chunk, slots=slots, chips=chips
        ),
        [(2, planes, part, length)] * 2,
        [(rows, LANES)] * chips
        + [(blocks * 4, LANES)] * chips
        + [
            pltpu.SMEM(info.shape, info.dtype),
            (blocks, LANES),
            (blocks, LANES),
            shift.shape,
            pltpu.VMEM(tables.shape, tables.dtype),
            (chips, 2 * length * planes, length),
            own,
            own,
            pltpu.SemaphoreType.DMA((5 + chips,)),
        ],
        operands,
        48 * planes * length**3,
        "inverse",
        hbm=range(1, len(operands)),
        fixed=range(1, 7),
    )


def sums_kernel(*refs, terms):
    term_refs = refs[:terms]
    p_ref, r_ref, normal_ref, out_ref = refs[terms:]
    shape = p_ref.shape

    def add(plane, held):
        held = list(held)
        for ri in range(2):
            normal = term_refs[0][ri, plane]
            for term in term_refs[1:]:
                normal = normal + term[ri, plane]
            normal_ref[ri, plane] = normal
            p = p_ref[ri, plane]
            r = r_ref[ri, plane]
            for at, product in enumerate((r * r, p * normal, r * normal, normal * normal)):
                held[at] = held[at] + jnp.sum(product.reshape(-1, 8, LANES), axis=0)
        return tuple(held)

    start = tuple(jnp.zeros((8, LANES), jnp.float32) for _ in range(4))
    held = lax.fori_loop(0, shape[1], add, start, unroll=4)
    lane = lax.broadcasted_iota(jnp.int32, out_ref.shape, 1)
    found = jnp.zeros(out_ref.shape, jnp.float32)
    for at in range(4):
        found = jnp.where(lane == at, jnp.sum(held[at]), found)
    out_ref[...] = found


def sums(terms, p, r, devices):
    kernel = functools.partial(sums_kernel, terms=len(terms))
    return call(kernel, [p.shape, (devices, LANES)], [], [*terms, p, r], 10**7, "sums")


def finish_kernel(total_ref, x_ref, r_ref, p_ref, normal_ref, x_out, r_out, p_out):
    total = jnp.sum(total_ref[...], axis=0, keepdims=True)
    r_r, p_n, r_n, n_n = (total[:, at : at + 1] for at in range(4))
    alpha = r_r / p_n
    beta = (r_r + alpha * (alpha * n_n - 2.0 * r_n)) / r_r
    for plane in range(x_ref.shape[1]):
        for ri in range(2):
            p = p_ref[ri, plane]
            next_r = r_ref[ri, plane] - alpha * normal_ref[ri, plane]
            x_out[ri, plane] = x_ref[ri, plane] + alpha * p
            r_out[ri, plane] = next_r
            p_out[ri, plane] = next_r + beta * p


def finish(total, x, r, p, normal):
    return call(finish_kernel, [x.shape] * 3, [], [total, x, r, p, normal], 10**7, "finish")


def matrices_kernel(info_hbm, weights_ref, out_ref, held, info, sem, *, slots):
    base = lax.axis_index("tile") * slots
    copy = pltpu.make_async_copy(info_hbm, info, sem)
    copy.start()
    copy.wait()

    def one(block, carry):
        w_x = weights_ref[block, 0]
        w_y = weights_ref[block, 1]
        w_z = weights_ref[block, 2]
        twice = jnp.concatenate([w_x, w_x], axis=0)
        rolled = [twice] + [pltpu.roll(twice, 8 - d, 0) for d in range(1, 4)]
        low = lax.broadcasted_iota(jnp.int32, (8, LANES), 0) < 4
        along_x = [twice * jnp.where(low, rolled[d], rolled[d + 1]) for d in (0, 2)]
        right = []
        for f in range(4):
            for d_z in range(4):
                other = (f + d_z) % 4
                along_z = w_z[f : f + 1] * w_z[other : other + 1]
                right += [along * along_z for along in along_x]
        turned = pltpu.roll(
            jnp.concatenate([w_y, w_y], axis=0), info[1, base + block] % 4, 0
        )[:4]
        left = halves(jnp.concatenate([turned * turned[e : e + 1] for e in range(4)], axis=0))
        high, low = halves(jnp.concatenate(right, axis=0))
        both = dot_bf16(jnp.concatenate(left, axis=0), high, ((1,), (1,)))
        done = both[:16] + both[16:] + dot_bf16(left[0], low, ((1,), (1,)))
        for f in range(4):
            lanes = done[:, f // 2 * LANES : (f // 2 + 1) * LANES]
            if f % 2:
                lanes = pltpu.roll(lanes, LANES // 2, 1)
            held[pl.ds(f * slots + block, 16, stride=LANES), :] = lanes
        return carry

    lax.fori_loop(0, slots, one, 0, unroll=4)

    def turn(pair, carry):
        at = pl.ds(pl.multiple_of(pair * LANES, LANES), LANES)
        rows = held[at, :64].T
        for group in range(16):
            four = rows[4 * group : 4 * group + 4]
            out_ref[pl.ds(pl.multiple_of(pair * LANES + 8 * group, 8), 8), :] = jnp.concatenate(
                [four, four], axis=0
            )
        return carry

    lax.fori_loop(0, 16, turn, 0, unroll=2)


def block_matrices(info, weights):
    return call(
        functools.partial(matrices_kernel, slots=weights.shape[0]),
        [(16 * LANES, LANES)],
        [(16 * LANES, LANES), pltpu.SMEM(info.shape, info.dtype), pltpu.SemaphoreType.DMA],
        [info, weights],
        10**9,
        "matrices",
        hbm=[0],
    )[0]


def block_offsets(gathered, slots, ntile, capacity):
    owners = gathered[:, 0, 3 * capacity : 3 * capacity + slots]
    lists = gathered[:, :, : 3 * capacity].reshape(ntile, ntile, 3, capacity)
    earlier = jnp.tril(jnp.ones((slots, slots), jnp.int32), -1)
    same = (owners[:, :, None] == owners[:, None, :]).astype(jnp.int32)
    ranks = jnp.sum(same * earlier[None], axis=2)
    wanted = owners * capacity + ranks
    lists = jnp.transpose(lists, (2, 1, 0, 3)).reshape(3, ntile, 1, ntile * capacity)
    hit = wanted[:, :, None] == jnp.arange(ntile * capacity, dtype=jnp.int32)
    found = jnp.sum(jnp.where(hit[None], lists, 0), axis=3)
    return found[0], found[1] + owners * (LANES // ntile), found[2]


def shards(image_p, image_x, image_r, sensitivity, kb_weights, block_owner, owner_list):
    ntile = lax.axis_size("tile")
    ncoil = lax.axis_size("coil")
    chips = ncoil // 2
    slots = kb_weights.shape[0]
    capacity = owner_list.shape[3]
    planes, length = image_p.shape[1], image_p.shape[3]
    part = image_p.shape[2]
    chunk = LANES // (2 * planes)
    tile = lax.axis_index("tile")
    smap = sensitivity[0]
    tables = fourier_tables(length)

    def from_chip(values, by):
        pairs = [
            (a * 2 + k, (a - by) % chips * 2 + k) for a in range(chips) for k in range(2)
        ]
        return lax.ppermute(values, "coil", pairs)

    def other_core(values):
        pairs = [(a * 2 + k, a * 2 + 1 - k) for a in range(chips) for k in range(2)]
        return lax.ppermute(values, "coil", pairs)

    p_same = [image_p] + [from_chip(image_p, by) for by in range(1, chips)]
    p_other = [other_core(image_p)]
    gathered = lax.all_to_all(message(block_owner, owner_list), "tile", 0, 0, tiled=True)
    far_rows = map_rows(smap, chips)
    off_x, off_y, off_z = block_offsets(gathered, slots, ntile, capacity)
    info = jnp.stack(
        [(off_y // chunk * length + off_z).reshape(-1), (off_y % chunk).reshape(-1)]
    )
    lane = jnp.arange(LANES, dtype=jnp.int32)
    lane_ri = lane // (LANES // 2)
    lane_q = lane // planes % chunk
    lane_x = lane % planes + tile * planes
    unit = 2.0 * math.pi / length
    angle = unit * (off_x.reshape(-1, 1) * lane_x[None] % length).astype(jnp.float32)
    phases = (jnp.cos(angle), jnp.sin(angle) * jnp.where(lane_ri == 0, 1.0, -1.0)[None])
    row = jnp.arange(32, dtype=jnp.int32)[:, None]
    row_q, row_ri, row_i = row // 8, row // 4 % 2, row % 4
    angle = unit * (row_i * lane_x[None] % length).astype(jnp.float32)
    sine = jnp.where(row_ri == 0, 1.0, -1.0) * jnp.sin(angle)
    shift = jnp.where(row_ri == lane_ri[None], jnp.cos(angle), sine)
    shift = jnp.where(lane_q[None] % 4 == row_q, shift / math.sqrt(length), 0.0)
    p_far, far_rows, info, phases, shift = lax.optimization_barrier(
        (p_same[1:], far_rows, info, phases, shift)
    )
    p_other += [other_core(piece) for piece in p_far]
    far_maps = [from_chip(rows, by) for by, rows in enumerate(far_rows, 1)]
    partial = forward([image_p, *p_far, *p_other], smap, tables, info, phases, shift, chunk, slots)
    partial, weights = lax.optimization_barrier((partial, kb_weights))
    parts = lax.all_to_all(partial, "tile", 0, 0, tiled=True)
    done = regrid(parts, block_matrices(info, weights), chips * ntile)
    groups = [
        [at * ntile + t for at in range(ncoil) if at % 2 == k for t in range(ntile)]
        for k in range(2)
    ]
    spread = lax.all_to_all(
        done, ("coil", "tile"), 0, 0, axis_index_groups=groups, tiled=True
    )
    sent, kept = inverse(
        spread, info, phases, shift, tables, smap, far_maps, part, chunk, slots
    )
    normal, found = sums([kept, other_core(sent)], image_p, image_r, ncoil * ntile)
    total = lax.all_to_all(found, ("coil", "tile"), 0, 0, tiled=True)
    return tuple(finish(total, image_x, image_r, image_p, normal))


def solution(mesh):
    return jax.shard_map(
        shards,
        mesh=mesh,
        in_specs=(
            P(None, "tile", "coil", None),
            P(None, "tile", "coil", None),
            P(None, "tile", "coil", None),
            P("coil", None, "tile", None, None),
            P("tile", None, None, None),
            P("tile"),
            P(None, "tile", None, None),
        ),
        out_specs=(
            P(None, "tile", "coil", None),
            P(None, "tile", "coil", None),
            P(None, "tile", "coil", None),
        ),
        check_vma=False,
    )
```

```python
import functools
import math

import jax
import jax.numpy as jnp
import ml_dtypes
import numpy as np
from jax import lax
from jax.experimental import pallas as pl
from jax.experimental.pallas import tpu as pltpu
from jax.sharding import PartitionSpec as P

LANES = 128
VMEM = 24 * 1024 * 1024


def halves(values):
    high = values.astype(jnp.bfloat16)
    low = (values - high.astype(jnp.float32)).astype(jnp.bfloat16)
    return high, low


def dot_bf16(left, right, dims):
    return lax.dot_general(left, right, (dims, ((), ())), preferred_element_type=jnp.float32)


def dot_left(table, values, dims=((1,), (0,))):
    high, low = halves(values)
    return (
        dot_bf16(table[0], high, dims)
        + dot_bf16(table[0], low, dims)
        + dot_bf16(table[1], high, dims)
    )


def dot_right(values, table, dims=((1,), (0,))):
    high, low = halves(values)
    return (
        dot_bf16(high, table[0], dims)
        + dot_bf16(low, table[0], dims)
        + dot_bf16(high, table[1], dims)
    )


def fourier_tables(length):
    cells = np.arange(length)
    angle = 2.0 * math.pi / length * (cells[:, None] * cells[None, :] % length)
    cos_t = np.cos(angle) / math.sqrt(length)
    sin_t = np.sin(angle) / math.sqrt(length)
    found = []
    for sign in (1.0, -1.0):
        whole = np.block([[cos_t, -sign * sin_t], [sign * sin_t, cos_t]])
        high = whole.astype(ml_dtypes.bfloat16)
        low = (whole - high.astype(np.float64)).astype(ml_dtypes.bfloat16)
        found += [high, low]
    return jnp.asarray(np.stack(found))


def shift_tables(length, planes, chunk):
    row = np.arange(32)[:, None]
    lane = np.arange(LANES)[None, :]
    row_q, row_ri, row_i = row // 8, row // 4 % 2, row % 4
    lane_ri, lane_q, lane_x = lane // (LANES // 2), lane // planes % chunk, lane % planes
    found = []
    for tile in range(length // planes):
        angle = 2.0 * math.pi / length * (row_i * (lane_x + tile * planes) % length)
        sine = np.where(row_ri == 0, 1.0, -1.0) * np.sin(angle)
        table = np.where(row_ri == lane_ri, np.cos(angle), sine) / math.sqrt(length)
        found.append(np.where(lane_q % 4 == row_q, table, 0.0))
    return jnp.asarray(np.stack(found), jnp.float32)


def band_of_lane(planes, chunk):
    return lax.broadcasted_iota(jnp.int32, (4, LANES), 1) // planes % chunk


def in_window(band, first, chunk):
    past = band - first
    if chunk == 4:
        here = past >= 0
        return here, jnp.logical_not(here)
    here = jnp.logical_and(past >= 0, past < 4)
    return here, past < 4 - chunk


def call(kernel, outs, scratch, operands, flops, name, hbm=(), hbm_outs=(), vmem=(), fixed=(), spaces=()):
    spaces = dict(spaces)
    operands = list(operands)
    for listed, space in ((fixed, pltpu.HBM), (vmem, pltpu.VMEM)):
        for at in listed:
            operands[at] = pltpu.with_memory_space_constraint(operands[at], space)
    here = pl.BlockSpec(memory_space=pltpu.VMEM)
    there = pl.BlockSpec(memory_space=pltpu.HBM)
    moved = sum(math.prod(a.shape) * a.dtype.itemsize for a in operands)
    return pl.pallas_call(
        kernel,
        out_shape=[
            spaces[at](shape, jnp.float32)
            if at in spaces
            else jax.ShapeDtypeStruct(shape, jnp.float32)
            for at, shape in enumerate(outs)
        ],
        in_specs=[there if at in hbm else here for at in range(len(operands))],
        out_specs=[there if at in hbm_outs else here for at in range(len(outs))],
        scratch_shapes=[
            pltpu.VMEM(shape, jnp.float32) if isinstance(shape, tuple) else shape
            for shape in scratch
        ],
        compiler_params=pltpu.CompilerParams(vmem_limit_bytes=VMEM),
        cost_estimate=pl.CostEstimate(flops=flops, bytes_accessed=moved, transcendentals=0),
        name=name,
    )(*operands)


def started(pairs, sems):
    copies = [
        pltpu.make_async_copy(source, to, sems.at[at]) for at, (source, to) in enumerate(pairs)
    ]
    for copy in copies:
        copy.start()
    return copies


def place_on_coil():
    coil = lax.axis_index("coil")
    return coil // 2, coil % 2


def quarters_of(chips, part):
    chip, core = place_on_coil()
    return [
        pl.multiple_of(((chip + hop) % chips * 2 + at) * part, part)
        for at in (core, 1 - core)
        for hop in range(chips)
    ]


def map_rows_kernel(s_ref, *refs, chips):
    outs, (held, sems) = refs[:-2], refs[-2:]
    chip, _ = place_on_coil()
    own = s_ref.shape[2] // chips
    for by in range(1, chips):
        rows = pl.ds(pl.multiple_of((chip + chips - by) % chips * own, own), own)
        for copy in started([(s_ref.at[:, :, rows, :], held)], sems):
            copy.wait()
        for copy in started([(held, outs[by - 1])], sems):
            copy.wait()


def map_rows(smap, chips):
    _, planes, length, _ = smap.shape
    shape = (2, planes, length // chips, length)
    return call(
        functools.partial(map_rows_kernel, chips=chips),
        [shape] * (chips - 1),
        [shape, pltpu.SemaphoreType.DMA((1,))],
        [smap],
        0,
        "map_rows",
        hbm=[0],
        fixed=[0],
        hbm_outs=range(chips - 1),
    )


def message_kernel(owner_ref, list_ref, out_ref):
    _, _, ntile, capacity = list_ref.shape
    out_ref[...] = jnp.zeros_like(out_ref)
    slots = owner_ref.shape[1]
    for to in range(ntile):
        for axis in range(3):
            out_ref[to, :, axis * capacity : (axis + 1) * capacity] = list_ref[axis, 0]
        out_ref[to, 0:1, 3 * capacity : 3 * capacity + slots] = owner_ref[...]


def message(block_owner, owner_list):
    ntile = owner_list.shape[2]
    return pl.pallas_call(
        message_kernel,
        out_shape=jax.ShapeDtypeStruct((ntile, ntile, LANES), jnp.int32),
        in_specs=[pl.BlockSpec(memory_space=pltpu.VMEM)] * 2,
        out_specs=pl.BlockSpec(memory_space=pltpu.VMEM),
        name="message",
    )(block_owner[None], owner_list)


def cut_boxes(info, grid, cos_ref, sin_ref, shift_ref, out_ref, gbuf, planes, chunk, slots):
    handlers = out_ref.shape[0]
    band = band_of_lane(planes, chunk)

    def cut(handler, carry):
        base = pl.multiple_of(handler * LANES, LANES)
        for slot in range(slots):
            block = handler * slots + slot
            here, after = in_window(band, info[1, block], chunk)
            first = grid[pl.ds(info[0, block], 4), :]
            second = grid[pl.ds(info[0, block] + LANES, 4), :]
            if chunk > 4:
                second = jnp.where(after, second, 0.0)
            gbuf[pl.ds(base + slot, 4, stride=slots), :] = jnp.where(here, first, second)
        return carry

    lax.fori_loop(0, handlers, cut, 0)
    high, low = halves(shift_ref[...])
    table = jnp.concatenate(
        [
            jnp.concatenate([high, high], axis=1),
            jnp.concatenate([low, jnp.zeros_like(low)], axis=1),
        ],
        axis=0,
    )
    for handler in range(handlers):
        rows = slice(handler * slots, (handler + 1) * slots)
        cos_b = jnp.concatenate([cos_ref[rows, :]] * 4, axis=0)
        sin_b = jnp.concatenate([sin_ref[rows, :]] * 4, axis=0)
        cells = gbuf[handler * LANES : (handler + 1) * LANES, :]
        turned = cells * cos_b + pltpu.roll(cells, LANES // 2, 1) * sin_b
        both = dot_bf16(table, jnp.concatenate(halves(turned), axis=1), ((1,), (1,)))
        out_ref[handler] = both[:32] + both[32:]


def forward_kernel(*refs, pieces, chunk, slots):
    p_hbm = refs[:pieces]
    s_hbm, table_hbm, info_hbm, cos_hbm, sin_hbm, shift_hbm, out_ref = refs[pieces : pieces + 7]
    pbuf, sbuf, tables, info, cos_ref, sin_ref, shift_ref = refs[pieces + 7 : pieces + 14]
    natural, ybuf, grid, gbuf, sems = refs[pieces + 14 :]
    _, planes, part, length = p_hbm[0].shape
    rows = length * planes
    starts = quarters_of(pieces // 2, part)
    order = [0, pieces // 2]
    order += [at for at in range(pieces) if at not in order]
    first = [(table_hbm.at[0:2], tables.at[0:2])]
    for at in order:
        first += [(p_hbm[at], pbuf.at[at]), (s_hbm.at[:, :, pl.ds(starts[at], part), :], sbuf.at[at])]
    last = [
        (table_hbm.at[2:4], tables.at[2:4]),
        (info_hbm, info),
        (cos_hbm, cos_ref),
        (sin_hbm, sin_ref),
        (shift_hbm.at[lax.axis_index("tile")], shift_ref),
    ]
    copies = started(first + last, sems)
    copies[0].wait()
    batch = min(planes, 256 // part)
    table = (tables[0], tables[1])
    for turn, at in enumerate(order):
        copies[1 + 2 * turn].wait()
        copies[2 + 2 * turn].wait()
        for base in range(0, planes, batch):
            bands = []
            for plane in range(base, base + batch):
                s_re = sbuf[at, 0, plane]
                s_im = sbuf[at, 1, plane]
                p_re = pbuf[at, 0, plane]
                p_im = pbuf[at, 1, plane]
                bands.append(
                    jnp.concatenate([s_re * p_re - s_im * p_im, s_re * p_im + s_im * p_re], axis=1)
                )
            done = dot_right(jnp.concatenate(bands, axis=0), table)
            for ri in range(2):
                half = done[:, ri * length : (ri + 1) * length]
                natural[ri, base : base + batch, pl.ds(starts[at], part), :] = half.reshape(
                    batch, part, length
                )
    for copy in copies[1 + 2 * pieces :]:
        copy.wait()
    table = (tables[2], tables[3])
    for pair in range(planes // 2):
        columns = [
            jnp.concatenate([natural[0, plane], natural[1, plane]], axis=0)
            for plane in (2 * pair, 2 * pair + 1)
        ]
        both = dot_left(table, jnp.concatenate(columns, axis=1))
        for inner in range(2):
            for ri in range(2):
                ybuf[pl.ds(ri * rows + 2 * pair + inner, length, stride=planes), :] = both[
                    ri * length : (ri + 1) * length, inner * LANES : (inner + 1) * LANES
                ]
    for band in range(length // chunk):
        re = ybuf[band * 64 : (band + 1) * 64, :]
        im = ybuf[rows + band * 64 : rows + (band + 1) * 64, :]
        grid[band * length : (band + 1) * length, :] = jnp.concatenate([re, im], axis=0).T
    cut_boxes(info, grid, cos_ref, sin_ref, shift_ref, out_ref, gbuf, planes, chunk, slots)


def forward(pieces, smap, tables, info, phases, shift, chunk, slots):
    _, planes, part, length = pieces[0].shape
    count = len(pieces)
    blocks = info.shape[1]
    operands = [*pieces, smap, tables, info, *phases, shift]
    return call(
        functools.partial(forward_kernel, pieces=count, chunk=chunk, slots=slots),
        [(blocks // slots, 32, LANES)],
        [
            (count, 2, planes, part, length),
            (count, 2, planes, part, length),
            pltpu.VMEM(tables.shape, tables.dtype),
            pltpu.SMEM(info.shape, info.dtype),
            (blocks, LANES),
            (blocks, LANES),
            shift.shape[1:],
            (2, planes, length, length),
            (2 * length * planes, length),
            (length * (length // chunk + 1), LANES),
            (blocks * 4, LANES),
            pltpu.SemaphoreType.DMA((2 * count + 6,)),
        ],
        operands,
        48 * planes * length**3,
        "forward",
        hbm=range(len(operands)),
        fixed=range(count, len(operands)),
    )[0]


def regrid_kernel(parts_ref, matrix_ref, out_ref):
    total = parts_ref[0]
    for at in range(1, parts_ref.shape[0]):
        total = total + parts_ref[at]
    along = lax.broadcasted_iota(jnp.int32, (8, LANES), 0) % 4
    sums = [jnp.zeros((8, LANES), jnp.float32) for _ in range(4)]
    for source in range(4):
        for d_z in range(4):
            value = total[8 * source : 8 * source + 8]
            if d_z:
                value = pltpu.roll(value, LANES - 32 * d_z, 1)
            for d_x in range(4):
                moved = value
                if d_x:
                    moved = jnp.where(
                        along + d_x < 4, pltpu.roll(value, 8 - d_x, 0), pltpu.roll(value, 4 - d_x, 0)
                    )
                for e in range(4):
                    at = 8 * (((e * 4 + source) * 4 + d_z) * 4 + d_x)
                    sums[e] = sums[e] + matrix_ref[at : at + 8] * moved
    done = jnp.concatenate(sums, axis=0)
    for at in range(out_ref.shape[0]):
        out_ref[at] = done


def regrid(parts, matrix, copies):
    return call(
        regrid_kernel,
        [(copies,) + parts.shape[1:]],
        [],
        [parts, matrix],
        10**7,
        "regrid",
        vmem=[1],
        spaces={0: pltpu.VMEM},
    )[0]


def place_boxes(info, chip, u_ref, cos_ref, sin_ref, shift_ref, outs, gbufs, planes, chunk, slots):
    chips = len(outs)
    handlers = u_ref.shape[0] // chips
    high, low = halves(shift_ref[...])
    table = jnp.concatenate([high, high, low, jnp.zeros_like(low)], axis=0)
    for handler in range(handlers):
        rows = slice(handler * slots, (handler + 1) * slots)
        cos_b = jnp.concatenate([cos_ref[rows, :]] * 4, axis=0)
        sin_b = jnp.concatenate([sin_ref[rows, :]] * 4, axis=0)
        for hop in range(chips):
            u_hi, u_lo = (
                half.astype(jnp.float32) for half in halves(u_ref[(chip + hop) % chips * handlers + handler])
            )
            stack = jnp.concatenate([u_hi, u_lo, u_hi, jnp.zeros_like(u_hi)], axis=0)
            cells = dot_bf16(stack.T.astype(jnp.bfloat16), table, ((1,), (0,)))
            turned = cells * cos_b - pltpu.roll(cells, LANES // 2, 1) * sin_b
            gbufs[hop][handler * LANES : (handler + 1) * LANES, :] = turned
    band = band_of_lane(planes, chunk)

    def put(handler, carry):
        base = pl.multiple_of(handler * LANES, LANES)
        for slot in range(slots):
            block = handler * slots + slot
            here, after = in_window(band, info[1, block], chunk)
            first = pl.ds(info[0, block], 4)
            second = pl.ds(info[0, block] + LANES, 4)
            for hop in range(chips):
                cells = gbufs[hop][pl.ds(base + slot, 4, stride=slots), :]
                old_first = outs[hop][first, :]
                old_second = outs[hop][second, :]
                outs[hop][first, :] = old_first + jnp.where(here, cells, 0.0)
                outs[hop][second, :] = old_second + jnp.where(after, cells, 0.0)
        return carry

    lax.fori_loop(0, handlers, put, 0)


def inverse_kernel(*refs, part, length, chunk, slots, chips):
    u_ref, info_hbm, cos_hbm, sin_hbm, shift_hbm, table_hbm, s_hbm = refs[:7]
    far_maps = refs[7 : 6 + chips]
    outs = refs[6 + chips : 8 + chips]
    refs = refs[8 + chips :]
    grids, gbufs, refs = refs[:chips], refs[chips : 2 * chips], refs[2 * chips :]
    info, cos_ref, sin_ref, shift_ref, table_ref, ybuf, images, maps, sems = refs
    planes = s_hbm.shape[1]
    rows = length * planes
    own = length // chips
    chip, core = place_on_coil()
    own_rows = pl.multiple_of(chip * own, own)
    pairs = [
        (info_hbm, info),
        (cos_hbm, cos_ref),
        (sin_hbm, sin_ref),
        (shift_hbm.at[lax.axis_index("tile")], shift_ref),
        (table_hbm, table_ref),
        (s_hbm.at[:, :, pl.ds(own_rows, own), :], maps.at[0]),
    ]
    pairs += [(far_map, maps.at[at]) for at, far_map in enumerate(far_maps, 1)]
    copies = started(pairs, sems)
    for grid in grids:
        grid[...] = jnp.zeros_like(grid)
    for copy in copies[:4]:
        copy.wait()
    place_boxes(info, chip, u_ref, cos_ref, sin_ref, shift_ref, grids, gbufs, planes, chunk, slots)
    for copy in copies[4:]:
        copy.wait()
    table = []
    for half in range(2):
        bands = [
            table_ref[half, pl.ds(pl.multiple_of(ri * length + own_rows, own), own), :]
            for ri in range(2)
        ]
        table.append(jnp.concatenate(bands, axis=0))
    for hop in range(chips):
        for band in range(length // chunk):
            tile = grids[hop][band * length : (band + 1) * length, :].T
            ybuf[hop, band * 64 : (band + 1) * 64, :] = tile[:64]
            ybuf[hop, rows + band * 64 : rows + (band + 1) * 64, :] = tile[64:]
        for pair in range(planes // 2):
            columns = [
                jnp.concatenate(
                    [
                        ybuf[hop, pl.ds(ri * rows + plane, length, stride=planes), :]
                        for ri in range(2)
                    ],
                    axis=0,
                )
                for plane in (2 * pair, 2 * pair + 1)
            ]
            done = dot_left(table, jnp.concatenate(columns, axis=1))
            for inner in range(2):
                for ri in range(2):
                    images[hop, ri, 2 * pair + inner] = done[
                        ri * own : (ri + 1) * own, inner * LANES : (inner + 1) * LANES
                    ]
    table = (table_ref[2], table_ref[3])
    batch = min(planes, 256 // part)
    for at, half in enumerate((1 - core, core)):
        local = pl.ds(pl.multiple_of(half * part, part), part)
        for base in range(0, planes, batch):
            total_re, total_im = 0.0, 0.0
            for hop in range(chips):
                bands = [
                    jnp.concatenate([images[hop, ri, plane, local, :] for ri in range(2)], axis=1)
                    for plane in range(base, base + batch)
                ]
                done = dot_right(jnp.concatenate(bands, axis=0), table)
                i_re = done[:, :length].reshape(batch, part, length)
                i_im = done[:, length:].reshape(batch, part, length)
                s_re = maps[hop, 0, base : base + batch, local, :]
                s_im = maps[hop, 1, base : base + batch, local, :]
                total_re = total_re + (s_re * i_re + s_im * i_im)
                total_im = total_im + (s_re * i_im - s_im * i_re)
            outs[at][0, base : base + batch] = total_re
            outs[at][1, base : base + batch] = total_im


def inverse(spread, info, phases, shift, tables, smap, far_maps, part, chunk, slots):
    _, planes, length, _ = smap.shape
    chips = len(far_maps) + 1
    blocks = info.shape[1]
    rows = length * (length // chunk + 1)
    own = (chips, 2, planes, 2 * part, length)
    operands = [spread, info, *phases, shift, tables, smap, *far_maps]
    return call(
        functools.partial(
            inverse_kernel, part=part, length=length, chunk=chunk, slots=slots, chips=chips
        ),
        [(2, planes, part, length)] * 2,
        [(rows, LANES)] * chips
        + [(blocks * 4, LANES)] * chips
        + [
            pltpu.SMEM(info.shape, info.dtype),
            (blocks, LANES),
            (blocks, LANES),
            shift.shape[1:],
            pltpu.VMEM(tables.shape, tables.dtype),
            (chips, 2 * length * planes, length),
            own,
            own,
            pltpu.SemaphoreType.DMA((5 + chips,)),
        ],
        operands,
        48 * planes * length**3,
        "inverse",
        hbm=range(1, len(operands)),
        fixed=range(1, 7),
    )


def sums_kernel(*refs, terms):
    term_refs = refs[:terms]
    p_ref, r_ref, normal_ref, out_ref = refs[terms:]
    shape = p_ref.shape

    def add(plane, held):
        held = list(held)
        for ri in range(2):
            normal = term_refs[0][ri, plane]
            for term in term_refs[1:]:
                normal = normal + term[ri, plane]
            normal_ref[ri, plane] = normal
            p = p_ref[ri, plane]
            r = r_ref[ri, plane]
            for at, product in enumerate((r * r, p * normal, r * normal, normal * normal)):
                held[at] = held[at] + jnp.sum(product.reshape(-1, 8, LANES), axis=0)
        return tuple(held)

    start = tuple(jnp.zeros((8, LANES), jnp.float32) for _ in range(4))
    held = lax.fori_loop(0, shape[1], add, start, unroll=4)
    lane = lax.broadcasted_iota(jnp.int32, out_ref.shape, 1)
    found = jnp.zeros(out_ref.shape, jnp.float32)
    for at in range(4):
        found = jnp.where(lane == at, jnp.sum(held[at]), found)
    out_ref[...] = found


def sums(terms, p, r, devices):
    kernel = functools.partial(sums_kernel, terms=len(terms))
    return call(kernel, [p.shape, (devices, LANES)], [], [*terms, p, r], 10**7, "sums")


def finish_kernel(total_ref, x_ref, r_ref, p_ref, normal_ref, x_out, r_out, p_out):
    total = jnp.sum(total_ref[...], axis=0, keepdims=True)
    r_r, p_n, r_n, n_n = (total[:, at : at + 1] for at in range(4))
    alpha = r_r / p_n
    beta = (r_r + alpha * (alpha * n_n - 2.0 * r_n)) / r_r
    for plane in range(x_ref.shape[1]):
        for ri in range(2):
            p = p_ref[ri, plane]
            next_r = r_ref[ri, plane] - alpha * normal_ref[ri, plane]
            x_out[ri, plane] = x_ref[ri, plane] + alpha * p
            r_out[ri, plane] = next_r
            p_out[ri, plane] = next_r + beta * p


def finish(total, x, r, p, normal):
    return call(finish_kernel, [x.shape] * 3, [], [total, x, r, p, normal], 10**7, "finish")


def matrices_kernel(info_hbm, weights_ref, out_ref, held, info, sem, *, slots):
    base = lax.axis_index("tile") * slots
    copy = pltpu.make_async_copy(info_hbm, info, sem)
    copy.start()
    copy.wait()

    def one(block, carry):
        w_x = weights_ref[block, 0]
        w_y = weights_ref[block, 1]
        w_z = weights_ref[block, 2]
        twice = jnp.concatenate([w_x, w_x], axis=0)
        rolled = [twice] + [pltpu.roll(twice, 8 - d, 0) for d in range(1, 4)]
        low = lax.broadcasted_iota(jnp.int32, (8, LANES), 0) < 4
        along_x = [twice * jnp.where(low, rolled[d], rolled[d + 1]) for d in (0, 2)]
        right = []
        for f in range(4):
            for d_z in range(4):
                other = (f + d_z) % 4
                along_z = w_z[f : f + 1] * w_z[other : other + 1]
                right += [along * along_z for along in along_x]
        turned = pltpu.roll(
            jnp.concatenate([w_y, w_y], axis=0), info[1, base + block] % 4, 0
        )[:4]
        left = halves(jnp.concatenate([turned * turned[e : e + 1] for e in range(4)], axis=0))
        high, low = halves(jnp.concatenate(right, axis=0))
        both = dot_bf16(jnp.concatenate(left, axis=0), high, ((1,), (1,)))
        done = both[:16] + both[16:] + dot_bf16(left[0], low, ((1,), (1,)))
        for f in range(4):
            lanes = done[:, f // 2 * LANES : (f // 2 + 1) * LANES]
            if f % 2:
                lanes = pltpu.roll(lanes, LANES // 2, 1)
            held[pl.ds(f * slots + block, 16, stride=LANES), :] = lanes
        return carry

    lax.fori_loop(0, slots, one, 0, unroll=4)

    def turn(pair, carry):
        at = pl.ds(pl.multiple_of(pair * LANES, LANES), LANES)
        rows = held[at, :64].T
        for group in range(16):
            four = rows[4 * group : 4 * group + 4]
            out_ref[pl.ds(pl.multiple_of(pair * LANES + 8 * group, 8), 8), :] = jnp.concatenate(
                [four, four], axis=0
            )
        return carry

    lax.fori_loop(0, 16, turn, 0, unroll=2)


def block_matrices(info, weights):
    return call(
        functools.partial(matrices_kernel, slots=weights.shape[0]),
        [(16 * LANES, LANES)],
        [(16 * LANES, LANES), pltpu.SMEM(info.shape, info.dtype), pltpu.SemaphoreType.DMA],
        [info, weights],
        10**9,
        "matrices",
        hbm=[0],
    )[0]


def block_offsets(gathered, slots, ntile, capacity):
    owners = gathered[:, 0, 3 * capacity : 3 * capacity + slots]
    lists = gathered[:, :, : 3 * capacity].reshape(ntile, ntile, 3, capacity)
    earlier = jnp.tril(jnp.ones((slots, slots), jnp.int32), -1)
    same = (owners[:, :, None] == owners[:, None, :]).astype(jnp.int32)
    ranks = jnp.sum(same * earlier[None], axis=2)
    wanted = owners * capacity + ranks
    lists = jnp.transpose(lists, (2, 1, 0, 3)).reshape(3, ntile, 1, ntile * capacity)
    hit = wanted[:, :, None] == jnp.arange(ntile * capacity, dtype=jnp.int32)
    found = jnp.sum(jnp.where(hit[None], lists, 0), axis=3)
    return found[0], found[1] + owners * (LANES // ntile), found[2]


def shards(image_p, image_x, image_r, sensitivity, kb_weights, block_owner, owner_list):
    ntile = lax.axis_size("tile")
    ncoil = lax.axis_size("coil")
    chips = ncoil // 2
    slots = kb_weights.shape[0]
    capacity = owner_list.shape[3]
    planes, length = image_p.shape[1], image_p.shape[3]
    part = image_p.shape[2]
    chunk = LANES // (2 * planes)
    tile = lax.axis_index("tile")
    smap = sensitivity[0]
    tables = fourier_tables(length)

    def from_chip(values, by):
        pairs = [
            (a * 2 + k, (a - by) % chips * 2 + k) for a in range(chips) for k in range(2)
        ]
        return lax.ppermute(values, "coil", pairs)

    def other_core(values):
        pairs = [(a * 2 + k, a * 2 + 1 - k) for a in range(chips) for k in range(2)]
        return lax.ppermute(values, "coil", pairs)

    p_same = [image_p] + [from_chip(image_p, by) for by in range(1, chips)]
    p_other = [other_core(image_p)]
    gathered = lax.all_to_all(message(block_owner, owner_list), "tile", 0, 0, tiled=True)
    far_rows = map_rows(smap, chips)
    off_x, off_y, off_z = block_offsets(gathered, slots, ntile, capacity)
    info = jnp.stack(
        [(off_y // chunk * length + off_z).reshape(-1), (off_y % chunk).reshape(-1)]
    )
    lane = jnp.arange(LANES, dtype=jnp.int32)
    lane_ri = lane // (LANES // 2)
    lane_x = lane % planes + tile * planes
    unit = 2.0 * math.pi / length
    angle = unit * (off_x.reshape(-1, 1) * lane_x[None] % length).astype(jnp.float32)
    phases = (jnp.cos(angle), jnp.sin(angle) * jnp.where(lane_ri == 0, 1.0, -1.0)[None])
    shift = shift_tables(length, planes, chunk)
    p_far, far_rows, info, phases = lax.optimization_barrier(
        (p_same[1:], far_rows, info, phases)
    )
    p_other += [other_core(piece) for piece in p_far]
    far_maps = [from_chip(rows, by) for by, rows in enumerate(far_rows, 1)]
    partial = forward([image_p, *p_far, *p_other], smap, tables, info, phases, shift, chunk, slots)
    partial, weights = lax.optimization_barrier((partial, kb_weights))
    parts = lax.all_to_all(partial, "tile", 0, 0, tiled=True)
    done = regrid(parts, block_matrices(info, weights), chips * ntile)
    groups = [
        [at * ntile + t for at in range(ncoil) if at % 2 == k for t in range(ntile)]
        for k in range(2)
    ]
    spread = lax.all_to_all(
        done, ("coil", "tile"), 0, 0, axis_index_groups=groups, tiled=True
    )
    sent, kept = inverse(
        spread, info, phases, shift, tables, smap, far_maps, part, chunk, slots
    )
    normal, found = sums([kept, other_core(sent)], image_p, image_r, ncoil * ntile)
    total = lax.all_to_all(found, ("coil", "tile"), 0, 0, tiled=True)
    return tuple(finish(total, image_x, image_r, image_p, normal))


def solution(mesh):
    return jax.shard_map(
        shards,
        mesh=mesh,
        in_specs=(
            P(None, "tile", "coil", None),
            P(None, "tile", "coil", None),
            P(None, "tile", "coil", None),
            P("coil", None, "tile", None, None),
            P("tile", None, None, None),
            P("tile"),
            P(None, "tile", None, None),
        ),
        out_specs=(
            P(None, "tile", "coil", None),
            P(None, "tile", "coil", None),
            P(None, "tile", "coil", None),
        ),
        check_vma=False,
    )
```

```python
import functools
import math

import jax
import jax.numpy as jnp
import ml_dtypes
import numpy as np
from jax import lax
from jax.experimental import pallas as pl
from jax.experimental.pallas import tpu as pltpu
from jax.sharding import PartitionSpec as P

LANES = 128
VMEM = 24 * 1024 * 1024


def halves(values):
    high = values.astype(jnp.bfloat16)
    low = (values - high.astype(jnp.float32)).astype(jnp.bfloat16)
    return high, low


def dot_bf16(left, right, dims):
    return lax.dot_general(left, right, (dims, ((), ())), preferred_element_type=jnp.float32)


def dot_left(table, values, dims=((1,), (0,))):
    high, low = halves(values)
    return (
        dot_bf16(table[0], high, dims)
        + dot_bf16(table[0], low, dims)
        + dot_bf16(table[1], high, dims)
    )


def dot_right(values, table, dims=((1,), (0,))):
    high, low = halves(values)
    return (
        dot_bf16(high, table[0], dims)
        + dot_bf16(low, table[0], dims)
        + dot_bf16(high, table[1], dims)
    )


def fourier_tables(length):
    cells = np.arange(length)
    angle = 2.0 * math.pi / length * (cells[:, None] * cells[None, :] % length)
    cos_t = np.cos(angle) / math.sqrt(length)
    sin_t = np.sin(angle) / math.sqrt(length)
    found = []
    for sign in (1.0, -1.0):
        whole = np.block([[cos_t, -sign * sin_t], [sign * sin_t, cos_t]])
        high = whole.astype(ml_dtypes.bfloat16)
        low = (whole - high.astype(np.float64)).astype(ml_dtypes.bfloat16)
        found += [high, low]
    return jnp.asarray(np.stack(found))


def shift_tables(length, planes, chunk):
    row = np.arange(32)[:, None]
    lane = np.arange(LANES)[None, :]
    row_q, row_ri, row_i = row // 8, row // 4 % 2, row % 4
    lane_ri, lane_q, lane_x = lane // (LANES // 2), lane // planes % chunk, lane % planes
    found = []
    for tile in range(length // planes):
        angle = 2.0 * math.pi / length * (row_i * (lane_x + tile * planes) % length)
        sine = np.where(row_ri == 0, 1.0, -1.0) * np.sin(angle)
        table = np.where(row_ri == lane_ri, np.cos(angle), sine) / math.sqrt(length)
        found.append(np.where(lane_q % 4 == row_q, table, 0.0))
    return jnp.asarray(np.stack(found), jnp.float32)


def band_of_lane(planes, chunk):
    return lax.broadcasted_iota(jnp.int32, (4, LANES), 1) // planes % chunk


def in_window(band, first, chunk):
    past = band - first
    if chunk == 4:
        here = past >= 0
        return here, jnp.logical_not(here)
    here = jnp.logical_and(past >= 0, past < 4)
    return here, past < 4 - chunk


def call(kernel, outs, scratch, operands, flops, name, hbm=(), hbm_outs=(), vmem=(), fixed=(), spaces=()):
    spaces = dict(spaces)
    operands = list(operands)
    for listed, space in ((fixed, pltpu.HBM), (vmem, pltpu.VMEM)):
        for at in listed:
            operands[at] = pltpu.with_memory_space_constraint(operands[at], space)
    here = pl.BlockSpec(memory_space=pltpu.VMEM)
    there = pl.BlockSpec(memory_space=pltpu.HBM)
    moved = sum(math.prod(a.shape) * a.dtype.itemsize for a in operands)
    return pl.pallas_call(
        kernel,
        out_shape=[
            spaces[at](shape, jnp.float32)
            if at in spaces
            else jax.ShapeDtypeStruct(shape, jnp.float32)
            for at, shape in enumerate(outs)
        ],
        in_specs=[there if at in hbm else here for at in range(len(operands))],
        out_specs=[there if at in hbm_outs else here for at in range(len(outs))],
        scratch_shapes=[
            pltpu.VMEM(shape, jnp.float32) if isinstance(shape, tuple) else shape
            for shape in scratch
        ],
        compiler_params=pltpu.CompilerParams(vmem_limit_bytes=VMEM),
        cost_estimate=pl.CostEstimate(flops=flops, bytes_accessed=moved, transcendentals=0),
        name=name,
    )(*operands)


def started(pairs, sems):
    copies = [
        pltpu.make_async_copy(source, to, sems.at[at]) for at, (source, to) in enumerate(pairs)
    ]
    for copy in copies:
        copy.start()
    return copies


def place_on_coil():
    coil = lax.axis_index("coil")
    return coil // 2, coil % 2


def quarters_of(chips, part):
    chip, core = place_on_coil()
    return [
        pl.multiple_of(((chip + hop) % chips * 2 + at) * part, part)
        for at in (core, 1 - core)
        for hop in range(chips)
    ]


def map_rows_kernel(s_ref, *refs, chips):
    outs, (held, sems) = refs[:-2], refs[-2:]
    chip, _ = place_on_coil()
    own = s_ref.shape[2] // chips
    for by in range(1, chips):
        rows = pl.ds(pl.multiple_of((chip + chips - by) % chips * own, own), own)
        for copy in started([(s_ref.at[:, :, rows, :], held)], sems):
            copy.wait()
        for copy in started([(held, outs[by - 1])], sems):
            copy.wait()


def map_rows(smap, chips):
    _, planes, length, _ = smap.shape
    shape = (2, planes, length // chips, length)
    return call(
        functools.partial(map_rows_kernel, chips=chips),
        [shape] * (chips - 1),
        [shape, pltpu.SemaphoreType.DMA((1,))],
        [smap],
        0,
        "map_rows",
        hbm=[0],
        fixed=[0],
        hbm_outs=range(chips - 1),
    )


def message_kernel(owner_ref, list_ref, out_ref):
    _, _, ntile, capacity = list_ref.shape
    out_ref[...] = jnp.zeros_like(out_ref)
    slots = owner_ref.shape[1]
    for to in range(ntile):
        for axis in range(3):
            out_ref[to, :, axis * capacity : (axis + 1) * capacity] = list_ref[axis, 0]
        out_ref[to, 0:1, 3 * capacity : 3 * capacity + slots] = owner_ref[...]


def message(block_owner, owner_list):
    ntile = owner_list.shape[2]
    return pl.pallas_call(
        message_kernel,
        out_shape=jax.ShapeDtypeStruct((ntile, ntile, LANES), jnp.int32),
        in_specs=[pl.BlockSpec(memory_space=pltpu.VMEM)] * 2,
        out_specs=pl.BlockSpec(memory_space=pltpu.VMEM),
        name="message",
    )(block_owner[None], owner_list)


def cut_boxes(info, grid, cos_ref, sin_ref, shift_ref, out_ref, gbuf, planes, chunk, slots):
    handlers = out_ref.shape[0]
    band = band_of_lane(planes, chunk)

    def cut(handler, carry):
        base = pl.multiple_of(handler * LANES, LANES)
        for slot in range(slots):
            block = handler * slots + slot
            here, after = in_window(band, info[1, block], chunk)
            first = grid[pl.ds(info[0, block], 4), :]
            second = grid[pl.ds(info[0, block] + LANES, 4), :]
            if chunk > 4:
                second = jnp.where(after, second, 0.0)
            gbuf[pl.ds(base + slot, 4, stride=slots), :] = jnp.where(here, first, second)
        return carry

    lax.fori_loop(0, handlers, cut, 0)
    high, low = halves(shift_ref[...])
    table = jnp.concatenate(
        [
            jnp.concatenate([high, high], axis=1),
            jnp.concatenate([low, jnp.zeros_like(low)], axis=1),
        ],
        axis=0,
    )
    for handler in range(handlers):
        rows = slice(handler * slots, (handler + 1) * slots)
        cos_b = jnp.concatenate([cos_ref[rows, :]] * 4, axis=0)
        sin_b = jnp.concatenate([sin_ref[rows, :]] * 4, axis=0)
        cells = gbuf[handler * LANES : (handler + 1) * LANES, :]
        turned = cells * cos_b + pltpu.roll(cells, LANES // 2, 1) * sin_b
        both = dot_bf16(table, jnp.concatenate(halves(turned), axis=1), ((1,), (1,)))
        out_ref[handler] = both[:32] + both[32:]


def forward_kernel(*refs, pieces, chunk, slots):
    p_refs = refs[:pieces]
    s_hbm, table_hbm, info_hbm, cos_hbm, sin_hbm, shift_hbm, weights_ref = refs[pieces : pieces + 7]
    out_ref, turned_ref = refs[pieces + 7 : pieces + 9]
    sbuf, tables, info, cos_ref, sin_ref, shift_ref = refs[pieces + 9 : pieces + 15]
    natural, ybuf, grid, gbuf, sems = refs[pieces + 15 :]
    _, planes, part, length = p_refs[0].shape
    rows = length * planes
    starts = quarters_of(pieces // 2, part)
    order = [0, pieces // 2]
    order += [at for at in range(pieces) if at not in order]
    first = [(table_hbm.at[0:2], tables.at[0:2])]
    for at in order:
        first.append((s_hbm.at[:, :, pl.ds(starts[at], part), :], sbuf.at[at]))
    last = [
        (table_hbm.at[2:4], tables.at[2:4]),
        (info_hbm, info),
        (cos_hbm, cos_ref),
        (sin_hbm, sin_ref),
        (shift_hbm.at[lax.axis_index("tile")], shift_ref),
    ]
    copies = started(first + last, sems)
    copies[0].wait()
    batch = min(planes, 256 // part)
    table = (tables[0], tables[1])
    for turn, at in enumerate(order):
        copies[1 + turn].wait()
        for base in range(0, planes, batch):
            bands = []
            for plane in range(base, base + batch):
                s_re = sbuf[at, 0, plane]
                s_im = sbuf[at, 1, plane]
                p_re = p_refs[at][0, plane]
                p_im = p_refs[at][1, plane]
                bands.append(
                    jnp.concatenate([s_re * p_re - s_im * p_im, s_re * p_im + s_im * p_re], axis=1)
                )
            done = dot_right(jnp.concatenate(bands, axis=0), table)
            for ri in range(2):
                half = done[:, ri * length : (ri + 1) * length]
                natural[ri, base : base + batch, pl.ds(starts[at], part), :] = half.reshape(
                    batch, part, length
                )
    for copy in copies[1 + pieces :]:
        copy.wait()
    own = lax.axis_index("tile") * slots
    for block in range(slots):
        w_y = weights_ref[block, 1]
        turned_ref[block] = pltpu.roll(
            jnp.concatenate([w_y, w_y], axis=0), info[1, own + block] % 4, 0
        )
    table = (tables[2], tables[3])
    for pair in range(planes // 2):
        columns = [
            jnp.concatenate([natural[0, plane], natural[1, plane]], axis=0)
            for plane in (2 * pair, 2 * pair + 1)
        ]
        both = dot_left(table, jnp.concatenate(columns, axis=1))
        for inner in range(2):
            for ri in range(2):
                ybuf[pl.ds(ri * rows + 2 * pair + inner, length, stride=planes), :] = both[
                    ri * length : (ri + 1) * length, inner * LANES : (inner + 1) * LANES
                ]
    for band in range(length // chunk):
        re = ybuf[band * 64 : (band + 1) * 64, :]
        im = ybuf[rows + band * 64 : rows + (band + 1) * 64, :]
        grid[band * length : (band + 1) * length, :] = jnp.concatenate([re, im], axis=0).T
    cut_boxes(info, grid, cos_ref, sin_ref, shift_ref, out_ref, gbuf, planes, chunk, slots)


def forward(pieces, smap, tables, info, phases, shift, weights, chunk, slots):
    _, planes, part, length = pieces[0].shape
    count = len(pieces)
    blocks = info.shape[1]
    operands = [*pieces, smap, tables, info, *phases, shift, weights]
    return call(
        functools.partial(forward_kernel, pieces=count, chunk=chunk, slots=slots),
        [(blocks // slots, 32, LANES), (slots, 8, LANES)],
        [
            (count, 2, planes, part, length),
            pltpu.VMEM(tables.shape, tables.dtype),
            pltpu.SMEM(info.shape, info.dtype),
            (blocks, LANES),
            (blocks, LANES),
            shift.shape[1:],
            (2, planes, length, length),
            (2 * length * planes, length),
            (length * (length // chunk + 1), LANES),
            (blocks * 4, LANES),
            pltpu.SemaphoreType.DMA((count + 6,)),
        ],
        operands,
        48 * planes * length**3,
        "forward",
        hbm=range(count, len(operands) - 1),
        fixed=range(count, len(operands) - 1),
    )


def regrid_kernel(parts_ref, matrix_ref, out_ref):
    total = parts_ref[0]
    for at in range(1, parts_ref.shape[0]):
        total = total + parts_ref[at]
    along = lax.broadcasted_iota(jnp.int32, (8, LANES), 0) % 4
    sums = [jnp.zeros((8, LANES), jnp.float32) for _ in range(4)]
    for source in range(4):
        for d_z in range(4):
            value = total[8 * source : 8 * source + 8]
            if d_z:
                value = pltpu.roll(value, LANES - 32 * d_z, 1)
            for d_x in range(4):
                moved = value
                if d_x:
                    moved = jnp.where(
                        along + d_x < 4, pltpu.roll(value, 8 - d_x, 0), pltpu.roll(value, 4 - d_x, 0)
                    )
                for e in range(4):
                    at = 8 * (((e * 4 + source) * 4 + d_z) * 4 + d_x)
                    sums[e] = sums[e] + matrix_ref[at : at + 8] * moved
    done = jnp.concatenate(sums, axis=0)
    for at in range(out_ref.shape[0]):
        out_ref[at] = done


def regrid(parts, matrix, copies):
    return call(
        regrid_kernel,
        [(copies,) + parts.shape[1:]],
        [],
        [parts, matrix],
        10**7,
        "regrid",
        vmem=[1],
        spaces={0: pltpu.VMEM},
    )[0]


def place_boxes(info, chip, u_ref, cos_ref, sin_ref, shift_ref, outs, gbufs, planes, chunk, slots):
    chips = len(outs)
    handlers = u_ref.shape[0] // chips
    high, low = halves(shift_ref[...])
    table = jnp.concatenate([high, high, low, jnp.zeros_like(low)], axis=0)
    for handler in range(handlers):
        rows = slice(handler * slots, (handler + 1) * slots)
        cos_b = jnp.concatenate([cos_ref[rows, :]] * 4, axis=0)
        sin_b = jnp.concatenate([sin_ref[rows, :]] * 4, axis=0)
        for hop in range(chips):
            u_hi, u_lo = (
                half.astype(jnp.float32) for half in halves(u_ref[(chip + hop) % chips * handlers + handler])
            )
            stack = jnp.concatenate([u_hi, u_lo, u_hi, jnp.zeros_like(u_hi)], axis=0)
            cells = dot_bf16(stack.T.astype(jnp.bfloat16), table, ((1,), (0,)))
            turned = cells * cos_b - pltpu.roll(cells, LANES // 2, 1) * sin_b
            gbufs[hop][handler * LANES : (handler + 1) * LANES, :] = turned
    band = band_of_lane(planes, chunk)

    def put(handler, carry):
        base = pl.multiple_of(handler * LANES, LANES)
        for slot in range(slots):
            block = handler * slots + slot
            here, after = in_window(band, info[1, block], chunk)
            first = pl.ds(info[0, block], 4)
            second = pl.ds(info[0, block] + LANES, 4)
            for hop in range(chips):
                cells = gbufs[hop][pl.ds(base + slot, 4, stride=slots), :]
                old_first = outs[hop][first, :]
                old_second = outs[hop][second, :]
                outs[hop][first, :] = old_first + jnp.where(here, cells, 0.0)
                outs[hop][second, :] = old_second + jnp.where(after, cells, 0.0)
        return carry

    lax.fori_loop(0, handlers, put, 0)


def inverse_kernel(*refs, part, length, chunk, slots, chips):
    u_ref, info_hbm, cos_hbm, sin_hbm, shift_hbm, table_hbm, s_hbm = refs[:7]
    far_maps = refs[7 : 6 + chips]
    outs = refs[6 + chips : 8 + chips]
    refs = refs[8 + chips :]
    grids, gbufs, refs = refs[:chips], refs[chips : 2 * chips], refs[2 * chips :]
    info, cos_ref, sin_ref, shift_ref, table_ref, ybuf, images, maps, sems = refs
    planes = s_hbm.shape[1]
    rows = length * planes
    own = length // chips
    chip, core = place_on_coil()
    own_rows = pl.multiple_of(chip * own, own)
    pairs = [
        (info_hbm, info),
        (cos_hbm, cos_ref),
        (sin_hbm, sin_ref),
        (shift_hbm.at[lax.axis_index("tile")], shift_ref),
        (table_hbm, table_ref),
        (s_hbm.at[:, :, pl.ds(own_rows, own), :], maps.at[0]),
    ]
    pairs += [(far_map, maps.at[at]) for at, far_map in enumerate(far_maps, 1)]
    copies = started(pairs, sems)
    for grid in grids:
        grid[...] = jnp.zeros_like(grid)
    for copy in copies[:4]:
        copy.wait()
    place_boxes(info, chip, u_ref, cos_ref, sin_ref, shift_ref, grids, gbufs, planes, chunk, slots)
    for copy in copies[4:]:
        copy.wait()
    table = []
    for half in range(2):
        bands = [
            table_ref[half, pl.ds(pl.multiple_of(ri * length + own_rows, own), own), :]
            for ri in range(2)
        ]
        table.append(jnp.concatenate(bands, axis=0))
    for hop in range(chips):
        for band in range(length // chunk):
            tile = grids[hop][band * length : (band + 1) * length, :].T
            ybuf[hop, band * 64 : (band + 1) * 64, :] = tile[:64]
            ybuf[hop, rows + band * 64 : rows + (band + 1) * 64, :] = tile[64:]
        for pair in range(planes // 2):
            columns = [
                jnp.concatenate(
                    [
                        ybuf[hop, pl.ds(ri * rows + plane, length, stride=planes), :]
                        for ri in range(2)
                    ],
                    axis=0,
                )
                for plane in (2 * pair, 2 * pair + 1)
            ]
            done = dot_left(table, jnp.concatenate(columns, axis=1))
            for inner in range(2):
                for ri in range(2):
                    images[hop, ri, 2 * pair + inner] = done[
                        ri * own : (ri + 1) * own, inner * LANES : (inner + 1) * LANES
                    ]
    table = (table_ref[2], table_ref[3])
    batch = min(planes, 256 // part)
    for at, half in enumerate((1 - core, core)):
        local = pl.ds(pl.multiple_of(half * part, part), part)
        for base in range(0, planes, batch):
            total_re, total_im = 0.0, 0.0
            for hop in range(chips):
                bands = [
                    jnp.concatenate([images[hop, ri, plane, local, :] for ri in range(2)], axis=1)
                    for plane in range(base, base + batch)
                ]
                done = dot_right(jnp.concatenate(bands, axis=0), table)
                i_re = done[:, :length].reshape(batch, part, length)
                i_im = done[:, length:].reshape(batch, part, length)
                s_re = maps[hop, 0, base : base + batch, local, :]
                s_im = maps[hop, 1, base : base + batch, local, :]
                total_re = total_re + (s_re * i_re + s_im * i_im)
                total_im = total_im + (s_re * i_im - s_im * i_re)
            outs[at][0, base : base + batch] = total_re
            outs[at][1, base : base + batch] = total_im


def inverse(spread, info, phases, shift, tables, smap, far_maps, part, chunk, slots):
    _, planes, length, _ = smap.shape
    chips = len(far_maps) + 1
    blocks = info.shape[1]
    rows = length * (length // chunk + 1)
    own = (chips, 2, planes, 2 * part, length)
    operands = [spread, info, *phases, shift, tables, smap, *far_maps]
    return call(
        functools.partial(
            inverse_kernel, part=part, length=length, chunk=chunk, slots=slots, chips=chips
        ),
        [(2, planes, part, length)] * 2,
        [(rows, LANES)] * chips
        + [(blocks * 4, LANES)] * chips
        + [
            pltpu.SMEM(info.shape, info.dtype),
            (blocks, LANES),
            (blocks, LANES),
            shift.shape[1:],
            pltpu.VMEM(tables.shape, tables.dtype),
            (chips, 2 * length * planes, length),
            own,
            own,
            pltpu.SemaphoreType.DMA((5 + chips,)),
        ],
        operands,
        48 * planes * length**3,
        "inverse",
        hbm=range(1, len(operands)),
        fixed=range(1, 7),
    )


def sums_kernel(*refs, terms):
    term_refs = refs[:terms]
    p_ref, r_ref, normal_ref, out_ref = refs[terms:]
    shape = p_ref.shape

    def add(plane, held):
        held = list(held)
        for ri in range(2):
            normal = term_refs[0][ri, plane]
            for term in term_refs[1:]:
                normal = normal + term[ri, plane]
            normal_ref[ri, plane] = normal
            p = p_ref[ri, plane]
            r = r_ref[ri, plane]
            for at, product in enumerate((r * r, p * normal, r * normal, normal * normal)):
                held[at] = held[at] + jnp.sum(product.reshape(-1, 8, LANES), axis=0)
        return tuple(held)

    start = tuple(jnp.zeros((8, LANES), jnp.float32) for _ in range(4))
    held = lax.fori_loop(0, shape[1], add, start, unroll=4)
    lane = lax.broadcasted_iota(jnp.int32, out_ref.shape, 1)
    found = jnp.zeros(out_ref.shape, jnp.float32)
    for at in range(4):
        found = jnp.where(lane == at, jnp.sum(held[at]), found)
    out_ref[...] = found


def sums(terms, p, r, devices):
    kernel = functools.partial(sums_kernel, terms=len(terms))
    return call(kernel, [p.shape, (devices, LANES)], [], [*terms, p, r], 10**7, "sums")


def finish_kernel(total_ref, x_ref, r_ref, p_ref, normal_ref, x_out, r_out, p_out):
    total = jnp.sum(total_ref[...], axis=0, keepdims=True)
    r_r, p_n, r_n, n_n = (total[:, at : at + 1] for at in range(4))
    alpha = r_r / p_n
    beta = (r_r + alpha * (alpha * n_n - 2.0 * r_n)) / r_r
    for plane in range(x_ref.shape[1]):
        for ri in range(2):
            p = p_ref[ri, plane]
            next_r = r_ref[ri, plane] - alpha * normal_ref[ri, plane]
            x_out[ri, plane] = x_ref[ri, plane] + alpha * p
            r_out[ri, plane] = next_r
            p_out[ri, plane] = next_r + beta * p


def finish(total, x, r, p, normal):
    return call(finish_kernel, [x.shape] * 3, [], [total, x, r, p, normal], 10**7, "finish")


def matrices_kernel(weights_ref, turned_ref, out_ref, held, *, slots):
    def one(block, carry):
        w_x = weights_ref[block, 0]
        w_z = weights_ref[block, 2]
        twice = jnp.concatenate([w_x, w_x], axis=0)
        rolled = [twice] + [pltpu.roll(twice, 8 - d, 0) for d in range(1, 4)]
        low = lax.broadcasted_iota(jnp.int32, (8, LANES), 0) < 4
        along_x = [twice * jnp.where(low, rolled[d], rolled[d + 1]) for d in (0, 2)]
        right = []
        for f in range(4):
            for d_z in range(4):
                other = (f + d_z) % 4
                along_z = w_z[f : f + 1] * w_z[other : other + 1]
                right += [along * along_z for along in along_x]
        turned = turned_ref[block, 0:4]
        left = halves(jnp.concatenate([turned * turned[e : e + 1] for e in range(4)], axis=0))
        high, low = halves(jnp.concatenate(right, axis=0))
        both = dot_bf16(jnp.concatenate(left, axis=0), high, ((1,), (1,)))
        done = both[:16] + both[16:] + dot_bf16(left[0], low, ((1,), (1,)))
        for f in range(4):
            lanes = done[:, f // 2 * LANES : (f // 2 + 1) * LANES]
            if f % 2:
                lanes = pltpu.roll(lanes, LANES // 2, 1)
            held[pl.ds(f * slots + block, 16, stride=LANES), :] = lanes
        return carry

    lax.fori_loop(0, slots, one, 0, unroll=4)

    def turn(pair, carry):
        at = pl.ds(pl.multiple_of(pair * LANES, LANES), LANES)
        rows = held[at, :64].T
        for group in range(16):
            four = rows[4 * group : 4 * group + 4]
            out_ref[pl.ds(pl.multiple_of(pair * LANES + 8 * group, 8), 8), :] = jnp.concatenate(
                [four, four], axis=0
            )
        return carry

    lax.fori_loop(0, 16, turn, 0, unroll=2)


def block_matrices(weights, turned):
    return call(
        functools.partial(matrices_kernel, slots=weights.shape[0]),
        [(16 * LANES, LANES)],
        [(16 * LANES, LANES)],
        [weights, turned],
        10**9,
        "matrices",
    )[0]


def block_offsets(gathered, slots, ntile, capacity):
    owners = gathered[:, 0, 3 * capacity : 3 * capacity + slots]
    lists = gathered[:, :, : 3 * capacity].reshape(ntile, ntile, 3, capacity)
    earlier = jnp.tril(jnp.ones((slots, slots), jnp.int32), -1)
    same = (owners[:, :, None] == owners[:, None, :]).astype(jnp.int32)
    ranks = jnp.sum(same * earlier[None], axis=2)
    wanted = owners * capacity + ranks
    lists = jnp.transpose(lists, (2, 1, 0, 3)).reshape(3, ntile, 1, ntile * capacity)
    hit = wanted[:, :, None] == jnp.arange(ntile * capacity, dtype=jnp.int32)
    found = jnp.sum(jnp.where(hit[None], lists, 0), axis=3)
    return found[0], found[1] + owners * (LANES // ntile), found[2]


def shards(image_p, image_x, image_r, sensitivity, kb_weights, block_owner, owner_list):
    ntile = lax.axis_size("tile")
    ncoil = lax.axis_size("coil")
    chips = ncoil // 2
    slots = kb_weights.shape[0]
    capacity = owner_list.shape[3]
    planes, length = image_p.shape[1], image_p.shape[3]
    part = image_p.shape[2]
    chunk = LANES // (2 * planes)
    tile = lax.axis_index("tile")
    smap = sensitivity[0]
    tables = fourier_tables(length)

    def from_chip(values, by):
        pairs = [
            (a * 2 + k, (a - by) % chips * 2 + k) for a in range(chips) for k in range(2)
        ]
        return lax.ppermute(values, "coil", pairs)

    def other_core(values):
        pairs = [(a * 2 + k, a * 2 + 1 - k) for a in range(chips) for k in range(2)]
        return lax.ppermute(values, "coil", pairs)

    p_same = [image_p] + [from_chip(image_p, by) for by in range(1, chips)]
    p_other = [other_core(image_p)]
    gathered = lax.all_to_all(message(block_owner, owner_list), "tile", 0, 0, tiled=True)
    far_rows = map_rows(smap, chips)
    off_x, off_y, off_z = block_offsets(gathered, slots, ntile, capacity)
    info = jnp.stack(
        [(off_y // chunk * length + off_z).reshape(-1), (off_y % chunk).reshape(-1)]
    )
    lane = jnp.arange(LANES, dtype=jnp.int32)
    lane_ri = lane // (LANES // 2)
    lane_x = lane % planes + tile * planes
    unit = 2.0 * math.pi / length
    angle = unit * (off_x.reshape(-1, 1) * lane_x[None] % length).astype(jnp.float32)
    phases = (jnp.cos(angle), jnp.sin(angle) * jnp.where(lane_ri == 0, 1.0, -1.0)[None])
    shift = shift_tables(length, planes, chunk)
    p_far, far_rows, info, phases = lax.optimization_barrier(
        (p_same[1:], far_rows, info, phases)
    )
    p_other += [other_core(piece) for piece in p_far]
    far_maps = [from_chip(rows, by) for by, rows in enumerate(far_rows, 1)]
    partial, turned = forward(
        [image_p, *p_far, *p_other], smap, tables, info, phases, shift, kb_weights, chunk, slots
    )
    partial, turned = lax.optimization_barrier((partial, turned))
    parts = lax.all_to_all(partial, "tile", 0, 0, tiled=True)
    done = regrid(parts, block_matrices(kb_weights, turned), chips * ntile)
    groups = [
        [at * ntile + t for at in range(ncoil) if at % 2 == k for t in range(ntile)]
        for k in range(2)
    ]
    spread = lax.all_to_all(
        done, ("coil", "tile"), 0, 0, axis_index_groups=groups, tiled=True
    )
    sent, kept = inverse(
        spread, info, phases, shift, tables, smap, far_maps, part, chunk, slots
    )
    normal, found = sums([kept, other_core(sent)], image_p, image_r, ncoil * ntile)
    total = lax.all_to_all(found, ("coil", "tile"), 0, 0, tiled=True)
    return tuple(finish(total, image_x, image_r, image_p, normal))


def solution(mesh):
    return jax.shard_map(
        shards,
        mesh=mesh,
        in_specs=(
            P(None, "tile", "coil", None),
            P(None, "tile", "coil", None),
            P(None, "tile", "coil", None),
            P("coil", None, "tile", None, None),
            P("tile", None, None, None),
            P("tile"),
            P(None, "tile", None, None),
        ),
        out_specs=(
            P(None, "tile", "coil", None),
            P(None, "tile", "coil", None),
            P(None, "tile", "coil", None),
        ),
        check_vma=False,
    )
```

```python
import functools
import math

import jax
import jax.numpy as jnp
import ml_dtypes
import numpy as np
from jax import lax
from jax.experimental import pallas as pl
from jax.experimental.pallas import tpu as pltpu
from jax.sharding import PartitionSpec as P

LANES = 128
VMEM = 24 * 1024 * 1024


def halves(values):
    high = values.astype(jnp.bfloat16)
    low = (values - high.astype(jnp.float32)).astype(jnp.bfloat16)
    return high, low


def dot_bf16(left, right, dims):
    return lax.dot_general(left, right, (dims, ((), ())), preferred_element_type=jnp.float32)


def dot_left(table, values, dims=((1,), (0,))):
    high, low = halves(values)
    return (
        dot_bf16(table[0], high, dims)
        + dot_bf16(table[0], low, dims)
        + dot_bf16(table[1], high, dims)
    )


def dot_right(values, table, dims=((1,), (0,))):
    high, low = halves(values)
    return (
        dot_bf16(high, table[0], dims)
        + dot_bf16(low, table[0], dims)
        + dot_bf16(high, table[1], dims)
    )


def fourier_tables(length):
    cells = np.arange(length)
    angle = 2.0 * math.pi / length * (cells[:, None] * cells[None, :] % length)
    cos_t = np.cos(angle) / math.sqrt(length)
    sin_t = np.sin(angle) / math.sqrt(length)
    found = []
    for sign in (1.0, -1.0):
        whole = np.block([[cos_t, -sign * sin_t], [sign * sin_t, cos_t]])
        high = whole.astype(ml_dtypes.bfloat16)
        low = (whole - high.astype(np.float64)).astype(ml_dtypes.bfloat16)
        found += [high, low]
    return jnp.asarray(np.stack(found))


def shift_tables(length, planes, chunk):
    row = np.arange(32)[:, None]
    lane = np.arange(LANES)[None, :]
    row_q, row_ri, row_i = row // 8, row // 4 % 2, row % 4
    lane_ri, lane_q, lane_x = lane // (LANES // 2), lane // planes % chunk, lane % planes
    found = []
    for tile in range(length // planes):
        angle = 2.0 * math.pi / length * (row_i * (lane_x + tile * planes) % length)
        sine = np.where(row_ri == 0, 1.0, -1.0) * np.sin(angle)
        table = np.where(row_ri == lane_ri, np.cos(angle), sine) / math.sqrt(length)
        found.append(np.where(lane_q % 4 == row_q, table, 0.0))
    return jnp.asarray(np.stack(found), jnp.float32)


def band_of_lane(planes, chunk):
    return lax.broadcasted_iota(jnp.int32, (4, LANES), 1) // planes % chunk


def in_window(band, first, chunk):
    past = band - first
    if chunk == 4:
        here = past >= 0
        return here, jnp.logical_not(here)
    here = jnp.logical_and(past >= 0, past < 4)
    return here, past < 4 - chunk


def call(kernel, outs, scratch, operands, flops, name, hbm=(), hbm_outs=(), vmem=(), fixed=(), spaces=()):
    spaces = dict(spaces)
    operands = list(operands)
    for listed, space in ((fixed, pltpu.HBM), (vmem, pltpu.VMEM)):
        for at in listed:
            operands[at] = pltpu.with_memory_space_constraint(operands[at], space)
    here = pl.BlockSpec(memory_space=pltpu.VMEM)
    there = pl.BlockSpec(memory_space=pltpu.HBM)
    moved = sum(math.prod(a.shape) * a.dtype.itemsize for a in operands)
    return pl.pallas_call(
        kernel,
        out_shape=[
            spaces[at](shape, jnp.float32)
            if at in spaces
            else jax.ShapeDtypeStruct(shape, jnp.float32)
            for at, shape in enumerate(outs)
        ],
        in_specs=[there if at in hbm else here for at in range(len(operands))],
        out_specs=[there if at in hbm_outs else here for at in range(len(outs))],
        scratch_shapes=[
            pltpu.VMEM(shape, jnp.float32) if isinstance(shape, tuple) else shape
            for shape in scratch
        ],
        compiler_params=pltpu.CompilerParams(vmem_limit_bytes=VMEM),
        cost_estimate=pl.CostEstimate(flops=flops, bytes_accessed=moved, transcendentals=0),
        name=name,
    )(*operands)


def started(pairs, sems):
    copies = [
        pltpu.make_async_copy(source, to, sems.at[at]) for at, (source, to) in enumerate(pairs)
    ]
    for copy in copies:
        copy.start()
    return copies


def place_on_coil():
    coil = lax.axis_index("coil")
    return coil // 2, coil % 2


def quarters_of(chips, part):
    chip, core = place_on_coil()
    return [
        pl.multiple_of(((chip + hop) % chips * 2 + at) * part, part)
        for at in (core, 1 - core)
        for hop in range(chips)
    ]


def map_rows_kernel(s_ref, *refs, chips):
    outs, (held, sems) = refs[:-2], refs[-2:]
    chip, _ = place_on_coil()
    own = s_ref.shape[2] // chips
    for by in range(1, chips):
        rows = pl.ds(pl.multiple_of((chip + chips - by) % chips * own, own), own)
        for copy in started([(s_ref.at[:, :, rows, :], held)], sems):
            copy.wait()
        for copy in started([(held, outs[by - 1])], sems):
            copy.wait()


def map_rows(smap, chips):
    _, planes, length, _ = smap.shape
    shape = (2, planes, length // chips, length)
    return call(
        functools.partial(map_rows_kernel, chips=chips),
        [shape] * (chips - 1),
        [shape, pltpu.SemaphoreType.DMA((1,))],
        [smap],
        0,
        "map_rows",
        hbm=[0],
        fixed=[0],
        hbm_outs=range(chips - 1),
    )


def message_kernel(owner_ref, list_ref, out_ref):
    _, _, ntile, capacity = list_ref.shape
    out_ref[...] = jnp.zeros_like(out_ref)
    slots = owner_ref.shape[1]
    for to in range(ntile):
        for axis in range(3):
            out_ref[to, :, axis * capacity : (axis + 1) * capacity] = list_ref[axis, 0]
        out_ref[to, 0:1, 3 * capacity : 3 * capacity + slots] = owner_ref[...]


def message(block_owner, owner_list):
    ntile = owner_list.shape[2]
    return pl.pallas_call(
        message_kernel,
        out_shape=jax.ShapeDtypeStruct((ntile, ntile, LANES), jnp.int32),
        in_specs=[pl.BlockSpec(memory_space=pltpu.VMEM)] * 2,
        out_specs=pl.BlockSpec(memory_space=pltpu.VMEM),
        name="message",
    )(block_owner[None], owner_list)


def cut_boxes(info, grid, cos_ref, sin_ref, shift_ref, out_ref, gbuf, planes, chunk, slots):
    handlers = out_ref.shape[0]
    band = band_of_lane(planes, chunk)

    def cut(handler, carry):
        base = pl.multiple_of(handler * LANES, LANES)
        for slot in range(slots):
            block = handler * slots + slot
            here, after = in_window(band, info[1, block], chunk)
            first = grid[pl.ds(info[0, block], 4), :]
            second = grid[pl.ds(info[0, block] + LANES, 4), :]
            if chunk > 4:
                second = jnp.where(after, second, 0.0)
            gbuf[pl.ds(base + slot, 4, stride=slots), :] = jnp.where(here, first, second)
        return carry

    lax.fori_loop(0, handlers, cut, 0)
    high, low = halves(shift_ref[...])
    table = jnp.concatenate(
        [
            jnp.concatenate([high, high], axis=1),
            jnp.concatenate([low, jnp.zeros_like(low)], axis=1),
        ],
        axis=0,
    )
    for handler in range(handlers):
        rows = slice(handler * slots, (handler + 1) * slots)
        cos_b = jnp.concatenate([cos_ref[rows, :]] * 4, axis=0)
        sin_b = jnp.concatenate([sin_ref[rows, :]] * 4, axis=0)
        cells = gbuf[handler * LANES : (handler + 1) * LANES, :]
        turned = cells * cos_b + pltpu.roll(cells, LANES // 2, 1) * sin_b
        both = dot_bf16(table, jnp.concatenate(halves(turned), axis=1), ((1,), (1,)))
        out_ref[handler] = both[:32] + both[32:]


def forward_kernel(*refs, pieces, chunk, slots):
    p_refs = refs[:pieces]
    s_hbm, table_hbm, info_hbm, cos_hbm, sin_hbm, shift_hbm, weights_ref = refs[pieces : pieces + 7]
    out_ref, turned_ref = refs[pieces + 7 : pieces + 9]
    sbuf, tables, info, cos_ref, sin_ref, shift_ref = refs[pieces + 9 : pieces + 15]
    natural, ybuf, grid, gbuf, sems = refs[pieces + 15 :]
    _, planes, part, length = p_refs[0].shape
    rows = length * planes
    starts = quarters_of(pieces // 2, part)
    order = [0, pieces // 2]
    order += [at for at in range(pieces) if at not in order]
    first = [(table_hbm.at[0:2], tables.at[0:2])]
    for at in order:
        first.append((s_hbm.at[:, :, pl.ds(starts[at], part), :], sbuf.at[at]))
    last = [
        (table_hbm.at[2:4], tables.at[2:4]),
        (info_hbm, info),
        (cos_hbm, cos_ref),
        (sin_hbm, sin_ref),
        (shift_hbm.at[lax.axis_index("tile")], shift_ref),
    ]
    copies = started(first + last, sems)
    copies[0].wait()
    batch = min(planes, 256 // part)
    table = (tables[0], tables[1])
    for turn, at in enumerate(order):
        copies[1 + turn].wait()
        for base in range(0, planes, batch):
            bands = []
            for plane in range(base, base + batch):
                s_re = sbuf[at, 0, plane]
                s_im = sbuf[at, 1, plane]
                p_re = p_refs[at][0, plane]
                p_im = p_refs[at][1, plane]
                bands.append(
                    jnp.concatenate([s_re * p_re - s_im * p_im, s_re * p_im + s_im * p_re], axis=1)
                )
            done = dot_right(jnp.concatenate(bands, axis=0), table)
            for ri in range(2):
                half = done[:, ri * length : (ri + 1) * length]
                natural[ri, base : base + batch, pl.ds(starts[at], part), :] = half.reshape(
                    batch, part, length
                )
    for copy in copies[1 + pieces :]:
        copy.wait()
    own = lax.axis_index("tile") * slots
    for block in range(slots):
        w_y = weights_ref[block, 1]
        turned_ref[block] = pltpu.roll(
            jnp.concatenate([w_y, w_y], axis=0), info[1, own + block] % 4, 0
        )
    table = (tables[2], tables[3])
    for pair in range(planes // 2):
        columns = [
            jnp.concatenate([natural[0, plane], natural[1, plane]], axis=0)
            for plane in (2 * pair, 2 * pair + 1)
        ]
        both = dot_left(table, jnp.concatenate(columns, axis=1))
        for inner in range(2):
            for ri in range(2):
                ybuf[pl.ds(ri * rows + 2 * pair + inner, length, stride=planes), :] = both[
                    ri * length : (ri + 1) * length, inner * LANES : (inner + 1) * LANES
                ]
    for band in range(length // chunk):
        re = ybuf[band * 64 : (band + 1) * 64, :]
        im = ybuf[rows + band * 64 : rows + (band + 1) * 64, :]
        grid[band * length : (band + 1) * length, :] = jnp.concatenate([re, im], axis=0).T
    cut_boxes(info, grid, cos_ref, sin_ref, shift_ref, out_ref, gbuf, planes, chunk, slots)


def forward(pieces, smap, tables, info, phases, shift, weights, chunk, slots):
    _, planes, part, length = pieces[0].shape
    count = len(pieces)
    blocks = info.shape[1]
    operands = [*pieces, smap, tables, info, *phases, shift, weights]
    return call(
        functools.partial(forward_kernel, pieces=count, chunk=chunk, slots=slots),
        [(blocks // slots, 32, LANES), (slots, 8, LANES)],
        [
            (count, 2, planes, part, length),
            pltpu.VMEM(tables.shape, tables.dtype),
            pltpu.SMEM(info.shape, info.dtype),
            (blocks, LANES),
            (blocks, LANES),
            shift.shape[1:],
            (2, planes, length, length),
            (2 * length * planes, length),
            (length * (length // chunk + 1), LANES),
            (blocks * 4, LANES),
            pltpu.SemaphoreType.DMA((count + 6,)),
        ],
        operands,
        48 * planes * length**3,
        "forward",
        hbm=range(count, len(operands) - 1),
        fixed=range(count, len(operands) - 1),
    )


def regrid_kernel(parts_ref, matrix_ref, out_ref):
    total = parts_ref[0]
    for at in range(1, parts_ref.shape[0]):
        total = total + parts_ref[at]
    along = lax.broadcasted_iota(jnp.int32, (8, LANES), 0) % 4
    sums = [jnp.zeros((8, LANES), jnp.float32) for _ in range(4)]
    for source in range(4):
        for d_z in range(4):
            value = total[8 * source : 8 * source + 8]
            if d_z:
                value = pltpu.roll(value, LANES - 32 * d_z, 1)
            for d_x in range(4):
                moved = value
                if d_x:
                    moved = jnp.where(
                        along + d_x < 4, pltpu.roll(value, 8 - d_x, 0), pltpu.roll(value, 4 - d_x, 0)
                    )
                for e in range(4):
                    at = 8 * (((e * 4 + source) * 4 + d_z) * 4 + d_x)
                    sums[e] = sums[e] + matrix_ref[at : at + 8] * moved
    done = jnp.concatenate(sums, axis=0)
    for at in range(out_ref.shape[0]):
        out_ref[at] = done


def regrid(parts, matrix, copies):
    return call(
        regrid_kernel,
        [(copies,) + parts.shape[1:]],
        [],
        [parts, matrix],
        10**7,
        "regrid",
        vmem=[1],
        spaces={0: pltpu.VMEM},
    )[0]


def place_boxes(info, chip, u_ref, cos_ref, sin_ref, shift_ref, outs, gbufs, planes, chunk, slots):
    chips = len(outs)
    handlers = u_ref.shape[0] // chips
    high, low = halves(shift_ref[...])
    table = jnp.concatenate([high, high, low, jnp.zeros_like(low)], axis=0)
    for handler in range(handlers):
        rows = slice(handler * slots, (handler + 1) * slots)
        cos_b = jnp.concatenate([cos_ref[rows, :]] * 4, axis=0)
        sin_b = jnp.concatenate([sin_ref[rows, :]] * 4, axis=0)
        for hop in range(chips):
            u_hi, u_lo = (
                half.astype(jnp.float32) for half in halves(u_ref[(chip + hop) % chips * handlers + handler])
            )
            stack = jnp.concatenate([u_hi, u_lo, u_hi, jnp.zeros_like(u_hi)], axis=0)
            cells = dot_bf16(stack.T.astype(jnp.bfloat16), table, ((1,), (0,)))
            turned = cells * cos_b - pltpu.roll(cells, LANES // 2, 1) * sin_b
            gbufs[hop][handler * LANES : (handler + 1) * LANES, :] = turned
    band = band_of_lane(planes, chunk)

    def put(handler, carry):
        base = pl.multiple_of(handler * LANES, LANES)
        for slot in range(slots):
            block = handler * slots + slot
            here, after = in_window(band, info[1, block], chunk)
            first = pl.ds(info[0, block], 4)
            second = pl.ds(info[0, block] + LANES, 4)
            for hop in range(chips):
                cells = gbufs[hop][pl.ds(base + slot, 4, stride=slots), :]
                old_first = outs[hop][first, :]
                old_second = outs[hop][second, :]
                outs[hop][first, :] = old_first + jnp.where(here, cells, 0.0)
                outs[hop][second, :] = old_second + jnp.where(after, cells, 0.0)
        return carry

    lax.fori_loop(0, handlers, put, 0)


def inverse_kernel(*refs, part, length, chunk, slots, chips):
    u_ref, info_hbm, cos_hbm, sin_hbm, shift_hbm, table_hbm, s_hbm = refs[:7]
    far_maps = refs[7 : 6 + chips]
    outs = refs[6 + chips : 8 + chips]
    refs = refs[8 + chips :]
    grids, gbufs, refs = refs[:chips], refs[chips : 2 * chips], refs[2 * chips :]
    info, cos_ref, sin_ref, shift_ref, table_ref, ybuf, images, maps, sems = refs
    planes = s_hbm.shape[1]
    rows = length * planes
    own = length // chips
    chip, core = place_on_coil()
    own_rows = pl.multiple_of(chip * own, own)
    pairs = [
        (info_hbm, info),
        (cos_hbm, cos_ref),
        (sin_hbm, sin_ref),
        (shift_hbm.at[lax.axis_index("tile")], shift_ref),
        (table_hbm, table_ref),
        (s_hbm.at[:, :, pl.ds(own_rows, own), :], maps.at[0]),
    ]
    pairs += [(far_map, maps.at[at]) for at, far_map in enumerate(far_maps, 1)]
    copies = started(pairs, sems)
    for grid in grids:
        grid[...] = jnp.zeros_like(grid)
    for copy in copies[:4]:
        copy.wait()
    place_boxes(info, chip, u_ref, cos_ref, sin_ref, shift_ref, grids, gbufs, planes, chunk, slots)
    for copy in copies[4:]:
        copy.wait()
    table = []
    for half in range(2):
        bands = [
            table_ref[half, pl.ds(pl.multiple_of(ri * length + own_rows, own), own), :]
            for ri in range(2)
        ]
        table.append(jnp.concatenate(bands, axis=0))
    for hop in range(chips):
        for band in range(length // chunk):
            tile = grids[hop][band * length : (band + 1) * length, :].T
            ybuf[hop, band * 64 : (band + 1) * 64, :] = tile[:64]
            ybuf[hop, rows + band * 64 : rows + (band + 1) * 64, :] = tile[64:]
        for pair in range(planes // 2):
            columns = [
                jnp.concatenate(
                    [
                        ybuf[hop, pl.ds(ri * rows + plane, length, stride=planes), :]
                        for ri in range(2)
                    ],
                    axis=0,
                )
                for plane in (2 * pair, 2 * pair + 1)
            ]
            done = dot_left(table, jnp.concatenate(columns, axis=1))
            for inner in range(2):
                for ri in range(2):
                    images[hop, ri, 2 * pair + inner] = done[
                        ri * own : (ri + 1) * own, inner * LANES : (inner + 1) * LANES
                    ]
    table = (table_ref[2], table_ref[3])
    batch = min(planes, 256 // part)
    for at, half in enumerate((1 - core, core)):
        local = pl.ds(pl.multiple_of(half * part, part), part)
        for base in range(0, planes, batch):
            total_re, total_im = 0.0, 0.0
            for hop in range(chips):
                bands = [
                    jnp.concatenate([images[hop, ri, plane, local, :] for ri in range(2)], axis=1)
                    for plane in range(base, base + batch)
                ]
                done = dot_right(jnp.concatenate(bands, axis=0), table)
                i_re = done[:, :length].reshape(batch, part, length)
                i_im = done[:, length:].reshape(batch, part, length)
                s_re = maps[hop, 0, base : base + batch, local, :]
                s_im = maps[hop, 1, base : base + batch, local, :]
                total_re = total_re + (s_re * i_re + s_im * i_im)
                total_im = total_im + (s_re * i_im - s_im * i_re)
            outs[at][0, base : base + batch] = total_re
            outs[at][1, base : base + batch] = total_im


def inverse(spread, info, phases, shift, tables, smap, far_maps, part, chunk, slots):
    _, planes, length, _ = smap.shape
    chips = len(far_maps) + 1
    blocks = info.shape[1]
    rows = length * (length // chunk + 1)
    own = (chips, 2, planes, 2 * part, length)
    operands = [spread, info, *phases, shift, tables, smap, *far_maps]
    return call(
        functools.partial(
            inverse_kernel, part=part, length=length, chunk=chunk, slots=slots, chips=chips
        ),
        [(2, planes, part, length)] * 2,
        [(rows, LANES)] * chips
        + [(blocks * 4, LANES)] * chips
        + [
            pltpu.SMEM(info.shape, info.dtype),
            (blocks, LANES),
            (blocks, LANES),
            shift.shape[1:],
            pltpu.VMEM(tables.shape, tables.dtype),
            (chips, 2 * length * planes, length),
            own,
            own,
            pltpu.SemaphoreType.DMA((5 + chips,)),
        ],
        operands,
        48 * planes * length**3,
        "inverse",
        hbm=range(1, len(operands)),
        fixed=range(1, 7),
    )


def sums_kernel(*refs, terms):
    term_refs = refs[:terms]
    p_ref, r_ref, normal_ref, out_ref = refs[terms:]
    shape = p_ref.shape

    def add(plane, held):
        held = list(held)
        for ri in range(2):
            normal = term_refs[0][ri, plane]
            for term in term_refs[1:]:
                normal = normal + term[ri, plane]
            normal_ref[ri, plane] = normal
            p = p_ref[ri, plane]
            r = r_ref[ri, plane]
            for at, product in enumerate((r * r, p * normal, r * normal, normal * normal)):
                held[at] = held[at] + jnp.sum(product.reshape(-1, 8, LANES), axis=0)
        return tuple(held)

    start = tuple(jnp.zeros((8, LANES), jnp.float32) for _ in range(4))
    held = lax.fori_loop(0, shape[1], add, start, unroll=4)
    lane = lax.broadcasted_iota(jnp.int32, out_ref.shape, 1)
    found = jnp.zeros(out_ref.shape, jnp.float32)
    for at in range(4):
        found = jnp.where(lane == at, jnp.sum(held[at]), found)
    out_ref[...] = found


def sums(terms, p, r, devices):
    kernel = functools.partial(sums_kernel, terms=len(terms))
    return call(kernel, [p.shape, (devices, LANES)], [], [*terms, p, r], 10**7, "sums")


def finish_kernel(total_ref, x_ref, r_ref, p_ref, normal_ref, x_out, r_out, p_out):
    total = jnp.sum(total_ref[...], axis=0, keepdims=True)
    r_r, p_n, r_n, n_n = (total[:, at : at + 1] for at in range(4))
    alpha = r_r / p_n
    beta = (r_r + alpha * (alpha * n_n - 2.0 * r_n)) / r_r
    for plane in range(x_ref.shape[1]):
        for ri in range(2):
            p = p_ref[ri, plane]
            next_r = r_ref[ri, plane] - alpha * normal_ref[ri, plane]
            x_out[ri, plane] = x_ref[ri, plane] + alpha * p
            r_out[ri, plane] = next_r
            p_out[ri, plane] = next_r + beta * p


def finish(total, x, r, p, normal):
    return call(finish_kernel, [x.shape] * 3, [], [total, x, r, p, normal], 10**7, "finish")


def matrices_kernel(weights_ref, turned_ref, out_ref, held, *, slots):
    def one(block, carry):
        w_x = weights_ref[block, 0]
        w_z = weights_ref[block, 2]
        twice = jnp.concatenate([w_x, w_x], axis=0)
        rolled = [twice] + [pltpu.roll(twice, 8 - d, 0) for d in range(1, 4)]
        low = lax.broadcasted_iota(jnp.int32, (8, LANES), 0) < 4
        along_x = [twice * jnp.where(low, rolled[d], rolled[d + 1]) for d in (0, 2)]
        right = []
        for f in range(4):
            for d_z in range(4):
                other = (f + d_z) % 4
                along_z = w_z[f : f + 1] * w_z[other : other + 1]
                right += [along * along_z for along in along_x]
        turned = turned_ref[block, 0:4]
        left = halves(jnp.concatenate([turned * turned[e : e + 1] for e in range(4)], axis=0))
        high, low = halves(jnp.concatenate(right, axis=0))
        both = dot_bf16(jnp.concatenate(left, axis=0), high, ((1,), (1,)))
        done = both[:16] + both[16:] + dot_bf16(left[0], low, ((1,), (1,)))
        for f in range(4):
            lanes = done[:, f // 2 * LANES : (f // 2 + 1) * LANES]
            if f % 2:
                lanes = pltpu.roll(lanes, LANES // 2, 1)
            held[pl.ds(f * slots + block, 16, stride=LANES), :] = lanes
        return carry

    lax.fori_loop(0, slots, one, 0, unroll=4)

    def turn(pair, carry):
        at = pl.ds(pl.multiple_of(pair * LANES, LANES), LANES)
        rows = held[at, :64].T
        for group in range(16):
            four = rows[4 * group : 4 * group + 4]
            out_ref[pl.ds(pl.multiple_of(pair * LANES + 8 * group, 8), 8), :] = jnp.concatenate(
                [four, four], axis=0
            )
        return carry

    lax.fori_loop(0, 16, turn, 0, unroll=2)


def block_matrices(weights, turned):
    return call(
        functools.partial(matrices_kernel, slots=weights.shape[0]),
        [(16 * LANES, LANES)],
        [(16 * LANES, LANES)],
        [weights, turned],
        10**9,
        "matrices",
    )[0]


def block_offsets(gathered, slots, ntile, capacity):
    owners = gathered[:, 0, 3 * capacity : 3 * capacity + slots]
    lists = gathered[:, :, : 3 * capacity].reshape(ntile, ntile, 3, capacity)
    earlier = jnp.tril(jnp.ones((slots, slots), jnp.int32), -1)
    same = (owners[:, :, None] == owners[:, None, :]).astype(jnp.int32)
    ranks = jnp.sum(same * earlier[None], axis=2)
    wanted = owners * capacity + ranks
    lists = jnp.transpose(lists, (2, 1, 0, 3)).reshape(3, ntile, 1, ntile * capacity)
    hit = wanted[:, :, None] == jnp.arange(ntile * capacity, dtype=jnp.int32)
    found = jnp.sum(jnp.where(hit[None], lists, 0), axis=3)
    return found[0], found[1] + owners * (LANES // ntile), found[2]


def shards(image_p, image_x, image_r, sensitivity, kb_weights, block_owner, owner_list):
    ntile = lax.axis_size("tile")
    ncoil = lax.axis_size("coil")
    chips = ncoil // 2
    slots = kb_weights.shape[0]
    capacity = owner_list.shape[3]
    planes, length = image_p.shape[1], image_p.shape[3]
    part = image_p.shape[2]
    chunk = LANES // (2 * planes)
    tile = lax.axis_index("tile")
    smap = sensitivity[0]
    tables = fourier_tables(length)

    def from_chip(values, by):
        pairs = [
            (a * 2 + k, (a - by) % chips * 2 + k) for a in range(chips) for k in range(2)
        ]
        return lax.ppermute(values, "coil", pairs)

    def other_core(values):
        pairs = [(a * 2 + k, a * 2 + 1 - k) for a in range(chips) for k in range(2)]
        return lax.ppermute(values, "coil", pairs)

    p_same = [image_p] + [from_chip(image_p, by) for by in range(1, chips)]
    sent, p_later = lax.optimization_barrier((message(block_owner, owner_list), image_p))
    p_other = [other_core(p_later)]
    gathered = lax.all_to_all(sent, "tile", 0, 0, tiled=True)
    far_rows = map_rows(smap, chips)
    off_x, off_y, off_z = block_offsets(gathered, slots, ntile, capacity)
    info = jnp.stack(
        [(off_y // chunk * length + off_z).reshape(-1), (off_y % chunk).reshape(-1)]
    )
    lane = jnp.arange(LANES, dtype=jnp.int32)
    lane_ri = lane // (LANES // 2)
    lane_x = lane % planes + tile * planes
    unit = 2.0 * math.pi / length
    angle = unit * (off_x.reshape(-1, 1) * lane_x[None] % length).astype(jnp.float32)
    phases = (jnp.cos(angle), jnp.sin(angle) * jnp.where(lane_ri == 0, 1.0, -1.0)[None])
    shift = shift_tables(length, planes, chunk)
    p_far, far_rows, info, phases = lax.optimization_barrier(
        (p_same[1:], far_rows, info, phases)
    )
    p_other += [other_core(piece) for piece in p_far]
    far_maps = [from_chip(rows, by) for by, rows in enumerate(far_rows, 1)]
    partial, turned = forward(
        [image_p, *p_far, *p_other], smap, tables, info, phases, shift, kb_weights, chunk, slots
    )
    partial, turned = lax.optimization_barrier((partial, turned))
    parts = lax.all_to_all(partial, "tile", 0, 0, tiled=True)
    done = regrid(parts, block_matrices(kb_weights, turned), chips * ntile)
    groups = [
        [at * ntile + t for at in range(ncoil) if at % 2 == k for t in range(ntile)]
        for k in range(2)
    ]
    spread = lax.all_to_all(
        done, ("coil", "tile"), 0, 0, axis_index_groups=groups, tiled=True
    )
    sent, kept = inverse(
        spread, info, phases, shift, tables, smap, far_maps, part, chunk, slots
    )
    normal, found = sums([kept, other_core(sent)], image_p, image_r, ncoil * ntile)
    total = lax.all_to_all(found, ("coil", "tile"), 0, 0, tiled=True)
    return tuple(finish(total, image_x, image_r, image_p, normal))


def solution(mesh):
    return jax.shard_map(
        shards,
        mesh=mesh,
        in_specs=(
            P(None, "tile", "coil", None),
            P(None, "tile", "coil", None),
            P(None, "tile", "coil", None),
            P("coil", None, "tile", None, None),
            P("tile", None, None, None),
            P("tile"),
            P(None, "tile", None, None),
        ),
        out_specs=(
            P(None, "tile", "coil", None),
            P(None, "tile", "coil", None),
            P(None, "tile", "coil", None),
        ),
        check_vma=False,
    )
```
